32 devices in a mesh: scen: 2 (over x), row: 16 (over z, y, core).
Axes of the slice: x: 2, y: 2, z: 4, core: 2. Of those that a mesh axis runs over, the one named last changes fastest.
Arguments:
- basin_state: float32 [6, 256, 2048], P('scen', 'row'), parts along dimension 0, may hold values from -1.5 to 1.5
- basin_depth: float32 [256, 4096], P('row', 'scen'), parts along dimension 1, may hold values from 0.7 to 1.5
- coast_depth: float32 [16, 512, 256], P('row', 'scen'), parts along dimension 1, may hold values from 0.1 to 2
- coast_flow: float32 [16, 4, 256, 256], P('row', 'scen'), parts along dimension 1, may hold values from -0.4 to 0.4
- coast_link: int32 [16, 6], P('row', 'scen'), parts along dimension 1, may hold values from 0 to 2031, as said below
Outputs:
- basin_out: float32 [6, 256, 2048], P('scen', 'row'), parts along dimension 0
- coast_out: float32 [16, 6, 256, 256], P('row', 'scen'), parts along dimension 1
The draws below stay inside these ranges and needn't reach their ends.
There are 2 independent parts, one for each index of `scen`. The reference program is written for one: setup_inputs(seed, part) draws one part's arguments, and reference() takes and returns one part's arrays. A program takes and returns all parts, laid end to end along the dimension named above; each array names one. Nothing has to cross between parts.
Inputs may be any that keep to these rules, and one draw needn't show every extreme that they name: `coast_link`: column 0 is a basin row below 256, column 1 a column at most 2031, column 2 is 0 or 1; block 0 links to the last row and last start column, block 1 to row 0 and column 0.
All inputs are finite; a program needn't handle non-finite values.
Results may differ from the reference program's by a relative error of at most 0.0003.
Values sent between devices are 32-bit elements; how exact they have to be, the bound alone decides.
No kernel may reach another device: no remote copies, remote signals or barrier semaphores. Data moves between devices by JAX's collectives and lax.ppermute only.
A program may use at most 64 MiB of HBM per device.

```python
import jax
import jax.numpy as jnp
from jax import lax

BCOLS = 2048
BS = 256
BSTEPS = 8
CSTEPS = 10
STRIP = 17
NROWS = 256
NBLK = 16


def draw_coast_link(key, part):
    key = jax.random.fold_in(key, 11)
    key_row, key_col, key_wet = jax.random.split(key, 3)
    rows = jax.random.randint(key_row, (NBLK,), 0, NROWS)
    cols = jax.random.randint(key_col, (NBLK,), 0, BCOLS - STRIP + 1)
    wet = (jax.random.randint(key_wet, (NBLK,), 0, 4) > 0).astype(jnp.int32)
    rows = rows.at[0].set(NROWS - 1).at[1].set(0)
    cols = cols.at[0].set(BCOLS - STRIP).at[1].set(0)
    return jnp.stack([rows, cols, wet], axis=1).astype(jnp.int32)


def level_of(key, shape, shards, least, top_value):
    factor_of = 1.0
    for position, parts in shards:
        steps = jax.random.uniform(jax.random.fold_in(jax.random.fold_in(key, 6), position), (parts,), jnp.float32, least / len(shards), top_value / len(shards))
        factor_of = factor_of * jnp.repeat(jnp.exp(steps), shape[position] // parts).reshape((-1,) + (1,) * (len(shape) - 1 - position))
    return factor_of


def scatter_about(stream_key, dims, deviation, reach, shards=(), kind=jnp.bfloat16):
    loudness = level_of(stream_key, dims, shards, -0.22, 0.18) if shards else 1.0
    array = jax.random.normal(stream_key, dims, jnp.float32) * deviation * loudness
    return jnp.minimum(jnp.maximum(array, -reach), reach).astype(kind)


def setup_inputs(seed: int = 0, part: int = 0) -> dict:
    key_of = jax.random.split(jax.random.key(seed), 6)
    own_keys = jax.random.split(jax.random.fold_in(key_of[5], part), 6)
    return {
        "basin_state": scatter_about(own_keys[0], (3, NROWS, BCOLS), 0.5, 1.5, ((1, 16),), jnp.float32),
        "basin_depth": jnp.clip(0.7 + 0.8 * jax.random.uniform(own_keys[1], (NROWS, BCOLS), jnp.float32) ** level_of(own_keys[1], (NROWS, BCOLS), ((0, 16),), -0.2, 0.2), 0.7, 1.5),
        "coast_depth": jnp.clip(0.1 + 1.9 * jax.random.uniform(own_keys[2], (NBLK, BS, BS), jnp.float32) ** level_of(own_keys[2], (NBLK, BS, BS), ((0, 16),), -0.2, 0.2), 0.1, 2.0),
        "coast_flow": scatter_about(own_keys[3], (NBLK, 2, BS, BS), 0.1, 0.4, ((0, 16),), jnp.float32),
        "coast_link": draw_coast_link(jax.random.fold_in(jax.random.fold_in(key_of[5], part), 71), part),
    }


basin_courant = 0.5
coast_courant = 0.1
depth_floor = 0.2
ghost_level = 2.0

def basin_step(state, depth, inside):
    eta, east, north = (state[0], state[1], state[2])
    zcol = jnp.zeros((eta.shape[0], 1), jnp.float32)
    zrow = jnp.zeros((1, eta.shape[1]), jnp.float32)
    east_west = jnp.concatenate([zcol, east[:, :-1]], axis=1)
    north_south = jnp.concatenate([zrow, north[:-1]], axis=0)
    eta_new = (eta - basin_courant * (east - east_west + (north - north_south))) * inside
    eta_east = jnp.concatenate([eta_new[:, 1:], zcol], axis=1)
    eta_north = jnp.concatenate([eta_new[1:], zrow], axis=0)
    east_new = (east - basin_courant * depth * (eta_east - eta_new)) * inside
    north_new = (north - basin_courant * depth * (eta_north - eta_new)) * inside
    return jnp.stack([eta_new, east_new, north_new])

def interp_table(strip_len, cells):
    rows = jnp.arange(strip_len, dtype=jnp.int32)[:, None]
    cols = jnp.arange(cells, dtype=jnp.int32)[None, :]
    base = cols // 16
    weight = ((cols % 16).astype(jnp.float32) + 0.5) / 16.0
    return jnp.where(rows == base, 1.0 - weight, 0.0) + jnp.where(rows == base + 1, weight, 0.0)

def make_ghost(strip, cells):
    table = interp_table(strip.shape[1], cells)
    values = jnp.dot(strip, table, precision=lax.Precision.HIGHEST, preferred_element_type=jnp.float32)
    return jnp.stack([ghost_level + values[0], jnp.zeros((cells,), jnp.float32), values[1]])

def phys_flux(state, normal):
    depth = state[0]
    along = state[normal]
    across = state[3 - normal]
    speed_u = along / jnp.maximum(depth, depth_floor)
    press = along * speed_u + 0.5 * depth * depth
    cross = across * speed_u
    if normal == 1:
        flux = jnp.stack([along, press, cross])
    else:
        flux = jnp.stack([along, cross, press])
    return (flux, jnp.abs(speed_u) + jnp.sqrt(jnp.maximum(depth, 0.0)))

def rusanov(left, right, normal):
    flux_l, speed_l = phys_flux(left, normal)
    flux_r, speed_r = phys_flux(right, normal)
    speed = jnp.maximum(speed_l, speed_r)
    return 0.5 * (flux_l + flux_r) - 0.5 * speed * (right - left)

def coast_step(block, ghost):
    rows = jnp.concatenate([ghost[:, None, :], block, block[:, -1:, :]], axis=1)
    padded = jnp.concatenate([rows[:, :, :1], rows, rows[:, :, -1:]], axis=2)
    flux_x = rusanov(padded[:, 1:-1, :-1], padded[:, 1:-1, 1:], 1)
    flux_y = rusanov(padded[:, :-1, 1:-1], padded[:, 1:, 1:-1], 2)
    return block - coast_courant * (flux_x[:, :, 1:] - flux_x[:, :, :-1] + (flux_y[:, 1:, :] - flux_y[:, :-1, :]))

def coast_run(block, ghost, steps):
    return lax.fori_loop(0, steps, lambda step, value: coast_step(value, ghost), block)

def reference(basin_state, basin_depth, coast_depth, coast_flow, coast_link):
    inside = jnp.ones((basin_state.shape[1], 1), jnp.float32)
    state = basin_state
    for step in range(BSTEPS):
        state = basin_step(state, basin_depth, inside)
    surface_pair = jnp.stack([basin_state[0], basin_state[2]])
    blocks = jnp.concatenate([coast_depth[:, None], coast_flow], axis=1)

    def one_block(items):
        block, link = items
        strip = lax.dynamic_slice(surface_pair, (jnp.int32(0), link[0].astype(jnp.int32), link[1].astype(jnp.int32)), (2, 1, STRIP))[:, 0, :]
        ghost = make_ghost(strip, BS)
        return jnp.where(link[2] > 0, coast_run(block, ghost, CSTEPS), block)
    coast_out = lax.map(one_block, (blocks, coast_link))
    return (state, coast_out)
```

```python
import functools

import jax
import jax.numpy as jnp
from jax import lax
from jax.experimental import pallas as pl
from jax.experimental.pallas import tpu as pltpu
from jax.sharding import PartitionSpec as P

BSTEPS = 8
CSTEPS = 10

depth_floor = 0.2
ghost_level = 2.0

RATE = 0.05
DEPTH_UNIT = RATE * RATE
FLOW_UNIT = RATE * RATE * RATE
TINY = 1e-30

HALO = BSTEPS
SUB = 8
LANES = 128


def lane_ids():
    return lax.broadcasted_iota(jnp.int32, (SUB, LANES), 1)


def row_ids():
    return lax.broadcasted_iota(jnp.int32, (SUB, LANES), 0)


def split_columns(cells):
    rows = lax.broadcasted_iota(jnp.int32, (cells, cells), 0)
    cols = lax.broadcasted_iota(jnp.int32, (cells, cells), 1)
    half = cells // 2
    source = jnp.where(cols < half, 2 * cols, 2 * (cols - half) + 1)
    return (rows == source).astype(jnp.bfloat16)


def permute(values, table, transposed=False):
    dims = (((1,), (1 if transposed else 0,)), ((), ()))
    total = None
    rest = values
    for _ in range(3):
        part = rest.astype(jnp.bfloat16)
        rest = rest - part.astype(jnp.float32)
        term = lax.dot_general(part, table, dims, preferred_element_type=jnp.float32)
        total = term if total is None else total + term
    return total


def inverse(x):
    guess = pl.reciprocal(x, approx=True)
    return guess * (2.0 - x * guess)


def cell_terms(u):
    h, mu, mv = u
    r = inverse(jnp.maximum(h, depth_floor * DEPTH_UNIT))
    vx, vy = mu * r, mv * r
    hp = jnp.maximum(h, TINY)
    c = hp * lax.rsqrt(hp)
    p = (0.5 * h) * h
    cross = mu * vy
    return {
        "u": u,
        "fx": (mu, mu * vx + p, cross),
        "fy": (mv, cross, mv * vy + p),
        "sx": jnp.abs(vx) + c,
        "sy": jnp.abs(vy) + c,
    }


def x_part(even, odd, first, last):
    left = functools.partial(pltpu.roll, shift=LANES - 1, axis=1)
    right = functools.partial(pltpu.roll, shift=1, axis=1)
    next_u = [left(a) for a in even["u"]]
    next_f = [next_u[1], left(even["fx"][1]), left(even["fx"][2])]
    a_in = jnp.maximum(even["sx"], odd["sx"])
    a_out = jnp.where(last, 0.0, jnp.maximum(odd["sx"], left(even["sx"])))
    d_in = [a_in * (o - e) for e, o in zip(even["u"], odd["u"])]
    d_out = [a_out * (n - o) for o, n in zip(odd["u"], next_u)]
    new_even, new_odd = [], []
    for i in range(3):
        f_e, f_o = even["fx"][i], odd["fx"][i]
        f_next = jnp.where(last, f_o, next_f[i])
        f_back = jnp.where(first, f_e, right(f_o))
        new_even.append(even["u"][i] + ((d_in[i] - right(d_out[i])) - (f_o - f_back)))
        new_odd.append(odd["u"][i] + ((d_out[i] - d_in[i]) - (f_next - f_e)))
    return new_even, new_odd


def y_face(above, below):
    a = jnp.maximum(above["sy"], below["sy"])
    return [
        a * (ub - ua) - (fa + fb)
        for ua, ub, fa, fb in zip(above["u"], below["u"], above["fy"], below["fy"])
    ]


def coast_steps(state, rows, steps, ghost):
    lane, sub = lane_ids(), row_ids()
    first, last = lane == 0, lane == LANES - 1
    top, bottom = sub == 0, sub == SUB - 1

    def load(k):
        return [cell_terms([state[f, half, k] for f in range(3)]) for half in range(2)]

    def store(k, both):
        for half in range(2):
            for f in range(3):
                state[f, half, k] = both[half][f]

    def wrapped(tail, head):
        down = functools.partial(pltpu.roll, shift=1, axis=0)
        out = {"sy": jnp.where(top, head["sy"], down(tail["sy"]))}
        for name in ("u", "fy"):
            out[name] = [jnp.where(top, h, down(t)) for h, t in zip(head[name], tail[name])]
        return out

    def step(_, carry):
        tails = load(rows - 1)
        prev, acc, start = None, None, None
        for k in range(rows):
            cur = load(k)
            if k == 0:
                heads = cur if ghost is None else ghost
                above = [wrapped(t, h) for t, h in zip(tails, heads)]
                start = face = [y_face(a, b) for a, b in zip(above, cur)]
            else:
                face = [y_face(a, b) for a, b in zip(prev, cur)]
                store(k - 1, [[x + g for x, g in zip(xs, gs)] for xs, gs in zip(acc, face)])
            acc = x_part(cur[0], cur[1], first, last)
            acc = [[x - g for x, g in zip(xs, gs)] for xs, gs in zip(acc, face)]
            prev = cur
        end = [
            [
                jnp.where(bottom, -(f + f), pltpu.roll(g, SUB - 1, 0))
                for f, g in zip(cell["fy"], gs)
            ]
            for cell, gs in zip(prev, start)
        ]
        store(rows - 1, [[x + g for x, g in zip(xs, gs)] for xs, gs in zip(acc, end)])
        return carry

    lax.fori_loop(0, steps, step, 0)


def fold_in(source, tmp, state, table, unit, rows):
    split = permute(source[...], table) * unit
    for half in range(2):
        tmp[half] = split[:, half * LANES : (half + 1) * LANES]
        for k in range(rows):
            state[half, k] = tmp[half, pl.ds(k, SUB, stride=rows), :]


def unfold(state, tmp, table, unit, rows):
    for half in range(2):
        for k in range(rows):
            tmp[half, pl.ds(k, SUB, stride=rows), :] = state[half, k]
    flat = jnp.concatenate([tmp[0], tmp[1]], axis=1)
    return permute(flat * (1.0 / unit), table, transposed=True)


def coast_kernel(link, depth, flow, out, state, tmp):
    rows = depth.shape[0] // SUB
    cells = depth.shape[1]
    units = (DEPTH_UNIT, FLOW_UNIT, FLOW_UNIT)

    @pl.when(link[0, 2] > 0)
    def _():
        table = split_columns(cells)
        for f in range(3):
            source = depth if f == 0 else flow.at[f - 1]
            fold_in(source, tmp, state.at[f], table, units[f], rows)
        coast_steps(state, rows, CSTEPS, None)
        for f in range(3):
            out[f] = unfold(state.at[f], tmp, table, units[f], rows)

    @pl.when(link[0, 2] <= 0)
    def _():
        out[0] = depth[...]
        out[1] = flow[0]
        out[2] = flow[1]


def coast_bulk(link, depth, flow):
    cells = depth.shape[0]
    return pl.pallas_call(
        coast_kernel,
        out_shape=jax.ShapeDtypeStruct((3, cells, cells), jnp.float32),
        in_specs=[
            pl.BlockSpec(memory_space=pltpu.SMEM),
            pl.BlockSpec(memory_space=pltpu.VMEM),
            pl.BlockSpec(memory_space=pltpu.VMEM),
        ],
        out_specs=pl.BlockSpec(memory_space=pltpu.VMEM),
        scratch_shapes=[
            pltpu.VMEM((3, 2, cells // SUB, SUB, LANES), jnp.float32),
            pltpu.VMEM((2, cells, LANES), jnp.float32),
        ],
        compiler_params=pltpu.CompilerParams(vmem_limit_bytes=32 * 1024 * 1024),
        cost_estimate=pl.CostEstimate(
            flops=CSTEPS * 70 * cells * cells, bytes_accessed=24 * cells * cells, transcendentals=0
        ),
        name="coast_bulk",
    )(link, depth, flow)


EDGE = 3
EDGE_ROWS = EDGE * SUB
EDGE_OUT = 16


def edge_kernel(strip_rows, link, strips, depth, flow, before, out, state, tmp):
    cells = depth.shape[1]
    units = (DEPTH_UNIT, FLOW_UNIT, FLOW_UNIT)
    out[...] = before[...]

    @pl.when(link[0, 2] > 0)
    def _():
        table = split_columns(cells)
        for f in range(3):
            source = depth if f == 0 else flow.at[f - 1]
            fold_in(source, tmp, state.at[f], table, units[f], EDGE)
        strip = strips[link[0, 0] // strip_rows]
        rows = lax.broadcasted_iota(jnp.int32, (LANES, cells), 0)
        cols = lax.broadcasted_iota(jnp.int32, (LANES, cells), 1)
        half = cells // 2
        cols = jnp.where(cols < half, 2 * cols, 2 * (cols - half) + 1)
        base = cols // 16
        weight = ((cols % 16).astype(jnp.float32) + 0.5) / 16.0
        mix = jnp.where(rows == base, 1.0 - weight, 0.0) + jnp.where(rows == base + 1, weight, 0.0)
        values = jnp.dot(
            strip, mix, precision=lax.Precision.HIGHEST, preferred_element_type=jnp.float32
        )
        level = (ghost_level + values[0:1]) * DEPTH_UNIT
        inflow = values[1:2] * FLOW_UNIT
        ghost = []
        for at in (0, half):
            h = jnp.broadcast_to(level[:, at : at + half], (SUB, half))
            mv = jnp.broadcast_to(inflow[:, at : at + half], (SUB, half))
            ghost.append(cell_terms([h, jnp.zeros_like(h), mv]))
        coast_steps(state, EDGE, CSTEPS, ghost)
        keep = lax.broadcasted_iota(jnp.int32, (EDGE_OUT, cells), 0) < CSTEPS
        for f in range(3):
            done = unfold(state.at[f], tmp, table, units[f], EDGE)
            out[f] = jnp.where(keep, done[:EDGE_OUT], before[f])


def coast_edge(strip_rows, link, strips, depth, flow, before):
    cells = depth.shape[0]
    return pl.pallas_call(
        functools.partial(edge_kernel, strip_rows),
        out_shape=jax.ShapeDtypeStruct(before.shape, jnp.float32),
        grid=(1,),
        in_specs=[
            pl.BlockSpec(memory_space=pltpu.SMEM),
            pl.BlockSpec(strips.shape, lambda i: (0, 0, 0)),
            pl.BlockSpec((EDGE_ROWS, cells), lambda i: (0, 0)),
            pl.BlockSpec((2, EDGE_ROWS, cells), lambda i: (0, 0, 0)),
            pl.BlockSpec((3, EDGE_OUT, cells), lambda i: (0, 0, 0)),
        ],
        out_specs=pl.BlockSpec((3, EDGE_OUT, cells), lambda i: (0, 0, 0)),
        scratch_shapes=[
            pltpu.VMEM((3, 2, EDGE, SUB, LANES), jnp.float32),
            pltpu.VMEM((2, EDGE_ROWS, LANES), jnp.float32),
        ],
        input_output_aliases={4: 0},
        cost_estimate=pl.CostEstimate(
            flops=CSTEPS * 70 * EDGE_ROWS * cells, bytes_accessed=4 * 100 * cells, transcendentals=0
        ),
        name="coast_edge",
    )(link, strips, depth, flow, before)


def basin_kernel(inside, state, depth, south, north, out, eta, hu, hv, dep):
    rows = state.shape[1]
    width = state.shape[2]
    total = rows + 2 * HALO
    chunks = width // LANES
    for ref, field, unit in ((eta, 0, 1.0), (hu, 1, 0.5), (hv, 2, 0.5), (dep, 3, 0.25)):
        ref[:HALO] = south[field] * unit
        ref[HALO : HALO + rows] = (depth[...] if field == 3 else state[field]) * unit
        ref[HALO + rows :] = north[field] * unit
    lane = lax.broadcasted_iota(jnp.int32, (total, LANES), 1)
    first, last = lane == 0, lane == LANES - 1
    row = lax.broadcasted_iota(jnp.int32, (total, LANES), 0)
    kept = jnp.where(row < HALO + rows, 1.0, inside[0].astype(jnp.float32))

    def step(_, carry):
        prev_west = jnp.zeros((total, LANES), jnp.float32)
        prev_eta, prev_east, prev_hu = None, None, None
        for c in range(chunks + 1):
            if c < chunks:
                at = slice(c * LANES, (c + 1) * LANES)
                u, v = hu[:, at], hv[:, at]
                west = pltpu.roll(u, 1, 1)
                du = u - jnp.where(first, prev_west, west)
                dv = v - pltpu.roll(v, 1, 0)
                new = (eta[:, at] - (du + dv)) * kept
                eta[:, at] = new
                east = pltpu.roll(new, LANES - 1, 1)
                hv[:, at] = v - dep[:, at] * (pltpu.roll(new, total - 1, 0) - new)
            else:
                east = jnp.zeros((total, LANES), jnp.float32)
            if c > 0:
                back = slice((c - 1) * LANES, c * LANES)
                hu[:, back] = prev_hu - dep[:, back] * (jnp.where(last, east, prev_east) - prev_eta)
            prev_west, prev_eta, prev_east, prev_hu = west, new, east, u
        return carry

    lax.fori_loop(0, BSTEPS, step, 0)
    own = slice(HALO, HALO + rows)
    out[0] = eta[own]
    out[1] = hu[own] * 2.0
    out[2] = hv[own] * 2.0


def basin_run(inside, state, depth, south, north):
    rows, width = depth.shape
    total = rows + 2 * HALO
    vmem = pl.BlockSpec(memory_space=pltpu.VMEM)
    return pl.pallas_call(
        basin_kernel,
        out_shape=jax.ShapeDtypeStruct(state.shape, jnp.float32),
        in_specs=[pl.BlockSpec(memory_space=pltpu.SMEM), vmem, vmem, vmem, vmem],
        out_specs=vmem,
        scratch_shapes=[pltpu.VMEM((total, width), jnp.float32)] * 4,
        compiler_params=pltpu.CompilerParams(vmem_limit_bytes=32 * 1024 * 1024),
        cost_estimate=pl.CostEstimate(
            flops=BSTEPS * 16 * total * width, bytes_accessed=4 * 11 * rows * width, transcendentals=0
        ),
        name="basin_steps",
    )(inside, state, depth, south, north)


def strips_kernel(first_row, links, state, out):
    rows, width = state.shape[1], state.shape[2]
    count = out.shape[0]
    span = 2 * LANES
    top = first_row[0]

    def piece(b, carry):
        row = jnp.clip(links[b, 0] - top, 0, rows - 1)
        col = links[b, 1]
        start = jnp.clip(col // LANES, 0, width // LANES - 2) * LANES
        shift = lax.rem(span - (col - start), span)
        for i, f in enumerate((0, 2)):
            chunk = state[f, pl.ds(row, 1), pl.ds(pl.multiple_of(start, LANES), span)]
            moved = pltpu.roll(chunk, shift, 1)
            out[b, pl.ds(i, 1), :] = moved[:, :LANES]
        return carry

    lax.fori_loop(0, count, piece, 0, unroll=min(count, 16))


def make_strips(first_row, links, state):
    vmem = pl.BlockSpec(memory_space=pltpu.VMEM)
    smem = pl.BlockSpec(memory_space=pltpu.SMEM)
    return pl.pallas_call(
        strips_kernel,
        out_shape=jax.ShapeDtypeStruct((links.shape[0], 2, LANES), jnp.float32),
        in_specs=[smem, smem, vmem],
        out_specs=vmem,
        name="strips",
    )(first_row, links, state)


def local(basin_state, basin_depth, coast_depth, coast_flow, coast_link):
    strip_rows = basin_state.shape[1]
    devices = lax.axis_size("row")
    position = lax.axis_index("row")

    sent = jnp.broadcast_to(coast_link, (devices, 3))
    links = lax.all_to_all(sent, "row", 0, 0, tiled=True)

    def rows_of(start):
        return jnp.concatenate(
            [basin_state[:, start : start + HALO], basin_depth[None, start : start + HALO]], axis=0
        )

    south = lax.ppermute(
        rows_of(strip_rows - HALO), "row", [(i, i + 1) for i in range(devices - 1)]
    )
    north = lax.ppermute(rows_of(0), "row", [(i + 1, i) for i in range(devices - 1)])

    first_row = (position * strip_rows).astype(jnp.int32)[None]
    pieces = make_strips(first_row, links, basin_state)
    strips = lax.all_to_all(pieces, "row", 0, 0, tiled=True)

    depth, flow = coast_depth[0], coast_flow[0]
    bulk = coast_bulk(coast_link, depth, flow)
    inside = (position < devices - 1).astype(jnp.int32)[None]
    basin_out = basin_run(inside, basin_state, basin_depth, south, north)
    coast_out = coast_edge(strip_rows, coast_link, strips, depth, flow, bulk)
    return (basin_out, coast_out[None])


def solution(mesh):
    in_specs = (
        P("scen", "row", None),
        P("row", "scen"),
        P("row", "scen", None),
        P("row", "scen", None, None),
        P("row", "scen"),
    )
    out_specs = (P("scen", "row", None), P("row", "scen", None, None))
    return jax.shard_map(local, mesh=mesh, in_specs=in_specs, out_specs=out_specs, check_vma=False)
```

```python
import functools

import jax
import jax.numpy as jnp
from jax import lax
from jax.experimental import pallas as pl
from jax.experimental.pallas import tpu as pltpu
from jax.sharding import PartitionSpec as P

BSTEPS = 8
CSTEPS = 10

depth_floor = 0.2
ghost_level = 2.0

RATE = 0.05
DEPTH_UNIT = RATE * RATE
FLOW_UNIT = RATE * RATE * RATE
TINY = 1e-30

HALO = BSTEPS
SUB = 8
LANES = 128


def lane_ids():
    return lax.broadcasted_iota(jnp.int32, (SUB, LANES), 1)


def row_ids():
    return lax.broadcasted_iota(jnp.int32, (SUB, LANES), 0)


def split_columns(cells):
    rows = lax.broadcasted_iota(jnp.int32, (cells, cells), 0)
    cols = lax.broadcasted_iota(jnp.int32, (cells, cells), 1)
    half = cells // 2
    source = jnp.where(cols < half, 2 * cols, 2 * (cols - half) + 1)
    return (rows == source).astype(jnp.bfloat16)


def permute(values, table, transposed=False):
    dims = (((1,), (1 if transposed else 0,)), ((), ()))
    total = None
    rest = values
    for _ in range(3):
        part = rest.astype(jnp.bfloat16)
        rest = rest - part.astype(jnp.float32)
        term = lax.dot_general(part, table, dims, preferred_element_type=jnp.float32)
        total = term if total is None else total + term
    return total


def inverse(x):
    guess = pl.reciprocal(x, approx=True)
    return guess * (2.0 - x * guess)


def cell_terms(u):
    h, mu, mv = u
    r = inverse(jnp.maximum(h, depth_floor * DEPTH_UNIT))
    vx, vy = mu * r, mv * r
    hp = jnp.maximum(h, TINY)
    c = hp * lax.rsqrt(hp)
    p = (0.5 * h) * h
    cross = mu * vy
    return {
        "u": u,
        "fx": (mu, mu * vx + p, cross),
        "fy": (mv, cross, mv * vy + p),
        "sx": jnp.abs(vx) + c,
        "sy": jnp.abs(vy) + c,
    }


def x_part(even, odd, first, last):
    left = functools.partial(pltpu.roll, shift=LANES - 1, axis=1)
    right = functools.partial(pltpu.roll, shift=1, axis=1)
    next_u = [left(a) for a in even["u"]]
    next_f = [next_u[1], left(even["fx"][1]), left(even["fx"][2])]
    a_in = jnp.maximum(even["sx"], odd["sx"])
    a_out = jnp.where(last, 0.0, jnp.maximum(odd["sx"], left(even["sx"])))
    d_in = [a_in * (o - e) for e, o in zip(even["u"], odd["u"])]
    d_out = [a_out * (n - o) for o, n in zip(odd["u"], next_u)]
    new_even, new_odd = [], []
    for i in range(3):
        f_e, f_o = even["fx"][i], odd["fx"][i]
        f_next = jnp.where(last, f_o, next_f[i])
        f_back = jnp.where(first, f_e, right(f_o))
        new_even.append(even["u"][i] + ((d_in[i] - right(d_out[i])) - (f_o - f_back)))
        new_odd.append(odd["u"][i] + ((d_out[i] - d_in[i]) - (f_next - f_e)))
    return new_even, new_odd


def y_face(above, below):
    a = jnp.maximum(above["sy"], below["sy"])
    return [
        a * (ub - ua) - (fa + fb)
        for ua, ub, fa, fb in zip(above["u"], below["u"], above["fy"], below["fy"])
    ]


def coast_steps(here, there, rows, steps, ghost):
    lane, sub = lane_ids(), row_ids()
    first, last = lane == 0, lane == LANES - 1
    top, bottom = sub == 0, sub == SUB - 1

    def load(state, k):
        return [cell_terms([state[f, half, k] for f in range(3)]) for half in range(2)]

    def store(state, k, both):
        for half in range(2):
            for f in range(3):
                state[f, half, k] = both[half][f]

    def wrapped(tail, head):
        down = functools.partial(pltpu.roll, shift=1, axis=0)
        out = {"sy": jnp.where(top, head["sy"], down(tail["sy"]))}
        for name in ("u", "fy"):
            out[name] = [jnp.where(top, h, down(t)) for h, t in zip(head[name], tail[name])]
        return out

    def step(old, new):
        tails = load(old, rows - 1)
        prev, acc, start = None, None, None
        for k in range(rows):
            cur = load(old, k)
            if k == 0:
                heads = cur if ghost is None else ghost
                above = [wrapped(t, h) for t, h in zip(tails, heads)]
                start = face = [y_face(a, b) for a, b in zip(above, cur)]
            else:
                face = [y_face(a, b) for a, b in zip(prev, cur)]
                store(new, k - 1, [[x + g for x, g in zip(xs, gs)] for xs, gs in zip(acc, face)])
            acc = x_part(cur[0], cur[1], first, last)
            acc = [[x - g for x, g in zip(xs, gs)] for xs, gs in zip(acc, face)]
            prev = cur
        end = [
            [
                jnp.where(bottom, -(f + f), pltpu.roll(g, SUB - 1, 0))
                for f, g in zip(cell["fy"], gs)
            ]
            for cell, gs in zip(prev, start)
        ]
        store(new, rows - 1, [[x + g for x, g in zip(xs, gs)] for xs, gs in zip(acc, end)])

    def pair(_, carry):
        step(here, there)
        step(there, here)
        return carry

    lax.fori_loop(0, steps // 2, pair, 0)


EDGE = 3
EDGE_ROWS = EDGE * SUB
EDGE_OUT = 16
UNITS = (DEPTH_UNIT, FLOW_UNIT, FLOW_UNIT)


def unfold(state, tmp, table, unit, rows):
    for half in range(2):
        for k in range(rows):
            tmp[half, pl.ds(k, SUB, stride=rows), :] = state[half, k]
    flat = jnp.concatenate([tmp[0], tmp[1]], axis=1)
    return permute(flat * (1.0 / unit), table, transposed=True)


def coast_kernel(link, depth, flow, out, edge, keep, here, there, tmp):
    rows = depth.shape[0] // SUB
    cells = depth.shape[1]
    wet = link[0, 2] > 0
    kept = lax.broadcasted_iota(jnp.int32, keep.shape, 0) < jnp.where(wet, CSTEPS, 0)
    keep[...] = kept.astype(jnp.float32)

    @pl.when(wet)
    def _():
        table = split_columns(cells)
        for f in range(3):
            split = permute(depth[...] if f == 0 else flow[f - 1], table) * UNITS[f]
            for half in range(2):
                tmp[half] = split[:, half * LANES : (half + 1) * LANES]
                for k in range(rows):
                    here[f, half, k] = tmp[half, pl.ds(k, SUB, stride=rows), :]
                for k in range(EDGE):
                    edge[f, half, k] = tmp[half, pl.ds(k, SUB, stride=EDGE), :]
        coast_steps(here, there, rows, CSTEPS, None)
        for f in range(3):
            out[f] = unfold(here.at[f], tmp, table, UNITS[f], rows)

    @pl.when(jnp.logical_not(wet))
    def _():
        edge[...] = jnp.zeros_like(edge)
        out[0] = depth[...]
        out[1] = flow[0]
        out[2] = flow[1]


def coast_bulk(link, depth, flow):
    cells = depth.shape[0]
    vmem = pl.BlockSpec(memory_space=pltpu.VMEM)
    return pl.pallas_call(
        coast_kernel,
        out_shape=(
            jax.ShapeDtypeStruct((3, cells, cells), jnp.float32),
            jax.ShapeDtypeStruct((3, 2, EDGE, SUB, LANES), jnp.float32),
            jax.ShapeDtypeStruct((EDGE_OUT, cells), jnp.float32),
        ),
        in_specs=[pl.BlockSpec(memory_space=pltpu.SMEM), vmem, vmem],
        out_specs=(vmem, vmem, vmem),
        scratch_shapes=[
            pltpu.VMEM((3, 2, cells // SUB, SUB, LANES), jnp.float32),
            pltpu.VMEM((3, 2, cells // SUB, SUB, LANES), jnp.float32),
            pltpu.VMEM((2, cells, LANES), jnp.float32),
        ],
        compiler_params=pltpu.CompilerParams(vmem_limit_bytes=32 * 1024 * 1024),
        cost_estimate=pl.CostEstimate(
            flops=CSTEPS * 70 * cells * cells, bytes_accessed=24 * cells * cells, transcendentals=0
        ),
        name="coast_bulk",
    )(link, depth, flow)


def edge_kernel(ghosts, edge, keep, before, out, here, there, tmp):
    cells = keep.shape[1]
    half = cells // 2
    values = jnp.sum(ghosts[...], axis=0)
    level = (ghost_level + values[0:1]) * DEPTH_UNIT
    inflow = values[1:2] * FLOW_UNIT
    ghost = []
    for at in (0, half):
        h = jnp.broadcast_to(level[:, at : at + half], (SUB, half))
        mv = jnp.broadcast_to(inflow[:, at : at + half], (SUB, half))
        ghost.append(cell_terms([h, jnp.zeros_like(h), mv]))
    here[...] = edge[...]
    coast_steps(here, there, EDGE, CSTEPS, ghost)
    table = split_columns(cells)
    for f in range(3):
        done = unfold(here.at[f], tmp, table, UNITS[f], EDGE)
        out[f] = jnp.where(keep[...] > 0.0, done[:EDGE_OUT], before[f])


def coast_edge(ghosts, edge, keep, before):
    cells = before.shape[2]
    vmem = pl.BlockSpec(memory_space=pltpu.VMEM)
    top = pl.BlockSpec((3, EDGE_OUT, cells), lambda i: (0, 0, 0))
    return pl.pallas_call(
        edge_kernel,
        out_shape=jax.ShapeDtypeStruct(before.shape, jnp.float32),
        grid=(1,),
        in_specs=[vmem, vmem, vmem, top],
        out_specs=top,
        scratch_shapes=[
            pltpu.VMEM((3, 2, EDGE, SUB, LANES), jnp.float32),
            pltpu.VMEM((3, 2, EDGE, SUB, LANES), jnp.float32),
            pltpu.VMEM((2, EDGE_ROWS, LANES), jnp.float32),
        ],
        input_output_aliases={3: 0},
        cost_estimate=pl.CostEstimate(
            flops=CSTEPS * 70 * EDGE_ROWS * cells, bytes_accessed=4 * 100 * cells, transcendentals=0
        ),
        name="coast_edge",
    )(ghosts, edge, keep, before)


def basin_kernel(inside, state, depth, south, north, out, eta, hu, hv, dep):
    rows = state.shape[1]
    width = state.shape[2]
    total = rows + 2 * HALO
    chunks = width // LANES
    for ref, field, unit in ((eta, 0, 1.0), (hu, 1, 0.5), (hv, 2, 0.5), (dep, 3, 0.25)):
        ref[:HALO] = south[field] * unit
        ref[HALO : HALO + rows] = (depth[...] if field == 3 else state[field]) * unit
        ref[HALO + rows :] = north[field] * unit
    lane = lax.broadcasted_iota(jnp.int32, (total, LANES), 1)
    first, last = lane == 0, lane == LANES - 1
    row = lax.broadcasted_iota(jnp.int32, (total, LANES), 0)
    kept = jnp.where(row < HALO + rows, 1.0, inside[0].astype(jnp.float32))

    def step(_, carry):
        prev_west = jnp.zeros((total, LANES), jnp.float32)
        prev_eta, prev_east, prev_hu = None, None, None
        for c in range(chunks + 1):
            if c < chunks:
                at = slice(c * LANES, (c + 1) * LANES)
                u, v = hu[:, at], hv[:, at]
                west = pltpu.roll(u, 1, 1)
                du = u - jnp.where(first, prev_west, west)
                dv = v - pltpu.roll(v, 1, 0)
                new = (eta[:, at] - (du + dv)) * kept
                eta[:, at] = new
                east = pltpu.roll(new, LANES - 1, 1)
                hv[:, at] = v - dep[:, at] * (pltpu.roll(new, total - 1, 0) - new)
            else:
                east = jnp.zeros((total, LANES), jnp.float32)
            if c > 0:
                back = slice((c - 1) * LANES, c * LANES)
                hu[:, back] = prev_hu - dep[:, back] * (jnp.where(last, east, prev_east) - prev_eta)
            prev_west, prev_eta, prev_east, prev_hu = west, new, east, u
        return carry

    lax.fori_loop(0, BSTEPS, step, 0)
    own = slice(HALO, HALO + rows)
    out[0] = eta[own]
    out[1] = hu[own] * 2.0
    out[2] = hv[own] * 2.0


def basin_run(inside, state, depth, south, north):
    rows, width = depth.shape
    total = rows + 2 * HALO
    vmem = pl.BlockSpec(memory_space=pltpu.VMEM)
    return pl.pallas_call(
        basin_kernel,
        out_shape=jax.ShapeDtypeStruct(state.shape, jnp.float32),
        in_specs=[pl.BlockSpec(memory_space=pltpu.SMEM), vmem, vmem, vmem, vmem],
        out_specs=vmem,
        scratch_shapes=[pltpu.VMEM((total, width), jnp.float32)] * 4,
        compiler_params=pltpu.CompilerParams(vmem_limit_bytes=32 * 1024 * 1024),
        cost_estimate=pl.CostEstimate(
            flops=BSTEPS * 16 * total * width, bytes_accessed=4 * 11 * rows * width, transcendentals=0
        ),
        name="basin_steps",
    )(inside, state, depth, south, north)


def send_kernel(first_row, links, state, depth, ghosts, up, down, strips):
    rows, width = state.shape[1], state.shape[2]
    count, cells = ghosts.shape[0], ghosts.shape[2]
    span = 2 * LANES
    for f in range(3):
        up[f] = state[f, rows - HALO :]
        down[f] = state[f, :HALO]
    up[3] = depth[rows - HALO :]
    down[3] = depth[:HALO]

    def piece(b, carry):
        row = links[b, 0] - first_row[0]
        owned = jnp.logical_and(row >= 0, row < rows).astype(jnp.float32)
        row = jnp.clip(row, 0, rows - 1)
        col = links[b, 1]
        start = jnp.clip(col // LANES, 0, width // LANES - 2) * LANES
        shift = lax.rem(span - (col - start), span)
        for i, f in enumerate((0, 2)):
            chunk = state[f, pl.ds(row, 1), pl.ds(pl.multiple_of(start, LANES), span)]
            strips[pl.ds(2 * b + i, 1), :] = pltpu.roll(chunk, shift, 1)[:, :LANES] * owned
        return carry

    lax.fori_loop(0, count, piece, 0, unroll=min(count, 16))
    at = lax.broadcasted_iota(jnp.int32, (LANES, cells), 0)
    cols = lax.broadcasted_iota(jnp.int32, (LANES, cells), 1)
    half = cells // 2
    cols = jnp.where(cols < half, 2 * cols, 2 * (cols - half) + 1)
    base = cols // 16
    weight = ((cols % 16).astype(jnp.float32) + 0.5) / 16.0
    mix = jnp.where(at == base, 1.0 - weight, 0.0) + jnp.where(at == base + 1, weight, 0.0)
    values = jnp.dot(
        strips[...], mix, precision=lax.Precision.HIGHEST, preferred_element_type=jnp.float32
    )
    for b in range(count):
        ghosts[b] = values[2 * b : 2 * b + 2]


def to_send(first_row, links, state, depth, cells):
    count, width = links.shape[0], depth.shape[1]
    vmem = pl.BlockSpec(memory_space=pltpu.VMEM)
    smem = pl.BlockSpec(memory_space=pltpu.SMEM)
    halo = jax.ShapeDtypeStruct((4, HALO, width), jnp.float32)
    return pl.pallas_call(
        send_kernel,
        out_shape=(jax.ShapeDtypeStruct((count, 2, cells), jnp.float32), halo, halo),
        in_specs=[smem, smem, vmem, vmem],
        out_specs=(vmem, vmem, vmem),
        scratch_shapes=[pltpu.VMEM((2 * count, LANES), jnp.float32)],
        name="to_send",
    )(first_row, links, state, depth)


def local(basin_state, basin_depth, coast_depth, coast_flow, coast_link):
    strip_rows = basin_state.shape[1]
    devices = lax.axis_size("row")
    position = lax.axis_index("row")

    sent = jnp.broadcast_to(coast_link, (devices, 3))
    links = lax.all_to_all(sent, "row", 0, 0, tiled=True)

    first_row = (position * strip_rows).astype(jnp.int32)[None]
    depth, flow = coast_depth[0], coast_flow[0]
    ghosts, up, down = to_send(first_row, links, basin_state, basin_depth, depth.shape[1])
    ghosts = lax.all_to_all(ghosts, "row", 0, 0, tiled=True)
    south = lax.ppermute(up, "row", [(i, i + 1) for i in range(devices - 1)])
    north = lax.ppermute(down, "row", [(i + 1, i) for i in range(devices - 1)])

    bulk, edge, keep = coast_bulk(coast_link, depth, flow)
    inside = (position < devices - 1).astype(jnp.int32)[None]
    basin_out = basin_run(inside, basin_state, basin_depth, south, north)
    coast_out = coast_edge(ghosts, edge, keep, bulk)
    return (basin_out, coast_out[None])


def solution(mesh):
    in_specs = (
        P("scen", "row", None),
        P("row", "scen"),
        P("row", "scen", None),
        P("row", "scen", None, None),
        P("row", "scen"),
    )
    out_specs = (P("scen", "row", None), P("row", "scen", None, None))
    return jax.shard_map(local, mesh=mesh, in_specs=in_specs, out_specs=out_specs, check_vma=False)
```

```python
import functools

import jax
import jax.numpy as jnp
from jax import lax
from jax.experimental import pallas as pl
from jax.experimental.pallas import tpu as pltpu
from jax.sharding import PartitionSpec as P

BSTEPS = 8
CSTEPS = 10

depth_floor = 0.2
ghost_level = 2.0

RATE = 0.05
DEPTH_UNIT = RATE * RATE
FLOW_UNIT = RATE * RATE * RATE
TINY = 1e-30

HALO = BSTEPS
SUB = 8
LANES = 128


def lane_ids():
    return lax.broadcasted_iota(jnp.int32, (SUB, LANES), 1)


def row_ids():
    return lax.broadcasted_iota(jnp.int32, (SUB, LANES), 0)


def split_columns(cells):
    rows = lax.broadcasted_iota(jnp.int32, (cells, cells), 0)
    cols = lax.broadcasted_iota(jnp.int32, (cells, cells), 1)
    half = cells // 2
    source = jnp.where(cols < half, 2 * cols, 2 * (cols - half) + 1)
    return (rows == source).astype(jnp.bfloat16)


def permute(values, table, transposed=False):
    dims = (((1,), (1 if transposed else 0,)), ((), ()))
    total = None
    rest = values
    for _ in range(3):
        part = rest.astype(jnp.bfloat16)
        rest = rest - part.astype(jnp.float32)
        term = lax.dot_general(part, table, dims, preferred_element_type=jnp.float32)
        total = term if total is None else total + term
    return total


def inverse(x):
    guess = pl.reciprocal(x, approx=True)
    return guess * (2.0 - x * guess)


def cell_terms(u):
    h, mu, mv = u
    r = inverse(jnp.maximum(h, depth_floor * DEPTH_UNIT))
    vx, vy = mu * r, mv * r
    hp = jnp.maximum(h, TINY)
    c = hp * lax.rsqrt(hp)
    p = (0.5 * h) * h
    cross = mu * vy
    return {
        "u": u,
        "fx": (mu, mu * vx + p, cross),
        "fy": (mv, cross, mv * vy + p),
        "sx": jnp.abs(vx) + c,
        "sy": jnp.abs(vy) + c,
    }


def x_part(even, odd, first, last):
    left = functools.partial(pltpu.roll, shift=LANES - 1, axis=1)
    right = functools.partial(pltpu.roll, shift=1, axis=1)
    next_u = [left(a) for a in even["u"]]
    next_f = [next_u[1], left(even["fx"][1]), left(even["fx"][2])]
    a_in = jnp.maximum(even["sx"], odd["sx"])
    a_out = jnp.where(last, 0.0, jnp.maximum(odd["sx"], left(even["sx"])))
    d_in = [a_in * (o - e) for e, o in zip(even["u"], odd["u"])]
    d_out = [a_out * (n - o) for o, n in zip(odd["u"], next_u)]
    new_even, new_odd = [], []
    for i in range(3):
        f_e, f_o = even["fx"][i], odd["fx"][i]
        f_next = jnp.where(last, f_o, next_f[i])
        f_back = jnp.where(first, f_e, right(f_o))
        new_even.append(even["u"][i] + ((d_in[i] - right(d_out[i])) - (f_o - f_back)))
        new_odd.append(odd["u"][i] + ((d_out[i] - d_in[i]) - (f_next - f_e)))
    return new_even, new_odd


def y_face(above, below):
    a = jnp.maximum(above["sy"], below["sy"])
    return [
        a * (ub - ua) - (fa + fb)
        for ua, ub, fa, fb in zip(above["u"], below["u"], above["fy"], below["fy"])
    ]


def coast_steps(state, rows, group, steps, ghost):
    lane, sub = lane_ids(), row_ids()
    first, last = lane == 0, lane == LANES - 1
    top, bottom = sub == 0, sub == SUB - 1
    zero = jnp.zeros((SUB, LANES), jnp.float32)

    def load(k):
        return [cell_terms([state[f, half, 1 + k] for f in range(3)]) for half in range(2)]

    def store(k, both):
        for half in range(2):
            for f in range(3):
                state[f, half, 1 + k] = both[half][f]

    def faces_of(cells):
        return [
            {"u": list(cell["u"]), "fy": list(cell["fy"]), "sy": cell["sy"]} for cell in cells
        ]

    def wrapped(tail, head):
        down = functools.partial(pltpu.roll, shift=1, axis=0)
        out = {"sy": jnp.where(top, head["sy"], down(tail["sy"]))}
        for name in ("u", "fy"):
            out[name] = [jnp.where(top, h, down(t)) for h, t in zip(head[name], tail[name])]
        return out

    def step(_, carry):
        tails, heads = load(rows - 1), load(0)
        above = [wrapped(t, h) for t, h in zip(tails, heads if ghost is None else ghost)]
        start = [y_face(a, b) for a, b in zip(above, heads)]

        def rows_from(begin, prev, acc):
            for k in range(group):
                cur = load(begin + k)
                face = [y_face(a, b) for a, b in zip(prev, cur)]
                store(begin + k - 1, [[x + g for x, g in zip(*pair)] for pair in zip(acc, face)])
                acc = x_part(cur[0], cur[1], first, last)
                acc = [[x - g for x, g in zip(*pair)] for pair in zip(acc, face)]
                prev = faces_of(cur)
            return prev, acc

        prev, acc = lax.fori_loop(
            0,
            rows // group,
            lambda i, c: rows_from(i * group, *c),
            (above, [[zero] * 3 for _ in range(2)]),
        )
        end = [
            [
                jnp.where(bottom, -(f + f), pltpu.roll(g, SUB - 1, 0))
                for f, g in zip(cell["fy"], gs)
            ]
            for cell, gs in zip(prev, start)
        ]
        store(rows - 1, [[x + g for x, g in zip(*pair)] for pair in zip(acc, end)])
        return carry

    lax.fori_loop(0, steps, step, 0)


GROUP = 8
EDGE = 3
EDGE_ROWS = EDGE * SUB
EDGE_OUT = 16
UNITS = (DEPTH_UNIT, FLOW_UNIT, FLOW_UNIT)


def unfold(state, tmp, table, unit, rows):
    for half in range(2):
        for k in range(rows):
            tmp[half, pl.ds(k, SUB, stride=rows), :] = state[half, 1 + k]
    flat = jnp.concatenate([tmp[0], tmp[1]], axis=1)
    return permute(flat * (1.0 / unit), table, transposed=True)


def coast_kernel(link, depth, flow, out, edge, keep, state, tmp):
    rows = depth.shape[0] // SUB
    cells = depth.shape[1]
    wet = link[0, 2] > 0
    kept = lax.broadcasted_iota(jnp.int32, keep.shape, 0) < jnp.where(wet, CSTEPS, 0)
    keep[...] = kept.astype(jnp.float32)

    @pl.when(wet)
    def _():
        table = split_columns(cells)
        for f in range(3):
            split = permute(depth[...] if f == 0 else flow[f - 1], table) * UNITS[f]
            for half in range(2):
                tmp[half] = split[:, half * LANES : (half + 1) * LANES]
                for k in range(rows):
                    state[f, half, 1 + k] = tmp[half, pl.ds(k, SUB, stride=rows), :]
                for k in range(EDGE):
                    edge[f, half, k] = tmp[half, pl.ds(k, SUB, stride=EDGE), :]
        coast_steps(state, rows, GROUP, CSTEPS, None)
        for f in range(3):
            out[f] = unfold(state.at[f], tmp, table, UNITS[f], rows)

    @pl.when(jnp.logical_not(wet))
    def _():
        edge[...] = jnp.zeros_like(edge)
        out[0] = depth[...]
        out[1] = flow[0]
        out[2] = flow[1]


def coast_bulk(link, depth, flow):
    cells = depth.shape[0]
    vmem = pl.BlockSpec(memory_space=pltpu.VMEM)
    return pl.pallas_call(
        coast_kernel,
        out_shape=(
            jax.ShapeDtypeStruct((3, cells, cells), jnp.float32),
            jax.ShapeDtypeStruct((3, 2, EDGE, SUB, LANES), jnp.float32),
            jax.ShapeDtypeStruct((EDGE_OUT, cells), jnp.float32),
        ),
        in_specs=[pl.BlockSpec(memory_space=pltpu.SMEM), vmem, vmem],
        out_specs=(vmem, vmem, vmem),
        scratch_shapes=[
            pltpu.VMEM((3, 2, 1 + cells // SUB, SUB, LANES), jnp.float32),
            pltpu.VMEM((2, cells, LANES), jnp.float32),
        ],
        compiler_params=pltpu.CompilerParams(vmem_limit_bytes=32 * 1024 * 1024),
        cost_estimate=pl.CostEstimate(
            flops=CSTEPS * 70 * cells * cells, bytes_accessed=24 * cells * cells, transcendentals=0
        ),
        name="coast_bulk",
    )(link, depth, flow)


def edge_kernel(ghosts, edge, keep, before, out, state, tmp):
    cells = keep.shape[1]
    half = cells // 2
    values = jnp.sum(ghosts[...], axis=0)
    level = (ghost_level + values[0:1]) * DEPTH_UNIT
    inflow = values[1:2] * FLOW_UNIT
    ghost = []
    for at in (0, half):
        h = jnp.broadcast_to(level[:, at : at + half], (SUB, half))
        mv = jnp.broadcast_to(inflow[:, at : at + half], (SUB, half))
        ghost.append(cell_terms([h, jnp.zeros_like(h), mv]))
    state[:, :, 1:] = edge[...]
    coast_steps(state, EDGE, EDGE, CSTEPS, ghost)
    table = split_columns(cells)
    for f in range(3):
        done = unfold(state.at[f], tmp, table, UNITS[f], EDGE)
        out[f] = jnp.where(keep[...] > 0.0, done[:EDGE_OUT], before[f])


def coast_edge(ghosts, edge, keep, before):
    cells = before.shape[2]
    vmem = pl.BlockSpec(memory_space=pltpu.VMEM)
    top = pl.BlockSpec((3, EDGE_OUT, cells), lambda i: (0, 0, 0))
    return pl.pallas_call(
        edge_kernel,
        out_shape=jax.ShapeDtypeStruct(before.shape, jnp.float32),
        grid=(1,),
        in_specs=[vmem, vmem, vmem, top],
        out_specs=top,
        scratch_shapes=[
            pltpu.VMEM((3, 2, 1 + EDGE, SUB, LANES), jnp.float32),
            pltpu.VMEM((2, EDGE_ROWS, LANES), jnp.float32),
        ],
        input_output_aliases={3: 0},
        cost_estimate=pl.CostEstimate(
            flops=CSTEPS * 70 * EDGE_ROWS * cells, bytes_accessed=4 * 100 * cells, transcendentals=0
        ),
        name="coast_edge",
    )(ghosts, edge, keep, before)


def basin_kernel(inside, state, depth, south, north, out, eta, hu, hv, dep):
    rows = state.shape[1]
    width = state.shape[2]
    total = rows + 2 * HALO
    chunks = width // LANES
    for ref, field, unit in ((eta, 0, 1.0), (hu, 1, 0.5), (hv, 2, 0.5), (dep, 3, 0.25)):
        ref[:HALO] = south[field] * unit
        ref[HALO : HALO + rows] = (depth[...] if field == 3 else state[field]) * unit
        ref[HALO + rows :] = north[field] * unit
    lane = lax.broadcasted_iota(jnp.int32, (total, LANES), 1)
    first, last = lane == 0, lane == LANES - 1
    row = lax.broadcasted_iota(jnp.int32, (total, LANES), 0)
    kept = jnp.where(row < HALO + rows, 1.0, inside[0].astype(jnp.float32))

    def step(_, carry):
        prev_west = jnp.zeros((total, LANES), jnp.float32)
        prev_eta, prev_east, prev_hu = None, None, None
        for c in range(chunks + 1):
            if c < chunks:
                at = slice(c * LANES, (c + 1) * LANES)
                u, v = hu[:, at], hv[:, at]
                west = pltpu.roll(u, 1, 1)
                du = u - jnp.where(first, prev_west, west)
                dv = v - pltpu.roll(v, 1, 0)
                new = (eta[:, at] - (du + dv)) * kept
                eta[:, at] = new
                east = pltpu.roll(new, LANES - 1, 1)
                hv[:, at] = v - dep[:, at] * (pltpu.roll(new, total - 1, 0) - new)
            else:
                east = jnp.zeros((total, LANES), jnp.float32)
            if c > 0:
                back = slice((c - 1) * LANES, c * LANES)
                hu[:, back] = prev_hu - dep[:, back] * (jnp.where(last, east, prev_east) - prev_eta)
            prev_west, prev_eta, prev_east, prev_hu = west, new, east, u
        return carry

    lax.fori_loop(0, BSTEPS, step, 0)
    own = slice(HALO, HALO + rows)
    out[0] = eta[own]
    out[1] = hu[own] * 2.0
    out[2] = hv[own] * 2.0


def basin_run(inside, state, depth, south, north):
    rows, width = depth.shape
    total = rows + 2 * HALO
    vmem = pl.BlockSpec(memory_space=pltpu.VMEM)
    return pl.pallas_call(
        basin_kernel,
        out_shape=jax.ShapeDtypeStruct(state.shape, jnp.float32),
        in_specs=[pl.BlockSpec(memory_space=pltpu.SMEM), vmem, vmem, vmem, vmem],
        out_specs=vmem,
        scratch_shapes=[pltpu.VMEM((total, width), jnp.float32)] * 4,
        compiler_params=pltpu.CompilerParams(vmem_limit_bytes=32 * 1024 * 1024),
        cost_estimate=pl.CostEstimate(
            flops=BSTEPS * 16 * total * width, bytes_accessed=4 * 11 * rows * width, transcendentals=0
        ),
        name="basin_steps",
    )(inside, state, depth, south, north)


def send_kernel(first_row, links, state, depth, ghosts, up, down, strips):
    rows, width = state.shape[1], state.shape[2]
    count, cells = ghosts.shape[0], ghosts.shape[2]
    span = 2 * LANES
    for f in range(3):
        up[f] = state[f, rows - HALO :]
        down[f] = state[f, :HALO]
    up[3] = depth[rows - HALO :]
    down[3] = depth[:HALO]

    def piece(b, carry):
        row = links[b, 0] - first_row[0]
        owned = jnp.logical_and(row >= 0, row < rows).astype(jnp.float32)
        row = jnp.clip(row, 0, rows - 1)
        col = links[b, 1]
        start = jnp.clip(col // LANES, 0, width // LANES - 2) * LANES
        shift = lax.rem(span - (col - start), span)
        for i, f in enumerate((0, 2)):
            chunk = state[f, pl.ds(row, 1), pl.ds(pl.multiple_of(start, LANES), span)]
            strips[pl.ds(2 * b + i, 1), :] = pltpu.roll(chunk, shift, 1)[:, :LANES] * owned
        return carry

    lax.fori_loop(0, count, piece, 0, unroll=min(count, 16))
    at = lax.broadcasted_iota(jnp.int32, (LANES, cells), 0)
    cols = lax.broadcasted_iota(jnp.int32, (LANES, cells), 1)
    half = cells // 2
    cols = jnp.where(cols < half, 2 * cols, 2 * (cols - half) + 1)
    base = cols // 16
    weight = ((cols % 16).astype(jnp.float32) + 0.5) / 16.0
    mix = jnp.where(at == base, 1.0 - weight, 0.0) + jnp.where(at == base + 1, weight, 0.0)
    values = jnp.dot(
        strips[...], mix, precision=lax.Precision.HIGHEST, preferred_element_type=jnp.float32
    )
    for b in range(count):
        ghosts[b] = values[2 * b : 2 * b + 2]


def to_send(first_row, links, state, depth, cells):
    count, width = links.shape[0], depth.shape[1]
    vmem = pl.BlockSpec(memory_space=pltpu.VMEM)
    smem = pl.BlockSpec(memory_space=pltpu.SMEM)
    halo = jax.ShapeDtypeStruct((4, HALO, width), jnp.float32)
    return pl.pallas_call(
        send_kernel,
        out_shape=(jax.ShapeDtypeStruct((count, 2, cells), jnp.float32), halo, halo),
        in_specs=[smem, smem, vmem, vmem],
        out_specs=(vmem, vmem, vmem),
        scratch_shapes=[pltpu.VMEM((2 * count, LANES), jnp.float32)],
        name="to_send",
    )(first_row, links, state, depth)


def local(basin_state, basin_depth, coast_depth, coast_flow, coast_link):
    strip_rows = basin_state.shape[1]
    devices = lax.axis_size("row")
    position = lax.axis_index("row")

    sent = jnp.broadcast_to(coast_link, (devices, 3))
    links = lax.all_to_all(sent, "row", 0, 0, tiled=True)

    first_row = (position * strip_rows).astype(jnp.int32)[None]
    depth, flow = coast_depth[0], coast_flow[0]
    ghosts, up, down = to_send(first_row, links, basin_state, basin_depth, depth.shape[1])
    ghosts = lax.all_to_all(ghosts, "row", 0, 0, tiled=True)
    south = lax.ppermute(up, "row", [(i, i + 1) for i in range(devices - 1)])
    north = lax.ppermute(down, "row", [(i + 1, i) for i in range(devices - 1)])

    bulk, edge, keep = coast_bulk(coast_link, depth, flow)
    inside = (position < devices - 1).astype(jnp.int32)[None]
    basin_out = basin_run(inside, basin_state, basin_depth, south, north)
    coast_out = coast_edge(ghosts, edge, keep, bulk)
    return (basin_out, coast_out[None])


def solution(mesh):
    in_specs = (
        P("scen", "row", None),
        P("row", "scen"),
        P("row", "scen", None),
        P("row", "scen", None, None),
        P("row", "scen"),
    )
    out_specs = (P("scen", "row", None), P("row", "scen", None, None))
    return jax.shard_map(local, mesh=mesh, in_specs=in_specs, out_specs=out_specs, check_vma=False)
```

```python
import functools

import jax
import jax.numpy as jnp
from jax import lax
from jax.experimental import pallas as pl
from jax.experimental.pallas import tpu as pltpu
from jax.sharding import PartitionSpec as P

BSTEPS = 8
CSTEPS = 10

depth_floor = 0.2
ghost_level = 2.0

RATE = 0.05
DEPTH_UNIT = RATE * RATE
FLOW_UNIT = RATE * RATE * RATE
TINY = 1e-30

HALO = BSTEPS
SUB = 8
LANES = 128


def lane_ids():
    return lax.broadcasted_iota(jnp.int32, (SUB, LANES), 1)


def row_ids():
    return lax.broadcasted_iota(jnp.int32, (SUB, LANES), 0)


def inverse(x):
    guess = pl.reciprocal(x, approx=True)
    return guess * (2.0 - x * guess)


def cell_terms(u):
    h, mu, mv = u
    r = inverse(jnp.maximum(h, depth_floor * DEPTH_UNIT))
    vx, vy = mu * r, mv * r
    hp = jnp.maximum(h, TINY)
    c = hp * lax.rsqrt(hp)
    p = (0.5 * h) * h
    cross = mu * vy
    return {
        "u": u,
        "fx": (mu, mu * vx + p, cross),
        "fy": (mv, cross, mv * vy + p),
        "sx": jnp.abs(vx) + c,
        "sy": jnp.abs(vy) + c,
    }


def x_part(west, east, first, last):
    left = functools.partial(pltpu.roll, shift=LANES - 1, axis=1)
    right = functools.partial(pltpu.roll, shift=1, axis=1)

    def following(w, e):
        lw, le = left(w), left(e)
        return jnp.where(last, le, lw), jnp.where(last, e, le)

    next_s = following(west["sx"], east["sx"])
    next_u = [following(w, e) for w, e in zip(west["u"], east["u"])]
    next_f = [next_u[1]] + [following(west["fx"][i], east["fx"][i]) for i in (1, 2)]
    a_w = jnp.maximum(west["sx"], next_s[0])
    a_e = jnp.maximum(east["sx"], next_s[1])
    new_west, new_east = [], []
    for i in range(3):
        g_w = a_w * (next_u[i][0] - west["u"][i]) - (west["fx"][i] + next_f[i][0])
        g_e = a_e * (next_u[i][1] - east["u"][i]) - (east["fx"][i] + next_f[i][1])
        rw, re = right(g_w), right(g_e)
        new_west.append(west["u"][i] + (g_w - jnp.where(first, -2.0 * west["fx"][i], rw)))
        new_east.append(east["u"][i] + (g_e - jnp.where(first, rw, re)))
    return new_west, new_east


def y_face(above, below):
    a = jnp.maximum(above["sy"], below["sy"])
    return [
        a * (ub - ua) - (fa + fb)
        for ua, ub, fa, fb in zip(above["u"], below["u"], above["fy"], below["fy"])
    ]


def coast_steps(state, rows, group, steps, ghost):
    lane, sub = lane_ids(), row_ids()
    first, last = lane == 0, lane == LANES - 1
    top, bottom = sub == 0, sub == SUB - 1
    zero = jnp.zeros((SUB, LANES), jnp.float32)

    def load(k):
        return [cell_terms([state[f, half, 1 + k] for f in range(3)]) for half in range(2)]

    def store(k, both):
        for half in range(2):
            for f in range(3):
                state[f, half, 1 + k] = both[half][f]

    def faces_of(cells):
        return [
            {"u": list(cell["u"]), "fy": list(cell["fy"]), "sy": cell["sy"]} for cell in cells
        ]

    def wrapped(tail, head):
        down = functools.partial(pltpu.roll, shift=1, axis=0)
        out = {"sy": jnp.where(top, head["sy"], down(tail["sy"]))}
        for name in ("u", "fy"):
            out[name] = [jnp.where(top, h, down(t)) for h, t in zip(head[name], tail[name])]
        return out

    def step(_, carry):
        tails, heads = load(rows - 1), load(0)
        above = [wrapped(t, h) for t, h in zip(tails, heads if ghost is None else ghost)]
        start = [y_face(a, b) for a, b in zip(above, heads)]

        def rows_from(begin, prev, acc):
            for k in range(group):
                cur = load(begin + k)
                face = [y_face(a, b) for a, b in zip(prev, cur)]
                store(begin + k - 1, [[x + g for x, g in zip(*pair)] for pair in zip(acc, face)])
                acc = x_part(cur[0], cur[1], first, last)
                acc = [[x - g for x, g in zip(*pair)] for pair in zip(acc, face)]
                prev = faces_of(cur)
            return prev, acc

        prev, acc = lax.fori_loop(
            0,
            rows // group,
            lambda i, c: rows_from(i * group, *c),
            (above, [[zero] * 3 for _ in range(2)]),
        )
        end = [
            [
                jnp.where(bottom, -(f + f), pltpu.roll(g, SUB - 1, 0))
                for f, g in zip(cell["fy"], gs)
            ]
            for cell, gs in zip(prev, start)
        ]
        store(rows - 1, [[x + g for x, g in zip(*pair)] for pair in zip(acc, end)])
        return carry

    lax.fori_loop(0, steps, step, 0)


GROUP = 8
EDGE = 3
EDGE_ROWS = EDGE * SUB
EDGE_OUT = 16
UNITS = (DEPTH_UNIT, FLOW_UNIT, FLOW_UNIT)


def coast_kernel(link, depth, flow, out, edge, keep, state, tmp):
    rows = depth.shape[0] // SUB
    wet = link[0, 2] > 0
    kept = lax.broadcasted_iota(jnp.int32, keep.shape, 0) < jnp.where(wet, CSTEPS, 0)
    keep[...] = kept.astype(jnp.float32)
    halves = (slice(0, LANES), slice(LANES, 2 * LANES))
    tall = 32

    def copy_in(i, carry):
        at = pl.ds(pl.multiple_of(i * tall, tall), tall)
        for f in range(3):
            raw = depth[at] if f == 0 else flow[f - 1, at]
            out[f, at] = raw
            for p in range(2):
                tmp[f, p, at] = raw[:, halves[p]] * UNITS[f]
        return carry

    def fold(k, carry):
        for f in range(3):
            for p in range(2):
                state[f, p, 1 + k] = tmp[f, p, pl.ds(k, SUB, stride=rows), :]
        return carry

    def unfold(k, carry):
        for f in range(3):
            for p in range(2):
                tmp[f, p, pl.ds(k, SUB, stride=rows), :] = state[f, p, 1 + k]
        return carry

    def copy_out(i, carry):
        at = pl.ds(pl.multiple_of(i * tall, tall), tall)
        for f in range(3):
            for p in range(2):
                out[f, at, halves[p]] = tmp[f, p, at] * (1.0 / UNITS[f])
        return carry

    lax.fori_loop(0, depth.shape[0] // tall, copy_in, 0)
    for f in range(3):
        for p in range(2):
            for k in range(EDGE):
                edge[f, p, k] = tmp[f, p, pl.ds(k, SUB, stride=EDGE), :]

    @pl.when(wet)
    def _():
        lax.fori_loop(0, rows, fold, 0, unroll=2)
        coast_steps(state, rows, GROUP, CSTEPS, None)
        lax.fori_loop(0, rows, unfold, 0, unroll=2)
        lax.fori_loop(0, depth.shape[0] // tall, copy_out, 0)


VMEM_LIMIT = 12 * 1024 * 1024


def coast_bulk(link, depth, flow):
    cells = depth.shape[0]
    vmem = pl.BlockSpec(memory_space=pltpu.VMEM)
    return pl.pallas_call(
        coast_kernel,
        out_shape=(
            jax.ShapeDtypeStruct((3, cells, cells), jnp.float32),
            jax.ShapeDtypeStruct((3, 2, EDGE, SUB, LANES), jnp.float32),
            jax.ShapeDtypeStruct((EDGE_OUT, cells), jnp.float32),
        ),
        in_specs=[pl.BlockSpec(memory_space=pltpu.SMEM), vmem, vmem],
        out_specs=(vmem, vmem, vmem),
        scratch_shapes=[
            pltpu.VMEM((3, 2, 1 + cells // SUB, SUB, LANES), jnp.float32),
            pltpu.VMEM((3, 2, cells, LANES), jnp.float32),
        ],
        compiler_params=pltpu.CompilerParams(vmem_limit_bytes=VMEM_LIMIT),
        cost_estimate=pl.CostEstimate(
            flops=CSTEPS * 70 * cells * cells, bytes_accessed=24 * cells * cells, transcendentals=0
        ),
        name="coast_bulk",
    )(link, depth, flow)


def edge_kernel(ghosts, edge, keep, before, out, state, tmp):
    values = jnp.sum(ghosts[...], axis=0)
    level = (ghost_level + values[0:1]) * DEPTH_UNIT
    inflow = values[1:2] * FLOW_UNIT
    halves = (slice(0, LANES), slice(LANES, 2 * LANES))
    ghost = []
    for half in halves:
        h = jnp.broadcast_to(level[:, half], (SUB, LANES))
        mv = jnp.broadcast_to(inflow[:, half], (SUB, LANES))
        ghost.append(cell_terms([h, jnp.zeros_like(h), mv]))
    state[:, :, 1:] = edge[...]
    coast_steps(state, EDGE, EDGE, CSTEPS, ghost)
    for f in range(3):
        for p, half in enumerate(halves):
            for k in range(EDGE):
                tmp[pl.ds(k, SUB, stride=EDGE), :] = state[f, p, 1 + k]
            done = tmp[:EDGE_OUT] * (1.0 / UNITS[f])
            out[f, :, half] = jnp.where(keep[:, half] > 0.0, done, before[f, :, half])


def coast_edge(ghosts, edge, keep, before):
    cells = before.shape[2]
    vmem = pl.BlockSpec(memory_space=pltpu.VMEM)
    top = pl.BlockSpec((3, EDGE_OUT, cells), lambda i: (0, 0, 0))
    return pl.pallas_call(
        edge_kernel,
        out_shape=jax.ShapeDtypeStruct(before.shape, jnp.float32),
        grid=(1,),
        in_specs=[vmem, vmem, vmem, top],
        out_specs=top,
        scratch_shapes=[
            pltpu.VMEM((3, 2, 1 + EDGE, SUB, LANES), jnp.float32),
            pltpu.VMEM((EDGE_ROWS, LANES), jnp.float32),
        ],
        input_output_aliases={3: 0},
        compiler_params=pltpu.CompilerParams(vmem_limit_bytes=VMEM_LIMIT),
        cost_estimate=pl.CostEstimate(
            flops=CSTEPS * 70 * EDGE_ROWS * cells, bytes_accessed=4 * 100 * cells, transcendentals=0
        ),
        name="coast_edge",
    )(ghosts, edge, keep, before)


def basin_kernel(inside, state, depth, south, north, out, eta, hu, hv, dep):
    rows = state.shape[1]
    width = state.shape[2]
    total = rows + 2 * HALO
    chunks = width // LANES
    for ref, field, unit in ((eta, 0, 1.0), (hu, 1, 0.5), (hv, 2, 0.5), (dep, 3, 0.25)):
        ref[:HALO] = south[field] * unit
        ref[HALO : HALO + rows] = (depth[...] if field == 3 else state[field]) * unit
        ref[HALO + rows :] = north[field] * unit
    lane = lax.broadcasted_iota(jnp.int32, (total, LANES), 1)
    first, last = lane == 0, lane == LANES - 1
    row = lax.broadcasted_iota(jnp.int32, (total, LANES), 0)
    kept = jnp.where(row < HALO + rows, 1.0, inside[0].astype(jnp.float32))

    def step(_, carry):
        prev_west = jnp.zeros((total, LANES), jnp.float32)
        prev_eta, prev_east, prev_hu = None, None, None
        for c in range(chunks + 1):
            if c < chunks:
                at = slice(c * LANES, (c + 1) * LANES)
                u, v = hu[:, at], hv[:, at]
                west = pltpu.roll(u, 1, 1)
                du = u - jnp.where(first, prev_west, west)
                dv = v - pltpu.roll(v, 1, 0)
                new = (eta[:, at] - (du + dv)) * kept
                eta[:, at] = new
                east = pltpu.roll(new, LANES - 1, 1)
                hv[:, at] = v - dep[:, at] * (pltpu.roll(new, total - 1, 0) - new)
            else:
                east = jnp.zeros((total, LANES), jnp.float32)
            if c > 0:
                back = slice((c - 1) * LANES, c * LANES)
                hu[:, back] = prev_hu - dep[:, back] * (jnp.where(last, east, prev_east) - prev_eta)
            prev_west, prev_eta, prev_east, prev_hu = west, new, east, u
        return carry

    lax.fori_loop(0, BSTEPS, step, 0)
    own = slice(HALO, HALO + rows)
    out[0] = eta[own]
    out[1] = hu[own] * 2.0
    out[2] = hv[own] * 2.0


def basin_run(inside, state, depth, south, north):
    rows, width = depth.shape
    total = rows + 2 * HALO
    vmem = pl.BlockSpec(memory_space=pltpu.VMEM)
    return pl.pallas_call(
        basin_kernel,
        out_shape=jax.ShapeDtypeStruct(state.shape, jnp.float32),
        in_specs=[pl.BlockSpec(memory_space=pltpu.SMEM), vmem, vmem, vmem, vmem],
        out_specs=vmem,
        scratch_shapes=[pltpu.VMEM((total, width), jnp.float32)] * 4,
        compiler_params=pltpu.CompilerParams(vmem_limit_bytes=VMEM_LIMIT),
        cost_estimate=pl.CostEstimate(
            flops=BSTEPS * 16 * total * width, bytes_accessed=4 * 11 * rows * width, transcendentals=0
        ),
        name="basin_steps",
    )(inside, state, depth, south, north)


def send_kernel(first_row, links, state, depth, ghosts, up, down, strips):
    rows, width = state.shape[1], state.shape[2]
    count, cells = ghosts.shape[0], ghosts.shape[2]
    span = 2 * LANES
    for f in range(3):
        up[f] = state[f, rows - HALO :]
        down[f] = state[f, :HALO]
    up[3] = depth[rows - HALO :]
    down[3] = depth[:HALO]

    def piece(b, carry):
        row = links[b, 0] - first_row[0]
        owned = jnp.logical_and(row >= 0, row < rows).astype(jnp.float32)
        row = jnp.clip(row, 0, rows - 1)
        col = links[b, 1]
        start = jnp.clip(col // LANES, 0, width // LANES - 2) * LANES
        shift = lax.rem(span - (col - start), span)
        for i, f in enumerate((0, 2)):
            chunk = state[f, pl.ds(row, 1), pl.ds(pl.multiple_of(start, LANES), span)]
            strips[pl.ds(2 * b + i, 1), :] = pltpu.roll(chunk, shift, 1)[:, :LANES] * owned
        return carry

    lax.fori_loop(0, count, piece, 0, unroll=min(count, 16))
    at = lax.broadcasted_iota(jnp.int32, (LANES, cells), 0)
    cols = lax.broadcasted_iota(jnp.int32, (LANES, cells), 1)
    base = cols // 16
    weight = ((cols % 16).astype(jnp.float32) + 0.5) / 16.0
    mix = jnp.where(at == base, 1.0 - weight, 0.0) + jnp.where(at == base + 1, weight, 0.0)
    values = jnp.dot(
        strips[...], mix, precision=lax.Precision.HIGHEST, preferred_element_type=jnp.float32
    )
    for b in range(count):
        ghosts[b] = values[2 * b : 2 * b + 2]


def to_send(first_row, links, state, depth, cells):
    count, width = links.shape[0], depth.shape[1]
    vmem = pl.BlockSpec(memory_space=pltpu.VMEM)
    smem = pl.BlockSpec(memory_space=pltpu.SMEM)
    halo = jax.ShapeDtypeStruct((4, HALO, width), jnp.float32)
    return pl.pallas_call(
        send_kernel,
        out_shape=(jax.ShapeDtypeStruct((count, 2, cells), jnp.float32), halo, halo),
        in_specs=[smem, smem, vmem, vmem],
        out_specs=(vmem, vmem, vmem),
        scratch_shapes=[pltpu.VMEM((2 * count, LANES), jnp.float32)],
        compiler_params=pltpu.CompilerParams(vmem_limit_bytes=VMEM_LIMIT),
        name="to_send",
    )(first_row, links, state, depth)


def local(basin_state, basin_depth, coast_depth, coast_flow, coast_link):
    strip_rows = basin_state.shape[1]
    devices = lax.axis_size("row")
    position = lax.axis_index("row")

    sent = jnp.broadcast_to(coast_link, (devices, 3))
    links = lax.all_to_all(sent, "row", 0, 0, tiled=True)
    depth, flow = coast_depth[0], coast_flow[0]
    bulk, edge, keep = coast_bulk(coast_link, depth, flow)

    first_row = (position * strip_rows).astype(jnp.int32)[None]
    first_row, bulk = lax.optimization_barrier((first_row, bulk))
    ghosts, up, down = to_send(first_row, links, basin_state, basin_depth, depth.shape[1])
    ghosts = lax.all_to_all(ghosts, "row", 0, 0, tiled=True)
    south = lax.ppermute(up, "row", [(i, i + 1) for i in range(devices - 1)])
    north = lax.ppermute(down, "row", [(i + 1, i) for i in range(devices - 1)])

    inside = (position < devices - 1).astype(jnp.int32)[None]
    basin_out = basin_run(inside, basin_state, basin_depth, south, north)
    coast_out = coast_edge(ghosts, edge, keep, bulk)
    return (basin_out, coast_out[None])


def solution(mesh):
    in_specs = (
        P("scen", "row", None),
        P("row", "scen"),
        P("row", "scen", None),
        P("row", "scen", None, None),
        P("row", "scen"),
    )
    out_specs = (P("scen", "row", None), P("row", "scen", None, None))
    return jax.shard_map(local, mesh=mesh, in_specs=in_specs, out_specs=out_specs, check_vma=False)
```

```python
import functools

import jax
import jax.numpy as jnp
from jax import lax
from jax.experimental import pallas as pl
from jax.experimental.pallas import tpu as pltpu
from jax.sharding import PartitionSpec as P

BSTEPS = 8
CSTEPS = 10

depth_floor = 0.2
ghost_level = 2.0

RATE = 0.05
DEPTH_UNIT = RATE * RATE
FLOW_UNIT = RATE * RATE * RATE
TINY = 1e-30

HALO = BSTEPS
SUB = 8
LANES = 128


def lane_ids():
    return lax.broadcasted_iota(jnp.int32, (SUB, LANES), 1)


def row_ids():
    return lax.broadcasted_iota(jnp.int32, (SUB, LANES), 0)


def cell_terms(u):
    h, mu, mv = u
    r = pl.reciprocal(jnp.maximum(h, depth_floor * DEPTH_UNIT), approx=True)
    vx, vy = mu * r, mv * r
    hp = jnp.maximum(h, TINY)
    c = hp * lax.rsqrt(hp)
    p = (0.5 * h) * h
    cross = mu * vy
    return {
        "u": u,
        "fx": (mu, mu * vx + p, cross),
        "fy": (mv, cross, mv * vy + p),
        "sx": jnp.abs(vx) + c,
        "sy": jnp.abs(vy) + c,
    }


def x_part(even, odd, first, last):
    left = functools.partial(pltpu.roll, shift=LANES - 1, axis=1)
    right = functools.partial(pltpu.roll, shift=1, axis=1)
    after = cell_terms([jnp.where(last, o, left(e)) for e, o in zip(even["u"], odd["u"])])
    a_in = jnp.maximum(even["sx"], odd["sx"])
    a_out = jnp.maximum(odd["sx"], after["sx"])
    new_even, new_odd = [], []
    for i in range(3):
        e, o, n = even["u"][i], odd["u"][i], after["u"][i]
        f_e, f_o, f_n = even["fx"][i], odd["fx"][i], after["fx"][i]
        g_in = a_in * (o - e) - (f_e + f_o)
        g_out = a_out * (n - o) - (f_o + f_n)
        g_back = jnp.where(first, -2.0 * f_e, right(g_out))
        new_even.append(e + (g_in - g_back))
        new_odd.append(o + (g_out - g_in))
    return new_even, new_odd


def y_face(above, below):
    a = jnp.maximum(above["sy"], below["sy"])
    return [
        a * (ub - ua) - (fa + fb)
        for ua, ub, fa, fb in zip(above["u"], below["u"], above["fy"], below["fy"])
    ]


def coast_steps(state, rows, group, steps, ghost):
    lane, sub = lane_ids(), row_ids()
    first, last = lane == 0, lane == LANES - 1
    top, bottom = sub == 0, sub == SUB - 1
    zero = jnp.zeros((SUB, LANES), jnp.float32)

    def load(k):
        return [cell_terms([state[f, half, 1 + k] for f in range(3)]) for half in range(2)]

    def store(k, both):
        for half in range(2):
            for f in range(3):
                state[f, half, 1 + k] = both[half][f]

    def faces_of(cells):
        return [
            {"u": list(cell["u"]), "fy": list(cell["fy"]), "sy": cell["sy"]} for cell in cells
        ]

    def wrapped(tail, head):
        down = functools.partial(pltpu.roll, shift=1, axis=0)
        out = {"sy": jnp.where(top, head["sy"], down(tail["sy"]))}
        for name in ("u", "fy"):
            out[name] = [jnp.where(top, h, down(t)) for h, t in zip(head[name], tail[name])]
        return out

    def step(_, carry):
        tails, heads = load(rows - 1), load(0)
        above = [wrapped(t, h) for t, h in zip(tails, ghost)]
        start = [y_face(a, b) for a, b in zip(above, heads)]

        def rows_from(begin, prev, acc):
            for k in range(group):
                cur = load(begin + k)
                face = [y_face(a, b) for a, b in zip(prev, cur)]
                store(begin + k - 1, [[x + g for x, g in zip(*pair)] for pair in zip(acc, face)])
                acc = x_part(cur[0], cur[1], first, last)
                acc = [[x - g for x, g in zip(*pair)] for pair in zip(acc, face)]
                prev = faces_of(cur)
            return prev, acc

        prev, acc = lax.fori_loop(
            0,
            rows // group,
            lambda i, c: rows_from(i * group, *c),
            (above, [[zero] * 3 for _ in range(2)]),
        )
        end = [
            [
                jnp.where(bottom, -(f + f), pltpu.roll(g, SUB - 1, 0))
                for f, g in zip(cell["fy"], gs)
            ]
            for cell, gs in zip(prev, start)
        ]
        store(rows - 1, [[x + g for x, g in zip(*pair)] for pair in zip(acc, end)])
        return carry

    lax.fori_loop(0, steps, step, 0)


GROUP = 8
UNITS = (DEPTH_UNIT, FLOW_UNIT, FLOW_UNIT)
VMEM_LIMIT = 12 * 1024 * 1024
HALF = LANES // 2


def pick(values, ids):
    return jnp.take_along_axis(values, ids, axis=1, mode="promise_in_bounds")


def split_columns(west, east):
    lane = lane_ids()
    low = lane < HALF
    twice = 2 * jnp.where(low, lane, lane - HALF)
    w = pick(west, jnp.where(low, twice, twice + 1))
    e = pick(east, jnp.where(low, twice + 1, twice))
    return jnp.where(low, w, e), pltpu.roll(jnp.where(low, e, w), HALF, 1)


def join_columns(even, odd):
    lane = lane_ids()
    low = lane < HALF
    odd = pltpu.roll(odd, HALF, 1)
    w, e = jnp.where(low, even, odd), jnp.where(low, odd, even)
    half, is_odd = lane // 2, lane % 2
    return pick(w, half + HALF * is_odd), pick(e, half + HALF * (1 - is_odd))


def coast_kernel(link, ghosts, depth, flow, out, state, tmp):
    rows = depth.shape[0] // SUB
    halves = (slice(0, LANES), slice(LANES, 2 * LANES))
    tall = 32

    def copy_in(i, carry):
        at = pl.ds(pl.multiple_of(i * tall, tall), tall)
        for f in range(3):
            raw = depth[at] if f == 0 else flow[f - 1, at]
            out[f, at] = raw
            for p in range(2):
                tmp[f, p, at] = raw[:, halves[p]] * UNITS[f]
        return carry

    def fold(k, carry):
        for f in range(3):
            both = split_columns(*[tmp[f, p, pl.ds(k, SUB, stride=rows), :] for p in range(2)])
            for p in range(2):
                state[f, p, 1 + k] = both[p]
        return carry

    def unfold(k, carry):
        for f in range(3):
            both = join_columns(state[f, 0, 1 + k], state[f, 1, 1 + k])
            for p in range(2):
                tmp[f, p, pl.ds(k, SUB, stride=rows), :] = both[p]
        return carry

    def copy_out(i, carry):
        at = pl.ds(pl.multiple_of(i * tall, tall), tall)
        for f in range(3):
            for p in range(2):
                out[f, at, halves[p]] = tmp[f, p, at] * (1.0 / UNITS[f])
        return carry

    lax.fori_loop(0, depth.shape[0] // tall, copy_in, 0)

    @pl.when(link[0, 2] > 0)
    def _():
        lax.fori_loop(0, rows, fold, 0, unroll=4)
        values = jnp.sum(ghosts[...], axis=0)
        level = (ghost_level + values[0:1]) * DEPTH_UNIT
        inflow = values[1:2] * FLOW_UNIT
        spread = [jnp.broadcast_to(v[:, half], (SUB, LANES)) for v in (level, inflow) for half in halves]
        h, mv = split_columns(*spread[:2]), split_columns(*spread[2:])
        ghost = [cell_terms([h[p], jnp.zeros_like(h[p]), mv[p]]) for p in range(2)]
        coast_steps(state, rows, GROUP, CSTEPS, ghost)
        lax.fori_loop(0, rows, unfold, 0, unroll=4)
        lax.fori_loop(0, depth.shape[0] // tall, copy_out, 0)


def coast_run(link, ghosts, depth, flow):
    cells = depth.shape[0]
    vmem = pl.BlockSpec(memory_space=pltpu.VMEM)
    return pl.pallas_call(
        coast_kernel,
        out_shape=jax.ShapeDtypeStruct((3, cells, cells), jnp.float32),
        in_specs=[pl.BlockSpec(memory_space=pltpu.SMEM), vmem, vmem, vmem],
        out_specs=vmem,
        scratch_shapes=[
            pltpu.VMEM((3, 2, 1 + cells // SUB, SUB, LANES), jnp.float32),
            pltpu.VMEM((3, 2, cells, LANES), jnp.float32),
        ],
        compiler_params=pltpu.CompilerParams(vmem_limit_bytes=VMEM_LIMIT),
        cost_estimate=pl.CostEstimate(
            flops=CSTEPS * 70 * cells * cells, bytes_accessed=24 * cells * cells, transcendentals=0
        ),
        name="coast_steps",
    )(link, ghosts, depth, flow)


def basin_kernel(inside, state, depth, south, north, out, eta, hu, hv, dep):
    rows = state.shape[1]
    width = state.shape[2]
    total = rows + 2 * HALO
    chunks = width // LANES
    for ref, field, unit in ((eta, 0, 1.0), (hu, 1, 0.5), (hv, 2, 0.5), (dep, 3, 0.25)):
        ref[:HALO] = south[field] * unit
        ref[HALO : HALO + rows] = (depth[...] if field == 3 else state[field]) * unit
        ref[HALO + rows :] = north[field] * unit
    lane = lax.broadcasted_iota(jnp.int32, (total, LANES), 1)
    first, last = lane == 0, lane == LANES - 1
    row = lax.broadcasted_iota(jnp.int32, (total, LANES), 0)
    kept = jnp.where(row < HALO + rows, 1.0, inside[0].astype(jnp.float32))

    def step(_, carry):
        prev_west = jnp.zeros((total, LANES), jnp.float32)
        prev_eta, prev_east, prev_hu = None, None, None
        for c in range(chunks + 1):
            if c < chunks:
                at = slice(c * LANES, (c + 1) * LANES)
                u, v = hu[:, at], hv[:, at]
                west = pltpu.roll(u, 1, 1)
                du = u - jnp.where(first, prev_west, west)
                dv = v - pltpu.roll(v, 1, 0)
                new = (eta[:, at] - (du + dv)) * kept
                eta[:, at] = new
                east = pltpu.roll(new, LANES - 1, 1)
                hv[:, at] = v - dep[:, at] * (pltpu.roll(new, total - 1, 0) - new)
            else:
                east = jnp.zeros((total, LANES), jnp.float32)
            if c > 0:
                back = slice((c - 1) * LANES, c * LANES)
                hu[:, back] = prev_hu - dep[:, back] * (jnp.where(last, east, prev_east) - prev_eta)
            prev_west, prev_eta, prev_east, prev_hu = west, new, east, u
        return carry

    lax.fori_loop(0, BSTEPS, step, 0)
    own = slice(HALO, HALO + rows)
    out[0] = eta[own]
    out[1] = hu[own] * 2.0
    out[2] = hv[own] * 2.0


def basin_run(inside, state, depth, south, north):
    rows, width = depth.shape
    total = rows + 2 * HALO
    vmem = pl.BlockSpec(memory_space=pltpu.VMEM)
    return pl.pallas_call(
        basin_kernel,
        out_shape=jax.ShapeDtypeStruct(state.shape, jnp.float32),
        in_specs=[pl.BlockSpec(memory_space=pltpu.SMEM), vmem, vmem, vmem, vmem],
        out_specs=vmem,
        scratch_shapes=[pltpu.VMEM((total, width), jnp.float32)] * 4,
        compiler_params=pltpu.CompilerParams(vmem_limit_bytes=VMEM_LIMIT),
        cost_estimate=pl.CostEstimate(
            flops=BSTEPS * 16 * total * width, bytes_accessed=4 * 11 * rows * width, transcendentals=0
        ),
        name="basin_steps",
    )(inside, state, depth, south, north)


def pack_kernel(after, state, depth, up, down):
    rows = depth.shape[0]
    for f in range(4):
        source = depth if f == 3 else state.at[f]
        up[f] = source[rows - HALO :]
        down[f] = source[:HALO]


def pack_halos(after, state, depth):
    vmem = pl.BlockSpec(memory_space=pltpu.VMEM)
    halo = jax.ShapeDtypeStruct((4, HALO, depth.shape[1]), jnp.float32)
    return pl.pallas_call(
        pack_kernel,
        out_shape=(halo, halo),
        in_specs=[pl.BlockSpec(memory_space=pl.ANY), vmem, vmem],
        out_specs=(vmem, vmem),
        compiler_params=pltpu.CompilerParams(vmem_limit_bytes=VMEM_LIMIT),
        name="pack_halos",
    )(after, state, depth)


def strips_kernel(first_row, links, state, ghosts, strips):
    rows, width = state.shape[1], state.shape[2]
    count, cells = ghosts.shape[0], ghosts.shape[2]
    span = 2 * LANES

    def piece(b, carry):
        row = links[b, 0, 0] - first_row[0]
        owned = jnp.logical_and(row >= 0, row < rows).astype(jnp.float32)
        row = jnp.clip(row, 0, rows - 1)
        col = links[b, 0, 1]
        start = jnp.clip(col // LANES, 0, width // LANES - 2) * LANES
        shift = lax.rem(span - (col - start), span)
        for i, f in enumerate((0, 2)):
            chunk = state[f, pl.ds(row, 1), pl.ds(pl.multiple_of(start, LANES), span)]
            strips[pl.ds(2 * b + i, 1), :] = pltpu.roll(chunk, shift, 1)[:, :LANES] * owned
        return carry

    lax.fori_loop(0, count, piece, 0, unroll=min(count, 16))
    at = lax.broadcasted_iota(jnp.int32, (LANES, cells), 0)
    cols = lax.broadcasted_iota(jnp.int32, (LANES, cells), 1)
    base = cols // 16
    weight = ((cols % 16).astype(jnp.float32) + 0.5) / 16.0
    mix = jnp.where(at == base, 1.0 - weight, 0.0) + jnp.where(at == base + 1, weight, 0.0)
    values = jnp.dot(
        strips[...], mix, precision=lax.Precision.HIGHEST, preferred_element_type=jnp.float32
    )
    for b in range(count):
        ghosts[b] = values[2 * b : 2 * b + 2]


def make_strips(first_row, links, state, cells):
    count = links.shape[0]
    vmem = pl.BlockSpec(memory_space=pltpu.VMEM)
    smem = pl.BlockSpec(memory_space=pltpu.SMEM)
    return pl.pallas_call(
        strips_kernel,
        out_shape=jax.ShapeDtypeStruct((count, 2, cells), jnp.float32),
        in_specs=[smem, smem, vmem],
        out_specs=vmem,
        scratch_shapes=[pltpu.VMEM((2 * count, LANES), jnp.float32)],
        compiler_params=pltpu.CompilerParams(vmem_limit_bytes=VMEM_LIMIT),
        name="strips",
    )(first_row, links, state)


def local(basin_state, basin_depth, coast_depth, coast_flow, coast_link):
    strip_rows = basin_state.shape[1]
    devices = lax.axis_size("row")
    position = lax.axis_index("row")

    sent = jnp.broadcast_to(coast_link, (devices,) + coast_link.shape)
    links = lax.all_to_all(sent, "row", 0, 0, tiled=True)

    up, down = pack_halos(sent, basin_state, basin_depth)
    south = lax.ppermute(up, "row", [(i, i + 1) for i in range(devices - 1)])
    north = lax.ppermute(down, "row", [(i + 1, i) for i in range(devices - 1)])

    first_row = (position * strip_rows).astype(jnp.int32)[None]
    ghosts = make_strips(first_row, links, basin_state, coast_depth.shape[2])
    ghosts = lax.all_to_all(ghosts, "row", 0, 0, tiled=True)

    inside = (position < devices - 1).astype(jnp.int32)[None]
    basin_out = basin_run(inside, basin_state, basin_depth, south, north)
    coast_link, basin_out = lax.optimization_barrier((coast_link, basin_out))
    coast_out = coast_run(coast_link, ghosts, coast_depth[0], coast_flow[0])
    return (basin_out, coast_out[None])


def solution(mesh):
    in_specs = (
        P("scen", "row", None),
        P("row", "scen"),
        P("row", "scen", None),
        P("row", "scen", None, None),
        P("row", "scen"),
    )
    out_specs = (P("scen", "row", None), P("row", "scen", None, None))
    return jax.shard_map(local, mesh=mesh, in_specs=in_specs, out_specs=out_specs, check_vma=False)
```

```python
import functools

import jax
import jax.numpy as jnp
from jax import lax
from jax.experimental import pallas as pl
from jax.experimental.pallas import tpu as pltpu
from jax.sharding import PartitionSpec as P

BSTEPS = 8
CSTEPS = 10

depth_floor = 0.2
ghost_level = 2.0

RATE = 0.05
DEPTH_UNIT = RATE * RATE
FLOW_UNIT = RATE * RATE * RATE
TINY = 1e-30

HALO = BSTEPS
SUB = 8
LANES = 128


def lane_ids():
    return lax.broadcasted_iota(jnp.int32, (SUB, LANES), 1)


def row_ids():
    return lax.broadcasted_iota(jnp.int32, (SUB, LANES), 0)


def cell_terms(u):
    h, mu, mv = u
    r = pl.reciprocal(jnp.maximum(h, depth_floor * DEPTH_UNIT), approx=True)
    vx, vy = mu * r, mv * r
    hp = jnp.maximum(h, TINY)
    c = hp * lax.rsqrt(hp)
    p = (0.5 * h) * h
    cross = mu * vy
    return {
        "u": u,
        "fx": (mu, mu * vx + p, cross),
        "fy": (mv, cross, mv * vy + p),
        "sx": jnp.abs(vx) + c,
        "sy": jnp.abs(vy) + c,
    }


def x_part(even, odd, first, last):
    left = functools.partial(pltpu.roll, shift=LANES - 1, axis=1)
    right = functools.partial(pltpu.roll, shift=1, axis=1)
    after = cell_terms([jnp.where(last, o, left(e)) for e, o in zip(even["u"], odd["u"])])
    a_in = jnp.maximum(even["sx"], odd["sx"])
    a_out = jnp.maximum(odd["sx"], after["sx"])
    new_even, new_odd = [], []
    for i in range(3):
        e, o, n = even["u"][i], odd["u"][i], after["u"][i]
        f_e, f_o, f_n = even["fx"][i], odd["fx"][i], after["fx"][i]
        g_in = a_in * (o - e) - (f_e + f_o)
        g_out = a_out * (n - o) - (f_o + f_n)
        g_back = jnp.where(first, -2.0 * f_e, right(g_out))
        new_even.append(e + (g_in - g_back))
        new_odd.append(o + (g_out - g_in))
    return new_even, new_odd


def y_face(above, below):
    a = jnp.maximum(above["sy"], below["sy"])
    return [
        a * (ub - ua) - (fa + fb)
        for ua, ub, fa, fb in zip(above["u"], below["u"], above["fy"], below["fy"])
    ]


def coast_steps(state, rows, group, steps, ghost):
    lane, sub = lane_ids(), row_ids()
    first, last = lane == 0, lane == LANES - 1
    top, bottom = sub == 0, sub == SUB - 1
    zero = jnp.zeros((SUB, LANES), jnp.float32)

    def load(k):
        return [cell_terms([state[f, half, 1 + k] for f in range(3)]) for half in range(2)]

    def store(k, both):
        for half in range(2):
            for f in range(3):
                state[f, half, 1 + k] = both[half][f]

    def faces_of(cells):
        return [
            {"u": list(cell["u"]), "fy": list(cell["fy"]), "sy": cell["sy"]} for cell in cells
        ]

    def wrapped(tail, head):
        down = functools.partial(pltpu.roll, shift=1, axis=0)
        out = {"sy": jnp.where(top, head["sy"], down(tail["sy"]))}
        for name in ("u", "fy"):
            out[name] = [jnp.where(top, h, down(t)) for h, t in zip(head[name], tail[name])]
        return out

    def step(_, carry):
        tails, heads = load(rows - 1), load(0)
        above = [wrapped(t, h) for t, h in zip(tails, heads if ghost is None else ghost)]
        start = [y_face(a, b) for a, b in zip(above, heads)]

        def rows_from(begin, prev, acc):
            for k in range(group):
                cur = load(begin + k)
                face = [y_face(a, b) for a, b in zip(prev, cur)]
                store(begin + k - 1, [[x + g for x, g in zip(*pair)] for pair in zip(acc, face)])
                acc = x_part(cur[0], cur[1], first, last)
                acc = [[x - g for x, g in zip(*pair)] for pair in zip(acc, face)]
                prev = faces_of(cur)
            return prev, acc

        prev, acc = lax.fori_loop(
            0,
            rows // group,
            lambda i, c: rows_from(i * group, *c),
            (above, [[zero] * 3 for _ in range(2)]),
        )
        end = [
            [
                jnp.where(bottom, -(f + f), pltpu.roll(g, SUB - 1, 0))
                for f, g in zip(cell["fy"], gs)
            ]
            for cell, gs in zip(prev, start)
        ]
        store(rows - 1, [[x + g for x, g in zip(*pair)] for pair in zip(acc, end)])
        return carry

    lax.fori_loop(0, steps, step, 0)


GROUP = 8
UNITS = (DEPTH_UNIT, FLOW_UNIT, FLOW_UNIT)
VMEM_LIMIT = 12 * 1024 * 1024
HALF = LANES // 2


def pick(values, ids):
    return jnp.take_along_axis(values, ids, axis=1, mode="promise_in_bounds")


def split_columns(west, east):
    lane = lane_ids()
    low = lane < HALF
    twice = 2 * jnp.where(low, lane, lane - HALF)
    w = pick(west, jnp.where(low, twice, twice + 1))
    e = pick(east, jnp.where(low, twice + 1, twice))
    return jnp.where(low, w, e), pltpu.roll(jnp.where(low, e, w), HALF, 1)


def join_columns(even, odd):
    lane = lane_ids()
    low = lane < HALF
    odd = pltpu.roll(odd, HALF, 1)
    w, e = jnp.where(low, even, odd), jnp.where(low, odd, even)
    half, is_odd = lane // 2, lane % 2
    return pick(w, half + HALF * is_odd), pick(e, half + HALF * (1 - is_odd))


EDGE = 3
EDGE_ROWS = EDGE * SUB
EDGE_OUT = 16
HALVES = (slice(0, LANES), slice(LANES, 2 * LANES))


def coast_kernel(link, depth, flow, out, edge, keep, state, tmp):
    rows = depth.shape[0] // SUB
    wet = link[0, 2] > 0
    kept = lax.broadcasted_iota(jnp.int32, keep.shape, 0) < jnp.where(wet, CSTEPS, 0)
    keep[...] = kept.astype(jnp.float32)
    tall = 32

    def copy_in(i, carry):
        at = pl.ds(pl.multiple_of(i * tall, tall), tall)
        for f in range(3):
            raw = depth[at] if f == 0 else flow[f - 1, at]
            out[f, at] = raw
            for p in range(2):
                tmp[f, p, at] = raw[:, HALVES[p]] * UNITS[f]
        return carry

    def fold(k, carry):
        for f in range(3):
            both = split_columns(*[tmp[f, p, pl.ds(k, SUB, stride=rows), :] for p in range(2)])
            for p in range(2):
                state[f, p, 1 + k] = both[p]
        return carry

    def fold_edge(k, carry):
        for f in range(3):
            both = split_columns(*[tmp[f, p, pl.ds(k, SUB, stride=EDGE), :] for p in range(2)])
            for p in range(2):
                edge[f, p, k] = both[p]
        return carry

    def unfold(k, carry):
        for f in range(3):
            both = join_columns(state[f, 0, 1 + k], state[f, 1, 1 + k])
            for p in range(2):
                tmp[f, p, pl.ds(k, SUB, stride=rows), :] = both[p]
        return carry

    def copy_out(i, carry):
        at = pl.ds(pl.multiple_of(i * tall, tall), tall)
        for f in range(3):
            for p in range(2):
                out[f, at, HALVES[p]] = tmp[f, p, at] * (1.0 / UNITS[f])
        return carry

    lax.fori_loop(0, depth.shape[0] // tall, copy_in, 0)
    lax.fori_loop(0, EDGE, fold_edge, 0)

    @pl.when(wet)
    def _():
        lax.fori_loop(0, rows, fold, 0, unroll=4)
        coast_steps(state, rows, GROUP, CSTEPS, None)
        lax.fori_loop(0, rows, unfold, 0, unroll=4)
        lax.fori_loop(0, depth.shape[0] // tall, copy_out, 0)


def coast_bulk(link, depth, flow):
    cells = depth.shape[0]
    vmem = pl.BlockSpec(memory_space=pltpu.VMEM)
    return pl.pallas_call(
        coast_kernel,
        out_shape=(
            jax.ShapeDtypeStruct((3, cells, cells), jnp.float32),
            jax.ShapeDtypeStruct((3, 2, EDGE, SUB, LANES), jnp.float32),
            jax.ShapeDtypeStruct((EDGE_OUT, cells), jnp.float32),
        ),
        in_specs=[pl.BlockSpec(memory_space=pltpu.SMEM), vmem, vmem],
        out_specs=(vmem, vmem, vmem),
        scratch_shapes=[
            pltpu.VMEM((3, 2, 1 + cells // SUB, SUB, LANES), jnp.float32),
            pltpu.VMEM((3, 2, cells, LANES), jnp.float32),
        ],
        compiler_params=pltpu.CompilerParams(vmem_limit_bytes=VMEM_LIMIT),
        cost_estimate=pl.CostEstimate(
            flops=CSTEPS * 70 * cells * cells, bytes_accessed=24 * cells * cells, transcendentals=0
        ),
        name="coast_bulk",
    )(link, depth, flow)


SLOT = 32


def edge_kernel(strip_rows, link, block, strips, edge, keep, before, out, state, tmp, tile, sem):
    cells = keep.shape[1]
    per_device = strips.shape[1]
    row = block[0] // 2
    copy = pltpu.make_async_copy(
        strips.at[link[0, 0] // strip_rows, pl.ds(pl.multiple_of(row // SUB * SUB, SUB), SUB)], tile, sem
    )
    copy.start()
    at = lax.broadcasted_iota(jnp.int32, (LANES, cells), 0)
    place = lax.broadcasted_iota(jnp.int32, (LANES, cells), 1)
    cols = jnp.where(place < LANES, 2 * place, 2 * (place - LANES) + 1)
    base = cols // 16
    weight = ((cols % 16).astype(jnp.float32) + 0.5) / 16.0
    mix = jnp.where(at == base, 1.0 - weight, 0.0) + jnp.where(at == base + 1, weight, 0.0)
    state[:, :, 1:] = edge[...]
    copy.wait()
    mine = tile[pl.ds(row % SUB, 1), :]
    mine = jnp.where(block[0] % 2 == 0, mine, pltpu.roll(mine, 2 * SLOT, 1))
    pair = jnp.concatenate([mine, pltpu.roll(mine, LANES - SLOT, 1)] + [mine] * (SUB - 2), axis=0)
    values = jnp.dot(pair, mix, precision=lax.Precision.HIGHEST, preferred_element_type=jnp.float32)
    level = (ghost_level + values[0:1]) * DEPTH_UNIT
    inflow = values[1:2] * FLOW_UNIT
    ghost = []
    for half in HALVES:
        h = jnp.broadcast_to(level[:, half], (SUB, LANES))
        mv = jnp.broadcast_to(inflow[:, half], (SUB, LANES))
        ghost.append(cell_terms([h, jnp.zeros_like(h), mv]))
    coast_steps(state, EDGE, EDGE, CSTEPS, ghost)
    for f in range(3):
        for k in range(EDGE):
            both = join_columns(state[f, 0, 1 + k], state[f, 1, 1 + k])
            for p in range(2):
                tmp[p, pl.ds(k, SUB, stride=EDGE), :] = both[p]
        for p, half in enumerate(HALVES):
            done = tmp[p, :EDGE_OUT] * (1.0 / UNITS[f])
            out[f, :, half] = jnp.where(keep[:, half] > 0.0, done, before[f, :, half])


def coast_edge(strip_rows, link, block, strips, edge, keep, before):
    cells = before.shape[2]
    vmem = pl.BlockSpec(memory_space=pltpu.VMEM)
    smem = pl.BlockSpec(memory_space=pltpu.SMEM)
    top = pl.BlockSpec((3, EDGE_OUT, cells), lambda i: (0, 0, 0))
    return pl.pallas_call(
        functools.partial(edge_kernel, strip_rows),
        out_shape=jax.ShapeDtypeStruct(before.shape, jnp.float32),
        grid=(1,),
        in_specs=[smem, smem, pl.BlockSpec(memory_space=pl.ANY), vmem, vmem, top],
        out_specs=top,
        scratch_shapes=[
            pltpu.VMEM((3, 2, 1 + EDGE, SUB, LANES), jnp.float32),
            pltpu.VMEM((2, EDGE_ROWS, LANES), jnp.float32),
            pltpu.VMEM((SUB, LANES), jnp.float32),
            pltpu.SemaphoreType.DMA,
        ],
        input_output_aliases={5: 0},
        compiler_params=pltpu.CompilerParams(vmem_limit_bytes=VMEM_LIMIT),
        cost_estimate=pl.CostEstimate(
            flops=CSTEPS * 70 * EDGE_ROWS * cells, bytes_accessed=4 * 100 * cells, transcendentals=0
        ),
        name="coast_edge",
    )(link, block, strips, edge, keep, before)


def basin_kernel(inside, state, depth, south, north, out, eta, hu, hv, dep):
    rows = state.shape[1]
    width = state.shape[2]
    total = rows + 2 * HALO
    chunks = width // LANES
    for ref, field, unit in ((eta, 0, 1.0), (hu, 1, 0.5), (hv, 2, 0.5), (dep, 3, 0.25)):
        ref[:HALO] = south[field] * unit
        ref[HALO : HALO + rows] = (depth[...] if field == 3 else state[field]) * unit
        ref[HALO + rows :] = north[field] * unit
    lane = lax.broadcasted_iota(jnp.int32, (total, LANES), 1)
    first, last = lane == 0, lane == LANES - 1
    row = lax.broadcasted_iota(jnp.int32, (total, LANES), 0)
    kept = jnp.where(row < HALO + rows, 1.0, inside[0].astype(jnp.float32))

    def step(_, carry):
        prev_west = jnp.zeros((total, LANES), jnp.float32)
        prev_eta, prev_east, prev_hu = None, None, None
        for c in range(chunks + 1):
            if c < chunks:
                at = slice(c * LANES, (c + 1) * LANES)
                u, v = hu[:, at], hv[:, at]
                west = pltpu.roll(u, 1, 1)
                du = u - jnp.where(first, prev_west, west)
                dv = v - pltpu.roll(v, 1, 0)
                new = (eta[:, at] - (du + dv)) * kept
                eta[:, at] = new
                east = pltpu.roll(new, LANES - 1, 1)
                hv[:, at] = v - dep[:, at] * (pltpu.roll(new, total - 1, 0) - new)
            else:
                east = jnp.zeros((total, LANES), jnp.float32)
            if c > 0:
                back = slice((c - 1) * LANES, c * LANES)
                hu[:, back] = prev_hu - dep[:, back] * (jnp.where(last, east, prev_east) - prev_eta)
            prev_west, prev_eta, prev_east, prev_hu = west, new, east, u
        return carry

    lax.fori_loop(0, BSTEPS, step, 0)
    own = slice(HALO, HALO + rows)
    out[0] = eta[own]
    out[1] = hu[own] * 2.0
    out[2] = hv[own] * 2.0


def basin_run(inside, state, depth, south, north):
    rows, width = depth.shape
    total = rows + 2 * HALO
    vmem = pl.BlockSpec(memory_space=pltpu.VMEM)
    return pl.pallas_call(
        basin_kernel,
        out_shape=jax.ShapeDtypeStruct(state.shape, jnp.float32),
        in_specs=[pl.BlockSpec(memory_space=pltpu.SMEM), vmem, vmem, vmem, vmem],
        out_specs=vmem,
        scratch_shapes=[pltpu.VMEM((total, width), jnp.float32)] * 4,
        compiler_params=pltpu.CompilerParams(vmem_limit_bytes=VMEM_LIMIT),
        cost_estimate=pl.CostEstimate(
            flops=BSTEPS * 16 * total * width, bytes_accessed=4 * 11 * rows * width, transcendentals=0
        ),
        name="basin_steps",
    )(inside, state, depth, south, north)


def pack_kernel(after, state, depth, up, down):
    rows = depth.shape[0]
    for f in range(4):
        source = depth if f == 3 else state.at[f]
        up[f] = source[rows - HALO :]
        down[f] = source[:HALO]


def pack_halos(after, state, depth):
    vmem = pl.BlockSpec(memory_space=pltpu.VMEM)
    halo = jax.ShapeDtypeStruct((4, HALO, depth.shape[1]), jnp.float32)
    return pl.pallas_call(
        pack_kernel,
        out_shape=(halo, halo),
        in_specs=[pl.BlockSpec(memory_space=pl.ANY), vmem, vmem],
        out_specs=(vmem, vmem),
        compiler_params=pltpu.CompilerParams(vmem_limit_bytes=VMEM_LIMIT),
        name="pack_halos",
    )(after, state, depth)


def strips_kernel(count, first_row, links, state, out):
    rows, width = state.shape[1], state.shape[2]
    span = 2 * LANES
    lane = lax.broadcasted_iota(jnp.int32, (1, LANES), 1)

    def pair(i, carry):
        total = jnp.zeros((1, LANES), jnp.float32)
        for j in range(2):
            b = 2 * i + j
            row = links[b, 0] - first_row[0]
            owned = jnp.logical_and(row >= 0, row < rows).astype(jnp.float32)
            row = jnp.clip(row, 0, rows - 1)
            col = links[b, 1]
            start = jnp.clip(col // LANES, 0, width // LANES - 2) * LANES
            for f in range(2):
                slot = (2 * j + f) * SLOT
                shift = lax.rem(span - (col - start) + slot, span)
                chunk = state[2 * f, pl.ds(row, 1), pl.ds(pl.multiple_of(start, LANES), span)]
                moved = pltpu.roll(chunk, shift, 1)[:, :LANES] * owned
                inside = jnp.logical_and(lane >= slot, lane < slot + SLOT)
                total = jnp.where(inside, moved, total)
        out[pl.ds(i, 1), :] = total
        return carry

    lax.fori_loop(0, count // 2, pair, 0, unroll=min(count // 2, 8))


def make_strips(count, first_row, links, state):
    vmem = pl.BlockSpec(memory_space=pltpu.VMEM)
    smem = pl.BlockSpec(memory_space=pltpu.SMEM)
    return pl.pallas_call(
        functools.partial(strips_kernel, count),
        out_shape=jax.ShapeDtypeStruct((count // 2, LANES), jnp.float32),
        in_specs=[smem, smem, vmem],
        out_specs=vmem,
        compiler_params=pltpu.CompilerParams(vmem_limit_bytes=VMEM_LIMIT),
        name="strips",
    )(first_row, links, state)


def local(basin_state, basin_depth, coast_depth, coast_flow, coast_link):
    strip_rows = basin_state.shape[1]
    devices = lax.axis_size("row")
    position = lax.axis_index("row")

    sent = jnp.pad(coast_link, ((0, SUB - 1), (0, LANES - coast_link.shape[1])))
    links = lax.all_gather(sent, "row", axis=0, tiled=True)
    links = links.reshape(devices, SUB, LANES)[:, 0, :2]

    bulk, edge, keep = coast_bulk(coast_link, coast_depth[0], coast_flow[0])
    first_row = (position * strip_rows).astype(jnp.int32)[None]
    first_row, bulk = lax.optimization_barrier((first_row, bulk))
    strips = make_strips(devices, first_row, links, basin_state)
    all_strips = lax.all_gather(strips, "row", axis=0, tiled=False)

    up, down = pack_halos(strips, basin_state, basin_depth)
    south = lax.ppermute(up, "row", [(i, i + 1) for i in range(devices - 1)])
    north = lax.ppermute(down, "row", [(i + 1, i) for i in range(devices - 1)])
    inside = (position < devices - 1).astype(jnp.int32)[None]
    basin_out = basin_run(inside, basin_state, basin_depth, south, north)
    block = position.astype(jnp.int32)[None]
    block, basin_out = lax.optimization_barrier((block, basin_out))
    coast_out = coast_edge(strip_rows, coast_link, block, all_strips, edge, keep, bulk)
    return (basin_out, coast_out[None])


def solution(mesh):
    in_specs = (
        P("scen", "row", None),
        P("row", "scen"),
        P("row", "scen", None),
        P("row", "scen", None, None),
        P("row", "scen"),
    )
    out_specs = (P("scen", "row", None), P("row", "scen", None, None))
    return jax.shard_map(local, mesh=mesh, in_specs=in_specs, out_specs=out_specs, check_vma=False)
```

```python
import functools

import jax
import jax.numpy as jnp
from jax import lax
from jax.experimental import pallas as pl
from jax.experimental.pallas import tpu as pltpu
from jax.sharding import PartitionSpec as P

BSTEPS = 8
CSTEPS = 10

depth_floor = 0.2
ghost_level = 2.0

RATE = 0.05
DEPTH_UNIT = RATE * RATE
FLOW_UNIT = RATE * RATE * RATE
TINY = 1e-30

HALO = BSTEPS
SUB = 8
LANES = 128


def lane_ids():
    return lax.broadcasted_iota(jnp.int32, (SUB, LANES), 1)


def row_ids():
    return lax.broadcasted_iota(jnp.int32, (SUB, LANES), 0)


def cell_terms(u):
    h, mu, mv = u
    r = pl.reciprocal(jnp.maximum(h, depth_floor * DEPTH_UNIT), approx=True)
    vx, vy = mu * r, mv * r
    hp = jnp.maximum(h, TINY)
    c = hp * lax.rsqrt(hp)
    p = (0.5 * h) * h
    cross = mu * vy
    return {
        "u": u,
        "fx": (mu, mu * vx + p, cross),
        "fy": (mv, cross, mv * vy + p),
        "sx": jnp.abs(vx) + c,
        "sy": jnp.abs(vy) + c,
    }


def x_part(even, odd, first, last):
    left = functools.partial(pltpu.roll, shift=LANES - 1, axis=1)
    right = functools.partial(pltpu.roll, shift=1, axis=1)
    after = cell_terms([jnp.where(last, o, left(e)) for e, o in zip(even["u"], odd["u"])])
    a_in = jnp.maximum(even["sx"], odd["sx"])
    a_out = jnp.maximum(odd["sx"], after["sx"])
    new_even, new_odd = [], []
    for i in range(3):
        e, o, n = even["u"][i], odd["u"][i], after["u"][i]
        f_e, f_o, f_n = even["fx"][i], odd["fx"][i], after["fx"][i]
        g_in = a_in * (o - e) - (f_e + f_o)
        g_out = a_out * (n - o) - (f_o + f_n)
        g_back = jnp.where(first, -2.0 * f_e, right(g_out))
        new_even.append(e + (g_in - g_back))
        new_odd.append(o + (g_out - g_in))
    return new_even, new_odd


def y_face(above, below):
    a = jnp.maximum(above["sy"], below["sy"])
    return [
        a * (ub - ua) - (fa + fb)
        for ua, ub, fa, fb in zip(above["u"], below["u"], above["fy"], below["fy"])
    ]


def coast_steps(state, rows, group, steps, ghost):
    lane, sub = lane_ids(), row_ids()
    first, last = lane == 0, lane == LANES - 1
    top, bottom = sub == 0, sub == SUB - 1
    zero = jnp.zeros((SUB, LANES), jnp.float32)

    def load(k):
        return [cell_terms([state[f, half, 1 + k] for f in range(3)]) for half in range(2)]

    def store(k, both):
        for half in range(2):
            for f in range(3):
                state[f, half, 1 + k] = both[half][f]

    def faces_of(cells):
        return [
            {"u": list(cell["u"]), "fy": list(cell["fy"]), "sy": cell["sy"]} for cell in cells
        ]

    def wrapped(tail, head):
        down = functools.partial(pltpu.roll, shift=1, axis=0)
        out = {"sy": jnp.where(top, head["sy"], down(tail["sy"]))}
        for name in ("u", "fy"):
            out[name] = [jnp.where(top, h, down(t)) for h, t in zip(head[name], tail[name])]
        return out

    def step(_, carry):
        tails, heads = load(rows - 1), load(0)
        above = [wrapped(t, h) for t, h in zip(tails, ghost)]
        start = [y_face(a, b) for a, b in zip(above, heads)]

        def rows_from(begin, prev, acc):
            for k in range(group):
                cur = load(begin + k)
                face = [y_face(a, b) for a, b in zip(prev, cur)]
                store(begin + k - 1, [[x + g for x, g in zip(*pair)] for pair in zip(acc, face)])
                acc = x_part(cur[0], cur[1], first, last)
                acc = [[x - g for x, g in zip(*pair)] for pair in zip(acc, face)]
                prev = faces_of(cur)
            return prev, acc

        prev, acc = lax.fori_loop(
            0,
            rows // group,
            lambda i, c: rows_from(i * group, *c),
            (above, [[zero] * 3 for _ in range(2)]),
        )
        end = [
            [
                jnp.where(bottom, -(f + f), pltpu.roll(g, SUB - 1, 0))
                for f, g in zip(cell["fy"], gs)
            ]
            for cell, gs in zip(prev, start)
        ]
        store(rows - 1, [[x + g for x, g in zip(*pair)] for pair in zip(acc, end)])
        return carry

    lax.fori_loop(0, steps, step, 0)


GROUP = 16
UNITS = (DEPTH_UNIT, FLOW_UNIT, FLOW_UNIT)
VMEM_LIMIT = 12 * 1024 * 1024
HALF = LANES // 2


def pick(values, ids):
    return jnp.take_along_axis(values, ids, axis=1, mode="promise_in_bounds")


def split_columns(west, east):
    lane = lane_ids()
    low = lane < HALF
    twice = 2 * jnp.where(low, lane, lane - HALF)
    w = pick(west, jnp.where(low, twice, twice + 1))
    e = pick(east, jnp.where(low, twice + 1, twice))
    return jnp.where(low, w, e), pltpu.roll(jnp.where(low, e, w), HALF, 1)


def join_columns(even, odd):
    lane = lane_ids()
    low = lane < HALF
    odd = pltpu.roll(odd, HALF, 1)
    w, e = jnp.where(low, even, odd), jnp.where(low, odd, even)
    half, is_odd = lane // 2, lane % 2
    return pick(w, half + HALF * is_odd), pick(e, half + HALF * (1 - is_odd))


def coast_kernel(link, ghosts, depth, flow, out, state, tmp):
    rows = depth.shape[0] // SUB
    halves = (slice(0, LANES), slice(LANES, 2 * LANES))
    tall = 32

    def copy_in(i, carry):
        at = pl.ds(pl.multiple_of(i * tall, tall), tall)
        for f in range(3):
            raw = depth[at] if f == 0 else flow[f - 1, at]
            out[f, at] = raw
            for p in range(2):
                tmp[f, p, at] = raw[:, halves[p]] * UNITS[f]
        return carry

    def fold(k, carry):
        for f in range(3):
            both = split_columns(*[tmp[f, p, pl.ds(k, SUB, stride=rows), :] for p in range(2)])
            for p in range(2):
                state[f, p, 1 + k] = both[p]
        return carry

    def unfold(k, carry):
        for f in range(3):
            both = join_columns(state[f, 0, 1 + k], state[f, 1, 1 + k])
            for p in range(2):
                tmp[f, p, pl.ds(k, SUB, stride=rows), :] = both[p]
        return carry

    def copy_out(i, carry):
        at = pl.ds(pl.multiple_of(i * tall, tall), tall)
        for f in range(3):
            for p in range(2):
                out[f, at, halves[p]] = tmp[f, p, at] * (1.0 / UNITS[f])
        return carry

    lax.fori_loop(0, depth.shape[0] // tall, copy_in, 0)

    @pl.when(link[0, 2] > 0)
    def _():
        lax.fori_loop(0, rows, fold, 0, unroll=4)
        values = jnp.sum(ghosts[...], axis=0)
        level = (ghost_level + values[0:1]) * DEPTH_UNIT
        inflow = values[1:2] * FLOW_UNIT
        spread = [jnp.broadcast_to(v[:, half], (SUB, LANES)) for v in (level, inflow) for half in halves]
        h, mv = split_columns(*spread[:2]), split_columns(*spread[2:])
        ghost = [cell_terms([h[p], jnp.zeros_like(h[p]), mv[p]]) for p in range(2)]
        coast_steps(state, rows, GROUP, CSTEPS, ghost)
        lax.fori_loop(0, rows, unfold, 0, unroll=4)
        lax.fori_loop(0, depth.shape[0] // tall, copy_out, 0)


def coast_run(link, ghosts, depth, flow):
    cells = depth.shape[0]
    vmem = pl.BlockSpec(memory_space=pltpu.VMEM)
    return pl.pallas_call(
        coast_kernel,
        out_shape=jax.ShapeDtypeStruct((3, cells, cells), jnp.float32),
        in_specs=[pl.BlockSpec(memory_space=pltpu.SMEM), vmem, vmem, vmem],
        out_specs=vmem,
        scratch_shapes=[
            pltpu.VMEM((3, 2, 1 + cells // SUB, SUB, LANES), jnp.float32),
            pltpu.VMEM((3, 2, cells, LANES), jnp.float32),
        ],
        compiler_params=pltpu.CompilerParams(vmem_limit_bytes=VMEM_LIMIT),
        cost_estimate=pl.CostEstimate(
            flops=CSTEPS * 70 * cells * cells, bytes_accessed=24 * cells * cells, transcendentals=0
        ),
        name="coast_steps",
    )(link, ghosts, depth, flow)


def basin_kernel(own, pair, edge, out, eta, hu, hv, dep):
    rows, width = own.shape[1], own.shape[2]
    total = rows + 2 * HALO
    chunks = width // LANES
    position = lax.axis_index("row")
    odd = position % 2
    north_inside = (position < lax.axis_size("row") - 1).astype(jnp.float32)
    pair_from = pl.multiple_of(odd * (rows - HALO), HALO)
    pair_at = pl.multiple_of((1 - odd) * (HALO + rows), HALO)
    edge_at = pl.multiple_of(odd * (HALO + rows), HALO)
    for ref, field, unit in ((eta, 0, 1.0), (hu, 1, 0.5), (hv, 2, 0.5), (dep, 3, 0.25)):
        ref[HALO : HALO + rows] = own[field] * unit
        ref[pl.ds(pair_at, HALO)] = pair[field, pl.ds(pair_from, HALO)] * unit
        ref[pl.ds(edge_at, HALO)] = edge[field] * unit
    lane = lax.broadcasted_iota(jnp.int32, (total, LANES), 1)
    first, last = lane == 0, lane == LANES - 1
    row = lax.broadcasted_iota(jnp.int32, (total, LANES), 0)
    kept = jnp.where(row < HALO + rows, 1.0, north_inside)

    def step(_, carry):
        prev_west = jnp.zeros((total, LANES), jnp.float32)
        prev_eta, prev_east, prev_hu = None, None, None
        for c in range(chunks + 1):
            if c < chunks:
                at = slice(c * LANES, (c + 1) * LANES)
                u, v = hu[:, at], hv[:, at]
                west = pltpu.roll(u, 1, 1)
                du = u - jnp.where(first, prev_west, west)
                dv = v - pltpu.roll(v, 1, 0)
                new = (eta[:, at] - (du + dv)) * kept
                eta[:, at] = new
                east = pltpu.roll(new, LANES - 1, 1)
                hv[:, at] = v - dep[:, at] * (pltpu.roll(new, total - 1, 0) - new)
            else:
                east = jnp.zeros((total, LANES), jnp.float32)
            if c > 0:
                back = slice((c - 1) * LANES, c * LANES)
                hu[:, back] = prev_hu - dep[:, back] * (jnp.where(last, east, prev_east) - prev_eta)
            prev_west, prev_eta, prev_east, prev_hu = west, new, east, u
        return carry

    lax.fori_loop(0, BSTEPS, step, 0)
    own = slice(HALO, HALO + rows)
    out[0] = eta[own]
    out[1] = hu[own] * 2.0
    out[2] = hv[own] * 2.0


def basin_run(own, pair, edge):
    rows, width = own.shape[1:]
    total = rows + 2 * HALO
    vmem = pl.BlockSpec(memory_space=pltpu.VMEM)
    return pl.pallas_call(
        basin_kernel,
        out_shape=jax.ShapeDtypeStruct((3, rows, width), jnp.float32),
        in_specs=[vmem, vmem, vmem],
        out_specs=vmem,
        scratch_shapes=[pltpu.VMEM((total, width), jnp.float32)] * 4,
        compiler_params=pltpu.CompilerParams(vmem_limit_bytes=VMEM_LIMIT),
        cost_estimate=pl.CostEstimate(
            flops=BSTEPS * 16 * total * width, bytes_accessed=4 * 11 * rows * width, transcendentals=0
        ),
        name="basin_steps",
    )(own, pair, edge)


def pack_kernel(link, state, depth, own, edge, sent, sems):
    rows = depth.shape[0]
    odd = lax.axis_index("row") % 2
    edge_rows = pl.ds(pl.multiple_of(odd * (rows - HALO), HALO), HALO)
    copies = [
        pltpu.make_async_copy(state, own.at[:3], sems.at[0]),
        pltpu.make_async_copy(depth, own.at[3], sems.at[1]),
        pltpu.make_async_copy(state.at[:, edge_rows], edge.at[:3], sems.at[2]),
        pltpu.make_async_copy(depth.at[edge_rows], edge.at[3], sems.at[3]),
    ]
    for copy in copies:
        copy.start()
    for b in range(sent.shape[0]):
        sent[b] = link[...]
    for copy in copies:
        copy.wait()


def pack(link, state, depth, peers):
    vmem = pl.BlockSpec(memory_space=pltpu.VMEM)
    hbm = pl.BlockSpec(memory_space=pltpu.HBM)
    rows, width = depth.shape
    return pl.pallas_call(
        pack_kernel,
        out_shape=(
            jax.ShapeDtypeStruct((4, rows, width), jnp.float32),
            jax.ShapeDtypeStruct((4, HALO, width), jnp.float32),
            jax.ShapeDtypeStruct((peers,) + link.shape, link.dtype),
        ),
        in_specs=[vmem, hbm, hbm],
        out_specs=(vmem, vmem, vmem),
        scratch_shapes=[pltpu.SemaphoreType.DMA((4,))],
        compiler_params=pltpu.CompilerParams(vmem_limit_bytes=VMEM_LIMIT),
        name="pack",
    )(link, state, depth)


def strips_kernel(links, own, pair, ghosts, strips):
    rows, width = own.shape[1], own.shape[2]
    count, cells = ghosts.shape[0], ghosts.shape[2]
    span = 2 * LANES
    position = lax.axis_index("row")
    tops = (position * rows, (position + 1 - 2 * (position % 2)) * rows)

    def piece(b, carry):
        col = links[b, 0, 1]
        start = jnp.clip(col // LANES, 0, width // LANES - 2) * LANES
        shift = lax.rem(span - (col - start), span)
        at = pl.ds(pl.multiple_of(start, LANES), span)
        for i, f in enumerate((0, 2)):
            chunk = None
            for source, top in zip((own, pair), tops):
                row = links[b, 0, 0] - top
                owned = jnp.logical_and(row >= 0, row < rows).astype(jnp.float32)
                part = source[f, pl.ds(jnp.clip(row, 0, rows - 1), 1), at] * owned
                chunk = part if chunk is None else chunk + part
            strips[pl.ds(2 * b + i, 1), :] = pltpu.roll(chunk, shift, 1)[:, :LANES]
        return carry

    lax.fori_loop(0, count, piece, 0, unroll=8)
    at = lax.broadcasted_iota(jnp.int32, (LANES, cells), 0)
    cols = lax.broadcasted_iota(jnp.int32, (LANES, cells), 1)
    base = cols // 16
    weight = ((cols % 16).astype(jnp.float32) + 0.5) / 16.0
    mix = jnp.where(at == base, 1.0 - weight, 0.0) + jnp.where(at == base + 1, weight, 0.0)
    values = jnp.dot(
        strips[...], mix, precision=lax.Precision.HIGHEST, preferred_element_type=jnp.float32
    )
    for b in range(count):
        ghosts[b] = values[2 * b : 2 * b + 2]


def make_strips(links, own, pair, cells):
    count = links.shape[0]
    vmem = pl.BlockSpec(memory_space=pltpu.VMEM)
    smem = pl.BlockSpec(memory_space=pltpu.SMEM)
    return pl.pallas_call(
        strips_kernel,
        out_shape=jax.ShapeDtypeStruct((count, 2, cells), jnp.float32),
        in_specs=[smem, vmem, vmem],
        out_specs=vmem,
        scratch_shapes=[pltpu.VMEM((2 * count, LANES), jnp.float32)],
        compiler_params=pltpu.CompilerParams(vmem_limit_bytes=VMEM_LIMIT),
        name="strips",
    )(links, own, pair)


def local(basin_state, basin_depth, coast_depth, coast_flow, coast_link):
    devices = lax.axis_size("row")
    parity = [list(range(p, devices, 2)) for p in range(2)]
    swap = [(i, i ^ 1) for i in range(devices)]
    across = [(i, i + 1) for i in range(1, devices - 1, 2)]
    across += [(j, i) for i, j in across]

    own, edge, sent = pack(coast_link, basin_state, basin_depth, devices // 2)
    pair = lax.ppermute(own, "row", swap)
    edge = lax.ppermute(edge, "row", across)
    links = lax.all_to_all(sent, "row", 0, 0, axis_index_groups=parity, tiled=True)

    basin_out = basin_run(own, pair, edge)
    own, basin_out = lax.optimization_barrier((own, basin_out))
    ghosts = make_strips(links, own, pair, coast_depth.shape[2])
    ghosts = lax.all_to_all(ghosts, "row", 0, 0, axis_index_groups=parity, tiled=True)
    coast_out = coast_run(coast_link, ghosts, coast_depth[0], coast_flow[0])
    return (basin_out, coast_out[None])


def solution(mesh):
    in_specs = (
        P("scen", "row", None),
        P("row", "scen"),
        P("row", "scen", None),
        P("row", "scen", None, None),
        P("row", "scen"),
    )
    out_specs = (P("scen", "row", None), P("row", "scen", None, None))
    return jax.shard_map(local, mesh=mesh, in_specs=in_specs, out_specs=out_specs, check_vma=False)
```

```python
import functools

import jax
import jax.numpy as jnp
from jax import lax
from jax.experimental import pallas as pl
from jax.experimental.pallas import tpu as pltpu
from jax.sharding import PartitionSpec as P

BSTEPS = 8
CSTEPS = 10

depth_floor = 0.2
ghost_level = 2.0

RATE = 0.05
DEPTH_UNIT = RATE * RATE
FLOW_UNIT = RATE * RATE * RATE
TINY = 1e-30

HALO = BSTEPS
SUB = 8
LANES = 128


def lane_ids():
    return lax.broadcasted_iota(jnp.int32, (SUB, LANES), 1)


def row_ids():
    return lax.broadcasted_iota(jnp.int32, (SUB, LANES), 0)


def cell_terms(u):
    h, mu, mv = u
    r = pl.reciprocal(jnp.maximum(h, depth_floor * DEPTH_UNIT), approx=True)
    vx, vy = mu * r, mv * r
    hp = jnp.maximum(h, TINY)
    c = hp * lax.rsqrt(hp)
    p = (0.5 * h) * h
    cross = mu * vy
    return {
        "u": u,
        "fx": (mu, mu * vx + p, cross),
        "fy": (mv, cross, mv * vy + p),
        "sx": jnp.abs(vx) + c,
        "sy": jnp.abs(vy) + c,
    }


def x_part(even, odd, first, last):
    left = functools.partial(pltpu.roll, shift=LANES - 1, axis=1)
    right = functools.partial(pltpu.roll, shift=1, axis=1)
    after = cell_terms([jnp.where(last, o, left(e)) for e, o in zip(even["u"], odd["u"])])
    a_in = jnp.maximum(even["sx"], odd["sx"])
    a_out = jnp.maximum(odd["sx"], after["sx"])
    new_even, new_odd = [], []
    for i in range(3):
        e, o, n = even["u"][i], odd["u"][i], after["u"][i]
        f_e, f_o, f_n = even["fx"][i], odd["fx"][i], after["fx"][i]
        g_in = a_in * (o - e) - (f_e + f_o)
        g_out = a_out * (n - o) - (f_o + f_n)
        g_back = jnp.where(first, -2.0 * f_e, right(g_out))
        new_even.append(e + (g_in - g_back))
        new_odd.append(o + (g_out - g_in))
    return new_even, new_odd


def y_face(above, below):
    a = jnp.maximum(above["sy"], below["sy"])
    return [
        a * (ub - ua) - (fa + fb)
        for ua, ub, fa, fb in zip(above["u"], below["u"], above["fy"], below["fy"])
    ]


def coast_steps(state, rows, group, steps, ghost):
    lane, sub = lane_ids(), row_ids()
    first, last = lane == 0, lane == LANES - 1
    top, bottom = sub == 0, sub == SUB - 1
    zero = jnp.zeros((SUB, LANES), jnp.float32)
    trips = rows // group

    def load(k):
        return [cell_terms([state[f, half, 1 + k] for f in range(3)]) for half in range(2)]

    def store(k, both):
        for half in range(2):
            for f in range(3):
                state[f, half, 1 + k] = both[half][f]

    def added(xs, ys):
        return [[x + y for x, y in zip(*pair)] for pair in zip(xs, ys)]

    def faces_of(cells):
        return [
            {"u": list(cell["u"]), "fy": list(cell["fy"]), "sy": cell["sy"]} for cell in cells
        ]

    def wrapped(tail, head):
        down = functools.partial(pltpu.roll, shift=1, axis=0)
        out = {"sy": jnp.where(top, head["sy"], down(tail["sy"]))}
        for name in ("u", "fy"):
            out[name] = [jnp.where(top, h, down(t)) for h, t in zip(head[name], tail[name])]
        return out

    def trip(j, carry):
        prev, acc, over = carry
        i = lax.rem(j, trips)
        opening = jnp.broadcast_to(i, (SUB, LANES)) == 0
        above = [wrapped(t, g) for t, g in zip(load(rows - 1), ghost)]
        prev = jax.tree.map(lambda a, p: jnp.where(opening, a, p), above, prev)
        for k in range(group):
            cur = load(i * group + k)
            face = [y_face(a, b) for a, b in zip(prev, cur)]
            if k == 0:
                over = [
                    [jnp.where(opening, pltpu.roll(g, SUB - 1, 0), o) for g, o in zip(*pair)]
                    for pair in zip(face, over)
                ]
            store(i * group + k - 1, added(acc, face))
            acc = x_part(cur[0], cur[1], first, last)
            acc = [[x - g for x, g in zip(*pair)] for pair in zip(acc, face)]
            prev = faces_of(cur)
        end = [
            [jnp.where(bottom, -2.0 * f, o) for f, o in zip(cell["fy"], os)]
            for cell, os in zip(prev, over)
        ]
        store(jnp.where(i == trips - 1, rows - 1, -1), added(acc, end))
        return prev, acc, over

    blank = {"u": [zero] * 3, "fy": [zero] * 3, "sy": zero}
    nothing = [[zero] * 3 for _ in range(2)]
    lax.fori_loop(0, steps * trips, trip, ([blank, blank], nothing, nothing))


GROUP = 16
UNITS = (DEPTH_UNIT, FLOW_UNIT, FLOW_UNIT)
VMEM_LIMIT = 12 * 1024 * 1024
HALF = LANES // 2


def pick(values, ids):
    return jnp.take_along_axis(values, ids, axis=1, mode="promise_in_bounds")


def split_columns(west, east):
    lane = lane_ids()
    low = lane < HALF
    twice = 2 * jnp.where(low, lane, lane - HALF)
    w = pick(west, jnp.where(low, twice, twice + 1))
    e = pick(east, jnp.where(low, twice + 1, twice))
    return jnp.where(low, w, e), pltpu.roll(jnp.where(low, e, w), HALF, 1)


def join_columns(even, odd):
    lane = lane_ids()
    low = lane < HALF
    odd = pltpu.roll(odd, HALF, 1)
    w, e = jnp.where(low, even, odd), jnp.where(low, odd, even)
    half, is_odd = lane // 2, lane % 2
    return pick(w, half + HALF * is_odd), pick(e, half + HALF * (1 - is_odd))


def coast_kernel(links, ghosts, depth, flow, out, state, tmp):
    rows = depth.shape[0] // SUB
    halves = (slice(0, LANES), slice(LANES, 2 * LANES))
    tall = 32
    wet = links[0, 0, 2] > 0

    def copy_in(i, carry):
        at = pl.ds(pl.multiple_of(i * tall, tall), tall)
        for f in range(3):
            raw = depth[at] if f == 0 else flow[f - 1, at]
            for p in range(2):
                tmp[f, p, at] = raw[:, halves[p]] * UNITS[f]
        return carry

    def copy_dry(i, carry):
        at = pl.ds(pl.multiple_of(i * tall, tall), tall)
        for f in range(3):
            out[f, at] = depth[at] if f == 0 else flow[f - 1, at]
        return carry

    def fold(k, carry):
        for f in range(3):
            both = split_columns(*[tmp[f, p, pl.ds(k, SUB, stride=rows), :] for p in range(2)])
            for p in range(2):
                state[f, p, 1 + k] = both[p]
        return carry

    def unfold(k, carry):
        for f in range(3):
            both = join_columns(state[f, 0, 1 + k], state[f, 1, 1 + k])
            for p in range(2):
                tmp[f, p, pl.ds(k, SUB, stride=rows), :] = both[p]
        return carry

    def copy_out(i, carry):
        at = pl.ds(pl.multiple_of(i * tall, tall), tall)
        for f in range(3):
            for p in range(2):
                out[f, at, halves[p]] = tmp[f, p, at] * (1.0 / UNITS[f])
        return carry

    @pl.when(jnp.logical_not(wet))
    def _():
        lax.fori_loop(0, depth.shape[0] // tall, copy_dry, 0)

    @pl.when(wet)
    def _():
        lax.fori_loop(0, depth.shape[0] // tall, copy_in, 0)
        lax.fori_loop(0, rows, fold, 0, unroll=16)
        values = ghosts[0]
        level = (ghost_level + values[0:1]) * DEPTH_UNIT
        inflow = values[1:2] * FLOW_UNIT
        spread = [jnp.broadcast_to(v[:, half], (SUB, LANES)) for v in (level, inflow) for half in halves]
        h, mv = split_columns(*spread[:2]), split_columns(*spread[2:])
        ghost = [cell_terms([h[p], jnp.zeros_like(h[p]), mv[p]]) for p in range(2)]
        coast_steps(state, rows, GROUP, CSTEPS, ghost)
        lax.fori_loop(0, rows, unfold, 0, unroll=16)
        lax.fori_loop(0, depth.shape[0] // tall, copy_out, 0)


def coast_run(links, ghosts, depth, flow):
    cells = depth.shape[0]
    vmem = pl.BlockSpec(memory_space=pltpu.VMEM)
    return pl.pallas_call(
        coast_kernel,
        out_shape=jax.ShapeDtypeStruct((3, cells, cells), jnp.float32),
        in_specs=[pl.BlockSpec(memory_space=pltpu.SMEM), vmem, vmem, vmem],
        out_specs=vmem,
        scratch_shapes=[
            pltpu.VMEM((3, 2, 1 + cells // SUB, SUB, LANES), jnp.float32),
            pltpu.VMEM((3, 2, cells, LANES), jnp.float32),
        ],
        compiler_params=pltpu.CompilerParams(vmem_limit_bytes=VMEM_LIMIT),
        cost_estimate=pl.CostEstimate(
            flops=CSTEPS * 70 * cells * cells, bytes_accessed=24 * cells * cells, transcendentals=0
        ),
        name="coast_steps",
    )(links, ghosts, depth, flow)


def basin_kernel(state, depth, pair_state, pair_depth, edge, out, eta, hu, hv, dep):
    rows, width = depth.shape
    total = rows + 2 * HALO
    chunks = width // LANES
    position = lax.axis_index("row")
    odd = position % 2
    north_inside = (position < lax.axis_size("row") - 1).astype(jnp.float32)
    pair_from = pl.multiple_of(odd * (rows - HALO), HALO)
    pair_at = pl.multiple_of((1 - odd) * (HALO + rows), HALO)
    edge_at = pl.multiple_of(odd * (HALO + rows), HALO)
    for ref, field, unit in ((eta, 0, 1.0), (hu, 1, 0.5), (hv, 2, 0.5), (dep, 3, 0.25)):
        own, pair = (depth, pair_depth) if field == 3 else (state.at[field], pair_state.at[field])
        ref[HALO : HALO + rows] = own[...] * unit
        ref[pl.ds(pair_at, HALO)] = pair[pl.ds(pair_from, HALO)] * unit
        ref[pl.ds(edge_at, HALO)] = edge[field] * unit
    lane = lax.broadcasted_iota(jnp.int32, (total, LANES), 1)
    first, last = lane == 0, lane == LANES - 1
    row = lax.broadcasted_iota(jnp.int32, (total, LANES), 0)
    kept = jnp.where(row < HALO + rows, 1.0, north_inside)

    def step(_, carry):
        prev_west = jnp.zeros((total, LANES), jnp.float32)
        prev_eta, prev_east, prev_hu = None, None, None
        for c in range(chunks + 1):
            if c < chunks:
                at = slice(c * LANES, (c + 1) * LANES)
                u, v = hu[:, at], hv[:, at]
                west = pltpu.roll(u, 1, 1)
                du = u - jnp.where(first, prev_west, west)
                dv = v - pltpu.roll(v, 1, 0)
                new = (eta[:, at] - (du + dv)) * kept
                eta[:, at] = new
                east = pltpu.roll(new, LANES - 1, 1)
                hv[:, at] = v - dep[:, at] * (pltpu.roll(new, total - 1, 0) - new)
            else:
                east = jnp.zeros((total, LANES), jnp.float32)
            if c > 0:
                back = slice((c - 1) * LANES, c * LANES)
                hu[:, back] = prev_hu - dep[:, back] * (jnp.where(last, east, prev_east) - prev_eta)
            prev_west, prev_eta, prev_east, prev_hu = west, new, east, u
        return carry

    lax.fori_loop(0, BSTEPS, step, 0)
    own = slice(HALO, HALO + rows)
    out[0] = eta[own]
    out[1] = hu[own] * 2.0
    out[2] = hv[own] * 2.0


def basin_run(state, depth, pair_state, pair_depth, edge):
    rows, width = depth.shape
    total = rows + 2 * HALO
    vmem = pl.BlockSpec(memory_space=pltpu.VMEM)
    return pl.pallas_call(
        basin_kernel,
        out_shape=jax.ShapeDtypeStruct((3, rows, width), jnp.float32),
        in_specs=[vmem] * 5,
        out_specs=vmem,
        scratch_shapes=[pltpu.VMEM((total, width), jnp.float32)] * 4,
        compiler_params=pltpu.CompilerParams(vmem_limit_bytes=VMEM_LIMIT),
        cost_estimate=pl.CostEstimate(
            flops=BSTEPS * 16 * total * width, bytes_accessed=4 * 11 * rows * width, transcendentals=0
        ),
        name="basin_steps",
    )(state, depth, pair_state, pair_depth, edge)


def strips_kernel(links, own, pair, near, far, strips):
    rows, width = own.shape[1], own.shape[2]
    count, cells = links.shape[0], near.shape[2]
    span = 2 * LANES
    position = lax.axis_index("row")
    tops = (position * rows, (position + 1 - 2 * (position % 2)) * rows)

    def piece(b, carry):
        col = links[b, 0, 1]
        start = jnp.clip(col // LANES, 0, width // LANES - 2) * LANES
        shift = lax.rem(span - (col - start), span)
        at = pl.ds(pl.multiple_of(start, LANES), span)
        for i, f in enumerate((0, 2)):
            chunk = None
            for source, top in zip((own, pair), tops):
                row = links[b, 0, 0] - top
                owned = jnp.logical_and(row >= 0, row < rows).astype(jnp.float32)
                part = source[f, pl.ds(jnp.clip(row, 0, rows - 1), 1), at] * owned
                chunk = part if chunk is None else chunk + part
            strips[pl.ds(2 * b + i, 1), :] = pltpu.roll(chunk, shift, 1)[:, :LANES]
        return carry

    lax.fori_loop(0, count, piece, 0, unroll=8)
    at = lax.broadcasted_iota(jnp.int32, (LANES, cells), 0)
    cols = lax.broadcasted_iota(jnp.int32, (LANES, cells), 1)
    base = cols // 16
    weight = ((cols % 16).astype(jnp.float32) + 0.5) / 16.0
    mix = jnp.where(at == base, 1.0 - weight, 0.0) + jnp.where(at == base + 1, weight, 0.0)
    values = jnp.dot(
        strips[...], mix, precision=lax.Precision.HIGHEST, preferred_element_type=jnp.float32
    )
    for b in range(count // 2):
        near[b] = values[2 * b : 2 * b + 2]
        far[b] = values[count + 2 * b : count + 2 * b + 2]


def make_strips(links, own, pair, cells):
    count = links.shape[0]
    vmem = pl.BlockSpec(memory_space=pltpu.VMEM)
    smem = pl.BlockSpec(memory_space=pltpu.SMEM)
    return pl.pallas_call(
        strips_kernel,
        out_shape=(jax.ShapeDtypeStruct((count // 2, 2, cells), jnp.float32),) * 2,
        in_specs=[smem, vmem, vmem],
        out_specs=(vmem, vmem),
        scratch_shapes=[pltpu.VMEM((2 * count, LANES), jnp.float32)],
        compiler_params=pltpu.CompilerParams(vmem_limit_bytes=VMEM_LIMIT),
        name="strips",
    )(links, own, pair)


def swap(values, bit):
    count = lax.axis_size("row")
    return lax.ppermute(values, "row", [(i, i ^ bit) for i in range(count)])


def local(basin_state, basin_depth, coast_depth, coast_flow, coast_link):
    devices = lax.axis_size("row")
    odd = lax.axis_index("row") % 2
    chips = devices // 2
    assert chips & (chips - 1) == 0
    bits = [1 << r for r in range(chips.bit_length() - 1)]

    links = coast_link[None]
    for bit in bits:
        links = jnp.concatenate([links, swap(links, 2 * bit)], axis=0)

    pair_state, pair_depth = swap(basin_state, 1), swap(basin_depth, 1)
    rows = basin_depth.shape[0]
    whole = jnp.concatenate([basin_state, basin_depth[None]], axis=0)
    edge = jnp.where(odd == 1, whole[:, rows - HALO :], whole[:, :HALO])
    across = [(i, i + 1) for i in range(1, devices - 1, 2)]
    edge = lax.ppermute(edge, "row", across + [(j, i) for i, j in across])

    ghosts, far = make_strips(links, basin_state, pair_state, coast_depth.shape[2])
    for bit in reversed(bits):
        ghosts = ghosts + swap(far, 2 * bit)
        ghosts, far = ghosts[: bit // 2], ghosts[bit // 2 :]
    basin_out = basin_run(basin_state, basin_depth, pair_state, pair_depth, edge)
    coast_out = coast_run(links, far, coast_depth[0], coast_flow[0])
    return (basin_out, coast_out[None])


def solution(mesh):
    in_specs = (
        P("scen", "row", None),
        P("row", "scen"),
        P("row", "scen", None),
        P("row", "scen", None, None),
        P("row", "scen"),
    )
    out_specs = (P("scen", "row", None), P("row", "scen", None, None))
    return jax.shard_map(local, mesh=mesh, in_specs=in_specs, out_specs=out_specs, check_vma=False)
```

```python
import functools

import jax
import jax.numpy as jnp
from jax import lax
from jax.experimental import pallas as pl
from jax.experimental.pallas import tpu as pltpu
from jax.sharding import PartitionSpec as P

BSTEPS = 8
CSTEPS = 10

depth_floor = 0.2
ghost_level = 2.0

RATE = 0.05
DEPTH_UNIT = RATE * RATE
FLOW_UNIT = RATE * RATE * RATE
TINY = 1e-30

HALO = BSTEPS
SUB = 8
LANES = 128


def lane_ids():
    return lax.broadcasted_iota(jnp.int32, (SUB, LANES), 1)


def row_ids():
    return lax.broadcasted_iota(jnp.int32, (SUB, LANES), 0)


def cell_terms(u):
    h, mu, mv = u
    r = pl.reciprocal(jnp.maximum(h, depth_floor * DEPTH_UNIT), approx=True)
    vx, vy = mu * r, mv * r
    hp = jnp.maximum(h, TINY)
    c = hp * lax.rsqrt(hp)
    p = (0.5 * h) * h
    cross = mu * vy
    return {
        "u": u,
        "fx": (mu, mu * vx + p, cross),
        "fy": (mv, cross, mv * vy + p),
        "sx": jnp.abs(vx) + c,
        "sy": jnp.abs(vy) + c,
    }


def x_part(even, odd, first, last):
    left = functools.partial(pltpu.roll, shift=LANES - 1, axis=1)
    right = functools.partial(pltpu.roll, shift=1, axis=1)
    after = {
        "u": [jnp.where(last, o, left(e)) for e, o in zip(even["u"], odd["u"])],
        "sx": jnp.where(last, odd["sx"], left(even["sx"])),
    }
    after["fx"] = [after["u"][1]] + [
        jnp.where(last, odd["fx"][i], left(even["fx"][i])) for i in (1, 2)
    ]
    a_in = jnp.maximum(even["sx"], odd["sx"])
    a_out = jnp.maximum(odd["sx"], after["sx"])
    new_even, new_odd = [], []
    for i in range(3):
        e, o, n = even["u"][i], odd["u"][i], after["u"][i]
        f_e, f_o, f_n = even["fx"][i], odd["fx"][i], after["fx"][i]
        g_in = a_in * (o - e) - (f_e + f_o)
        g_out = a_out * (n - o) - (f_o + f_n)
        g_back = jnp.where(first, -2.0 * f_e, right(g_out))
        new_even.append(e + (g_in - g_back))
        new_odd.append(o + (g_out - g_in))
    return new_even, new_odd


def y_face(above, below):
    a = jnp.maximum(above["sy"], below["sy"])
    return [
        a * (ub - ua) - (fa + fb)
        for ua, ub, fa, fb in zip(above["u"], below["u"], above["fy"], below["fy"])
    ]


def coast_steps(state, rows, group, steps, ghost):
    lane, sub = lane_ids(), row_ids()
    first, last = lane == 0, lane == LANES - 1
    top, bottom = sub == 0, sub == SUB - 1
    zero = jnp.zeros((SUB, LANES), jnp.float32)

    def load(k):
        return [cell_terms([state[f, half, 1 + k] for f in range(3)]) for half in range(2)]

    def store(k, both):
        for half in range(2):
            for f in range(3):
                state[f, half, 1 + k] = both[half][f]

    def faces_of(cells):
        return [
            {"u": list(cell["u"]), "fy": list(cell["fy"]), "sy": cell["sy"]} for cell in cells
        ]

    def wrapped(tail, head):
        down = functools.partial(pltpu.roll, shift=1, axis=0)
        out = {"sy": jnp.where(top, head["sy"], down(tail["sy"]))}
        for name in ("u", "fy"):
            out[name] = [jnp.where(top, h, down(t)) for h, t in zip(head[name], tail[name])]
        return out

    def step(_, carry):
        tails, heads = load(rows - 1), load(0)
        above = [wrapped(t, h) for t, h in zip(tails, ghost)]
        start = [y_face(a, b) for a, b in zip(above, heads)]

        def rows_from(begin, prev, acc):
            for k in range(group):
                cur = load(begin + k)
                face = [y_face(a, b) for a, b in zip(prev, cur)]
                store(begin + k - 1, [[x + g for x, g in zip(*pair)] for pair in zip(acc, face)])
                acc = x_part(cur[0], cur[1], first, last)
                acc = [[x - g for x, g in zip(*pair)] for pair in zip(acc, face)]
                prev = faces_of(cur)
            return prev, acc

        prev, acc = lax.fori_loop(
            0,
            rows // group,
            lambda i, c: rows_from(i * group, *c),
            (above, [[zero] * 3 for _ in range(2)]),
        )
        end = [
            [
                jnp.where(bottom, -(f + f), pltpu.roll(g, SUB - 1, 0))
                for f, g in zip(cell["fy"], gs)
            ]
            for cell, gs in zip(prev, start)
        ]
        store(rows - 1, [[x + g for x, g in zip(*pair)] for pair in zip(acc, end)])
        return carry

    lax.fori_loop(0, steps, step, 0)


GROUP = 16
UNITS = (DEPTH_UNIT, FLOW_UNIT, FLOW_UNIT)
VMEM_LIMIT = 12 * 1024 * 1024
HALF = LANES // 2


def pick(values, ids):
    return jnp.take_along_axis(values, ids, axis=1, mode="promise_in_bounds")


def split_columns(west, east):
    lane = lane_ids()
    low = lane < HALF
    twice = 2 * jnp.where(low, lane, lane - HALF)
    w = pick(west, jnp.where(low, twice, twice + 1))
    e = pick(east, jnp.where(low, twice + 1, twice))
    return jnp.where(low, w, e), pltpu.roll(jnp.where(low, e, w), HALF, 1)


def join_columns(even, odd):
    lane = lane_ids()
    low = lane < HALF
    odd = pltpu.roll(odd, HALF, 1)
    w, e = jnp.where(low, even, odd), jnp.where(low, odd, even)
    half, is_odd = lane // 2, lane % 2
    return pick(w, half + HALF * is_odd), pick(e, half + HALF * (1 - is_odd))


def coast_kernel(links, ghosts, depth, flow, out, state, tmp):
    rows = depth.shape[0] // SUB
    halves = (slice(0, LANES), slice(LANES, 2 * LANES))
    tall = 32
    wet = links[0, 0, 2] > 0

    def copy_in(i, carry):
        at = pl.ds(pl.multiple_of(i * tall, tall), tall)
        for f in range(3):
            raw = depth[at] if f == 0 else flow[f - 1, at]
            for p in range(2):
                tmp[f, p, at] = raw[:, halves[p]] * UNITS[f]
        return carry

    def copy_dry(i, carry):
        at = pl.ds(pl.multiple_of(i * tall, tall), tall)
        for f in range(3):
            out[f, at] = depth[at] if f == 0 else flow[f - 1, at]
        return carry

    def fold(k, carry):
        for f in range(3):
            both = split_columns(*[tmp[f, p, pl.ds(k, SUB, stride=rows), :] for p in range(2)])
            for p in range(2):
                state[f, p, 1 + k] = both[p]
        return carry

    def unfold(k, carry):
        for f in range(3):
            both = join_columns(state[f, 0, 1 + k], state[f, 1, 1 + k])
            for p in range(2):
                tmp[f, p, pl.ds(k, SUB, stride=rows), :] = both[p]
        return carry

    def copy_out(i, carry):
        at = pl.ds(pl.multiple_of(i * tall, tall), tall)
        for f in range(3):
            for p in range(2):
                out[f, at, halves[p]] = tmp[f, p, at] * (1.0 / UNITS[f])
        return carry

    @pl.when(jnp.logical_not(wet))
    def _():
        lax.fori_loop(0, depth.shape[0] // tall, copy_dry, 0)

    @pl.when(wet)
    def _():
        lax.fori_loop(0, depth.shape[0] // tall, copy_in, 0)
        lax.fori_loop(0, rows, fold, 0, unroll=4)
        values = jnp.sum(ghosts[...], axis=0)
        level = (ghost_level + values[0:1]) * DEPTH_UNIT
        inflow = values[1:2] * FLOW_UNIT
        spread = [jnp.broadcast_to(v[:, half], (SUB, LANES)) for v in (level, inflow) for half in halves]
        h, mv = split_columns(*spread[:2]), split_columns(*spread[2:])
        ghost = [cell_terms([h[p], jnp.zeros_like(h[p]), mv[p]]) for p in range(2)]
        coast_steps(state, rows, GROUP, CSTEPS, ghost)
        lax.fori_loop(0, rows, unfold, 0, unroll=4)
        lax.fori_loop(0, depth.shape[0] // tall, copy_out, 0)


def coast_run(links, ghosts, depth, flow):
    cells = depth.shape[0]
    vmem = pl.BlockSpec(memory_space=pltpu.VMEM)
    return pl.pallas_call(
        coast_kernel,
        out_shape=jax.ShapeDtypeStruct((3, cells, cells), jnp.float32),
        in_specs=[pl.BlockSpec(memory_space=pltpu.SMEM), vmem, vmem, vmem],
        out_specs=vmem,
        scratch_shapes=[
            pltpu.VMEM((3, 2, 1 + cells // SUB, SUB, LANES), jnp.float32),
            pltpu.VMEM((3, 2, cells, LANES), jnp.float32),
        ],
        compiler_params=pltpu.CompilerParams(vmem_limit_bytes=VMEM_LIMIT),
        cost_estimate=pl.CostEstimate(
            flops=CSTEPS * 70 * cells * cells, bytes_accessed=24 * cells * cells, transcendentals=0
        ),
        name="coast_steps",
    )(links, ghosts, depth, flow)


def basin_kernel(state, depth, pair_state, pair_depth, edge, out, eta, hu, hv, dep):
    rows, width = depth.shape
    total = rows + 2 * HALO
    chunks = width // LANES
    position = lax.axis_index("row")
    odd = position % 2
    north_inside = (position < lax.axis_size("row") - 1).astype(jnp.float32)
    pair_from = pl.multiple_of(odd * (rows - HALO), HALO)
    pair_at = pl.multiple_of((1 - odd) * (HALO + rows), HALO)
    edge_at = pl.multiple_of(odd * (HALO + rows), HALO)
    for ref, field, unit in ((eta, 0, 1.0), (hu, 1, 0.5), (hv, 2, 0.5), (dep, 3, 0.25)):
        own, pair = (depth, pair_depth) if field == 3 else (state.at[field], pair_state.at[field])
        ref[HALO : HALO + rows] = own[...] * unit
        ref[pl.ds(pair_at, HALO)] = pair[pl.ds(pair_from, HALO)] * unit
        ref[pl.ds(edge_at, HALO)] = edge[field] * unit
    lane = lax.broadcasted_iota(jnp.int32, (total, LANES), 1)
    first, last = lane == 0, lane == LANES - 1
    row = lax.broadcasted_iota(jnp.int32, (total, LANES), 0)
    kept = jnp.where(row < HALO + rows, 1.0, north_inside)

    def step(_, carry):
        prev_west = jnp.zeros((total, LANES), jnp.float32)
        prev_eta, prev_east, prev_hu = None, None, None
        for c in range(chunks + 1):
            if c < chunks:
                at = slice(c * LANES, (c + 1) * LANES)
                u, v = hu[:, at], hv[:, at]
                west = pltpu.roll(u, 1, 1)
                du = u - jnp.where(first, prev_west, west)
                dv = v - pltpu.roll(v, 1, 0)
                new = (eta[:, at] - (du + dv)) * kept
                eta[:, at] = new
                east = pltpu.roll(new, LANES - 1, 1)
                hv[:, at] = v - dep[:, at] * (pltpu.roll(new, total - 1, 0) - new)
            else:
                east = jnp.zeros((total, LANES), jnp.float32)
            if c > 0:
                back = slice((c - 1) * LANES, c * LANES)
                hu[:, back] = prev_hu - dep[:, back] * (jnp.where(last, east, prev_east) - prev_eta)
            prev_west, prev_eta, prev_east, prev_hu = west, new, east, u
        return carry

    lax.fori_loop(0, BSTEPS, step, 0)
    own = slice(HALO, HALO + rows)
    out[0] = eta[own]
    out[1] = hu[own] * 2.0
    out[2] = hv[own] * 2.0


def basin_run(state, depth, pair_state, pair_depth, edge):
    rows, width = depth.shape
    total = rows + 2 * HALO
    vmem = pl.BlockSpec(memory_space=pltpu.VMEM)
    return pl.pallas_call(
        basin_kernel,
        out_shape=jax.ShapeDtypeStruct((3, rows, width), jnp.float32),
        in_specs=[vmem] * 5,
        out_specs=vmem,
        scratch_shapes=[pltpu.VMEM((total, width), jnp.float32)] * 4,
        compiler_params=pltpu.CompilerParams(vmem_limit_bytes=VMEM_LIMIT),
        cost_estimate=pl.CostEstimate(
            flops=BSTEPS * 16 * total * width, bytes_accessed=4 * 11 * rows * width, transcendentals=0
        ),
        name="basin_steps",
    )(state, depth, pair_state, pair_depth, edge)


def strips_kernel(links, own, pair, ghosts, strips):
    rows, width = own.shape[1], own.shape[2]
    count, cells = ghosts.shape[0], ghosts.shape[2]
    span = 2 * LANES
    position = lax.axis_index("row")
    tops = (position * rows, (position + 1 - 2 * (position % 2)) * rows)

    def piece(b, carry):
        col = links[b, 0, 1]
        start = jnp.clip(col // LANES, 0, width // LANES - 2) * LANES
        shift = lax.rem(span - (col - start), span)
        at = pl.ds(pl.multiple_of(start, LANES), span)
        for i, f in enumerate((0, 2)):
            chunk = None
            for source, top in zip((own, pair), tops):
                row = links[b, 0, 0] - top
                owned = jnp.logical_and(row >= 0, row < rows).astype(jnp.float32)
                part = source[f, pl.ds(jnp.clip(row, 0, rows - 1), 1), at] * owned
                chunk = part if chunk is None else chunk + part
            strips[pl.ds(2 * b + i, 1), :] = pltpu.roll(chunk, shift, 1)[:, :LANES]
        return carry

    lax.fori_loop(0, count, piece, 0, unroll=8)
    at = lax.broadcasted_iota(jnp.int32, (LANES, cells), 0)
    cols = lax.broadcasted_iota(jnp.int32, (LANES, cells), 1)
    base = cols // 16
    weight = ((cols % 16).astype(jnp.float32) + 0.5) / 16.0
    mix = jnp.where(at == base, 1.0 - weight, 0.0) + jnp.where(at == base + 1, weight, 0.0)
    values = jnp.dot(
        strips[...], mix, precision=lax.Precision.HIGHEST, preferred_element_type=jnp.float32
    )
    for b in range(count):
        ghosts[b] = values[2 * b : 2 * b + 2]


def make_strips(links, own, pair, cells):
    count = links.shape[0]
    vmem = pl.BlockSpec(memory_space=pltpu.VMEM)
    smem = pl.BlockSpec(memory_space=pltpu.SMEM)
    return pl.pallas_call(
        strips_kernel,
        out_shape=jax.ShapeDtypeStruct((count, 2, cells), jnp.float32),
        in_specs=[smem, vmem, vmem],
        out_specs=vmem,
        scratch_shapes=[pltpu.VMEM((2 * count, LANES), jnp.float32)],
        compiler_params=pltpu.CompilerParams(vmem_limit_bytes=VMEM_LIMIT),
        name="strips",
    )(links, own, pair)


def local(basin_state, basin_depth, coast_depth, coast_flow, coast_link):
    devices = lax.axis_size("row")
    odd = lax.axis_index("row") % 2
    parity = [list(range(p, devices, 2)) for p in range(2)]
    sent = jnp.broadcast_to(coast_link, (devices // 2,) + coast_link.shape)
    links = lax.all_to_all(sent, "row", 0, 0, axis_index_groups=parity, tiled=True)

    twins = [(i, i ^ 1) for i in range(devices)]
    pair_state, pair_depth = [lax.ppermute(a, "row", twins) for a in (basin_state, basin_depth)]
    rows = basin_depth.shape[0]
    whole = jnp.concatenate([basin_state, basin_depth[None]], axis=0)
    edge = jnp.where(odd == 1, whole[:, rows - HALO :], whole[:, :HALO])
    across = [(i, i + 1) for i in range(1, devices - 1, 2)]
    edge = lax.ppermute(edge, "row", across + [(j, i) for i, j in across])

    ghosts = make_strips(links, basin_state, pair_state, coast_depth.shape[2])
    edge, ghosts = lax.optimization_barrier((edge, ghosts))
    ghosts = lax.all_to_all(ghosts, "row", 0, 0, axis_index_groups=parity, tiled=True)
    basin_out = basin_run(basin_state, basin_depth, pair_state, pair_depth, edge)
    coast_out = coast_run(sent, ghosts, coast_depth[0], coast_flow[0])
    return (basin_out, coast_out[None])


def solution(mesh):
    in_specs = (
        P("scen", "row", None),
        P("row", "scen"),
        P("row", "scen", None),
        P("row", "scen", None, None),
        P("row", "scen"),
    )
    out_specs = (P("scen", "row", None), P("row", "scen", None, None))
    return jax.shard_map(local, mesh=mesh, in_specs=in_specs, out_specs=out_specs, check_vma=False)
```

```python
import functools

import jax
import jax.numpy as jnp
from jax import lax
from jax.experimental import pallas as pl
from jax.experimental.pallas import tpu as pltpu
from jax.sharding import PartitionSpec as P

BSTEPS = 8
CSTEPS = 10

depth_floor = 0.2
ghost_level = 2.0

RATE = 0.05
DEPTH_UNIT = RATE * RATE
FLOW_UNIT = RATE * RATE * RATE
TINY = 1e-30

HALO = BSTEPS
SUB = 8
LANES = 128


def lane_ids():
    return lax.broadcasted_iota(jnp.int32, (SUB, LANES), 1)


def row_ids():
    return lax.broadcasted_iota(jnp.int32, (SUB, LANES), 0)


def cell_terms(u):
    h, mu, mv = u
    r = pl.reciprocal(jnp.maximum(h, depth_floor * DEPTH_UNIT), approx=True)
    vx, vy = mu * r, mv * r
    hp = jnp.maximum(h, TINY)
    c = hp * lax.rsqrt(hp)
    p = (0.5 * h) * h
    cross = mu * vy
    return {
        "u": u,
        "fx": (mu, mu * vx + p, cross),
        "fy": (mv, cross, mv * vy + p),
        "sx": jnp.abs(vx) + c,
        "sy": jnp.abs(vy) + c,
    }


def y_face(above, below):
    a = jnp.maximum(above["sy"], below["sy"])
    return [
        a * (ub - ua) - (fa + fb)
        for ua, ub, fa, fb in zip(above["u"], below["u"], above["fy"], below["fy"])
    ]


def coast_steps(state, terms, after, parts, rows, group, steps, ghost):
    lane, sub = lane_ids(), row_ids()
    first, last = lane == 0, lane == LANES - 1
    top, bottom = sub == 0, sub == SUB - 1
    zero = jnp.zeros((SUB, LANES), jnp.float32)
    left = functools.partial(pltpu.roll, shift=LANES - 1, axis=1)
    right = functools.partial(pltpu.roll, shift=1, axis=1)

    def load(k):
        return [[state[f, half, 1 + k] for f in range(3)] for half in range(2)]

    def store(k, both):
        for half in range(2):
            for f in range(3):
                state[f, half, 1 + k] = both[half][f]

    def wrapped(tail, head):
        down = functools.partial(pltpu.roll, shift=1, axis=0)
        out = {"sy": jnp.where(top, head["sy"], down(tail["sy"]))}
        for name in ("u", "fy"):
            out[name] = [jnp.where(top, h, down(t)) for h, t in zip(head[name], tail[name])]
        return out

    def terms_of(begin, k):
        even, odd = [cell_terms(u) for u in load(begin + k)]
        for half, cell in enumerate((even, odd)):
            for q, value in enumerate((cell["sx"], cell["sy"], cell["fx"][1], cell["fy"][2], cell["fx"][2])):
                terms[half, k, q] = value
        moved = zip(even["u"] + [even["sx"]] + list(even["fx"][1:]), odd["u"] + [odd["sx"]] + list(odd["fx"][1:]))
        for q, (e, o) in enumerate(moved):
            after[k, q] = jnp.where(last, o, left(e))

    def x_faces(begin, k):
        even, odd = load(begin + k)
        following = [after[k, f] for f in range(3)]
        sx_e, sx_o, sx_n = terms[0, k, 0], terms[1, k, 0], after[k, 3]
        fx_e = [even[1], terms[0, k, 2], terms[0, k, 4]]
        fx_o = [odd[1], terms[1, k, 2], terms[1, k, 4]]
        fx_n = [following[1], after[k, 4], after[k, 5]]
        a_in, a_out = jnp.maximum(sx_e, sx_o), jnp.maximum(sx_o, sx_n)
        for f in range(3):
            g_in = a_in * (odd[f] - even[f]) - (fx_e[f] + fx_o[f])
            g_out = a_out * (following[f] - odd[f]) - (fx_o[f] + fx_n[f])
            parts[k, f] = even[f] + g_in
            parts[k, 3 + f] = odd[f] + (g_out - g_in)
            parts[k, 6 + f] = jnp.where(first, -2.0 * fx_e[f], right(g_out))

    def y_cells(begin, k):
        return [
            {"u": u, "fy": [u[2], terms[half, k, 4], terms[half, k, 3]], "sy": terms[half, k, 1]}
            for half, u in enumerate(load(begin + k))
        ]

    def step(_, carry):
        tails, heads = [[cell_terms(u) for u in load(k)] for k in (rows - 1, 0)]
        above = [wrapped(t, g) for t, g in zip(tails, ghost)]
        start = [y_face(a, b) for a, b in zip(above, heads)]

        def rows_from(begin, prev, acc):
            for k in range(group):
                terms_of(begin, k)
            for k in range(group):
                x_faces(begin, k)
            for k in range(group):
                cur = y_cells(begin, k)
                face = [y_face(a, b) for a, b in zip(prev, cur)]
                store(begin + k - 1, [[x + g for x, g in zip(*pair)] for pair in zip(acc, face)])
                acc = [
                    [parts[k, f] - (parts[k, 6 + f] + face[0][f]) for f in range(3)],
                    [parts[k, 3 + f] - face[1][f] for f in range(3)],
                ]
                prev = cur
            return prev, acc

        prev, acc = lax.fori_loop(
            0,
            rows // group,
            lambda i, c: rows_from(i * group, *c),
            (above, [[zero] * 3 for _ in range(2)]),
        )
        end = [
            [
                jnp.where(bottom, -(f + f), pltpu.roll(g, SUB - 1, 0))
                for f, g in zip(cell["fy"], gs)
            ]
            for cell, gs in zip(prev, start)
        ]
        store(rows - 1, [[x + g for x, g in zip(*pair)] for pair in zip(acc, end)])
        return carry

    lax.fori_loop(0, steps, step, 0)


GROUP = 16
UNITS = (DEPTH_UNIT, FLOW_UNIT, FLOW_UNIT)
VMEM_LIMIT = 12 * 1024 * 1024
HALF = LANES // 2


def pick(values, ids):
    return jnp.take_along_axis(values, ids, axis=1, mode="promise_in_bounds")


def split_columns(west, east):
    lane = lane_ids()
    low = lane < HALF
    twice = 2 * jnp.where(low, lane, lane - HALF)
    w = pick(west, jnp.where(low, twice, twice + 1))
    e = pick(east, jnp.where(low, twice + 1, twice))
    return jnp.where(low, w, e), pltpu.roll(jnp.where(low, e, w), HALF, 1)


def join_columns(even, odd):
    lane = lane_ids()
    low = lane < HALF
    odd = pltpu.roll(odd, HALF, 1)
    w, e = jnp.where(low, even, odd), jnp.where(low, odd, even)
    half, is_odd = lane // 2, lane % 2
    return pick(w, half + HALF * is_odd), pick(e, half + HALF * (1 - is_odd))


HALVES = (slice(0, LANES), slice(LANES, 2 * LANES))
TALL = 32


def fold_kernel(depth, flow, state, tmp):
    rows = depth.shape[0] // SUB

    def copy_in(i, carry):
        at = pl.ds(pl.multiple_of(i * TALL, TALL), TALL)
        for f in range(3):
            raw = depth[at] if f == 0 else flow[f - 1, at]
            for p in range(2):
                tmp[f, p, at] = raw[:, HALVES[p]] * UNITS[f]
        return carry

    def fold(k, carry):
        for f in range(3):
            both = split_columns(*[tmp[f, p, pl.ds(k, SUB, stride=rows), :] for p in range(2)])
            for p in range(2):
                state[f, p, k] = both[p]
        return carry

    lax.fori_loop(0, depth.shape[0] // TALL, copy_in, 0)
    lax.fori_loop(0, rows, fold, 0, unroll=4)


def coast_fold(depth, flow):
    cells = depth.shape[0]
    vmem = pl.BlockSpec(memory_space=pltpu.VMEM)
    return pl.pallas_call(
        fold_kernel,
        out_shape=jax.ShapeDtypeStruct((3, 2, cells // SUB, SUB, LANES), jnp.float32),
        in_specs=[vmem, vmem],
        out_specs=vmem,
        scratch_shapes=[pltpu.VMEM((3, 2, cells, LANES), jnp.float32)],
        compiler_params=pltpu.CompilerParams(vmem_limit_bytes=VMEM_LIMIT),
        cost_estimate=pl.CostEstimate(
            flops=CSTEPS * 70 * cells * cells, bytes_accessed=24 * cells * cells, transcendentals=0
        ),
        name="coast_fold",
    )(depth, flow)


def coast_kernel(links, ghosts, folded, depth, flow, out, state, terms, after, parts, tmp):
    rows = depth.shape[0] // SUB
    wet = links[0, 0, 2] > 0

    def copy_dry(i, carry):
        at = pl.ds(pl.multiple_of(i * TALL, TALL), TALL)
        for f in range(3):
            out[f, at] = depth[at] if f == 0 else flow[f - 1, at]
        return carry

    def copy_in(k, carry):
        for f in range(3):
            for p in range(2):
                state[f, p, 1 + k] = folded[f, p, k]
        return carry

    def unfold(k, carry):
        for f in range(3):
            both = join_columns(state[f, 0, 1 + k], state[f, 1, 1 + k])
            for p in range(2):
                tmp[f, p, pl.ds(k, SUB, stride=rows), :] = both[p]
        return carry

    def copy_out(i, carry):
        at = pl.ds(pl.multiple_of(i * TALL, TALL), TALL)
        for f in range(3):
            for p in range(2):
                out[f, at, HALVES[p]] = tmp[f, p, at] * (1.0 / UNITS[f])
        return carry

    @pl.when(jnp.logical_not(wet))
    def _():
        lax.fori_loop(0, depth.shape[0] // TALL, copy_dry, 0)

    @pl.when(wet)
    def _():
        lax.fori_loop(0, rows, copy_in, 0, unroll=4)
        values = jnp.sum(ghosts[...], axis=0)
        level = (ghost_level + values[0:1]) * DEPTH_UNIT
        inflow = values[1:2] * FLOW_UNIT
        spread = [jnp.broadcast_to(v[:, half], (SUB, LANES)) for v in (level, inflow) for half in HALVES]
        h, mv = split_columns(*spread[:2]), split_columns(*spread[2:])
        ghost = [cell_terms([h[p], jnp.zeros_like(h[p]), mv[p]]) for p in range(2)]
        coast_steps(state, terms, after, parts, rows, GROUP, CSTEPS, ghost)
        lax.fori_loop(0, rows, unfold, 0, unroll=4)
        lax.fori_loop(0, depth.shape[0] // TALL, copy_out, 0)


def coast_run(links, ghosts, folded, depth, flow):
    cells = depth.shape[0]
    vmem = pl.BlockSpec(memory_space=pltpu.VMEM)
    return pl.pallas_call(
        coast_kernel,
        out_shape=jax.ShapeDtypeStruct((3, cells, cells), jnp.float32),
        in_specs=[pl.BlockSpec(memory_space=pltpu.SMEM), vmem, vmem, vmem, vmem],
        out_specs=vmem,
        scratch_shapes=[
            pltpu.VMEM((3, 2, 1 + cells // SUB, SUB, LANES), jnp.float32),
            pltpu.VMEM((2, GROUP, 5, SUB, LANES), jnp.float32),
            pltpu.VMEM((GROUP, 6, SUB, LANES), jnp.float32),
            pltpu.VMEM((GROUP, 9, SUB, LANES), jnp.float32),
            pltpu.VMEM((3, 2, cells, LANES), jnp.float32),
        ],
        compiler_params=pltpu.CompilerParams(vmem_limit_bytes=VMEM_LIMIT),
        cost_estimate=pl.CostEstimate(
            flops=CSTEPS * 70 * cells * cells, bytes_accessed=24 * cells * cells, transcendentals=0
        ),
        name="coast_steps",
    )(links, ghosts, folded, depth, flow)


def basin_kernel(state, depth, pair_state, pair_depth, edge, out, eta, hu, hv, dep):
    rows, width = depth.shape
    total = rows + 2 * HALO
    chunks = width // LANES
    position = lax.axis_index("row")
    odd = position % 2
    north_inside = (position < lax.axis_size("row") - 1).astype(jnp.float32)
    pair_from = pl.multiple_of(odd * (rows - HALO), HALO)
    pair_at = pl.multiple_of((1 - odd) * (HALO + rows), HALO)
    edge_at = pl.multiple_of(odd * (HALO + rows), HALO)
    for ref, field, unit in ((eta, 0, 1.0), (hu, 1, 0.5), (hv, 2, 0.5), (dep, 3, 0.25)):
        own, pair = (depth, pair_depth) if field == 3 else (state.at[field], pair_state.at[field])
        ref[HALO : HALO + rows] = own[...] * unit
        ref[pl.ds(pair_at, HALO)] = pair[pl.ds(pair_from, HALO)] * unit
        ref[pl.ds(edge_at, HALO)] = edge[field] * unit
    lane = lax.broadcasted_iota(jnp.int32, (total, LANES), 1)
    first, last = lane == 0, lane == LANES - 1
    row = lax.broadcasted_iota(jnp.int32, (total, LANES), 0)
    kept = jnp.where(row < HALO + rows, 1.0, north_inside)

    def step(_, carry):
        prev_west = jnp.zeros((total, LANES), jnp.float32)
        prev_eta, prev_east, prev_hu = None, None, None
        for c in range(chunks + 1):
            if c < chunks:
                at = slice(c * LANES, (c + 1) * LANES)
                u, v = hu[:, at], hv[:, at]
                west = pltpu.roll(u, 1, 1)
                du = u - jnp.where(first, prev_west, west)
                dv = v - pltpu.roll(v, 1, 0)
                new = (eta[:, at] - (du + dv)) * kept
                eta[:, at] = new
                east = pltpu.roll(new, LANES - 1, 1)
                hv[:, at] = v - dep[:, at] * (pltpu.roll(new, total - 1, 0) - new)
            else:
                east = jnp.zeros((total, LANES), jnp.float32)
            if c > 0:
                back = slice((c - 1) * LANES, c * LANES)
                hu[:, back] = prev_hu - dep[:, back] * (jnp.where(last, east, prev_east) - prev_eta)
            prev_west, prev_eta, prev_east, prev_hu = west, new, east, u
        return carry

    lax.fori_loop(0, BSTEPS, step, 0)
    own = slice(HALO, HALO + rows)
    out[0] = eta[own]
    out[1] = hu[own] * 2.0
    out[2] = hv[own] * 2.0


def basin_run(state, depth, pair_state, pair_depth, edge):
    rows, width = depth.shape
    total = rows + 2 * HALO
    vmem = pl.BlockSpec(memory_space=pltpu.VMEM)
    return pl.pallas_call(
        basin_kernel,
        out_shape=jax.ShapeDtypeStruct((3, rows, width), jnp.float32),
        in_specs=[vmem] * 5,
        out_specs=vmem,
        scratch_shapes=[pltpu.VMEM((total, width), jnp.float32)] * 4,
        compiler_params=pltpu.CompilerParams(vmem_limit_bytes=VMEM_LIMIT),
        cost_estimate=pl.CostEstimate(
            flops=BSTEPS * 16 * total * width, bytes_accessed=4 * 11 * rows * width, transcendentals=0
        ),
        name="basin_steps",
    )(state, depth, pair_state, pair_depth, edge)


def strips_kernel(links, own, pair, ghosts, strips):
    rows, width = own.shape[1], own.shape[2]
    count, cells = ghosts.shape[0], ghosts.shape[2]
    span = 2 * LANES
    position = lax.axis_index("row")
    tops = (position * rows, (position + 1 - 2 * (position % 2)) * rows)

    def piece(b, carry):
        col = links[b, 0, 1]
        start = jnp.clip(col // LANES, 0, width // LANES - 2) * LANES
        shift = lax.rem(span - (col - start), span)
        at = pl.ds(pl.multiple_of(start, LANES), span)
        for i, f in enumerate((0, 2)):
            chunk = None
            for source, top in zip((own, pair), tops):
                row = links[b, 0, 0] - top
                owned = jnp.logical_and(row >= 0, row < rows).astype(jnp.float32)
                part = source[f, pl.ds(jnp.clip(row, 0, rows - 1), 1), at] * owned
                chunk = part if chunk is None else chunk + part
            strips[pl.ds(2 * b + i, 1), :] = pltpu.roll(chunk, shift, 1)[:, :LANES]
        return carry

    lax.fori_loop(0, count, piece, 0, unroll=8)
    at = lax.broadcasted_iota(jnp.int32, (LANES, cells), 0)
    cols = lax.broadcasted_iota(jnp.int32, (LANES, cells), 1)
    base = cols // 16
    weight = ((cols % 16).astype(jnp.float32) + 0.5) / 16.0
    mix = jnp.where(at == base, 1.0 - weight, 0.0) + jnp.where(at == base + 1, weight, 0.0)
    values = jnp.dot(
        strips[...], mix, precision=lax.Precision.HIGHEST, preferred_element_type=jnp.float32
    )
    for b in range(count):
        ghosts[b] = values[2 * b : 2 * b + 2]


def make_strips(links, own, pair, cells):
    count = links.shape[0]
    vmem = pl.BlockSpec(memory_space=pltpu.VMEM)
    smem = pl.BlockSpec(memory_space=pltpu.SMEM)
    return pl.pallas_call(
        strips_kernel,
        out_shape=jax.ShapeDtypeStruct((count, 2, cells), jnp.float32),
        in_specs=[smem, vmem, vmem],
        out_specs=vmem,
        scratch_shapes=[pltpu.VMEM((2 * count, LANES), jnp.float32)],
        compiler_params=pltpu.CompilerParams(vmem_limit_bytes=VMEM_LIMIT),
        name="strips",
    )(links, own, pair)


def local(basin_state, basin_depth, coast_depth, coast_flow, coast_link):
    devices = lax.axis_size("row")
    odd = lax.axis_index("row") % 2
    parity = [list(range(p, devices, 2)) for p in range(2)]
    sent = jnp.broadcast_to(coast_link, (devices // 2,) + coast_link.shape)
    links = lax.all_to_all(sent, "row", 0, 0, axis_index_groups=parity, tiled=True)

    depth, flow = coast_depth[0], coast_flow[0]
    folded = coast_fold(depth, flow)
    basin_state, folded = lax.optimization_barrier((basin_state, folded))

    twins = [(i, i ^ 1) for i in range(devices)]
    pair_state, pair_depth = [lax.ppermute(a, "row", twins) for a in (basin_state, basin_depth)]
    rows = basin_depth.shape[0]
    whole = jnp.concatenate([basin_state, basin_depth[None]], axis=0)
    edge = jnp.where(odd == 1, whole[:, rows - HALO :], whole[:, :HALO])
    across = [(i, i + 1) for i in range(1, devices - 1, 2)]
    edge = lax.ppermute(edge, "row", across + [(j, i) for i, j in across])

    ghosts = make_strips(links, basin_state, pair_state, coast_depth.shape[2])
    edge, ghosts = lax.optimization_barrier((edge, ghosts))
    ghosts = lax.all_to_all(ghosts, "row", 0, 0, axis_index_groups=parity, tiled=True)
    basin_out = basin_run(basin_state, basin_depth, pair_state, pair_depth, edge)
    folded, basin_out = lax.optimization_barrier((folded, basin_out))
    coast_out = coast_run(sent, ghosts, folded, depth, flow)
    return (basin_out, coast_out[None])


def solution(mesh):
    in_specs = (
        P("scen", "row", None),
        P("row", "scen"),
        P("row", "scen", None),
        P("row", "scen", None, None),
        P("row", "scen"),
    )
    out_specs = (P("scen", "row", None), P("row", "scen", None, None))
    return jax.shard_map(local, mesh=mesh, in_specs=in_specs, out_specs=out_specs, check_vma=False)
```

```python
import functools

import jax
import jax.numpy as jnp
from jax import lax
from jax.experimental import pallas as pl
from jax.experimental.pallas import tpu as pltpu
from jax.sharding import PartitionSpec as P

BSTEPS = 8
CSTEPS = 10

depth_floor = 0.2
ghost_level = 2.0

RATE = 0.05
DEPTH_UNIT = RATE * RATE
FLOW_UNIT = RATE * RATE * RATE
TINY = 1e-30

HALO = BSTEPS
SUB = 8
LANES = 128


def lane_ids():
    return lax.broadcasted_iota(jnp.int32, (SUB, LANES), 1)


def row_ids():
    return lax.broadcasted_iota(jnp.int32, (SUB, LANES), 0)


def cell_terms(u):
    h, mu, mv = u
    r = pl.reciprocal(jnp.maximum(h, depth_floor * DEPTH_UNIT), approx=True)
    vx, vy = mu * r, mv * r
    hp = jnp.maximum(h, TINY)
    c = hp * lax.rsqrt(hp)
    p = (0.5 * h) * h
    cross = mu * vy
    return {
        "u": u,
        "fx": (mu, mu * vx + p, cross),
        "fy": (mv, cross, mv * vy + p),
        "sx": jnp.abs(vx) + c,
        "sy": jnp.abs(vy) + c,
    }


def y_face(above, below):
    a = jnp.maximum(above["sy"], below["sy"])
    return [
        a * (ub - ua) - (fa + fb)
        for ua, ub, fa, fb in zip(above["u"], below["u"], above["fy"], below["fy"])
    ]


def coast_steps(state, terms, after, parts, opening, rows, group, steps, ghost):
    lane, sub = lane_ids(), row_ids()
    first, last = lane == 0, lane == LANES - 1
    top, bottom = sub == 0, sub == SUB - 1
    zero = jnp.zeros((SUB, LANES), jnp.float32)
    left = functools.partial(pltpu.roll, shift=LANES - 1, axis=1)
    right = functools.partial(pltpu.roll, shift=1, axis=1)

    def load(k):
        return [[state[f, half, 1 + k] for f in range(3)] for half in range(2)]

    def store(k, both):
        for half in range(2):
            for f in range(3):
                state[f, half, 1 + k] = both[half][f]

    def wrapped(tail, head):
        down = functools.partial(pltpu.roll, shift=1, axis=0)
        out = {"sy": jnp.where(top, head["sy"], down(tail["sy"]))}
        for name in ("u", "fy"):
            out[name] = [jnp.where(top, h, down(t)) for h, t in zip(head[name], tail[name])]
        return out

    def terms_of(begin, k):
        even, odd = [cell_terms(u) for u in load(begin + k)]
        for half, cell in enumerate((even, odd)):
            for q, value in enumerate((cell["sx"], cell["sy"], cell["fx"][1], cell["fy"][2], cell["fx"][2])):
                terms[half, k, q] = value
        moved = zip(even["u"] + [even["sx"]] + list(even["fx"][1:]), odd["u"] + [odd["sx"]] + list(odd["fx"][1:]))
        for q, (e, o) in enumerate(moved):
            after[k, q] = jnp.where(last, o, left(e))

    def x_faces(begin, k):
        even, odd = load(begin + k)
        following = [after[k, f] for f in range(3)]
        sx_e, sx_o, sx_n = terms[0, k, 0], terms[1, k, 0], after[k, 3]
        fx_e = [even[1], terms[0, k, 2], terms[0, k, 4]]
        fx_o = [odd[1], terms[1, k, 2], terms[1, k, 4]]
        fx_n = [following[1], after[k, 4], after[k, 5]]
        a_in, a_out = jnp.maximum(sx_e, sx_o), jnp.maximum(sx_o, sx_n)
        for f in range(3):
            g_in = a_in * (odd[f] - even[f]) - (fx_e[f] + fx_o[f])
            g_out = a_out * (following[f] - odd[f]) - (fx_o[f] + fx_n[f])
            parts[k, f] = even[f] + g_in
            parts[k, 3 + f] = odd[f] + (g_out - g_in)
            parts[k, 6 + f] = jnp.where(first, -2.0 * fx_e[f], right(g_out))

    def y_cells(begin, k):
        return [
            {"u": u, "fy": [u[2], terms[half, k, 4], terms[half, k, 3]], "sy": terms[half, k, 1]}
            for half, u in enumerate(load(begin + k))
        ]

    def step(_, carry):
        tails = [cell_terms(u) for u in load(rows - 1)]
        above = [wrapped(t, g) for t, g in zip(tails, ghost)]

        def rows_from(trip, prev, acc):
            begin = trip * group
            for k in range(group):
                terms_of(begin, k)
            for k in range(group):
                x_faces(begin, k)
            for k in range(group):
                cur = y_cells(begin, k)
                face = [y_face(a, b) for a, b in zip(prev, cur)]
                if k == 0:
                    for half in range(2):
                        for f in range(3):
                            opening[trip, half, f] = face[half][f]
                store(begin + k - 1, [[x + g for x, g in zip(*pair)] for pair in zip(acc, face)])
                acc = [
                    [parts[k, f] - (parts[k, 6 + f] + face[0][f]) for f in range(3)],
                    [parts[k, 3 + f] - face[1][f] for f in range(3)],
                ]
                prev = cur
            return prev, acc

        prev, acc = lax.fori_loop(
            0,
            rows // group,
            lambda i, c: rows_from(i, *c),
            (above, [[zero] * 3 for _ in range(2)]),
        )
        end = [
            [
                jnp.where(bottom, -(f + f), pltpu.roll(opening[0, half, i], SUB - 1, 0))
                for i, f in enumerate(cell["fy"])
            ]
            for half, cell in enumerate(prev)
        ]
        store(rows - 1, [[x + g for x, g in zip(*pair)] for pair in zip(acc, end)])
        return carry

    lax.fori_loop(0, steps, step, 0)


GROUP = 16
UNITS = (DEPTH_UNIT, FLOW_UNIT, FLOW_UNIT)
VMEM_LIMIT = 12 * 1024 * 1024
HALF = LANES // 2


def pick(values, ids):
    return jnp.take_along_axis(values, ids, axis=1, mode="promise_in_bounds")


def split_columns(west, east):
    lane = lane_ids()
    low = lane < HALF
    twice = 2 * jnp.where(low, lane, lane - HALF)
    w = pick(west, jnp.where(low, twice, twice + 1))
    e = pick(east, jnp.where(low, twice + 1, twice))
    return jnp.where(low, w, e), pltpu.roll(jnp.where(low, e, w), HALF, 1)


def join_columns(even, odd):
    lane = lane_ids()
    low = lane < HALF
    odd = pltpu.roll(odd, HALF, 1)
    w, e = jnp.where(low, even, odd), jnp.where(low, odd, even)
    half, is_odd = lane // 2, lane % 2
    return pick(w, half + HALF * is_odd), pick(e, half + HALF * (1 - is_odd))


HALVES = (slice(0, LANES), slice(LANES, 2 * LANES))
TALL = 32


def fold_kernel(depth, flow, state, tmp):
    rows = depth.shape[0] // SUB

    def copy_in(i, carry):
        at = pl.ds(pl.multiple_of(i * TALL, TALL), TALL)
        for f in range(3):
            raw = depth[at] if f == 0 else flow[f - 1, at]
            for p in range(2):
                tmp[f, p, at] = raw[:, HALVES[p]] * UNITS[f]
        return carry

    def fold(k, carry):
        for f in range(3):
            both = split_columns(*[tmp[f, p, pl.ds(k, SUB, stride=rows), :] for p in range(2)])
            for p in range(2):
                state[f, p, k] = both[p]
        return carry

    lax.fori_loop(0, depth.shape[0] // TALL, copy_in, 0)
    lax.fori_loop(0, rows, fold, 0, unroll=4)


def coast_fold(depth, flow):
    cells = depth.shape[0]
    vmem = pl.BlockSpec(memory_space=pltpu.VMEM)
    return pl.pallas_call(
        fold_kernel,
        out_shape=jax.ShapeDtypeStruct((3, 2, cells // SUB, SUB, LANES), jnp.float32),
        in_specs=[vmem, vmem],
        out_specs=vmem,
        scratch_shapes=[pltpu.VMEM((3, 2, cells, LANES), jnp.float32)],
        compiler_params=pltpu.CompilerParams(vmem_limit_bytes=VMEM_LIMIT),
        cost_estimate=pl.CostEstimate(
            flops=CSTEPS * 70 * cells * cells, bytes_accessed=24 * cells * cells, transcendentals=0
        ),
        name="coast_fold",
    )(depth, flow)


def coast_kernel(
    links, ghosts, folded, depth, flow, out, state, terms, after, parts, opening, tmp, sems
):
    rows = depth.shape[0] // SUB
    wet = links[0, 0, 2] > 0

    def copy_in(k, carry):
        for f in range(3):
            for p in range(2):
                state[f, p, 1 + k] = folded[f, p, k]
        return carry

    @pl.when(jnp.logical_not(wet))
    def _():
        copies = [
            pltpu.make_async_copy(depth, out.at[0], sems.at[0, 0]),
            pltpu.make_async_copy(flow, out.at[1:], sems.at[0, 1]),
        ]
        for copy in copies:
            copy.start()
        for copy in copies:
            copy.wait()

    @pl.when(wet)
    def _():
        lax.fori_loop(0, rows, copy_in, 0, unroll=4)
        values = jnp.sum(ghosts[...], axis=0)
        level = (ghost_level + values[0:1]) * DEPTH_UNIT
        inflow = values[1:2] * FLOW_UNIT
        spread = [jnp.broadcast_to(v[:, half], (SUB, LANES)) for v in (level, inflow) for half in HALVES]
        h, mv = split_columns(*spread[:2]), split_columns(*spread[2:])
        ghost = [cell_terms([h[p], jnp.zeros_like(h[p]), mv[p]]) for p in range(2)]
        coast_steps(state, terms, after, parts, opening, rows, GROUP, CSTEPS, ghost)
        copies = []
        for f in range(3):

            def unfold(k, carry):
                both = join_columns(state[f, 0, 1 + k], state[f, 1, 1 + k])
                for p in range(2):
                    tmp[f, p, pl.ds(k, SUB, stride=rows), :] = both[p] * (1.0 / UNITS[f])
                return carry

            lax.fori_loop(0, rows, unfold, 0, unroll=8)
            for p in range(2):
                copies.append(
                    pltpu.make_async_copy(tmp.at[f, p], out.at[f, :, HALVES[p]], sems.at[f, p])
                )
                copies[-1].start()
        for copy in copies:
            copy.wait()


def coast_run(links, ghosts, folded, depth, flow):
    cells = depth.shape[0]
    vmem = pl.BlockSpec(memory_space=pltpu.VMEM)
    return pl.pallas_call(
        coast_kernel,
        out_shape=jax.ShapeDtypeStruct((3, cells, cells), jnp.float32),
        in_specs=[pl.BlockSpec(memory_space=pltpu.SMEM), vmem, vmem, vmem, vmem],
        out_specs=pl.BlockSpec(memory_space=pltpu.HBM),
        scratch_shapes=[
            pltpu.VMEM((3, 2, 1 + cells // SUB, SUB, LANES), jnp.float32),
            pltpu.VMEM((2, GROUP, 5, SUB, LANES), jnp.float32),
            pltpu.VMEM((GROUP, 6, SUB, LANES), jnp.float32),
            pltpu.VMEM((GROUP, 9, SUB, LANES), jnp.float32),
            pltpu.VMEM((cells // SUB // GROUP, 2, 3, SUB, LANES), jnp.float32),
            pltpu.VMEM((3, 2, cells, LANES), jnp.float32),
            pltpu.SemaphoreType.DMA((3, 2)),
        ],
        compiler_params=pltpu.CompilerParams(vmem_limit_bytes=VMEM_LIMIT),
        cost_estimate=pl.CostEstimate(
            flops=CSTEPS * 70 * cells * cells, bytes_accessed=24 * cells * cells, transcendentals=0
        ),
        name="coast_steps",
    )(links, ghosts, folded, depth, flow)


def basin_kernel(state, depth, pair_state, pair_depth, edge, out, eta, hu, hv, dep):
    rows, width = depth.shape
    total = rows + 2 * HALO
    chunks = width // LANES
    position = lax.axis_index("row")
    odd = position % 2
    north_inside = (position < lax.axis_size("row") - 1).astype(jnp.float32)
    pair_from = pl.multiple_of(odd * (rows - HALO), HALO)
    pair_at = pl.multiple_of((1 - odd) * (HALO + rows), HALO)
    edge_at = pl.multiple_of(odd * (HALO + rows), HALO)
    for ref, field, unit in ((eta, 0, 1.0), (hu, 1, 0.5), (hv, 2, 0.5), (dep, 3, 0.25)):
        own, pair = (depth, pair_depth) if field == 3 else (state.at[field], pair_state.at[field])
        ref[HALO : HALO + rows] = own[...] * unit
        ref[pl.ds(pair_at, HALO)] = pair[pl.ds(pair_from, HALO)] * unit
        ref[pl.ds(edge_at, HALO)] = edge[field] * unit
    lane = lax.broadcasted_iota(jnp.int32, (total, LANES), 1)
    first, last = lane == 0, lane == LANES - 1
    row = lax.broadcasted_iota(jnp.int32, (total, LANES), 0)
    kept = jnp.where(row < HALO + rows, 1.0, north_inside)

    def step(_, carry):
        prev_west = jnp.zeros((total, LANES), jnp.float32)
        prev_eta, prev_east, prev_hu = None, None, None
        for c in range(chunks + 1):
            if c < chunks:
                at = slice(c * LANES, (c + 1) * LANES)
                u, v = hu[:, at], hv[:, at]
                west = pltpu.roll(u, 1, 1)
                du = u - jnp.where(first, prev_west, west)
                dv = v - pltpu.roll(v, 1, 0)
                new = (eta[:, at] - (du + dv)) * kept
                eta[:, at] = new
                east = pltpu.roll(new, LANES - 1, 1)
                hv[:, at] = v - dep[:, at] * (pltpu.roll(new, total - 1, 0) - new)
            else:
                east = jnp.zeros((total, LANES), jnp.float32)
            if c > 0:
                back = slice((c - 1) * LANES, c * LANES)
                hu[:, back] = prev_hu - dep[:, back] * (jnp.where(last, east, prev_east) - prev_eta)
            prev_west, prev_eta, prev_east, prev_hu = west, new, east, u
        return carry

    lax.fori_loop(0, BSTEPS, step, 0)
    own = slice(HALO, HALO + rows)
    out[0] = eta[own]
    out[1] = hu[own] * 2.0
    out[2] = hv[own] * 2.0


def basin_run(state, depth, pair_state, pair_depth, edge):
    rows, width = depth.shape
    total = rows + 2 * HALO
    vmem = pl.BlockSpec(memory_space=pltpu.VMEM)
    return pl.pallas_call(
        basin_kernel,
        out_shape=jax.ShapeDtypeStruct((3, rows, width), jnp.float32),
        in_specs=[vmem] * 5,
        out_specs=vmem,
        scratch_shapes=[pltpu.VMEM((total, width), jnp.float32)] * 4,
        compiler_params=pltpu.CompilerParams(vmem_limit_bytes=VMEM_LIMIT),
        cost_estimate=pl.CostEstimate(
            flops=BSTEPS * 16 * total * width, bytes_accessed=4 * 11 * rows * width, transcendentals=0
        ),
        name="basin_steps",
    )(state, depth, pair_state, pair_depth, edge)


def strips_kernel(links, own, pair, ghosts, strips):
    rows, width = own.shape[1], own.shape[2]
    count, cells = ghosts.shape[0], ghosts.shape[2]
    span = 2 * LANES
    position = lax.axis_index("row")
    tops = (position * rows, (position + 1 - 2 * (position % 2)) * rows)

    def piece(b, carry):
        col = links[b, 0, 1]
        start = jnp.clip(col // LANES, 0, width // LANES - 2) * LANES
        shift = lax.rem(span - (col - start), span)
        at = pl.ds(pl.multiple_of(start, LANES), span)
        for i, f in enumerate((0, 2)):
            chunk = None
            for source, top in zip((own, pair), tops):
                row = links[b, 0, 0] - top
                owned = jnp.logical_and(row >= 0, row < rows).astype(jnp.float32)
                part = source[f, pl.ds(jnp.clip(row, 0, rows - 1), 1), at] * owned
                chunk = part if chunk is None else chunk + part
            strips[pl.ds(2 * b + i, 1), :] = pltpu.roll(chunk, shift, 1)[:, :LANES]
        return carry

    lax.fori_loop(0, count, piece, 0, unroll=8)
    at = lax.broadcasted_iota(jnp.int32, (LANES, cells), 0)
    cols = lax.broadcasted_iota(jnp.int32, (LANES, cells), 1)
    base = cols // 16
    weight = ((cols % 16).astype(jnp.float32) + 0.5) / 16.0
    mix = jnp.where(at == base, 1.0 - weight, 0.0) + jnp.where(at == base + 1, weight, 0.0)
    values = jnp.dot(
        strips[...], mix, precision=lax.Precision.HIGHEST, preferred_element_type=jnp.float32
    )
    for b in range(count):
        ghosts[b] = values[2 * b : 2 * b + 2]


def make_strips(links, own, pair, cells):
    count = links.shape[0]
    vmem = pl.BlockSpec(memory_space=pltpu.VMEM)
    smem = pl.BlockSpec(memory_space=pltpu.SMEM)
    return pl.pallas_call(
        strips_kernel,
        out_shape=jax.ShapeDtypeStruct((count, 2, cells), jnp.float32),
        in_specs=[smem, vmem, vmem],
        out_specs=vmem,
        scratch_shapes=[pltpu.VMEM((2 * count, LANES), jnp.float32)],
        compiler_params=pltpu.CompilerParams(vmem_limit_bytes=VMEM_LIMIT),
        name="strips",
    )(links, own, pair)


def local(basin_state, basin_depth, coast_depth, coast_flow, coast_link):
    devices = lax.axis_size("row")
    odd = lax.axis_index("row") % 2
    parity = [list(range(p, devices, 2))[::-1] for p in range(2)]
    sent = jnp.broadcast_to(coast_link, (devices // 2,) + coast_link.shape)
    links = lax.all_to_all(sent, "row", 0, 0, axis_index_groups=parity, tiled=True)

    depth, flow = coast_depth[0], coast_flow[0]
    folded = coast_fold(depth, flow)
    links, basin_state, folded = lax.optimization_barrier((links, basin_state, folded))

    twins = [(i, i ^ 1) for i in range(devices)]
    pair_state, pair_depth = [lax.ppermute(a, "row", twins) for a in (basin_state, basin_depth)]
    rows = basin_depth.shape[0]
    whole = jnp.concatenate([basin_state, basin_depth[None]], axis=0)
    edge = jnp.where(odd == 1, whole[:, rows - HALO :], whole[:, :HALO])
    across = [(i, i + 1) for i in range(1, devices - 1, 2)]
    edge = lax.ppermute(edge, "row", across + [(j, i) for i, j in across])

    ghosts = make_strips(links, basin_state, pair_state, coast_depth.shape[2])
    edge, ghosts = lax.optimization_barrier((edge, ghosts))
    ghosts = lax.all_to_all(ghosts, "row", 0, 0, axis_index_groups=parity, tiled=True)
    basin_out = basin_run(basin_state, basin_depth, pair_state, pair_depth, edge)
    folded, basin_out = lax.optimization_barrier((folded, basin_out))
    coast_out = coast_run(sent, ghosts, folded, depth, flow)
    return (basin_out, coast_out[None])


def solution(mesh):
    in_specs = (
        P("scen", "row", None),
        P("row", "scen"),
        P("row", "scen", None),
        P("row", "scen", None, None),
        P("row", "scen"),
    )
    out_specs = (P("scen", "row", None), P("row", "scen", None, None))
    return jax.shard_map(local, mesh=mesh, in_specs=in_specs, out_specs=out_specs, check_vma=False)
```

```python
import functools

import jax
import jax.numpy as jnp
from jax import lax
from jax.experimental import pallas as pl
from jax.experimental.pallas import tpu as pltpu
from jax.sharding import PartitionSpec as P

BSTEPS = 8
CSTEPS = 10

depth_floor = 0.2
ghost_level = 2.0

RATE = 0.05
DEPTH_UNIT = RATE * RATE
FLOW_UNIT = RATE * RATE * RATE
TINY = 1e-30

HALO = BSTEPS
SUB = 8
LANES = 128


def lane_ids():
    return lax.broadcasted_iota(jnp.int32, (SUB, LANES), 1)


def row_ids():
    return lax.broadcasted_iota(jnp.int32, (SUB, LANES), 0)


def cell_terms(u):
    h, mu, mv = u
    r = pl.reciprocal(jnp.maximum(h, depth_floor * DEPTH_UNIT), approx=True)
    vx, vy = mu * r, mv * r
    hp = jnp.maximum(h, TINY)
    c = hp * lax.rsqrt(hp)
    p = (0.5 * h) * h
    cross = mu * vy
    return {
        "u": u,
        "fx": (mu, mu * vx + p, cross),
        "fy": (mv, cross, mv * vy + p),
        "sx": jnp.abs(vx) + c,
        "sy": jnp.abs(vy) + c,
    }


def y_face(above, below):
    a = jnp.maximum(above["sy"], below["sy"])
    return [
        a * (ub - ua) - (fa + fb)
        for ua, ub, fa, fb in zip(above["u"], below["u"], above["fy"], below["fy"])
    ]


def coast_steps(state, terms, after, parts, opening, rows, group, steps, ghost):
    lane, sub = lane_ids(), row_ids()
    first, last = lane == 0, lane == LANES - 1
    top, bottom = sub == 0, sub == SUB - 1
    zero = jnp.zeros((SUB, LANES), jnp.float32)
    left = functools.partial(pltpu.roll, shift=LANES - 1, axis=1)
    right = functools.partial(pltpu.roll, shift=1, axis=1)

    def load(k):
        return [[state[f, half, 1 + k] for f in range(3)] for half in range(2)]

    def store(k, both):
        for half in range(2):
            for f in range(3):
                state[f, half, 1 + k] = both[half][f]

    def wrapped(tail, head):
        down = functools.partial(pltpu.roll, shift=1, axis=0)
        out = {"sy": jnp.where(top, head["sy"], down(tail["sy"]))}
        for name in ("u", "fy"):
            out[name] = [jnp.where(top, h, down(t)) for h, t in zip(head[name], tail[name])]
        return out

    def terms_of(begin, k):
        even, odd = [cell_terms(u) for u in load(begin + k)]
        for half, cell in enumerate((even, odd)):
            for q, value in enumerate((cell["sx"], cell["sy"], cell["fx"][1], cell["fy"][2], cell["fx"][2])):
                terms[half, k, q] = value
        moved = zip(even["u"] + [even["sx"]] + list(even["fx"][1:]), odd["u"] + [odd["sx"]] + list(odd["fx"][1:]))
        for q, (e, o) in enumerate(moved):
            after[k, q] = jnp.where(last, o, left(e))

    def x_faces(begin, k):
        even, odd = load(begin + k)
        following = [after[k, f] for f in range(3)]
        sx_e, sx_o, sx_n = terms[0, k, 0], terms[1, k, 0], after[k, 3]
        fx_e = [even[1], terms[0, k, 2], terms[0, k, 4]]
        fx_o = [odd[1], terms[1, k, 2], terms[1, k, 4]]
        fx_n = [following[1], after[k, 4], after[k, 5]]
        a_in, a_out = jnp.maximum(sx_e, sx_o), jnp.maximum(sx_o, sx_n)
        for f in range(3):
            g_in = a_in * (odd[f] - even[f]) - (fx_e[f] + fx_o[f])
            g_out = a_out * (following[f] - odd[f]) - (fx_o[f] + fx_n[f])
            parts[k, f] = even[f] + g_in
            parts[k, 3 + f] = odd[f] + (g_out - g_in)
            parts[k, 6 + f] = jnp.where(first, -2.0 * fx_e[f], right(g_out))

    def y_cells(begin, k):
        return [
            {"u": u, "fy": [u[2], terms[half, k, 4], terms[half, k, 3]], "sy": terms[half, k, 1]}
            for half, u in enumerate(load(begin + k))
        ]

    def step(_, carry):
        tails = [cell_terms(u) for u in load(rows - 1)]
        above = [wrapped(t, g) for t, g in zip(tails, ghost)]

        def rows_from(trip, prev, acc):
            begin = trip * group
            for k in range(group):
                terms_of(begin, k)
            for k in range(group):
                x_faces(begin, k)
            for k in range(group):
                cur = y_cells(begin, k)
                face = [y_face(a, b) for a, b in zip(prev, cur)]
                if k == 0:
                    for half in range(2):
                        for f in range(3):
                            opening[trip, half, f] = face[half][f]
                store(begin + k - 1, [[x + g for x, g in zip(*pair)] for pair in zip(acc, face)])
                acc = [
                    [parts[k, f] - (parts[k, 6 + f] + face[0][f]) for f in range(3)],
                    [parts[k, 3 + f] - face[1][f] for f in range(3)],
                ]
                prev = cur
            return prev, acc

        prev, acc = lax.fori_loop(
            0,
            rows // group,
            lambda i, c: rows_from(i, *c),
            (above, [[zero] * 3 for _ in range(2)]),
        )
        end = [
            [
                jnp.where(bottom, -(f + f), pltpu.roll(opening[0, half, i], SUB - 1, 0))
                for i, f in enumerate(cell["fy"])
            ]
            for half, cell in enumerate(prev)
        ]
        store(rows - 1, [[x + g for x, g in zip(*pair)] for pair in zip(acc, end)])
        return carry

    lax.fori_loop(0, steps, step, 0)


GROUP = 16
UNITS = (DEPTH_UNIT, FLOW_UNIT, FLOW_UNIT)
VMEM_LIMIT = 12 * 1024 * 1024
HALF = LANES // 2


def pick(values, ids):
    return jnp.take_along_axis(values, ids, axis=1, mode="promise_in_bounds")


def split_columns(west, east):
    lane = lane_ids()
    low = lane < HALF
    twice = 2 * jnp.where(low, lane, lane - HALF)
    w = pick(west, jnp.where(low, twice, twice + 1))
    e = pick(east, jnp.where(low, twice + 1, twice))
    return jnp.where(low, w, e), pltpu.roll(jnp.where(low, e, w), HALF, 1)


def join_columns(even, odd):
    lane = lane_ids()
    low = lane < HALF
    odd = pltpu.roll(odd, HALF, 1)
    w, e = jnp.where(low, even, odd), jnp.where(low, odd, even)
    half, is_odd = lane // 2, lane % 2
    return pick(w, half + HALF * is_odd), pick(e, half + HALF * (1 - is_odd))


HALVES = (slice(0, LANES), slice(LANES, 2 * LANES))
TALL = 32


def fold_kernel(depth, flow, state, tmp):
    rows = depth.shape[0] // SUB

    def copy_in(i, carry):
        at = pl.ds(pl.multiple_of(i * TALL, TALL), TALL)
        for f in range(3):
            raw = depth[at] if f == 0 else flow[f - 1, at]
            for p in range(2):
                tmp[f, p, at] = raw[:, HALVES[p]] * UNITS[f]
        return carry

    def fold(k, carry):
        for f in range(3):
            both = split_columns(*[tmp[f, p, pl.ds(k, SUB, stride=rows), :] for p in range(2)])
            for p in range(2):
                state[f, p, k] = both[p]
        return carry

    lax.fori_loop(0, depth.shape[0] // TALL, copy_in, 0)
    lax.fori_loop(0, rows, fold, 0, unroll=4)


def coast_fold(depth, flow):
    cells = depth.shape[0]
    vmem = pl.BlockSpec(memory_space=pltpu.VMEM)
    return pl.pallas_call(
        fold_kernel,
        out_shape=jax.ShapeDtypeStruct((3, 2, cells // SUB, SUB, LANES), jnp.float32),
        in_specs=[vmem, vmem],
        out_specs=vmem,
        scratch_shapes=[pltpu.VMEM((3, 2, cells, LANES), jnp.float32)],
        compiler_params=pltpu.CompilerParams(vmem_limit_bytes=VMEM_LIMIT),
        cost_estimate=pl.CostEstimate(
            flops=CSTEPS * 70 * cells * cells, bytes_accessed=24 * cells * cells, transcendentals=0
        ),
        name="coast_fold",
    )(depth, flow)


def coast_kernel(
    links, ghosts, folded, depth, flow, out, state, terms, after, parts, opening, tmp
):
    rows = depth.shape[0] // SUB
    wet = links[0, 0, 2] > 0

    def copy_dry(i, carry):
        at = pl.ds(pl.multiple_of(i * TALL, TALL), TALL)
        for f in range(3):
            out[f, at] = depth[at] if f == 0 else flow[f - 1, at]
        return carry

    def copy_in(k, carry):
        for f in range(3):
            for p in range(2):
                state[f, p, 1 + k] = folded[f, p, k]
        return carry

    def unfold(k, carry):
        for f in range(3):
            both = join_columns(state[f, 0, 1 + k], state[f, 1, 1 + k])
            for p in range(2):
                tmp[f, p, pl.ds(k, SUB, stride=rows), :] = both[p]
        return carry

    def copy_out(i, carry):
        at = pl.ds(pl.multiple_of(i * TALL, TALL), TALL)
        for f in range(3):
            for p in range(2):
                out[f, at, HALVES[p]] = tmp[f, p, at] * (1.0 / UNITS[f])
        return carry

    @pl.when(jnp.logical_not(wet))
    def _():
        lax.fori_loop(0, depth.shape[0] // TALL, copy_dry, 0)

    @pl.when(wet)
    def _():
        lax.fori_loop(0, rows, copy_in, 0, unroll=4)
        values = jnp.sum(ghosts[...], axis=0)
        level = (ghost_level + values[0:1]) * DEPTH_UNIT
        inflow = values[1:2] * FLOW_UNIT
        spread = [jnp.broadcast_to(v[:, half], (SUB, LANES)) for v in (level, inflow) for half in HALVES]
        h, mv = split_columns(*spread[:2]), split_columns(*spread[2:])
        ghost = [cell_terms([h[p], jnp.zeros_like(h[p]), mv[p]]) for p in range(2)]
        coast_steps(state, terms, after, parts, opening, rows, GROUP, CSTEPS, ghost)
        lax.fori_loop(0, rows, unfold, 0, unroll=4)
        lax.fori_loop(0, depth.shape[0] // TALL, copy_out, 0)


def coast_run(links, ghosts, folded, depth, flow):
    cells = depth.shape[0]
    vmem = pl.BlockSpec(memory_space=pltpu.VMEM)
    return pl.pallas_call(
        coast_kernel,
        out_shape=jax.ShapeDtypeStruct((3, cells, cells), jnp.float32),
        in_specs=[pl.BlockSpec(memory_space=pltpu.SMEM), vmem, vmem, vmem, vmem],
        out_specs=vmem,
        scratch_shapes=[
            pltpu.VMEM((3, 2, 1 + cells // SUB, SUB, LANES), jnp.float32),
            pltpu.VMEM((2, GROUP, 5, SUB, LANES), jnp.float32),
            pltpu.VMEM((GROUP, 6, SUB, LANES), jnp.float32),
            pltpu.VMEM((GROUP, 9, SUB, LANES), jnp.float32),
            pltpu.VMEM((cells // SUB // GROUP, 2, 3, SUB, LANES), jnp.float32),
            pltpu.VMEM((3, 2, cells, LANES), jnp.float32),
        ],
        compiler_params=pltpu.CompilerParams(vmem_limit_bytes=VMEM_LIMIT),
        cost_estimate=pl.CostEstimate(
            flops=CSTEPS * 70 * cells * cells, bytes_accessed=24 * cells * cells, transcendentals=0
        ),
        name="coast_steps",
    )(links, ghosts, folded, depth, flow)


def basin_kernel(state, depth, pair_state, pair_depth, edge, out, eta, hu, hv, dep):
    rows, width = depth.shape
    total = rows + 2 * HALO
    chunks = width // LANES
    position = lax.axis_index("row")
    odd = position % 2
    north_inside = (position < lax.axis_size("row") - 1).astype(jnp.float32)
    pair_from = pl.multiple_of(odd * (rows - HALO), HALO)
    pair_at = pl.multiple_of((1 - odd) * (HALO + rows), HALO)
    edge_at = pl.multiple_of(odd * (HALO + rows), HALO)
    for ref, field, unit in ((eta, 0, 1.0), (hu, 1, 0.5), (hv, 2, 0.5), (dep, 3, 0.25)):
        own, pair = (depth, pair_depth) if field == 3 else (state.at[field], pair_state.at[field])
        ref[HALO : HALO + rows] = own[...] * unit
        ref[pl.ds(pair_at, HALO)] = pair[pl.ds(pair_from, HALO)] * unit
        ref[pl.ds(edge_at, HALO)] = edge[field] * unit
    lane = lax.broadcasted_iota(jnp.int32, (total, LANES), 1)
    first, last = lane == 0, lane == LANES - 1
    row = lax.broadcasted_iota(jnp.int32, (total, LANES), 0)
    kept = jnp.where(row < HALO + rows, 1.0, north_inside)

    def step(_, carry):
        prev_west = jnp.zeros((total, LANES), jnp.float32)
        prev_eta, prev_east, prev_hu = None, None, None
        for c in range(chunks + 1):
            if c < chunks:
                at = slice(c * LANES, (c + 1) * LANES)
                u, v = hu[:, at], hv[:, at]
                west = pltpu.roll(u, 1, 1)
                du = u - jnp.where(first, prev_west, west)
                dv = v - pltpu.roll(v, 1, 0)
                new = (eta[:, at] - (du + dv)) * kept
                eta[:, at] = new
                east = pltpu.roll(new, LANES - 1, 1)
                hv[:, at] = v - dep[:, at] * (pltpu.roll(new, total - 1, 0) - new)
            else:
                east = jnp.zeros((total, LANES), jnp.float32)
            if c > 0:
                back = slice((c - 1) * LANES, c * LANES)
                hu[:, back] = prev_hu - dep[:, back] * (jnp.where(last, east, prev_east) - prev_eta)
            prev_west, prev_eta, prev_east, prev_hu = west, new, east, u
        return carry

    lax.fori_loop(0, BSTEPS, step, 0)
    own = slice(HALO, HALO + rows)
    out[0] = eta[own]
    out[1] = hu[own] * 2.0
    out[2] = hv[own] * 2.0


def basin_run(state, depth, pair_state, pair_depth, edge):
    rows, width = depth.shape
    total = rows + 2 * HALO
    vmem = pl.BlockSpec(memory_space=pltpu.VMEM)
    return pl.pallas_call(
        basin_kernel,
        out_shape=jax.ShapeDtypeStruct((3, rows, width), jnp.float32),
        in_specs=[vmem] * 5,
        out_specs=vmem,
        scratch_shapes=[pltpu.VMEM((total, width), jnp.float32)] * 4,
        compiler_params=pltpu.CompilerParams(vmem_limit_bytes=VMEM_LIMIT),
        cost_estimate=pl.CostEstimate(
            flops=BSTEPS * 16 * total * width, bytes_accessed=4 * 11 * rows * width, transcendentals=0
        ),
        name="basin_steps",
    )(state, depth, pair_state, pair_depth, edge)


PLACES = 32


def strips_kernel(links, own, pair, ghosts, strips):
    rows, width = own.shape[1], own.shape[2]
    count, cells = ghosts.shape[0], ghosts.shape[2]
    span = 2 * LANES
    position = lax.axis_index("row")
    tops = (position * rows, (position + 1 - 2 * (position % 2)) * rows)

    def piece(b, carry):
        col = links[b, 0, 1]
        start = jnp.clip(col // LANES, 0, width // LANES - 2) * LANES
        shift = lax.rem(span - (col - start), span)
        at = pl.ds(pl.multiple_of(start, LANES), span)
        for i, f in enumerate((0, 2)):
            chunk = None
            for source, top in zip((own, pair), tops):
                row = links[b, 0, 0] - top
                owned = jnp.logical_and(row >= 0, row < rows).astype(jnp.float32)
                part = source[f, pl.ds(jnp.clip(row, 0, rows - 1), 1), at] * owned
                chunk = part if chunk is None else chunk + part
            strips[pl.ds(2 * b + i, 1), :] = pltpu.roll(chunk, shift, 1)[:, :LANES]
        return carry

    lax.fori_loop(0, count, piece, 0, unroll=8)
    at = lax.broadcasted_iota(jnp.int32, (PLACES, cells), 0)
    cols = lax.broadcasted_iota(jnp.int32, (PLACES, cells), 1)
    base = cols // 16
    weight = ((cols % 16).astype(jnp.float32) + 0.5) / 16.0
    mix = jnp.where(at == base, 1.0 - weight, 0.0) + jnp.where(at == base + 1, weight, 0.0)
    parts, rest = [], strips[:, :PLACES]
    for _ in range(3):
        parts.append(rest.astype(jnp.bfloat16))
        rest = rest - parts[-1].astype(jnp.float32)
    products = jnp.dot(
        jnp.concatenate(parts, axis=0), mix.astype(jnp.bfloat16), preferred_element_type=jnp.float32
    )
    size = 2 * count
    values = products[:size] + (products[size : 2 * size] + products[2 * size :])
    for b in range(count):
        ghosts[b] = values[2 * b : 2 * b + 2]


def make_strips(links, own, pair, cells):
    count = links.shape[0]
    vmem = pl.BlockSpec(memory_space=pltpu.VMEM)
    smem = pl.BlockSpec(memory_space=pltpu.SMEM)
    return pl.pallas_call(
        strips_kernel,
        out_shape=jax.ShapeDtypeStruct((count, 2, cells), jnp.float32),
        in_specs=[smem, vmem, vmem],
        out_specs=vmem,
        scratch_shapes=[pltpu.VMEM((2 * count, LANES), jnp.float32)],
        compiler_params=pltpu.CompilerParams(vmem_limit_bytes=VMEM_LIMIT),
        name="strips",
    )(links, own, pair)


def local(basin_state, basin_depth, coast_depth, coast_flow, coast_link):
    devices = lax.axis_size("row")
    odd = lax.axis_index("row") % 2
    parity = [list(range(p, devices, 2))[::-1] for p in range(2)]
    sent = jnp.broadcast_to(coast_link, (devices // 2,) + coast_link.shape)
    links = lax.all_to_all(sent, "row", 0, 0, axis_index_groups=parity, tiled=True)

    depth, flow = coast_depth[0], coast_flow[0]
    folded = coast_fold(depth, flow)

    twins = [(i, i ^ 1) for i in range(devices)]
    pair_state, pair_depth = [lax.ppermute(a, "row", twins) for a in (basin_state, basin_depth)]
    rows = basin_depth.shape[0]
    whole = jnp.concatenate([basin_state, basin_depth[None]], axis=0)
    edge = jnp.where(odd == 1, whole[:, rows - HALO :], whole[:, :HALO])
    across = [(i, i + 1) for i in range(1, devices - 1, 2)]
    edge = lax.ppermute(edge, "row", across + [(j, i) for i, j in across])

    pair_state, folded = lax.optimization_barrier((pair_state, folded))
    ghosts = make_strips(links, basin_state, pair_state, coast_depth.shape[2])
    basin_depth, ghosts = lax.optimization_barrier((basin_depth, ghosts))
    ghosts = lax.all_to_all(ghosts, "row", 0, 0, axis_index_groups=parity, tiled=True)
    basin_out = basin_run(basin_state, basin_depth, pair_state, pair_depth, edge)
    folded, basin_out = lax.optimization_barrier((folded, basin_out))
    coast_out = coast_run(sent, ghosts, folded, depth, flow)
    return (basin_out, coast_out[None])


def solution(mesh):
    in_specs = (
        P("scen", "row", None),
        P("row", "scen"),
        P("row", "scen", None),
        P("row", "scen", None, None),
        P("row", "scen"),
    )
    out_specs = (P("scen", "row", None), P("row", "scen", None, None))
    return jax.shard_map(local, mesh=mesh, in_specs=in_specs, out_specs=out_specs, check_vma=False)
```

```python
import functools

import jax
import jax.numpy as jnp
from jax import lax
from jax.experimental import pallas as pl
from jax.experimental.pallas import tpu as pltpu
from jax.sharding import PartitionSpec as P

BSTEPS = 8
CSTEPS = 10

depth_floor = 0.2
ghost_level = 2.0

RATE = 0.05
DEPTH_UNIT = RATE * RATE
FLOW_UNIT = RATE * RATE * RATE
TINY = 1e-30

HALO = BSTEPS
SUB = 8
LANES = 128


def lane_ids():
    return lax.broadcasted_iota(jnp.int32, (SUB, LANES), 1)


def row_ids():
    return lax.broadcasted_iota(jnp.int32, (SUB, LANES), 0)


def cell_terms(u):
    h, mu, mv = u
    r = pl.reciprocal(jnp.maximum(h, depth_floor * DEPTH_UNIT), approx=True)
    vx, vy = mu * r, mv * r
    hp = jnp.maximum(h, TINY)
    c = hp * lax.rsqrt(hp)
    p = (0.5 * h) * h
    cross = mu * vy
    return {
        "u": u,
        "fx": (mu, mu * vx + p, cross),
        "fy": (mv, cross, mv * vy + p),
        "sx": jnp.abs(vx) + c,
        "sy": jnp.abs(vy) + c,
    }


def y_face(above, below):
    a = jnp.maximum(above["sy"], below["sy"])
    return [
        a * (ub - ua) - (fa + fb)
        for ua, ub, fa, fb in zip(above["u"], below["u"], above["fy"], below["fy"])
    ]


def coast_steps(state, terms, after, parts, opening, rows, group, steps, ghost):
    lane, sub = lane_ids(), row_ids()
    first, last = lane == 0, lane == LANES - 1
    top, bottom = sub == 0, sub == SUB - 1
    zero = jnp.zeros((SUB, LANES), jnp.float32)
    left = functools.partial(pltpu.roll, shift=LANES - 1, axis=1)
    right = functools.partial(pltpu.roll, shift=1, axis=1)

    def load(k):
        return [[state[f, half, 1 + k] for f in range(3)] for half in range(2)]

    def store(k, both):
        for half in range(2):
            for f in range(3):
                state[f, half, 1 + k] = both[half][f]

    def wrapped(tail, head):
        down = functools.partial(pltpu.roll, shift=1, axis=0)
        out = {"sy": jnp.where(top, head["sy"], down(tail["sy"]))}
        for name in ("u", "fy"):
            out[name] = [jnp.where(top, h, down(t)) for h, t in zip(head[name], tail[name])]
        return out

    def terms_of(begin, k):
        even, odd = [cell_terms(u) for u in load(begin + k)]
        for half, cell in enumerate((even, odd)):
            for q, value in enumerate((cell["sx"], cell["sy"], cell["fx"][1], cell["fy"][2], cell["fx"][2])):
                terms[half, k, q] = value
        moved = zip(even["u"] + [even["sx"]] + list(even["fx"][1:]), odd["u"] + [odd["sx"]] + list(odd["fx"][1:]))
        for q, (e, o) in enumerate(moved):
            after[k, q] = jnp.where(last, o, left(e))

    def x_faces(begin, k):
        even, odd = load(begin + k)
        following = [after[k, f] for f in range(3)]
        sx_e, sx_o, sx_n = terms[0, k, 0], terms[1, k, 0], after[k, 3]
        fx_e = [even[1], terms[0, k, 2], terms[0, k, 4]]
        fx_o = [odd[1], terms[1, k, 2], terms[1, k, 4]]
        fx_n = [following[1], after[k, 4], after[k, 5]]
        a_in, a_out = jnp.maximum(sx_e, sx_o), jnp.maximum(sx_o, sx_n)
        for f in range(3):
            g_in = a_in * (odd[f] - even[f]) - (fx_e[f] + fx_o[f])
            g_out = a_out * (following[f] - odd[f]) - (fx_o[f] + fx_n[f])
            parts[k, f] = even[f] + g_in
            parts[k, 3 + f] = odd[f] + (g_out - g_in)
            parts[k, 6 + f] = jnp.where(first, -2.0 * fx_e[f], right(g_out))

    def y_cells(begin, k):
        return [
            {"u": u, "fy": [u[2], terms[half, k, 4], terms[half, k, 3]], "sy": terms[half, k, 1]}
            for half, u in enumerate(load(begin + k))
        ]

    def step(_, carry):
        tails = [cell_terms(u) for u in load(rows - 1)]
        above = [wrapped(t, g) for t, g in zip(tails, ghost)]

        def rows_from(trip, prev, acc):
            begin = trip * group
            for k in range(group):
                terms_of(begin, k)
            for k in range(group):
                x_faces(begin, k)
            for k in range(group):
                cur = y_cells(begin, k)
                face = [y_face(a, b) for a, b in zip(prev, cur)]
                if k == 0:
                    for half in range(2):
                        for f in range(3):
                            opening[trip, half, f] = face[half][f]
                store(begin + k - 1, [[x + g for x, g in zip(*pair)] for pair in zip(acc, face)])
                acc = [
                    [parts[k, f] - (parts[k, 6 + f] + face[0][f]) for f in range(3)],
                    [parts[k, 3 + f] - face[1][f] for f in range(3)],
                ]
                prev = cur
            return prev, acc

        prev, acc = lax.fori_loop(
            0,
            rows // group,
            lambda i, c: rows_from(i, *c),
            (above, [[zero] * 3 for _ in range(2)]),
        )
        end = [
            [
                jnp.where(bottom, -(f + f), pltpu.roll(opening[0, half, i], SUB - 1, 0))
                for i, f in enumerate(cell["fy"])
            ]
            for half, cell in enumerate(prev)
        ]
        store(rows - 1, [[x + g for x, g in zip(*pair)] for pair in zip(acc, end)])
        return carry

    lax.fori_loop(0, steps, step, 0)


GROUP = 16
UNITS = (DEPTH_UNIT, FLOW_UNIT, FLOW_UNIT)
VMEM_LIMIT = 12 * 1024 * 1024
HALF = LANES // 2


def pick(values, ids):
    return jnp.take_along_axis(values, ids, axis=1, mode="promise_in_bounds")


def split_columns(west, east):
    lane = lane_ids()
    low = lane < HALF
    twice = 2 * jnp.where(low, lane, lane - HALF)
    w = pick(west, jnp.where(low, twice, twice + 1))
    e = pick(east, jnp.where(low, twice + 1, twice))
    return jnp.where(low, w, e), pltpu.roll(jnp.where(low, e, w), HALF, 1)


def join_columns(even, odd):
    lane = lane_ids()
    low = lane < HALF
    odd = pltpu.roll(odd, HALF, 1)
    w, e = jnp.where(low, even, odd), jnp.where(low, odd, even)
    half, is_odd = lane // 2, lane % 2
    return pick(w, half + HALF * is_odd), pick(e, half + HALF * (1 - is_odd))


HALVES = (slice(0, LANES), slice(LANES, 2 * LANES))
TALL = 32


def fold_kernel(depth, flow, state, tmp):
    rows = depth.shape[0] // SUB

    def copy_in(i, carry):
        at = pl.ds(pl.multiple_of(i * TALL, TALL), TALL)
        for f in range(3):
            raw = depth[at] if f == 0 else flow[f - 1, at]
            for p in range(2):
                tmp[f, p, at] = raw[:, HALVES[p]] * UNITS[f]
        return carry

    def fold(k, carry):
        for f in range(3):
            both = split_columns(*[tmp[f, p, pl.ds(k, SUB, stride=rows), :] for p in range(2)])
            for p in range(2):
                state[f, p, k] = both[p]
        return carry

    lax.fori_loop(0, depth.shape[0] // TALL, copy_in, 0)
    lax.fori_loop(0, rows, fold, 0, unroll=4)


def coast_fold(depth, flow):
    cells = depth.shape[0]
    vmem = pl.BlockSpec(memory_space=pltpu.VMEM)
    return pl.pallas_call(
        fold_kernel,
        out_shape=jax.ShapeDtypeStruct((3, 2, cells // SUB, SUB, LANES), jnp.float32),
        in_specs=[vmem, vmem],
        out_specs=vmem,
        scratch_shapes=[pltpu.VMEM((3, 2, cells, LANES), jnp.float32)],
        compiler_params=pltpu.CompilerParams(vmem_limit_bytes=VMEM_LIMIT),
        cost_estimate=pl.CostEstimate(
            flops=CSTEPS * 70 * cells * cells, bytes_accessed=24 * cells * cells, transcendentals=0
        ),
        name="coast_fold",
    )(depth, flow)


def coast_kernel(
    links, ghosts, folded, depth, flow, out, state, terms, after, parts, opening, tmp
):
    rows = depth.shape[0] // SUB
    wet = links[0, 0, 2] > 0

    def copy_dry(i, carry):
        at = pl.ds(pl.multiple_of(i * TALL, TALL), TALL)
        for f in range(3):
            out[f, at] = depth[at] if f == 0 else flow[f - 1, at]
        return carry

    def copy_in(k, carry):
        for f in range(3):
            for p in range(2):
                state[f, p, 1 + k] = folded[f, p, k]
        return carry

    def unfold(k, carry):
        for f in range(3):
            both = join_columns(state[f, 0, 1 + k], state[f, 1, 1 + k])
            for p in range(2):
                tmp[f, p, pl.ds(k, SUB, stride=rows), :] = both[p]
        return carry

    def copy_out(i, carry):
        at = pl.ds(pl.multiple_of(i * TALL, TALL), TALL)
        for f in range(3):
            for p in range(2):
                out[f, at, HALVES[p]] = tmp[f, p, at] * (1.0 / UNITS[f])
        return carry

    @pl.when(jnp.logical_not(wet))
    def _():
        lax.fori_loop(0, depth.shape[0] // TALL, copy_dry, 0)

    @pl.when(wet)
    def _():
        lax.fori_loop(0, rows, copy_in, 0, unroll=4)
        values = jnp.sum(ghosts[...], axis=0)
        level = (ghost_level + values[0:1]) * DEPTH_UNIT
        inflow = values[1:2] * FLOW_UNIT
        h, mv = [[jnp.broadcast_to(v[:, half], (SUB, LANES)) for half in HALVES] for v in (level, inflow)]
        ghost = [cell_terms([h[p], jnp.zeros_like(h[p]), mv[p]]) for p in range(2)]
        coast_steps(state, terms, after, parts, opening, rows, GROUP, CSTEPS, ghost)
        lax.fori_loop(0, rows, unfold, 0, unroll=4)
        lax.fori_loop(0, depth.shape[0] // TALL, copy_out, 0)


def coast_run(links, ghosts, folded, depth, flow):
    cells = depth.shape[0]
    vmem = pl.BlockSpec(memory_space=pltpu.VMEM)
    return pl.pallas_call(
        coast_kernel,
        out_shape=jax.ShapeDtypeStruct((3, cells, cells), jnp.float32),
        in_specs=[pl.BlockSpec(memory_space=pltpu.SMEM), vmem, vmem, vmem, vmem],
        out_specs=vmem,
        scratch_shapes=[
            pltpu.VMEM((3, 2, 1 + cells // SUB, SUB, LANES), jnp.float32),
            pltpu.VMEM((2, GROUP, 5, SUB, LANES), jnp.float32),
            pltpu.VMEM((GROUP, 6, SUB, LANES), jnp.float32),
            pltpu.VMEM((GROUP, 9, SUB, LANES), jnp.float32),
            pltpu.VMEM((cells // SUB // GROUP, 2, 3, SUB, LANES), jnp.float32),
            pltpu.VMEM((3, 2, cells, LANES), jnp.float32),
        ],
        compiler_params=pltpu.CompilerParams(vmem_limit_bytes=VMEM_LIMIT),
        cost_estimate=pl.CostEstimate(
            flops=CSTEPS * 70 * cells * cells, bytes_accessed=24 * cells * cells, transcendentals=0
        ),
        name="coast_steps",
    )(links, ghosts, folded, depth, flow)


def basin_kernel(state, depth, pair_state, pair_depth, edges, out, eta, hu, hv, dep):
    rows, width = depth.shape
    total = rows + 2 * HALO
    chunks = width // LANES
    position = lax.axis_index("row")
    odd = position % 2
    end = lax.axis_size("row") - 1
    north_inside = (position < end).astype(jnp.float32)
    edge_inside = jnp.logical_and(position > 0, position < end).astype(jnp.float32)
    pair_from = pl.multiple_of(odd * (rows - HALO), HALO)
    pair_at = pl.multiple_of((1 - odd) * (HALO + rows), HALO)
    edge_at = pl.multiple_of(odd * (HALO + rows), HALO)
    for ref, field, unit in ((eta, 0, 1.0), (hu, 1, 0.5), (hv, 2, 0.5), (dep, 3, 0.25)):
        own, pair = (depth, pair_depth) if field == 3 else (state.at[field], pair_state.at[field])
        ref[HALO : HALO + rows] = own[...] * unit
        ref[pl.ds(pair_at, HALO)] = pair[pl.ds(pair_from, HALO)] * unit
        ref[pl.ds(edge_at, HALO)] = edges[odd, field] * (unit * edge_inside)
    lane = lax.broadcasted_iota(jnp.int32, (total, LANES), 1)
    first, last = lane == 0, lane == LANES - 1
    row = lax.broadcasted_iota(jnp.int32, (total, LANES), 0)
    kept = jnp.where(row < HALO + rows, 1.0, north_inside)

    def step(_, carry):
        prev_west = jnp.zeros((total, LANES), jnp.float32)
        prev_eta, prev_east, prev_hu = None, None, None
        for c in range(chunks + 1):
            if c < chunks:
                at = slice(c * LANES, (c + 1) * LANES)
                u, v = hu[:, at], hv[:, at]
                west = pltpu.roll(u, 1, 1)
                du = u - jnp.where(first, prev_west, west)
                dv = v - pltpu.roll(v, 1, 0)
                new = (eta[:, at] - (du + dv)) * kept
                eta[:, at] = new
                east = pltpu.roll(new, LANES - 1, 1)
                hv[:, at] = v - dep[:, at] * (pltpu.roll(new, total - 1, 0) - new)
            else:
                east = jnp.zeros((total, LANES), jnp.float32)
            if c > 0:
                back = slice((c - 1) * LANES, c * LANES)
                hu[:, back] = prev_hu - dep[:, back] * (jnp.where(last, east, prev_east) - prev_eta)
            prev_west, prev_eta, prev_east, prev_hu = west, new, east, u
        return carry

    lax.fori_loop(0, BSTEPS, step, 0)
    own = slice(HALO, HALO + rows)
    out[0] = eta[own]
    out[1] = hu[own] * 2.0
    out[2] = hv[own] * 2.0


def basin_run(state, depth, pair_state, pair_depth, edges):
    rows, width = depth.shape
    total = rows + 2 * HALO
    vmem = pl.BlockSpec(memory_space=pltpu.VMEM)
    return pl.pallas_call(
        basin_kernel,
        out_shape=jax.ShapeDtypeStruct((3, rows, width), jnp.float32),
        in_specs=[vmem] * 5,
        out_specs=vmem,
        scratch_shapes=[pltpu.VMEM((total, width), jnp.float32)] * 4,
        compiler_params=pltpu.CompilerParams(vmem_limit_bytes=VMEM_LIMIT),
        cost_estimate=pl.CostEstimate(
            flops=BSTEPS * 16 * total * width, bytes_accessed=4 * 11 * rows * width, transcendentals=0
        ),
        name="basin_steps",
    )(state, depth, pair_state, pair_depth, edges)


def strips_kernel(links, own, pair, ghosts, strips):
    rows, width = own.shape[1], own.shape[2]
    count = ghosts.shape[0]
    span = 2 * LANES
    position = lax.axis_index("row")
    tops = (position * rows, (position + 1 - 2 * (position % 2)) * rows)

    def piece(b, carry):
        col = links[b, 0, 1]
        start = jnp.clip(col // LANES, 0, width // LANES - 2) * LANES
        shift = lax.rem(span - (col - start), span)
        at = pl.ds(pl.multiple_of(start, LANES), span)
        for i, f in enumerate((0, 2)):
            chunk = None
            for source, top in zip((own, pair), tops):
                row = links[b, 0, 0] - top
                owned = jnp.logical_and(row >= 0, row < rows).astype(jnp.float32)
                part = source[f, pl.ds(jnp.clip(row, 0, rows - 1), 1), at] * owned
                chunk = part if chunk is None else chunk + part
            strips[pl.ds(2 * b + i, 1), :] = pltpu.roll(chunk, shift, 1)[:, :LANES]
        return carry

    lax.fori_loop(0, count, piece, 0, unroll=8)
    lane = lane_ids()
    for b in range(0, count, SUB // 2):
        values = strips[2 * b : 2 * b + SUB, :]
        low, high = pick(values, lane // 8), pick(values, lane // 8 + 1)
        for p in range(2):
            weight = ((2 * lane + p) % 16).astype(jnp.float32) / 16.0 + 0.5 / 16.0
            both = (1.0 - weight) * low + weight * high
            for i in range(SUB // 2):
                ghosts[b + i, :, p * LANES : (p + 1) * LANES] = both[2 * i : 2 * i + 2]


def make_strips(links, own, pair, cells):
    count = links.shape[0]
    vmem = pl.BlockSpec(memory_space=pltpu.VMEM)
    smem = pl.BlockSpec(memory_space=pltpu.SMEM)
    return pl.pallas_call(
        strips_kernel,
        out_shape=jax.ShapeDtypeStruct((count, 2, cells), jnp.float32),
        in_specs=[smem, vmem, vmem],
        out_specs=vmem,
        scratch_shapes=[pltpu.VMEM((2 * count, LANES), jnp.float32)],
        compiler_params=pltpu.CompilerParams(vmem_limit_bytes=VMEM_LIMIT),
        name="strips",
    )(links, own, pair)


def local(basin_state, basin_depth, coast_depth, coast_flow, coast_link):
    devices = lax.axis_size("row")
    odd = lax.axis_index("row") % 2
    parity = [list(range(p, devices, 2))[::-1] for p in range(2)]
    sent = jnp.broadcast_to(coast_link, (devices // 2,) + coast_link.shape)
    links = lax.all_to_all(sent, "row", 0, 0, axis_index_groups=parity, tiled=True)

    depth, flow = coast_depth[0], coast_flow[0]
    folded = coast_fold(depth, flow)

    twins = [(i, i ^ 1) for i in range(devices)]
    pair_state, pair_depth = [lax.ppermute(a, "row", twins) for a in (basin_state, basin_depth)]
    rows = basin_depth.shape[0]
    whole = jnp.concatenate([basin_state, basin_depth[None]], axis=0)
    edge = jnp.where(odd == 1, whole[:, rows - HALO :], whole[:, :HALO])
    across = [[i, (i + 1) % devices] for i in range(1, devices, 2)]
    edges = lax.all_gather(edge, "row", axis_index_groups=across)

    pair_state, folded = lax.optimization_barrier((pair_state, folded))
    ghosts = make_strips(links, basin_state, pair_state, coast_depth.shape[2])
    basin_depth, ghosts = lax.optimization_barrier((basin_depth, ghosts))
    ghosts = lax.all_to_all(ghosts, "row", 0, 0, axis_index_groups=parity, tiled=True)
    basin_out = basin_run(basin_state, basin_depth, pair_state, pair_depth, edges)
    folded, basin_out = lax.optimization_barrier((folded, basin_out))
    coast_out = coast_run(sent, ghosts, folded, depth, flow)
    return (basin_out, coast_out[None])


def solution(mesh):
    in_specs = (
        P("scen", "row", None),
        P("row", "scen"),
        P("row", "scen", None),
        P("row", "scen", None, None),
        P("row", "scen"),
    )
    out_specs = (P("scen", "row", None), P("row", "scen", None, None))
    return jax.shard_map(local, mesh=mesh, in_specs=in_specs, out_specs=out_specs, check_vma=False)
```

```python
import functools

import jax
import jax.numpy as jnp
from jax import lax
from jax.experimental import pallas as pl
from jax.experimental.pallas import tpu as pltpu
from jax.sharding import PartitionSpec as P

BSTEPS = 8
CSTEPS = 10

depth_floor = 0.2
ghost_level = 2.0

RATE = 0.05
DEPTH_UNIT = RATE * RATE
FLOW_UNIT = RATE * RATE * RATE
TINY = 1e-30

HALO = BSTEPS
SUB = 8
LANES = 128


def lane_ids():
    return lax.broadcasted_iota(jnp.int32, (SUB, LANES), 1)


def row_ids():
    return lax.broadcasted_iota(jnp.int32, (SUB, LANES), 0)


def cell_terms(u):
    h, mu, mv = u
    r = pl.reciprocal(jnp.maximum(h, depth_floor * DEPTH_UNIT), approx=True)
    vx, vy = mu * r, mv * r
    hp = jnp.maximum(h, TINY)
    c = hp * lax.rsqrt(hp)
    p = (0.5 * h) * h
    cross = mu * vy
    return {
        "u": u,
        "fx": (mu, mu * vx + p, cross),
        "fy": (mv, cross, mv * vy + p),
        "sx": jnp.abs(vx) + c,
        "sy": jnp.abs(vy) + c,
    }


def y_face(above, below):
    a = jnp.maximum(above["sy"], below["sy"])
    return [
        a * (ub - ua) - (fa + fb)
        for ua, ub, fa, fb in zip(above["u"], below["u"], above["fy"], below["fy"])
    ]


def coast_steps(state, terms, after, parts, opening, rows, group, steps, ghost):
    lane, sub = lane_ids(), row_ids()
    first, last = lane == 0, lane == LANES - 1
    top, bottom = sub == 0, sub == SUB - 1
    zero = jnp.zeros((SUB, LANES), jnp.float32)
    left = functools.partial(pltpu.roll, shift=LANES - 1, axis=1)
    right = functools.partial(pltpu.roll, shift=1, axis=1)

    def load(k):
        return [[state[f, half, 1 + k] for f in range(3)] for half in range(2)]

    def store(k, both):
        for half in range(2):
            for f in range(3):
                state[f, half, 1 + k] = both[half][f]

    def wrapped(tail, head):
        down = functools.partial(pltpu.roll, shift=1, axis=0)
        out = {"sy": jnp.where(top, head["sy"], down(tail["sy"]))}
        for name in ("u", "fy"):
            out[name] = [jnp.where(top, h, down(t)) for h, t in zip(head[name], tail[name])]
        return out

    def terms_of(begin, k):
        even, odd = [cell_terms(u) for u in load(begin + k)]
        for half, cell in enumerate((even, odd)):
            for q, value in enumerate((cell["sx"], cell["sy"], cell["fx"][1], cell["fy"][2], cell["fx"][2])):
                terms[half, k, q] = value
        moved = zip(even["u"] + [even["sx"]] + list(even["fx"][1:]), odd["u"] + [odd["sx"]] + list(odd["fx"][1:]))
        for q, (e, o) in enumerate(moved):
            after[k, q] = jnp.where(last, o, left(e))

    def x_faces(begin, k):
        even, odd = load(begin + k)
        following = [after[k, f] for f in range(3)]
        sx_e, sx_o, sx_n = terms[0, k, 0], terms[1, k, 0], after[k, 3]
        fx_e = [even[1], terms[0, k, 2], terms[0, k, 4]]
        fx_o = [odd[1], terms[1, k, 2], terms[1, k, 4]]
        fx_n = [following[1], after[k, 4], after[k, 5]]
        a_in, a_out = jnp.maximum(sx_e, sx_o), jnp.maximum(sx_o, sx_n)
        for f in range(3):
            g_in = a_in * (odd[f] - even[f]) - (fx_e[f] + fx_o[f])
            g_out = a_out * (following[f] - odd[f]) - (fx_o[f] + fx_n[f])
            parts[k, f] = even[f] + g_in
            parts[k, 3 + f] = odd[f] + (g_out - g_in)
            parts[k, 6 + f] = jnp.where(first, -2.0 * fx_e[f], right(g_out))

    def y_cells(begin, k):
        return [
            {"u": u, "fy": [u[2], terms[half, k, 4], terms[half, k, 3]], "sy": terms[half, k, 1]}
            for half, u in enumerate(load(begin + k))
        ]

    def step(_, carry):
        tails = [cell_terms(u) for u in load(rows - 1)]
        above = [wrapped(t, g) for t, g in zip(tails, ghost)]

        def rows_from(trip, prev, acc):
            begin = trip * group
            for k in range(group):
                terms_of(begin, k)
            for k in range(group):
                x_faces(begin, k)
            for k in range(group):
                cur = y_cells(begin, k)
                face = [y_face(a, b) for a, b in zip(prev, cur)]
                if k == 0:
                    for half in range(2):
                        for f in range(3):
                            opening[trip, half, f] = face[half][f]
                store(begin + k - 1, [[x + g for x, g in zip(*pair)] for pair in zip(acc, face)])
                acc = [
                    [parts[k, f] - (parts[k, 6 + f] + face[0][f]) for f in range(3)],
                    [parts[k, 3 + f] - face[1][f] for f in range(3)],
                ]
                prev = cur
            return prev, acc

        prev, acc = lax.fori_loop(
            0,
            rows // group,
            lambda i, c: rows_from(i, *c),
            (above, [[zero] * 3 for _ in range(2)]),
        )
        end = [
            [
                jnp.where(bottom, -(f + f), pltpu.roll(opening[0, half, i], SUB - 1, 0))
                for i, f in enumerate(cell["fy"])
            ]
            for half, cell in enumerate(prev)
        ]
        store(rows - 1, [[x + g for x, g in zip(*pair)] for pair in zip(acc, end)])
        return carry

    lax.fori_loop(0, steps, step, 0)


GROUP = 16
UNITS = (DEPTH_UNIT, FLOW_UNIT, FLOW_UNIT)
VMEM_LIMIT = 12 * 1024 * 1024
HALF = LANES // 2


def pick(values, ids):
    return jnp.take_along_axis(values, ids, axis=1, mode="promise_in_bounds")


def split_columns(west, east):
    lane = lane_ids()
    low = lane < HALF
    twice = 2 * jnp.where(low, lane, lane - HALF)
    w = pick(west, jnp.where(low, twice, twice + 1))
    e = pick(east, jnp.where(low, twice + 1, twice))
    return jnp.where(low, w, e), pltpu.roll(jnp.where(low, e, w), HALF, 1)


def join_columns(even, odd):
    lane = lane_ids()
    low = lane < HALF
    odd = pltpu.roll(odd, HALF, 1)
    w, e = jnp.where(low, even, odd), jnp.where(low, odd, even)
    half, is_odd = lane // 2, lane % 2
    return pick(w, half + HALF * is_odd), pick(e, half + HALF * (1 - is_odd))


HALVES = (slice(0, LANES), slice(LANES, 2 * LANES))
TALL = 32


def fold_kernel(depth, flow, state, tmp):
    rows = depth.shape[0] // SUB

    def copy_in(i, carry):
        at = pl.ds(pl.multiple_of(i * TALL, TALL), TALL)
        for f in range(3):
            raw = depth[at] if f == 0 else flow[f - 1, at]
            for p in range(2):
                tmp[f, p, at] = raw[:, HALVES[p]] * UNITS[f]
        return carry

    def fold(k, carry):
        for f in range(3):
            both = split_columns(*[tmp[f, p, pl.ds(k, SUB, stride=rows), :] for p in range(2)])
            for p in range(2):
                state[f, p, k] = both[p]
        return carry

    lax.fori_loop(0, depth.shape[0] // TALL, copy_in, 0)
    lax.fori_loop(0, rows, fold, 0, unroll=4)


def coast_fold(depth, flow):
    cells = depth.shape[0]
    vmem = pl.BlockSpec(memory_space=pltpu.VMEM)
    return pl.pallas_call(
        fold_kernel,
        out_shape=jax.ShapeDtypeStruct((3, 2, cells // SUB, SUB, LANES), jnp.float32),
        in_specs=[vmem, vmem],
        out_specs=vmem,
        scratch_shapes=[pltpu.VMEM((3, 2, cells, LANES), jnp.float32)],
        compiler_params=pltpu.CompilerParams(vmem_limit_bytes=VMEM_LIMIT),
        cost_estimate=pl.CostEstimate(
            flops=CSTEPS * 70 * cells * cells, bytes_accessed=24 * cells * cells, transcendentals=0
        ),
        name="coast_fold",
    )(depth, flow)


def coast_kernel(
    links, ghosts, folded, depth, flow, out, state, terms, after, parts, opening, tmp
):
    rows = depth.shape[0] // SUB
    wet = links[0, 0, 2] > 0

    def copy_dry(i, carry):
        at = pl.ds(pl.multiple_of(i * TALL, TALL), TALL)
        for f in range(3):
            out[f, at] = depth[at] if f == 0 else flow[f - 1, at]
        return carry

    def copy_in(k, carry):
        for f in range(3):
            for p in range(2):
                state[f, p, 1 + k] = folded[f, p, k]
        return carry

    def unfold(k, carry):
        for f in range(3):
            both = join_columns(state[f, 0, 1 + k], state[f, 1, 1 + k])
            for p in range(2):
                tmp[f, p, pl.ds(k, SUB, stride=rows), :] = both[p]
        return carry

    def copy_out(i, carry):
        at = pl.ds(pl.multiple_of(i * TALL, TALL), TALL)
        for f in range(3):
            for p in range(2):
                out[f, at, HALVES[p]] = tmp[f, p, at] * (1.0 / UNITS[f])
        return carry

    @pl.when(jnp.logical_not(wet))
    def _():
        lax.fori_loop(0, depth.shape[0] // TALL, copy_dry, 0)

    @pl.when(wet)
    def _():
        lax.fori_loop(0, rows, copy_in, 0, unroll=4)
        values = jnp.sum(ghosts[...], axis=0)
        level = (ghost_level + values) * DEPTH_UNIT
        inflow = values * FLOW_UNIT
        h, mv = [
            [jnp.broadcast_to(v[i : i + 1], (SUB, LANES)) for i in range(at, at + 2)]
            for v, at in ((level, 0), (inflow, 2))
        ]
        ghost = [cell_terms([h[p], jnp.zeros_like(h[p]), mv[p]]) for p in range(2)]
        coast_steps(state, terms, after, parts, opening, rows, GROUP, CSTEPS, ghost)
        lax.fori_loop(0, rows, unfold, 0, unroll=4)
        lax.fori_loop(0, depth.shape[0] // TALL, copy_out, 0)


def coast_run(links, ghosts, folded, depth, flow):
    cells = depth.shape[0]
    vmem = pl.BlockSpec(memory_space=pltpu.VMEM)
    return pl.pallas_call(
        coast_kernel,
        out_shape=jax.ShapeDtypeStruct((3, cells, cells), jnp.float32),
        in_specs=[pl.BlockSpec(memory_space=pltpu.SMEM), vmem, vmem, vmem, vmem],
        out_specs=vmem,
        scratch_shapes=[
            pltpu.VMEM((3, 2, 1 + cells // SUB, SUB, LANES), jnp.float32),
            pltpu.VMEM((2, GROUP, 5, SUB, LANES), jnp.float32),
            pltpu.VMEM((GROUP, 6, SUB, LANES), jnp.float32),
            pltpu.VMEM((GROUP, 9, SUB, LANES), jnp.float32),
            pltpu.VMEM((cells // SUB // GROUP, 2, 3, SUB, LANES), jnp.float32),
            pltpu.VMEM((3, 2, cells, LANES), jnp.float32),
        ],
        compiler_params=pltpu.CompilerParams(vmem_limit_bytes=VMEM_LIMIT),
        cost_estimate=pl.CostEstimate(
            flops=CSTEPS * 70 * cells * cells, bytes_accessed=24 * cells * cells, transcendentals=0
        ),
        name="coast_steps",
    )(links, ghosts, folded, depth, flow)


def basin_kernel(state, depth, pair_state, pair_depth, edge, out, eta, hu, hv, dep):
    rows, width = depth.shape
    total = rows + 2 * HALO
    chunks = width // LANES
    position = lax.axis_index("row")
    odd = position % 2
    north_inside = (position < lax.axis_size("row") - 1).astype(jnp.float32)
    pair_from = pl.multiple_of(odd * (rows - HALO), HALO)
    pair_at = pl.multiple_of((1 - odd) * (HALO + rows), HALO)
    edge_at = pl.multiple_of(odd * (HALO + rows), HALO)
    for ref, field, unit in ((eta, 0, 1.0), (hu, 1, 0.5), (hv, 2, 0.5), (dep, 3, 0.25)):
        own, pair = (depth, pair_depth) if field == 3 else (state.at[field], pair_state.at[field])
        ref[HALO : HALO + rows] = own[...] * unit
        ref[pl.ds(pair_at, HALO)] = pair[pl.ds(pair_from, HALO)] * unit
        ref[pl.ds(edge_at, HALO)] = edge[field] * unit
    lane = lax.broadcasted_iota(jnp.int32, (total, LANES), 1)
    first, last = lane == 0, lane == LANES - 1
    row = lax.broadcasted_iota(jnp.int32, (total, LANES), 0)
    kept = jnp.where(row < HALO + rows, 1.0, north_inside)

    def step(_, carry):
        prev_west = jnp.zeros((total, LANES), jnp.float32)
        prev_eta, prev_east, prev_hu = None, None, None
        for c in range(chunks + 1):
            if c < chunks:
                at = slice(c * LANES, (c + 1) * LANES)
                u, v = hu[:, at], hv[:, at]
                west = pltpu.roll(u, 1, 1)
                du = u - jnp.where(first, prev_west, west)
                dv = v - pltpu.roll(v, 1, 0)
                new = (eta[:, at] - (du + dv)) * kept
                eta[:, at] = new
                east = pltpu.roll(new, LANES - 1, 1)
                hv[:, at] = v - dep[:, at] * (pltpu.roll(new, total - 1, 0) - new)
            else:
                east = jnp.zeros((total, LANES), jnp.float32)
            if c > 0:
                back = slice((c - 1) * LANES, c * LANES)
                hu[:, back] = prev_hu - dep[:, back] * (jnp.where(last, east, prev_east) - prev_eta)
            prev_west, prev_eta, prev_east, prev_hu = west, new, east, u
        return carry

    lax.fori_loop(0, BSTEPS, step, 0)
    own = slice(HALO, HALO + rows)
    out[0] = eta[own]
    out[1] = hu[own] * 2.0
    out[2] = hv[own] * 2.0


def basin_run(state, depth, pair_state, pair_depth, edge):
    rows, width = depth.shape
    total = rows + 2 * HALO
    vmem = pl.BlockSpec(memory_space=pltpu.VMEM)
    return pl.pallas_call(
        basin_kernel,
        out_shape=jax.ShapeDtypeStruct((3, rows, width), jnp.float32),
        in_specs=[vmem] * 5,
        out_specs=vmem,
        scratch_shapes=[pltpu.VMEM((total, width), jnp.float32)] * 4,
        compiler_params=pltpu.CompilerParams(vmem_limit_bytes=VMEM_LIMIT),
        cost_estimate=pl.CostEstimate(
            flops=BSTEPS * 16 * total * width, bytes_accessed=4 * 11 * rows * width, transcendentals=0
        ),
        name="basin_steps",
    )(state, depth, pair_state, pair_depth, edge)


def strips_kernel(links, own, pair, ghosts, strips):
    rows, width = own.shape[1], own.shape[2]
    count = ghosts.shape[0]
    span = 2 * LANES
    position = lax.axis_index("row")
    tops = (position * rows, (position + 1 - 2 * (position % 2)) * rows)
    lane = lane_ids()
    weight = ((2 * lane + row_ids() % 2) % 16).astype(jnp.float32) / 16.0 + 0.5 / 16.0

    def piece(b, carry):
        col = links[b, 0, 1]
        start = jnp.clip(col // LANES, 0, width // LANES - 2) * LANES
        shift = lax.rem(span - (col - start), span)
        at = pl.ds(pl.multiple_of(start, LANES), span)
        for i, f in enumerate((0, 2)):
            chunk = None
            for source, top in zip((own, pair), tops):
                row = links[b, 0, 0] - top
                owned = jnp.logical_and(row >= 0, row < rows).astype(jnp.float32)
                part = source[f, pl.ds(jnp.clip(row, 0, rows - 1), 1), at] * owned
                chunk = part if chunk is None else chunk + part
            moved = pltpu.roll(chunk, shift, 1)[:, :LANES]
            strips[b, 2 * i : 2 * i + 2] = jnp.broadcast_to(moved, (2, LANES))
        values = strips[b]
        low, high = pick(values, lane // 8), pick(values, lane // 8 + 1)
        ghosts[b] = (1.0 - weight) * low + weight * high
        return carry

    strips[...] = jnp.zeros_like(strips)
    lax.fori_loop(0, count, piece, 0, unroll=8)


def make_strips(links, own, pair):
    count = links.shape[0]
    tiles = (count, SUB, LANES)
    vmem = pl.BlockSpec(memory_space=pltpu.VMEM)
    smem = pl.BlockSpec(memory_space=pltpu.SMEM)
    return pl.pallas_call(
        strips_kernel,
        out_shape=jax.ShapeDtypeStruct(tiles, jnp.float32),
        in_specs=[smem, vmem, vmem],
        out_specs=vmem,
        scratch_shapes=[pltpu.VMEM(tiles, jnp.float32)],
        compiler_params=pltpu.CompilerParams(vmem_limit_bytes=VMEM_LIMIT),
        cost_estimate=pl.CostEstimate(
            flops=2 * own.size * CSTEPS * 70, bytes_accessed=8 * own.size, transcendentals=0
        ),
        name="strips",
    )(links, own, pair)


def local(basin_state, basin_depth, coast_depth, coast_flow, coast_link):
    devices = lax.axis_size("row")
    odd = lax.axis_index("row") % 2
    parity = [list(range(p, devices, 2))[::-1] for p in range(2)]
    sent = jnp.broadcast_to(coast_link, (devices // 2,) + coast_link.shape)
    links = lax.all_to_all(sent, "row", 0, 0, axis_index_groups=parity, tiled=True)

    depth, flow = coast_depth[0], coast_flow[0]
    folded = coast_fold(depth, flow)

    twins = [(i, i ^ 1) for i in range(devices)]
    pair_state, pair_depth = [lax.ppermute(a, "row", twins) for a in (basin_state, basin_depth)]
    rows = basin_depth.shape[0]
    whole = jnp.concatenate([basin_state, basin_depth[None]], axis=0)
    edge = jnp.where(odd == 1, whole[:, rows - HALO :], whole[:, :HALO])
    across = [(i, i + 1) for i in range(1, devices - 1, 2)]
    edge = lax.ppermute(edge, "row", across + [(j, i) for i, j in across])

    pair_state, folded = lax.optimization_barrier((pair_state, folded))
    ghosts = make_strips(links, basin_state, pair_state)
    basin_depth, ghosts = lax.optimization_barrier((basin_depth, ghosts))
    ghosts = lax.all_to_all(ghosts, "row", 0, 0, axis_index_groups=parity, tiled=True)
    basin_out = basin_run(basin_state, basin_depth, pair_state, pair_depth, edge)
    folded, basin_out = lax.optimization_barrier((folded, basin_out))
    coast_out = coast_run(sent, ghosts, folded, depth, flow)
    return (basin_out, coast_out[None])


def solution(mesh):
    in_specs = (
        P("scen", "row", None),
        P("row", "scen"),
        P("row", "scen", None),
        P("row", "scen", None, None),
        P("row", "scen"),
    )
    out_specs = (P("scen", "row", None), P("row", "scen", None, None))
    return jax.shard_map(local, mesh=mesh, in_specs=in_specs, out_specs=out_specs, check_vma=False)
```

```python
import functools

import jax
import jax.numpy as jnp
from jax import lax
from jax.experimental import pallas as pl
from jax.experimental.pallas import tpu as pltpu
from jax.sharding import PartitionSpec as P

BSTEPS = 8
CSTEPS = 10

depth_floor = 0.2
ghost_level = 2.0

RATE = 0.05
DEPTH_UNIT = RATE * RATE
FLOW_UNIT = RATE * RATE * RATE
TINY = 1e-30

HALO = BSTEPS
SUB = 8
LANES = 128


def lane_ids():
    return lax.broadcasted_iota(jnp.int32, (SUB, LANES), 1)


def row_ids():
    return lax.broadcasted_iota(jnp.int32, (SUB, LANES), 0)


def cell_terms(u):
    h, mu, mv = u
    r = pl.reciprocal(jnp.maximum(h, depth_floor * DEPTH_UNIT), approx=True)
    vx, vy = mu * r, mv * r
    hp = jnp.maximum(h, TINY)
    c = hp * lax.rsqrt(hp)
    p = (0.5 * h) * h
    cross = mu * vy
    return {
        "u": u,
        "fx": (mu, mu * vx + p, cross),
        "fy": (mv, cross, mv * vy + p),
        "sx": jnp.abs(vx) + c,
        "sy": jnp.abs(vy) + c,
    }


def y_face(above, below):
    a = jnp.maximum(above["sy"], below["sy"])
    return [
        a * (ub - ua) - (fa + fb)
        for ua, ub, fa, fb in zip(above["u"], below["u"], above["fy"], below["fy"])
    ]


def coast_steps(state, terms, after, parts, opening, rows, group, steps, ghost):
    lane, sub = lane_ids(), row_ids()
    first, last = lane == 0, lane == LANES - 1
    top, bottom = sub == 0, sub == SUB - 1
    zero = jnp.zeros((SUB, LANES), jnp.float32)
    left = functools.partial(pltpu.roll, shift=LANES - 1, axis=1)
    right = functools.partial(pltpu.roll, shift=1, axis=1)

    def load(k):
        return [[state[f, half, 1 + k] for f in range(3)] for half in range(2)]

    def store(k, both):
        for half in range(2):
            for f in range(3):
                state[f, half, 1 + k] = both[half][f]

    def wrapped(tail, head):
        down = functools.partial(pltpu.roll, shift=1, axis=0)
        out = {"sy": jnp.where(top, head["sy"], down(tail["sy"]))}
        for name in ("u", "fy"):
            out[name] = [jnp.where(top, h, down(t)) for h, t in zip(head[name], tail[name])]
        return out

    def terms_of(begin, k):
        even, odd = [cell_terms(u) for u in load(begin + k)]
        for half, cell in enumerate((even, odd)):
            for q, value in enumerate((cell["sx"], cell["sy"], cell["fx"][1], cell["fy"][2], cell["fx"][2])):
                terms[half, k, q] = value
        moved = zip(even["u"] + [even["sx"]] + list(even["fx"][1:]), odd["u"] + [odd["sx"]] + list(odd["fx"][1:]))
        for q, (e, o) in enumerate(moved):
            after[k, q] = jnp.where(last, o, left(e))

    def x_faces(begin, k):
        even, odd = load(begin + k)
        following = [after[k, f] for f in range(3)]
        sx_e, sx_o, sx_n = terms[0, k, 0], terms[1, k, 0], after[k, 3]
        fx_e = [even[1], terms[0, k, 2], terms[0, k, 4]]
        fx_o = [odd[1], terms[1, k, 2], terms[1, k, 4]]
        fx_n = [following[1], after[k, 4], after[k, 5]]
        a_in, a_out = jnp.maximum(sx_e, sx_o), jnp.maximum(sx_o, sx_n)
        for f in range(3):
            g_in = a_in * (odd[f] - even[f]) - (fx_e[f] + fx_o[f])
            g_out = a_out * (following[f] - odd[f]) - (fx_o[f] + fx_n[f])
            parts[k, f] = even[f] + g_in
            parts[k, 3 + f] = odd[f] + (g_out - g_in)
            parts[k, 6 + f] = jnp.where(first, -2.0 * fx_e[f], right(g_out))

    def y_cells(begin, k):
        return [
            {"u": u, "fy": [u[2], terms[half, k, 4], terms[half, k, 3]], "sy": terms[half, k, 1]}
            for half, u in enumerate(load(begin + k))
        ]

    def step(_, carry):
        tails = [cell_terms(u) for u in load(rows - 1)]
        above = [wrapped(t, g) for t, g in zip(tails, ghost)]

        def rows_from(trip, prev, acc):
            begin = trip * group
            for k in range(group):
                terms_of(begin, k)
            for k in range(group):
                x_faces(begin, k)
            for k in range(group):
                cur = y_cells(begin, k)
                face = [y_face(a, b) for a, b in zip(prev, cur)]
                if k == 0:
                    for half in range(2):
                        for f in range(3):
                            opening[trip, half, f] = face[half][f]
                store(begin + k - 1, [[x + g for x, g in zip(*pair)] for pair in zip(acc, face)])
                acc = [
                    [parts[k, f] - (parts[k, 6 + f] + face[0][f]) for f in range(3)],
                    [parts[k, 3 + f] - face[1][f] for f in range(3)],
                ]
                prev = cur
            return prev, acc

        prev, acc = lax.fori_loop(
            0,
            rows // group,
            lambda i, c: rows_from(i, *c),
            (above, [[zero] * 3 for _ in range(2)]),
        )
        end = [
            [
                jnp.where(bottom, -(f + f), pltpu.roll(opening[0, half, i], SUB - 1, 0))
                for i, f in enumerate(cell["fy"])
            ]
            for half, cell in enumerate(prev)
        ]
        store(rows - 1, [[x + g for x, g in zip(*pair)] for pair in zip(acc, end)])
        return carry

    lax.fori_loop(0, steps, step, 0)


GROUP = 16
UNITS = (DEPTH_UNIT, FLOW_UNIT, FLOW_UNIT)
VMEM_LIMIT = 12 * 1024 * 1024
HALF = LANES // 2


def pick(values, ids):
    return jnp.take_along_axis(values, ids, axis=1, mode="promise_in_bounds")


def split_columns(west, east):
    lane = lane_ids()
    low = lane < HALF
    twice = 2 * jnp.where(low, lane, lane - HALF)
    w = pick(west, jnp.where(low, twice, twice + 1))
    e = pick(east, jnp.where(low, twice + 1, twice))
    return jnp.where(low, w, e), pltpu.roll(jnp.where(low, e, w), HALF, 1)


def join_columns(even, odd):
    lane = lane_ids()
    low = lane < HALF
    odd = pltpu.roll(odd, HALF, 1)
    w, e = jnp.where(low, even, odd), jnp.where(low, odd, even)
    half, is_odd = lane // 2, lane % 2
    return pick(w, half + HALF * is_odd), pick(e, half + HALF * (1 - is_odd))


HALVES = (slice(0, LANES), slice(LANES, 2 * LANES))
TALL = 32


def fold_kernel(depth, flow, state, tmp):
    rows = depth.shape[0] // SUB

    def copy_in(i, carry):
        at = pl.ds(pl.multiple_of(i * TALL, TALL), TALL)
        for f in range(3):
            raw = depth[at] if f == 0 else flow[f - 1, at]
            for p in range(2):
                tmp[f, p, at] = raw[:, HALVES[p]] * UNITS[f]
        return carry

    def fold(k, carry):
        for f in range(3):
            both = split_columns(*[tmp[f, p, pl.ds(k, SUB, stride=rows), :] for p in range(2)])
            for p in range(2):
                state[f, p, k] = both[p]
        return carry

    lax.fori_loop(0, depth.shape[0] // TALL, copy_in, 0)
    lax.fori_loop(0, rows, fold, 0, unroll=4)


def coast_fold(depth, flow):
    cells = depth.shape[0]
    vmem = pl.BlockSpec(memory_space=pltpu.VMEM)
    return pl.pallas_call(
        fold_kernel,
        out_shape=jax.ShapeDtypeStruct((3, 2, cells // SUB, SUB, LANES), jnp.float32),
        in_specs=[vmem, vmem],
        out_specs=vmem,
        scratch_shapes=[pltpu.VMEM((3, 2, cells, LANES), jnp.float32)],
        compiler_params=pltpu.CompilerParams(vmem_limit_bytes=VMEM_LIMIT),
        cost_estimate=pl.CostEstimate(
            flops=CSTEPS * 70 * cells * cells, bytes_accessed=24 * cells * cells, transcendentals=0
        ),
        name="coast_fold",
    )(depth, flow)


def coast_kernel(
    links, ghosts, folded, depth, flow, out, state, terms, after, parts, opening, tmp
):
    rows = depth.shape[0] // SUB
    wet = links[0, 0, 2] > 0

    def copy_dry(i, carry):
        at = pl.ds(pl.multiple_of(i * TALL, TALL), TALL)
        for f in range(3):
            out[f, at] = depth[at] if f == 0 else flow[f - 1, at]
        return carry

    def copy_in(k, carry):
        for f in range(3):
            for p in range(2):
                state[f, p, 1 + k] = folded[f, p, k]
        return carry

    def unfold(k, carry):
        for f in range(3):
            both = join_columns(state[f, 0, 1 + k], state[f, 1, 1 + k])
            for p in range(2):
                tmp[f, p, pl.ds(k, SUB, stride=rows), :] = both[p]
        return carry

    def copy_out(i, carry):
        at = pl.ds(pl.multiple_of(i * TALL, TALL), TALL)
        for f in range(3):
            for p in range(2):
                out[f, at, HALVES[p]] = tmp[f, p, at] * (1.0 / UNITS[f])
        return carry

    @pl.when(jnp.logical_not(wet))
    def _():
        lax.fori_loop(0, depth.shape[0] // TALL, copy_dry, 0)

    @pl.when(wet)
    def _():
        lax.fori_loop(0, rows, copy_in, 0, unroll=4)
        values = jnp.sum(ghosts[...], axis=0)
        level = (ghost_level + values) * DEPTH_UNIT
        inflow = values * FLOW_UNIT
        h, mv = [
            [jnp.broadcast_to(v[i : i + 1], (SUB, LANES)) for i in range(at, at + 2)]
            for v, at in ((level, 0), (inflow, 2))
        ]
        ghost = [cell_terms([h[p], jnp.zeros_like(h[p]), mv[p]]) for p in range(2)]
        coast_steps(state, terms, after, parts, opening, rows, GROUP, CSTEPS, ghost)
        lax.fori_loop(0, rows, unfold, 0, unroll=4)
        lax.fori_loop(0, depth.shape[0] // TALL, copy_out, 0)


def coast_run(links, ghosts, folded, depth, flow):
    cells = depth.shape[0]
    vmem = pl.BlockSpec(memory_space=pltpu.VMEM)
    return pl.pallas_call(
        coast_kernel,
        out_shape=jax.ShapeDtypeStruct((3, cells, cells), jnp.float32),
        in_specs=[pl.BlockSpec(memory_space=pltpu.SMEM), vmem, vmem, vmem, vmem],
        out_specs=vmem,
        scratch_shapes=[
            pltpu.VMEM((3, 2, 1 + cells // SUB, SUB, LANES), jnp.float32),
            pltpu.VMEM((2, GROUP, 5, SUB, LANES), jnp.float32),
            pltpu.VMEM((GROUP, 6, SUB, LANES), jnp.float32),
            pltpu.VMEM((GROUP, 9, SUB, LANES), jnp.float32),
            pltpu.VMEM((cells // SUB // GROUP, 2, 3, SUB, LANES), jnp.float32),
            pltpu.VMEM((3, 2, cells, LANES), jnp.float32),
        ],
        compiler_params=pltpu.CompilerParams(vmem_limit_bytes=VMEM_LIMIT),
        cost_estimate=pl.CostEstimate(
            flops=CSTEPS * 70 * cells * cells, bytes_accessed=24 * cells * cells, transcendentals=0
        ),
        name="coast_steps",
    )(links, ghosts, folded, depth, flow)


def basin_kernel(state, depth, pair_state, pair_depth, edge, out, eta, hu, hv, dep):
    rows, width = depth.shape
    total = rows + 2 * HALO
    chunks = width // LANES
    position = lax.axis_index("row")
    odd = position % 2
    north_inside = (position < lax.axis_size("row") - 1).astype(jnp.float32)
    pair_from = pl.multiple_of(odd * (rows - HALO), HALO)
    pair_at = pl.multiple_of((1 - odd) * (HALO + rows), HALO)
    edge_at = pl.multiple_of(odd * (HALO + rows), HALO)
    for ref, field, unit in ((eta, 0, 1.0), (hu, 1, 0.5), (hv, 2, 0.5), (dep, 3, 0.25)):
        own, pair = (depth, pair_depth) if field == 3 else (state.at[field], pair_state.at[field])
        ref[HALO : HALO + rows] = own[...] * unit
        ref[pl.ds(pair_at, HALO)] = pair[pl.ds(pair_from, HALO)] * unit
        ref[pl.ds(edge_at, HALO)] = edge[field] * unit
    lane = lax.broadcasted_iota(jnp.int32, (total, LANES), 1)
    first, last = lane == 0, lane == LANES - 1
    row = lax.broadcasted_iota(jnp.int32, (total, LANES), 0)
    kept = jnp.where(row < HALO + rows, 1.0, north_inside)

    def step(_, carry):
        prev_west = jnp.zeros((total, LANES), jnp.float32)
        prev_eta, prev_east, prev_hu = None, None, None
        for c in range(chunks + 1):
            if c < chunks:
                at = slice(c * LANES, (c + 1) * LANES)
                u, v = hu[:, at], hv[:, at]
                west = pltpu.roll(u, 1, 1)
                du = u - jnp.where(first, prev_west, west)
                dv = v - pltpu.roll(v, 1, 0)
                new = (eta[:, at] - (du + dv)) * kept
                eta[:, at] = new
                east = pltpu.roll(new, LANES - 1, 1)
                hv[:, at] = v - dep[:, at] * (pltpu.roll(new, total - 1, 0) - new)
            else:
                east = jnp.zeros((total, LANES), jnp.float32)
            if c > 0:
                back = slice((c - 1) * LANES, c * LANES)
                hu[:, back] = prev_hu - dep[:, back] * (jnp.where(last, east, prev_east) - prev_eta)
            prev_west, prev_eta, prev_east, prev_hu = west, new, east, u
        return carry

    lax.fori_loop(0, BSTEPS, step, 0)
    own = slice(HALO, HALO + rows)
    out[0] = eta[own]
    out[1] = hu[own] * 2.0
    out[2] = hv[own] * 2.0


def basin_run(state, depth, pair_state, pair_depth, edge):
    rows, width = depth.shape
    total = rows + 2 * HALO
    vmem = pl.BlockSpec(memory_space=pltpu.VMEM)
    return pl.pallas_call(
        basin_kernel,
        out_shape=jax.ShapeDtypeStruct((3, rows, width), jnp.float32),
        in_specs=[vmem] * 5,
        out_specs=vmem,
        scratch_shapes=[pltpu.VMEM((total, width), jnp.float32)] * 4,
        compiler_params=pltpu.CompilerParams(vmem_limit_bytes=VMEM_LIMIT),
        cost_estimate=pl.CostEstimate(
            flops=BSTEPS * 16 * total * width, bytes_accessed=4 * 11 * rows * width, transcendentals=0
        ),
        name="basin_steps",
    )(state, depth, pair_state, pair_depth, edge)


def strips_kernel(links, own, pair, ghosts, strips):
    rows, width = own.shape[1], own.shape[2]
    count = ghosts.shape[0]
    span = 2 * LANES
    position = lax.axis_index("row")
    tops = (position * rows, (position + 1 - 2 * (position % 2)) * rows)
    lane = lane_ids()
    weight = ((2 * lane + row_ids() % 2) % 16).astype(jnp.float32) / 16.0 + 0.5 / 16.0

    def piece(b, carry):
        col = links[b, 0, 1]
        start = jnp.clip(col // LANES, 0, width // LANES - 2) * LANES
        shift = lax.rem(span - (col - start), span)
        at = pl.ds(pl.multiple_of(start, LANES), span)
        for i, f in enumerate((0, 2)):
            chunk = None
            for source, top in zip((own, pair), tops):
                row = links[b, 0, 0] - top
                owned = jnp.logical_and(row >= 0, row < rows).astype(jnp.float32)
                part = source[f, pl.ds(jnp.clip(row, 0, rows - 1), 1), at] * owned
                chunk = part if chunk is None else chunk + part
            moved = pltpu.roll(chunk, shift, 1)[:, :LANES]
            strips[b, 2 * i : 2 * i + 2] = jnp.broadcast_to(moved, (2, LANES))
        values = strips[b]
        low, high = pick(values, lane // 8), pick(values, lane // 8 + 1)
        ghosts[b] = (1.0 - weight) * low + weight * high
        return carry

    strips[...] = jnp.zeros_like(strips)
    lax.fori_loop(0, count, piece, 0, unroll=8)


def make_strips(links, own, pair):
    count = links.shape[0]
    tiles = (count, SUB, LANES)
    vmem = pl.BlockSpec(memory_space=pltpu.VMEM)
    smem = pl.BlockSpec(memory_space=pltpu.SMEM)
    return pl.pallas_call(
        strips_kernel,
        out_shape=jax.ShapeDtypeStruct(tiles, jnp.float32),
        in_specs=[smem, vmem, vmem],
        out_specs=vmem,
        scratch_shapes=[pltpu.VMEM(tiles, jnp.float32)],
        compiler_params=pltpu.CompilerParams(vmem_limit_bytes=VMEM_LIMIT),
        name="strips",
    )(links, own, pair)


def local(basin_state, basin_depth, coast_depth, coast_flow, coast_link):
    devices = lax.axis_size("row")
    odd = lax.axis_index("row") % 2
    parity = [list(range(p, devices, 2))[::-1] for p in range(2)]
    sent = jnp.broadcast_to(coast_link, (devices // 2,) + coast_link.shape)
    links = lax.all_to_all(sent, "row", 0, 0, axis_index_groups=parity, tiled=True)

    twins = [(i, i ^ 1) for i in range(devices)]
    pair_state, pair_depth = [lax.ppermute(a, "row", twins) for a in (basin_state, basin_depth)]
    ghosts = make_strips(links, basin_state, pair_state)

    coast_depth, ghosts = lax.optimization_barrier((coast_depth, ghosts))
    ghosts = lax.all_to_all(ghosts, "row", 0, 0, axis_index_groups=parity, tiled=True)
    depth, flow = coast_depth[0], coast_flow[0]
    folded = coast_fold(depth, flow)
    later_state, folded = lax.optimization_barrier((basin_state, folded))
    rows = basin_depth.shape[0]
    whole = jnp.concatenate([later_state, basin_depth[None]], axis=0)
    edge = jnp.where(odd == 1, whole[:, rows - HALO :], whole[:, :HALO])
    across = [(i, i + 1) for i in range(1, devices - 1, 2)]
    edge = lax.ppermute(edge, "row", across + [(j, i) for i, j in across])

    coast_out = coast_run(sent, ghosts, folded, depth, flow)
    basin_depth, coast_out = lax.optimization_barrier((basin_depth, coast_out))
    basin_out = basin_run(basin_state, basin_depth, pair_state, pair_depth, edge)
    return (basin_out, coast_out[None])


def solution(mesh):
    in_specs = (
        P("scen", "row", None),
        P("row", "scen"),
        P("row", "scen", None),
        P("row", "scen", None, None),
        P("row", "scen"),
    )
    out_specs = (P("scen", "row", None), P("row", "scen", None, None))
    return jax.shard_map(local, mesh=mesh, in_specs=in_specs, out_specs=out_specs, check_vma=False)
```

```python
import functools

import jax
import jax.numpy as jnp
from jax import lax
from jax.experimental import pallas as pl
from jax.experimental.pallas import tpu as pltpu
from jax.sharding import PartitionSpec as P

BSTEPS = 8
CSTEPS = 10

depth_floor = 0.2
ghost_level = 2.0

RATE = 0.05
DEPTH_UNIT = RATE * RATE
FLOW_UNIT = RATE * RATE * RATE
TINY = 1e-30

HALO = BSTEPS
SUB = 8
LANES = 128


def lane_ids():
    return lax.broadcasted_iota(jnp.int32, (SUB, LANES), 1)


def row_ids():
    return lax.broadcasted_iota(jnp.int32, (SUB, LANES), 0)


def cell_terms(u):
    h, mu, mv = u
    r = pl.reciprocal(jnp.maximum(h, depth_floor * DEPTH_UNIT), approx=True)
    vx, vy = mu * r, mv * r
    hp = jnp.maximum(h, TINY)
    c = hp * lax.rsqrt(hp)
    p = (0.5 * h) * h
    cross = mu * vy
    return {
        "u": u,
        "fx": (mu, mu * vx + p, cross),
        "fy": (mv, cross, mv * vy + p),
        "sx": jnp.abs(vx) + c,
        "sy": jnp.abs(vy) + c,
    }


def y_face(above, below):
    a = jnp.maximum(above["sy"], below["sy"])
    return [
        a * (ub - ua) - (fa + fb)
        for ua, ub, fa, fb in zip(above["u"], below["u"], above["fy"], below["fy"])
    ]


def coast_steps(state, terms, after, parts, opening, rows, group, steps, ghost):
    lane, sub = lane_ids(), row_ids()
    first, last = lane == 0, lane == LANES - 1
    top, bottom = sub == 0, sub == SUB - 1
    zero = jnp.zeros((SUB, LANES), jnp.float32)
    left = functools.partial(pltpu.roll, shift=LANES - 1, axis=1)
    right = functools.partial(pltpu.roll, shift=1, axis=1)

    def load(k):
        return [[state[f, half, 1 + k] for f in range(3)] for half in range(2)]

    def store(k, both):
        for half in range(2):
            for f in range(3):
                state[f, half, 1 + k] = both[half][f]

    def wrapped(tail, head):
        down = functools.partial(pltpu.roll, shift=1, axis=0)
        out = {"sy": jnp.where(top, head["sy"], down(tail["sy"]))}
        for name in ("u", "fy"):
            out[name] = [jnp.where(top, h, down(t)) for h, t in zip(head[name], tail[name])]
        return out

    def terms_of(begin, k):
        even, odd = [cell_terms(u) for u in load(begin + k)]
        for half, cell in enumerate((even, odd)):
            for q, value in enumerate((cell["sx"], cell["sy"], cell["fx"][1], cell["fy"][2], cell["fx"][2])):
                terms[half, k, q] = value
        moved = zip(even["u"] + [even["sx"]] + list(even["fx"][1:]), odd["u"] + [odd["sx"]] + list(odd["fx"][1:]))
        for q, (e, o) in enumerate(moved):
            after[k, q] = jnp.where(last, o, left(e))

    def x_faces(begin, k):
        even, odd = load(begin + k)
        following = [after[k, f] for f in range(3)]
        sx_e, sx_o, sx_n = terms[0, k, 0], terms[1, k, 0], after[k, 3]
        fx_e = [even[1], terms[0, k, 2], terms[0, k, 4]]
        fx_o = [odd[1], terms[1, k, 2], terms[1, k, 4]]
        fx_n = [following[1], after[k, 4], after[k, 5]]
        a_in, a_out = jnp.maximum(sx_e, sx_o), jnp.maximum(sx_o, sx_n)
        for f in range(3):
            g_in = a_in * (odd[f] - even[f]) - (fx_e[f] + fx_o[f])
            g_out = a_out * (following[f] - odd[f]) - (fx_o[f] + fx_n[f])
            parts[k, f] = even[f] + g_in
            parts[k, 3 + f] = odd[f] + (g_out - g_in)
            parts[k, 6 + f] = jnp.where(first, -2.0 * fx_e[f], right(g_out))

    def y_cells(begin, k):
        return [
            {"u": u, "fy": [u[2], terms[half, k, 4], terms[half, k, 3]], "sy": terms[half, k, 1]}
            for half, u in enumerate(load(begin + k))
        ]

    def step(_, carry):
        tails = [cell_terms(u) for u in load(rows - 1)]
        above = [wrapped(t, g) for t, g in zip(tails, ghost)]

        def rows_from(trip, prev, acc):
            begin = trip * group
            for k in range(group):
                terms_of(begin, k)
            for k in range(group):
                x_faces(begin, k)
            for k in range(group):
                cur = y_cells(begin, k)
                face = [y_face(a, b) for a, b in zip(prev, cur)]
                if k == 0:
                    for half in range(2):
                        for f in range(3):
                            opening[trip, half, f] = face[half][f]
                store(begin + k - 1, [[x + g for x, g in zip(*pair)] for pair in zip(acc, face)])
                acc = [
                    [parts[k, f] - (parts[k, 6 + f] + face[0][f]) for f in range(3)],
                    [parts[k, 3 + f] - face[1][f] for f in range(3)],
                ]
                prev = cur
            return prev, acc

        prev, acc = lax.fori_loop(
            0,
            rows // group,
            lambda i, c: rows_from(i, *c),
            (above, [[zero] * 3 for _ in range(2)]),
        )
        end = [
            [
                jnp.where(bottom, -(f + f), pltpu.roll(opening[0, half, i], SUB - 1, 0))
                for i, f in enumerate(cell["fy"])
            ]
            for half, cell in enumerate(prev)
        ]
        store(rows - 1, [[x + g for x, g in zip(*pair)] for pair in zip(acc, end)])
        return carry

    lax.fori_loop(0, steps, step, 0)


GROUP = 16
UNITS = (DEPTH_UNIT, FLOW_UNIT, FLOW_UNIT)
VMEM_LIMIT = 12 * 1024 * 1024
HALF = LANES // 2


def pick(values, ids):
    return jnp.take_along_axis(values, ids, axis=1, mode="promise_in_bounds")


def split_columns(west, east):
    lane = lane_ids()
    low = lane < HALF
    twice = 2 * jnp.where(low, lane, lane - HALF)
    w = pick(west, jnp.where(low, twice, twice + 1))
    e = pick(east, jnp.where(low, twice + 1, twice))
    return jnp.where(low, w, e), pltpu.roll(jnp.where(low, e, w), HALF, 1)


def join_columns(even, odd):
    lane = lane_ids()
    low = lane < HALF
    odd = pltpu.roll(odd, HALF, 1)
    w, e = jnp.where(low, even, odd), jnp.where(low, odd, even)
    half, is_odd = lane // 2, lane % 2
    return pick(w, half + HALF * is_odd), pick(e, half + HALF * (1 - is_odd))


HALVES = (slice(0, LANES), slice(LANES, 2 * LANES))
TALL = 32


def fold_kernel(link, depth, flow, state, wet, tmp):
    rows = depth.shape[0] // SUB
    wet[...] = jnp.broadcast_to(link[:, 2:3], wet.shape).astype(jnp.float32)

    def copy_in(i, carry):
        at = pl.ds(pl.multiple_of(i * TALL, TALL), TALL)
        for f in range(3):
            raw = depth[at] if f == 0 else flow[f - 1, at]
            for p in range(2):
                tmp[f, p, at] = raw[:, HALVES[p]] * UNITS[f]
        return carry

    def fold(k, carry):
        for f in range(3):
            both = split_columns(*[tmp[f, p, pl.ds(k, SUB, stride=rows), :] for p in range(2)])
            for p in range(2):
                state[f, p, k] = both[p]
        return carry

    lax.fori_loop(0, depth.shape[0] // TALL, copy_in, 0)
    lax.fori_loop(0, rows, fold, 0, unroll=4)


def coast_fold(link, depth, flow):
    cells = depth.shape[0]
    vmem = pl.BlockSpec(memory_space=pltpu.VMEM)
    return pl.pallas_call(
        fold_kernel,
        out_shape=(
            jax.ShapeDtypeStruct((3, 2, cells // SUB, SUB, LANES), jnp.float32),
            jax.ShapeDtypeStruct((SUB, LANES), jnp.float32),
        ),
        in_specs=[vmem, vmem, vmem],
        out_specs=(vmem, vmem),
        scratch_shapes=[pltpu.VMEM((3, 2, cells, LANES), jnp.float32)],
        compiler_params=pltpu.CompilerParams(vmem_limit_bytes=VMEM_LIMIT),
        cost_estimate=pl.CostEstimate(
            flops=CSTEPS * 70 * cells * cells, bytes_accessed=24 * cells * cells, transcendentals=0
        ),
        name="coast_fold",
    )(link, depth, flow)


def coast_kernel(
    wet, ghosts, folded, depth, flow, out, state, terms, after, parts, opening, tmp, done, sems
):
    rows = depth.shape[0] // SUB
    is_wet = jnp.max(wet[...]) > 0.0

    def copy_in(k, carry):
        for f in range(3):
            for p in range(2):
                state[f, p, 1 + k] = folded[f, p, k]
        return carry

    @pl.when(jnp.logical_not(is_wet))
    def _():
        copies = [
            pltpu.make_async_copy(depth, out.at[0], sems.at[0]),
            pltpu.make_async_copy(flow, out.at[1:], sems.at[1]),
        ]
        for copy in copies:
            copy.start()
        for copy in copies:
            copy.wait()

    @pl.when(is_wet)
    def _():
        lax.fori_loop(0, rows, copy_in, 0, unroll=4)
        values = jnp.sum(ghosts[...], axis=0)
        level = (ghost_level + values) * DEPTH_UNIT
        inflow = values * FLOW_UNIT
        h, mv = [
            [jnp.broadcast_to(v[i : i + 1], (SUB, LANES)) for i in range(at, at + 2)]
            for v, at in ((level, 0), (inflow, 2))
        ]
        ghost = [cell_terms([h[p], jnp.zeros_like(h[p]), mv[p]]) for p in range(2)]
        coast_steps(state, terms, after, parts, opening, rows, GROUP, CSTEPS, ghost)
        copies = []
        for f in range(3):

            def unfold(k, carry):
                both = join_columns(state[f, 0, 1 + k], state[f, 1, 1 + k])
                for p in range(2):
                    tmp[p, pl.ds(k, SUB, stride=rows), :] = both[p]
                return carry

            def copy_out(i, carry):
                at = pl.ds(pl.multiple_of(i * TALL, TALL), TALL)
                for p in range(2):
                    done[f, at, HALVES[p]] = tmp[p, at] * (1.0 / UNITS[f])
                return carry

            lax.fori_loop(0, rows, unfold, 0, unroll=8)
            lax.fori_loop(0, depth.shape[0] // TALL, copy_out, 0, unroll=2)
            copies.append(pltpu.make_async_copy(done.at[f], out.at[f], sems.at[f]))
            copies[-1].start()
        for copy in copies:
            copy.wait()


def coast_run(wet, ghosts, folded, depth, flow):
    cells = depth.shape[0]
    vmem = pl.BlockSpec(memory_space=pltpu.VMEM)
    return pl.pallas_call(
        coast_kernel,
        out_shape=jax.ShapeDtypeStruct((3, cells, cells), jnp.float32),
        in_specs=[vmem] * 5,
        out_specs=pl.BlockSpec(memory_space=pltpu.HBM),
        scratch_shapes=[
            pltpu.VMEM((3, 2, 1 + cells // SUB, SUB, LANES), jnp.float32),
            pltpu.VMEM((2, GROUP, 5, SUB, LANES), jnp.float32),
            pltpu.VMEM((GROUP, 6, SUB, LANES), jnp.float32),
            pltpu.VMEM((GROUP, 9, SUB, LANES), jnp.float32),
            pltpu.VMEM((cells // SUB // GROUP, 2, 3, SUB, LANES), jnp.float32),
            pltpu.VMEM((2, cells, LANES), jnp.float32),
            pltpu.VMEM((3, cells, cells), jnp.float32),
            pltpu.SemaphoreType.DMA((3,)),
        ],
        compiler_params=pltpu.CompilerParams(vmem_limit_bytes=VMEM_LIMIT),
        cost_estimate=pl.CostEstimate(
            flops=CSTEPS * 70 * cells * cells, bytes_accessed=24 * cells * cells, transcendentals=0
        ),
        name="coast_steps",
    )(wet, ghosts, folded, depth, flow)


def basin_kernel(state, depth, pair_state, pair_depth, edge, out, eta, hu, hv, dep):
    rows, width = depth.shape
    total = rows + 2 * HALO
    chunks = width // LANES
    position = lax.axis_index("row")
    odd = position % 2
    north_inside = (position < lax.axis_size("row") - 1).astype(jnp.float32)
    pair_from = pl.multiple_of(odd * (rows - HALO), HALO)
    pair_at = pl.multiple_of((1 - odd) * (HALO + rows), HALO)
    edge_at = pl.multiple_of(odd * (HALO + rows), HALO)
    def assemble(c, carry):
        at = pl.ds(pl.multiple_of(c * LANES, LANES), LANES)
        for ref, field, unit in ((eta, 0, 1.0), (hu, 1, 0.5), (hv, 2, 0.5), (dep, 3, 0.25)):
            own, pair = (depth, pair_depth) if field == 3 else (state.at[field], pair_state.at[field])
            ref[HALO : HALO + rows, at] = own[:, at] * unit
            ref[pl.ds(pair_at, HALO), at] = pair[pl.ds(pair_from, HALO), at] * unit
            ref[pl.ds(edge_at, HALO), at] = edge[field, :, at] * unit
        return carry

    lax.fori_loop(0, chunks, assemble, 0, unroll=2)
    lane = lax.broadcasted_iota(jnp.int32, (total, LANES), 1)
    first, last = lane == 0, lane == LANES - 1
    row = lax.broadcasted_iota(jnp.int32, (total, LANES), 0)
    kept = jnp.where(row < HALO + rows, 1.0, north_inside)

    def step(_, carry):
        prev_west = jnp.zeros((total, LANES), jnp.float32)
        prev_eta, prev_east, prev_hu = None, None, None
        for c in range(chunks + 1):
            if c < chunks:
                at = slice(c * LANES, (c + 1) * LANES)
                u, v = hu[:, at], hv[:, at]
                west = pltpu.roll(u, 1, 1)
                du = u - jnp.where(first, prev_west, west)
                dv = v - pltpu.roll(v, 1, 0)
                new = (eta[:, at] - (du + dv)) * kept
                eta[:, at] = new
                east = pltpu.roll(new, LANES - 1, 1)
                hv[:, at] = v - dep[:, at] * (pltpu.roll(new, total - 1, 0) - new)
            else:
                east = jnp.zeros((total, LANES), jnp.float32)
            if c > 0:
                back = slice((c - 1) * LANES, c * LANES)
                hu[:, back] = prev_hu - dep[:, back] * (jnp.where(last, east, prev_east) - prev_eta)
            prev_west, prev_eta, prev_east, prev_hu = west, new, east, u
        return carry

    lax.fori_loop(0, BSTEPS, step, 0)
    own = slice(HALO, HALO + rows)
    out[0] = eta[own]
    out[1] = hu[own] * 2.0
    out[2] = hv[own] * 2.0


def basin_run(state, depth, pair_state, pair_depth, edge):
    rows, width = depth.shape
    total = rows + 2 * HALO
    vmem = pl.BlockSpec(memory_space=pltpu.VMEM)
    return pl.pallas_call(
        basin_kernel,
        out_shape=jax.ShapeDtypeStruct((3, rows, width), jnp.float32),
        in_specs=[vmem] * 5,
        out_specs=vmem,
        scratch_shapes=[pltpu.VMEM((total, width), jnp.float32)] * 4,
        compiler_params=pltpu.CompilerParams(vmem_limit_bytes=VMEM_LIMIT),
        cost_estimate=pl.CostEstimate(
            flops=BSTEPS * 16 * total * width, bytes_accessed=4 * 11 * rows * width, transcendentals=0
        ),
        name="basin_steps",
    )(state, depth, pair_state, pair_depth, edge)


def strips_kernel(links, own, pair, ghosts, strips):
    rows, width = own.shape[1], own.shape[2]
    count = ghosts.shape[0]
    span = 2 * LANES
    position = lax.axis_index("row")
    tops = (position * rows, (position + 1 - 2 * (position % 2)) * rows)
    lane = lane_ids()
    weight = ((2 * lane + row_ids() % 2) % 16).astype(jnp.float32) / 16.0 + 0.5 / 16.0

    def piece(b, carry):
        col = links[b, 0, 1]
        start = jnp.clip(col // LANES, 0, width // LANES - 2) * LANES
        shift = lax.rem(span - (col - start), span)
        at = pl.ds(pl.multiple_of(start, LANES), span)
        for i, f in enumerate((0, 2)):
            chunk = None
            for source, top in zip((own, pair), tops):
                row = links[b, 0, 0] - top
                owned = jnp.logical_and(row >= 0, row < rows).astype(jnp.float32)
                part = source[f, pl.ds(jnp.clip(row, 0, rows - 1), 1), at] * owned
                chunk = part if chunk is None else chunk + part
            moved = pltpu.roll(chunk, shift, 1)[:, :LANES]
            strips[b, 2 * i : 2 * i + 2] = jnp.broadcast_to(moved, (2, LANES))
        values = strips[b]
        low, high = pick(values, lane // 8), pick(values, lane // 8 + 1)
        ghosts[b] = (1.0 - weight) * low + weight * high
        return carry

    strips[...] = jnp.zeros_like(strips)
    lax.fori_loop(0, count, piece, 0, unroll=8)


def make_strips(links, own, pair):
    count = links.shape[0]
    tiles = (count, SUB, LANES)
    vmem = pl.BlockSpec(memory_space=pltpu.VMEM)
    smem = pl.BlockSpec(memory_space=pltpu.SMEM)
    return pl.pallas_call(
        strips_kernel,
        out_shape=jax.ShapeDtypeStruct(tiles, jnp.float32),
        in_specs=[smem, vmem, vmem],
        out_specs=vmem,
        scratch_shapes=[pltpu.VMEM(tiles, jnp.float32)],
        compiler_params=pltpu.CompilerParams(vmem_limit_bytes=VMEM_LIMIT),
        name="strips",
    )(links, own, pair)


def local(basin_state, basin_depth, coast_depth, coast_flow, coast_link):
    devices = lax.axis_size("row")
    odd = lax.axis_index("row") % 2
    parity = [list(range(p, devices, 2))[::-1] for p in range(2)]
    sent = jnp.broadcast_to(coast_link, (devices // 2,) + coast_link.shape)
    links = lax.all_to_all(sent, "row", 0, 0, axis_index_groups=parity, tiled=True)

    twins = [(i, i ^ 1) for i in range(devices)]
    pair_state, pair_depth = [lax.ppermute(a, "row", twins) for a in (basin_state, basin_depth)]
    start = odd * (basin_depth.shape[0] - HALO)
    edge = jnp.concatenate(
        [
            lax.dynamic_slice_in_dim(basin_state, start, HALO, axis=1),
            lax.dynamic_slice_in_dim(basin_depth, start, HALO, axis=0)[None],
        ],
        axis=0,
    )
    across = [(i, i + 1) for i in range(1, devices - 1, 2)]
    edge = lax.ppermute(edge, "row", across + [(j, i) for i, j in across])

    basin_out = basin_run(basin_state, basin_depth, pair_state, pair_depth, edge)
    pair_state, basin_out = lax.optimization_barrier((pair_state, basin_out))
    ghosts = make_strips(links, basin_state, pair_state)
    coast_depth, ghosts = lax.optimization_barrier((coast_depth, ghosts))
    ghosts = lax.all_to_all(ghosts, "row", 0, 0, axis_index_groups=parity, tiled=True)
    depth, flow = coast_depth[0], coast_flow[0]
    folded, wet = coast_fold(coast_link, depth, flow)
    coast_out = coast_run(wet, ghosts, folded, depth, flow)
    return (basin_out, coast_out[None])


def solution(mesh):
    in_specs = (
        P("scen", "row", None),
        P("row", "scen"),
        P("row", "scen", None),
        P("row", "scen", None, None),
        P("row", "scen"),
    )
    out_specs = (P("scen", "row", None), P("row", "scen", None, None))
    return jax.shard_map(local, mesh=mesh, in_specs=in_specs, out_specs=out_specs, check_vma=False)
```

```python
import functools

import jax
import jax.numpy as jnp
from jax import lax
from jax.experimental import pallas as pl
from jax.experimental.pallas import tpu as pltpu
from jax.sharding import PartitionSpec as P

BSTEPS = 8
CSTEPS = 10

depth_floor = 0.2
ghost_level = 2.0

RATE = 0.05
DEPTH_UNIT = RATE * RATE
FLOW_UNIT = RATE * RATE * RATE
TINY = 1e-30

HALO = BSTEPS
SUB = 8
LANES = 128


def lane_ids():
    return lax.broadcasted_iota(jnp.int32, (SUB, LANES), 1)


def row_ids():
    return lax.broadcasted_iota(jnp.int32, (SUB, LANES), 0)


def cell_terms(u):
    h, mu, mv = u
    r = pl.reciprocal(jnp.maximum(h, depth_floor * DEPTH_UNIT), approx=True)
    vx, vy = mu * r, mv * r
    hp = jnp.maximum(h, TINY)
    c = hp * lax.rsqrt(hp)
    p = (0.5 * h) * h
    cross = mu * vy
    return {
        "u": u,
        "fx": (mu, mu * vx + p, cross),
        "fy": (mv, cross, mv * vy + p),
        "sx": jnp.abs(vx) + c,
        "sy": jnp.abs(vy) + c,
    }


def y_face(above, below):
    a = jnp.maximum(above["sy"], below["sy"])
    return [
        a * (ub - ua) - (fa + fb)
        for ua, ub, fa, fb in zip(above["u"], below["u"], above["fy"], below["fy"])
    ]


def coast_steps(state, terms, after, parts, opening, rows, group, steps, ghost):
    lane, sub = lane_ids(), row_ids()
    first, last = lane == 0, lane == LANES - 1
    top, bottom = sub == 0, sub == SUB - 1
    zero = jnp.zeros((SUB, LANES), jnp.float32)
    left = functools.partial(pltpu.roll, shift=LANES - 1, axis=1)
    right = functools.partial(pltpu.roll, shift=1, axis=1)

    def load(k):
        return [[state[f, half, 1 + k] for f in range(3)] for half in range(2)]

    def store(k, both):
        for half in range(2):
            for f in range(3):
                state[f, half, 1 + k] = both[half][f]

    def store_above(tails):
        store(-1, [[jnp.where(top, g, pltpu.roll(t, 1, 0)) for g, t in zip(*pair)] for pair in zip(ghost, tails)])

    def y_terms_of(begin, k):
        both = [cell_terms(u) for u in load(begin + k)]
        for half, cell in enumerate(both):
            terms[half, 1 + k, 0] = cell["sy"]
            terms[half, 1 + k, 1] = cell["fy"][2]
            terms[half, 1 + k, 2] = cell["fx"][2]
        return both

    def terms_of(begin, k):
        even, odd = y_terms_of(begin, k)
        for half, cell in enumerate((even, odd)):
            terms[half, 1 + k, 3] = cell["sx"]
            terms[half, 1 + k, 4] = cell["fx"][1]
        moved = zip(even["u"] + [even["sx"]] + list(even["fx"][1:]), odd["u"] + [odd["sx"]] + list(odd["fx"][1:]))
        for q, (e, o) in enumerate(moved):
            after[k, q] = jnp.where(last, o, left(e))

    def x_faces(begin, k):
        even, odd = load(begin + k)
        following = [after[k, f] for f in range(3)]
        sx_e, sx_o, sx_n = terms[0, 1 + k, 3], terms[1, 1 + k, 3], after[k, 3]
        fx_e = [even[1], terms[0, 1 + k, 4], terms[0, 1 + k, 2]]
        fx_o = [odd[1], terms[1, 1 + k, 4], terms[1, 1 + k, 2]]
        fx_n = [following[1], after[k, 4], after[k, 5]]
        a_in, a_out = jnp.maximum(sx_e, sx_o), jnp.maximum(sx_o, sx_n)
        for f in range(3):
            g_in = a_in * (odd[f] - even[f]) - (fx_e[f] + fx_o[f])
            g_out = a_out * (following[f] - odd[f]) - (fx_o[f] + fx_n[f])
            parts[k, f] = even[f] + g_in
            parts[k, 3 + f] = odd[f] + (g_out - g_in)
            parts[k, 6 + f] = jnp.where(first, -2.0 * fx_e[f], right(g_out))

    def y_cells(begin, k):
        return [
            {
                "u": u,
                "fy": [u[2], terms[half, 1 + k, 2], terms[half, 1 + k, 1]],
                "sy": terms[half, 1 + k, 0],
            }
            for half, u in enumerate(load(begin + k))
        ]

    def trip(i, acc):
        begin = i * group
        y_terms_of(begin, -1)
        for k in range(group):
            terms_of(begin, k)
        for k in range(group):
            x_faces(begin, k)
        prev = y_cells(begin, -1)
        for k in range(group):
            cur = y_cells(begin, k)
            face = [y_face(a, b) for a, b in zip(prev, cur)]
            if k == 0:
                for half in range(2):
                    for f in range(3):
                        opening[i, half, f] = pltpu.roll(face[half][f], SUB - 1, 0)
            store(begin + k - 1, [[x + g for x, g in zip(*pair)] for pair in zip(acc, face)])
            acc = [
                [parts[k, f] - (parts[k, 6 + f] + face[0][f]) for f in range(3)],
                [parts[k, 3 + f] - face[1][f] for f in range(3)],
            ]
            prev = cur
        return acc

    def step(_, carry):
        acc = lax.fori_loop(0, rows // group, trip, [[zero] * 3 for _ in range(2)])
        tails = [
            [
                x + jnp.where(bottom, -2.0 * f, opening[0, half, i])
                for i, (x, f) in enumerate(zip(xs, cell["fy"]))
            ]
            for half, (xs, cell) in enumerate(zip(acc, y_cells(rows - group, group - 1)))
        ]
        store(rows - 1, tails)
        store_above(tails)
        return carry

    store_above(load(rows - 1))
    lax.fori_loop(0, steps, step, 0)


GROUP = 16
UNITS = (DEPTH_UNIT, FLOW_UNIT, FLOW_UNIT)
VMEM_LIMIT = 12 * 1024 * 1024
HALF = LANES // 2


def pick(values, ids):
    return jnp.take_along_axis(values, ids, axis=1, mode="promise_in_bounds")


def split_columns(west, east):
    lane = lane_ids()
    low = lane < HALF
    twice = 2 * jnp.where(low, lane, lane - HALF)
    w = pick(west, jnp.where(low, twice, twice + 1))
    e = pick(east, jnp.where(low, twice + 1, twice))
    return jnp.where(low, w, e), pltpu.roll(jnp.where(low, e, w), HALF, 1)


def join_columns(even, odd):
    lane = lane_ids()
    low = lane < HALF
    odd = pltpu.roll(odd, HALF, 1)
    w, e = jnp.where(low, even, odd), jnp.where(low, odd, even)
    half, is_odd = lane // 2, lane % 2
    return pick(w, half + HALF * is_odd), pick(e, half + HALF * (1 - is_odd))


HALVES = (slice(0, LANES), slice(LANES, 2 * LANES))
TALL = 32


def fold_kernel(link, depth, flow, state, wet, tmp):
    rows = depth.shape[0] // SUB
    wet[...] = jnp.broadcast_to(link[:, 2:3], wet.shape).astype(jnp.float32)

    def copy_in(i, carry):
        at = pl.ds(pl.multiple_of(i * TALL, TALL), TALL)
        for f in range(3):
            raw = depth[at] if f == 0 else flow[f - 1, at]
            for p in range(2):
                tmp[f, p, at] = raw[:, HALVES[p]] * UNITS[f]
        return carry

    def fold(k, carry):
        for f in range(3):
            both = split_columns(*[tmp[f, p, pl.ds(k, SUB, stride=rows), :] for p in range(2)])
            for p in range(2):
                state[f, p, k] = both[p]
        return carry

    lax.fori_loop(0, depth.shape[0] // TALL, copy_in, 0)
    lax.fori_loop(0, rows, fold, 0, unroll=4)


def coast_fold(link, depth, flow):
    cells = depth.shape[0]
    vmem = pl.BlockSpec(memory_space=pltpu.VMEM)
    return pl.pallas_call(
        fold_kernel,
        out_shape=(
            jax.ShapeDtypeStruct((3, 2, cells // SUB, SUB, LANES), jnp.float32),
            jax.ShapeDtypeStruct((SUB, LANES), jnp.float32),
        ),
        in_specs=[vmem, vmem, vmem],
        out_specs=(vmem, vmem),
        scratch_shapes=[pltpu.VMEM((3, 2, cells, LANES), jnp.float32)],
        compiler_params=pltpu.CompilerParams(vmem_limit_bytes=VMEM_LIMIT),
        cost_estimate=pl.CostEstimate(
            flops=CSTEPS * 70 * cells * cells, bytes_accessed=24 * cells * cells, transcendentals=0
        ),
        name="coast_fold",
    )(link, depth, flow)


def coast_kernel(
    wet, ghosts, folded, depth, flow, out, state, terms, after, parts, opening, tmp, done, sems
):
    rows = depth.shape[0] // SUB
    is_wet = jnp.max(wet[...]) > 0.0

    def copy_in(k, carry):
        for f in range(3):
            for p in range(2):
                state[f, p, 1 + k] = folded[f, p, k]
        return carry

    @pl.when(jnp.logical_not(is_wet))
    def _():
        copies = [
            pltpu.make_async_copy(depth, out.at[0], sems.at[0]),
            pltpu.make_async_copy(flow, out.at[1:], sems.at[1]),
        ]
        for copy in copies:
            copy.start()
        for copy in copies:
            copy.wait()

    @pl.when(is_wet)
    def _():
        lax.fori_loop(0, rows, copy_in, 0, unroll=4)
        values = jnp.sum(ghosts[...], axis=0)
        level = (ghost_level + values) * DEPTH_UNIT
        inflow = values * FLOW_UNIT
        h, mv = [
            [jnp.broadcast_to(v[i : i + 1], (SUB, LANES)) for i in range(at, at + 2)]
            for v, at in ((level, 0), (inflow, 2))
        ]
        ghost = [[h[p], jnp.zeros_like(h[p]), mv[p]] for p in range(2)]
        coast_steps(state, terms, after, parts, opening, rows, GROUP, CSTEPS, ghost)

        def write(f):
            return pltpu.make_async_copy(done.at[f], out.at[f], sems.at[f])

        def finish(f, carry):
            scale = jnp.where(f == 0, 1.0 / DEPTH_UNIT, 1.0 / FLOW_UNIT)

            def unfold(k, carry):
                both = join_columns(state[f, 0, 1 + k], state[f, 1, 1 + k])
                for p in range(2):
                    tmp[p, pl.ds(k, SUB, stride=rows), :] = both[p] * scale
                return carry

            def copy_out(i, carry):
                at = pl.ds(pl.multiple_of(i * TALL, TALL), TALL)
                for p in range(2):
                    done[f, at, HALVES[p]] = tmp[p, at]
                return carry

            lax.fori_loop(0, rows, unfold, 0, unroll=16)
            lax.fori_loop(0, depth.shape[0] // TALL, copy_out, 0, unroll=4)
            write(f).start()
            return carry

        lax.fori_loop(0, 3, finish, 0)
        for f in range(3):
            write(f).wait()


def coast_run(wet, ghosts, folded, depth, flow):
    cells = depth.shape[0]
    vmem = pl.BlockSpec(memory_space=pltpu.VMEM)
    return pl.pallas_call(
        coast_kernel,
        out_shape=jax.ShapeDtypeStruct((3, cells, cells), jnp.float32),
        in_specs=[vmem] * 5,
        out_specs=pl.BlockSpec(memory_space=pltpu.HBM),
        scratch_shapes=[
            pltpu.VMEM((3, 2, 1 + cells // SUB, SUB, LANES), jnp.float32),
            pltpu.VMEM((2, 1 + GROUP, 5, SUB, LANES), jnp.float32),
            pltpu.VMEM((GROUP, 6, SUB, LANES), jnp.float32),
            pltpu.VMEM((GROUP, 9, SUB, LANES), jnp.float32),
            pltpu.VMEM((cells // SUB // GROUP, 2, 3, SUB, LANES), jnp.float32),
            pltpu.VMEM((2, cells, LANES), jnp.float32),
            pltpu.VMEM((3, cells, cells), jnp.float32),
            pltpu.SemaphoreType.DMA((3,)),
        ],
        compiler_params=pltpu.CompilerParams(vmem_limit_bytes=VMEM_LIMIT),
        cost_estimate=pl.CostEstimate(
            flops=CSTEPS * 70 * cells * cells, bytes_accessed=24 * cells * cells, transcendentals=0
        ),
        name="coast_steps",
    )(wet, ghosts, folded, depth, flow)


def basin_kernel(state, depth, pair_state, pair_depth, edge, out, eta, hu, hv, dep):
    rows, width = depth.shape
    total = rows + 2 * HALO
    chunks = width // LANES
    position = lax.axis_index("row")
    odd = position % 2
    north_inside = (position < lax.axis_size("row") - 1).astype(jnp.float32)
    pair_from = pl.multiple_of(odd * (rows - HALO), HALO)
    pair_at = pl.multiple_of((1 - odd) * (HALO + rows), HALO)
    edge_at = pl.multiple_of(odd * (HALO + rows), HALO)
    for ref, field, unit in ((eta, 0, 1.0), (hu, 1, 0.5), (hv, 2, 0.5), (dep, 3, 0.25)):
        own, pair = (depth, pair_depth) if field == 3 else (state.at[field], pair_state.at[field])
        ref[HALO : HALO + rows] = own[...] * unit
        ref[pl.ds(pair_at, HALO)] = pair[pl.ds(pair_from, HALO)] * unit
        ref[pl.ds(edge_at, HALO)] = edge[field] * unit
    lane = lax.broadcasted_iota(jnp.int32, (total, LANES), 1)
    first, last = lane == 0, lane == LANES - 1
    row = lax.broadcasted_iota(jnp.int32, (total, LANES), 0)
    kept = jnp.where(row < HALO + rows, 1.0, north_inside)

    def step(_, carry):
        prev_west = jnp.zeros((total, LANES), jnp.float32)
        prev_eta, prev_east, prev_hu = None, None, None
        for c in range(chunks + 1):
            if c < chunks:
                at = slice(c * LANES, (c + 1) * LANES)
                u, v = hu[:, at], hv[:, at]
                west = pltpu.roll(u, 1, 1)
                du = u - jnp.where(first, prev_west, west)
                dv = v - pltpu.roll(v, 1, 0)
                new = (eta[:, at] - (du + dv)) * kept
                eta[:, at] = new
                east = pltpu.roll(new, LANES - 1, 1)
                hv[:, at] = v - dep[:, at] * (pltpu.roll(new, total - 1, 0) - new)
            else:
                east = jnp.zeros((total, LANES), jnp.float32)
            if c > 0:
                back = slice((c - 1) * LANES, c * LANES)
                hu[:, back] = prev_hu - dep[:, back] * (jnp.where(last, east, prev_east) - prev_eta)
            prev_west, prev_eta, prev_east, prev_hu = west, new, east, u
        return carry

    lax.fori_loop(0, BSTEPS, step, 0)
    own = slice(HALO, HALO + rows)
    out[0] = eta[own]
    out[1] = hu[own] * 2.0
    out[2] = hv[own] * 2.0


def basin_run(state, depth, pair_state, pair_depth, edge):
    rows, width = depth.shape
    total = rows + 2 * HALO
    vmem = pl.BlockSpec(memory_space=pltpu.VMEM)
    return pl.pallas_call(
        basin_kernel,
        out_shape=jax.ShapeDtypeStruct((3, rows, width), jnp.float32),
        in_specs=[vmem] * 5,
        out_specs=vmem,
        scratch_shapes=[pltpu.VMEM((total, width), jnp.float32)] * 4,
        compiler_params=pltpu.CompilerParams(vmem_limit_bytes=VMEM_LIMIT),
        cost_estimate=pl.CostEstimate(
            flops=BSTEPS * 16 * total * width, bytes_accessed=4 * 11 * rows * width, transcendentals=0
        ),
        name="basin_steps",
    )(state, depth, pair_state, pair_depth, edge)


def strips_kernel(links, own, pair, ghosts, strips):
    rows, width = own.shape[1], own.shape[2]
    count = ghosts.shape[0]
    span = 2 * LANES
    position = lax.axis_index("row")
    tops = (position * rows, (position + 1 - 2 * (position % 2)) * rows)
    lane = lane_ids()
    weight = ((2 * lane + row_ids() % 2) % 16).astype(jnp.float32) / 16.0 + 0.5 / 16.0

    def piece(b, carry):
        col = links[b, 0, 1]
        start = jnp.clip(col // LANES, 0, width // LANES - 2) * LANES
        shift = lax.rem(span - (col - start), span)
        at = pl.ds(pl.multiple_of(start, LANES), span)
        for i, f in enumerate((0, 2)):
            chunk = None
            for source, top in zip((own, pair), tops):
                row = links[b, 0, 0] - top
                owned = jnp.logical_and(row >= 0, row < rows).astype(jnp.float32)
                part = source[f, pl.ds(jnp.clip(row, 0, rows - 1), 1), at] * owned
                chunk = part if chunk is None else chunk + part
            moved = pltpu.roll(chunk, shift, 1)[:, :LANES]
            strips[b, 2 * i : 2 * i + 2] = jnp.broadcast_to(moved, (2, LANES))
        values = strips[b]
        low, high = pick(values, lane // 8), pick(values, lane // 8 + 1)
        ghosts[b] = (1.0 - weight) * low + weight * high
        return carry

    strips[...] = jnp.zeros_like(strips)
    lax.fori_loop(0, count, piece, 0, unroll=8)


def make_strips(links, own, pair):
    count = links.shape[0]
    tiles = (count, SUB, LANES)
    vmem = pl.BlockSpec(memory_space=pltpu.VMEM)
    smem = pl.BlockSpec(memory_space=pltpu.SMEM)
    return pl.pallas_call(
        strips_kernel,
        out_shape=jax.ShapeDtypeStruct(tiles, jnp.float32),
        in_specs=[smem, vmem, vmem],
        out_specs=vmem,
        scratch_shapes=[pltpu.VMEM(tiles, jnp.float32)],
        compiler_params=pltpu.CompilerParams(vmem_limit_bytes=VMEM_LIMIT),
        name="strips",
    )(links, own, pair)


def local(basin_state, basin_depth, coast_depth, coast_flow, coast_link):
    devices = lax.axis_size("row")
    odd = lax.axis_index("row") % 2
    parity = [list(range(p, devices, 2))[::-1] for p in range(2)]
    sent = jnp.broadcast_to(coast_link, (devices // 2,) + coast_link.shape)
    links = lax.all_to_all(sent, "row", 0, 0, axis_index_groups=parity, tiled=True)

    twins = [(i, i ^ 1) for i in range(devices)]
    pair_state, pair_depth = [lax.ppermute(a, "row", twins) for a in (basin_state, basin_depth)]
    start = odd * (basin_depth.shape[0] - HALO)
    edge = jnp.concatenate(
        [
            lax.dynamic_slice_in_dim(basin_state, start, HALO, axis=1),
            lax.dynamic_slice_in_dim(basin_depth, start, HALO, axis=0)[None],
        ],
        axis=0,
    )
    across = [(i, i + 1) for i in range(1, devices - 1, 2)]
    edge = lax.ppermute(edge, "row", across + [(j, i) for i, j in across])

    basin_out = basin_run(basin_state, basin_depth, pair_state, pair_depth, edge)
    pair_state, basin_out = lax.optimization_barrier((pair_state, basin_out))
    ghosts = make_strips(links, basin_state, pair_state)
    coast_depth, ghosts = lax.optimization_barrier((coast_depth, ghosts))
    ghosts = lax.all_to_all(ghosts, "row", 0, 0, axis_index_groups=parity, tiled=True)
    depth, flow = coast_depth[0], coast_flow[0]
    folded, wet = coast_fold(coast_link, depth, flow)
    coast_out = coast_run(wet, ghosts, folded, depth, flow)
    return (basin_out, coast_out[None])


def solution(mesh):
    in_specs = (
        P("scen", "row", None),
        P("row", "scen"),
        P("row", "scen", None),
        P("row", "scen", None, None),
        P("row", "scen"),
    )
    out_specs = (P("scen", "row", None), P("row", "scen", None, None))
    return jax.shard_map(local, mesh=mesh, in_specs=in_specs, out_specs=out_specs, check_vma=False)
```

```python
import functools

import jax
import jax.numpy as jnp
from jax import lax
from jax.experimental import pallas as pl
from jax.experimental.pallas import tpu as pltpu
from jax.sharding import PartitionSpec as P

BSTEPS = 8
CSTEPS = 10

depth_floor = 0.2
ghost_level = 2.0

RATE = 0.05
DEPTH_UNIT = RATE * RATE
FLOW_UNIT = RATE * RATE * RATE
TINY = 1e-30

HALO = BSTEPS
SUB = 8
LANES = 128


def lane_ids():
    return lax.broadcasted_iota(jnp.int32, (SUB, LANES), 1)


def row_ids():
    return lax.broadcasted_iota(jnp.int32, (SUB, LANES), 0)


def cell_terms(u):
    h, mu, mv = u
    r = pl.reciprocal(jnp.maximum(h, depth_floor * DEPTH_UNIT), approx=True)
    vx, vy = mu * r, mv * r
    hp = jnp.maximum(h, TINY)
    c = hp * lax.rsqrt(hp)
    p = (0.5 * h) * h
    cross = mu * vy
    return {
        "u": u,
        "fx": (mu, mu * vx + p, cross),
        "fy": (mv, cross, mv * vy + p),
        "sx": jnp.abs(vx) + c,
        "sy": jnp.abs(vy) + c,
    }


def y_face(above, below):
    a = jnp.maximum(above["sy"], below["sy"])
    return [
        a * (ub - ua) - (fa + fb)
        for ua, ub, fa, fb in zip(above["u"], below["u"], above["fy"], below["fy"])
    ]


def coast_steps(state, terms, after, parts, opening, rows, group, steps, ghost):
    lane, sub = lane_ids(), row_ids()
    first, last = lane == 0, lane == LANES - 1
    top, bottom = sub == 0, sub == SUB - 1
    zero = jnp.zeros((SUB, LANES), jnp.float32)
    left = functools.partial(pltpu.roll, shift=LANES - 1, axis=1)
    right = functools.partial(pltpu.roll, shift=1, axis=1)

    def load(view, k):
        return [[view[f, half, 1 + k] for f in range(3)] for half in range(2)]

    def store(view, k, both):
        for half in range(2):
            for f in range(3):
                view[f, half, 1 + k] = both[half][f]

    def store_above(tails):
        store(state, -1, [[jnp.where(top, g, pltpu.roll(t, 1, 0)) for g, t in zip(*pair)] for pair in zip(ghost, tails)])

    def y_terms_of(view, k):
        both = [cell_terms(u) for u in load(view, k)]
        for half, cell in enumerate(both):
            terms[half, 1 + k, 0] = cell["sy"]
            terms[half, 1 + k, 1] = cell["fy"][2]
            terms[half, 1 + k, 2] = cell["fx"][2]
        return both

    def terms_of(view, k):
        even, odd = y_terms_of(view, k)
        for half, cell in enumerate((even, odd)):
            terms[half, 1 + k, 3] = cell["sx"]
            terms[half, 1 + k, 4] = cell["fx"][1]
        moved = zip(even["u"] + [even["sx"]] + list(even["fx"][1:]), odd["u"] + [odd["sx"]] + list(odd["fx"][1:]))
        for q, (e, o) in enumerate(moved):
            after[k, q] = jnp.where(last, o, left(e))

    def x_faces(view, k):
        even, odd = load(view, k)
        following = [after[k, f] for f in range(3)]
        sx_e, sx_o, sx_n = terms[0, 1 + k, 3], terms[1, 1 + k, 3], after[k, 3]
        fx_e = [even[1], terms[0, 1 + k, 4], terms[0, 1 + k, 2]]
        fx_o = [odd[1], terms[1, 1 + k, 4], terms[1, 1 + k, 2]]
        fx_n = [following[1], after[k, 4], after[k, 5]]
        a_in, a_out = jnp.maximum(sx_e, sx_o), jnp.maximum(sx_o, sx_n)
        for f in range(3):
            g_in = a_in * (odd[f] - even[f]) - (fx_e[f] + fx_o[f])
            g_out = a_out * (following[f] - odd[f]) - (fx_o[f] + fx_n[f])
            g_back = jnp.where(first, -2.0 * fx_e[f], right(g_out))
            parts[k, f] = even[f] + (g_in - g_back)
            parts[k, 3 + f] = odd[f] + (g_out - g_in)

    def y_cells(view, k):
        return [
            {
                "u": u,
                "fy": [u[2], terms[half, 1 + k, 2], terms[half, 1 + k, 1]],
                "sy": terms[half, 1 + k, 0],
            }
            for half, u in enumerate(load(view, k))
        ]

    def trip(i, acc):
        view = state.at[:, :, pl.ds(i * group, 1 + group)]
        y_terms_of(view, -1)
        for k in range(group):
            terms_of(view, k)
        for k in range(group):
            x_faces(view, k)
        prev = y_cells(view, -1)
        for k in range(group):
            cur = y_cells(view, k)
            face = [y_face(a, b) for a, b in zip(prev, cur)]
            if k == 0:
                for half in range(2):
                    for f in range(3):
                        opening[i, half, f] = pltpu.roll(face[half][f], SUB - 1, 0)
            store(view, k - 1, [[x + g for x, g in zip(*pair)] for pair in zip(acc, face)])
            acc = [[parts[k, 3 * half + f] - face[half][f] for f in range(3)] for half in range(2)]
            prev = cur
        return acc

    def step(_, carry):
        acc = lax.fori_loop(0, rows // group, trip, [[zero] * 3 for _ in range(2)])
        tails = [
            [
                x + jnp.where(bottom, -2.0 * f, opening[0, half, i])
                for i, (x, f) in enumerate(zip(xs, cell["fy"]))
            ]
            for half, (xs, cell) in enumerate(
                zip(acc, y_cells(state.at[:, :, rows - group :], group - 1))
            )
        ]
        store(state, rows - 1, tails)
        store_above(tails)
        return carry

    store_above(load(state, rows - 1))
    lax.fori_loop(0, steps, step, 0)


GROUP = 16
UNITS = (DEPTH_UNIT, FLOW_UNIT, FLOW_UNIT)
VMEM_LIMIT = 12 * 1024 * 1024
HALF = LANES // 2


def pick(values, ids):
    return jnp.take_along_axis(values, ids, axis=1, mode="promise_in_bounds")


def split_columns(west, east):
    lane = lane_ids()
    low = lane < HALF
    twice = 2 * jnp.where(low, lane, lane - HALF)
    w = pick(west, jnp.where(low, twice, twice + 1))
    e = pick(east, jnp.where(low, twice + 1, twice))
    return jnp.where(low, w, e), pltpu.roll(jnp.where(low, e, w), HALF, 1)


def join_columns(even, odd):
    lane = lane_ids()
    low = lane < HALF
    odd = pltpu.roll(odd, HALF, 1)
    w, e = jnp.where(low, even, odd), jnp.where(low, odd, even)
    half, is_odd = lane // 2, lane % 2
    return pick(w, half + HALF * is_odd), pick(e, half + HALF * (1 - is_odd))


HALVES = (slice(0, LANES), slice(LANES, 2 * LANES))
TALL = 32


def fold_kernel(link, depth, flow, state, wet, tmp):
    rows = depth.shape[0] // SUB
    wet[...] = jnp.broadcast_to(link[:, 2:3], wet.shape).astype(jnp.float32)

    def copy_in(i, carry):
        at = pl.ds(pl.multiple_of(i * TALL, TALL), TALL)
        for f in range(3):
            raw = depth[at] if f == 0 else flow[f - 1, at]
            for p in range(2):
                tmp[f, p, at] = raw[:, HALVES[p]] * UNITS[f]
        return carry

    def fold(k, carry):
        for f in range(3):
            both = split_columns(*[tmp[f, p, pl.ds(k, SUB, stride=rows), :] for p in range(2)])
            for p in range(2):
                state[f, p, k] = both[p]
        return carry

    lax.fori_loop(0, depth.shape[0] // TALL, copy_in, 0)
    lax.fori_loop(0, rows, fold, 0, unroll=4)


def coast_fold(link, depth, flow):
    cells = depth.shape[0]
    vmem = pl.BlockSpec(memory_space=pltpu.VMEM)
    return pl.pallas_call(
        fold_kernel,
        out_shape=(
            jax.ShapeDtypeStruct((3, 2, cells // SUB, SUB, LANES), jnp.float32),
            jax.ShapeDtypeStruct((SUB, LANES), jnp.float32),
        ),
        in_specs=[vmem, vmem, vmem],
        out_specs=(vmem, vmem),
        scratch_shapes=[pltpu.VMEM((3, 2, cells, LANES), jnp.float32)],
        compiler_params=pltpu.CompilerParams(vmem_limit_bytes=VMEM_LIMIT),
        cost_estimate=pl.CostEstimate(
            flops=CSTEPS * 70 * cells * cells, bytes_accessed=24 * cells * cells, transcendentals=0
        ),
        name="coast_fold",
    )(link, depth, flow)


def coast_kernel(
    wet, ghosts, folded, depth, flow, out, state, terms, after, parts, opening, tmp, done, sems
):
    rows = depth.shape[0] // SUB
    is_wet = jnp.max(wet[...]) > 0.0

    def copy_in(k, carry):
        for f in range(3):
            for p in range(2):
                state[f, p, 1 + k] = folded[f, p, k]
        return carry

    @pl.when(jnp.logical_not(is_wet))
    def _():
        copies = [
            pltpu.make_async_copy(depth, out.at[0], sems.at[0]),
            pltpu.make_async_copy(flow, out.at[1:], sems.at[1]),
        ]
        for copy in copies:
            copy.start()
        for copy in copies:
            copy.wait()

    @pl.when(is_wet)
    def _():
        lax.fori_loop(0, rows, copy_in, 0, unroll=4)
        values = jnp.sum(ghosts[...], axis=0)
        level = (ghost_level + values) * DEPTH_UNIT
        inflow = values * FLOW_UNIT
        h, mv = [
            [jnp.broadcast_to(v[i : i + 1], (SUB, LANES)) for i in range(at, at + 2)]
            for v, at in ((level, 0), (inflow, 2))
        ]
        ghost = [[h[p], jnp.zeros_like(h[p]), mv[p]] for p in range(2)]
        coast_steps(state, terms, after, parts, opening, rows, GROUP, CSTEPS, ghost)

        def write(f):
            return pltpu.make_async_copy(done.at[f], out.at[f], sems.at[f])

        def finish(f, carry):
            scale = jnp.where(f == 0, 1.0 / DEPTH_UNIT, 1.0 / FLOW_UNIT)

            def unfold(k, carry):
                both = join_columns(state[f, 0, 1 + k], state[f, 1, 1 + k])
                for p in range(2):
                    tmp[p, pl.ds(k, SUB, stride=rows), :] = both[p] * scale
                return carry

            def copy_out(i, carry):
                at = pl.ds(pl.multiple_of(i * TALL, TALL), TALL)
                for p in range(2):
                    done[f, at, HALVES[p]] = tmp[p, at]
                return carry

            lax.fori_loop(0, rows, unfold, 0, unroll=16)
            lax.fori_loop(0, depth.shape[0] // TALL, copy_out, 0, unroll=4)
            write(f).start()
            return carry

        lax.fori_loop(0, 3, finish, 0)
        for f in range(3):
            write(f).wait()


def coast_run(wet, ghosts, folded, depth, flow):
    cells = depth.shape[0]
    vmem = pl.BlockSpec(memory_space=pltpu.VMEM)
    return pl.pallas_call(
        coast_kernel,
        out_shape=jax.ShapeDtypeStruct((3, cells, cells), jnp.float32),
        in_specs=[vmem] * 5,
        out_specs=pl.BlockSpec(memory_space=pltpu.HBM),
        scratch_shapes=[
            pltpu.VMEM((3, 2, 1 + cells // SUB, SUB, LANES), jnp.float32),
            pltpu.VMEM((2, 1 + GROUP, 5, SUB, LANES), jnp.float32),
            pltpu.VMEM((GROUP, 6, SUB, LANES), jnp.float32),
            pltpu.VMEM((GROUP, 6, SUB, LANES), jnp.float32),
            pltpu.VMEM((cells // SUB // GROUP, 2, 3, SUB, LANES), jnp.float32),
            pltpu.VMEM((2, cells, LANES), jnp.float32),
            pltpu.VMEM((3, cells, cells), jnp.float32),
            pltpu.SemaphoreType.DMA((3,)),
        ],
        compiler_params=pltpu.CompilerParams(vmem_limit_bytes=VMEM_LIMIT),
        cost_estimate=pl.CostEstimate(
            flops=CSTEPS * 70 * cells * cells, bytes_accessed=24 * cells * cells, transcendentals=0
        ),
        name="coast_steps",
    )(wet, ghosts, folded, depth, flow)


def basin_kernel(state, depth, pair_state, pair_depth, edge, out, eta, hu, hv, dep):
    rows, width = depth.shape
    total = rows + 2 * HALO
    chunks = width // LANES
    position = lax.axis_index("row")
    odd = position % 2
    north_inside = (position < lax.axis_size("row") - 1).astype(jnp.float32)
    pair_from = pl.multiple_of(odd * (rows - HALO), HALO)
    pair_at = pl.multiple_of((1 - odd) * (HALO + rows), HALO)
    edge_at = pl.multiple_of(odd * (HALO + rows), HALO)
    for ref, field, unit in ((eta, 0, 1.0), (hu, 1, 0.5), (hv, 2, 0.5), (dep, 3, 0.25)):
        own, pair = (depth, pair_depth) if field == 3 else (state.at[field], pair_state.at[field])
        ref[HALO : HALO + rows] = own[...] * unit
        ref[pl.ds(pair_at, HALO)] = pair[pl.ds(pair_from, HALO)] * unit
        ref[pl.ds(edge_at, HALO)] = edge[field] * unit
    lane = lax.broadcasted_iota(jnp.int32, (total, LANES), 1)
    first, last = lane == 0, lane == LANES - 1
    row = lax.broadcasted_iota(jnp.int32, (total, LANES), 0)
    kept = jnp.where(row < HALO + rows, 1.0, north_inside)

    def step(_, carry):
        prev_west = jnp.zeros((total, LANES), jnp.float32)
        prev_eta, prev_east, prev_hu = None, None, None
        for c in range(chunks + 1):
            if c < chunks:
                at = slice(c * LANES, (c + 1) * LANES)
                u, v = hu[:, at], hv[:, at]
                west = pltpu.roll(u, 1, 1)
                du = u - jnp.where(first, prev_west, west)
                dv = v - pltpu.roll(v, 1, 0)
                new = (eta[:, at] - (du + dv)) * kept
                eta[:, at] = new
                east = pltpu.roll(new, LANES - 1, 1)
                hv[:, at] = v - dep[:, at] * (pltpu.roll(new, total - 1, 0) - new)
            else:
                east = jnp.zeros((total, LANES), jnp.float32)
            if c > 0:
                back = slice((c - 1) * LANES, c * LANES)
                hu[:, back] = prev_hu - dep[:, back] * (jnp.where(last, east, prev_east) - prev_eta)
            prev_west, prev_eta, prev_east, prev_hu = west, new, east, u
        return carry

    lax.fori_loop(0, BSTEPS, step, 0)
    own = slice(HALO, HALO + rows)
    out[0] = eta[own]
    out[1] = hu[own] * 2.0
    out[2] = hv[own] * 2.0


def basin_run(state, depth, pair_state, pair_depth, edge):
    rows, width = depth.shape
    total = rows + 2 * HALO
    vmem = pl.BlockSpec(memory_space=pltpu.VMEM)
    return pl.pallas_call(
        basin_kernel,
        out_shape=jax.ShapeDtypeStruct((3, rows, width), jnp.float32),
        in_specs=[vmem] * 5,
        out_specs=vmem,
        scratch_shapes=[pltpu.VMEM((total, width), jnp.float32)] * 4,
        compiler_params=pltpu.CompilerParams(vmem_limit_bytes=VMEM_LIMIT),
        cost_estimate=pl.CostEstimate(
            flops=BSTEPS * 16 * total * width, bytes_accessed=4 * 11 * rows * width, transcendentals=0
        ),
        name="basin_steps",
    )(state, depth, pair_state, pair_depth, edge)


def strips_kernel(links, own, pair, ghosts, strips):
    rows, width = own.shape[1], own.shape[2]
    count = ghosts.shape[0]
    span = 2 * LANES
    position = lax.axis_index("row")
    tops = (position * rows, (position + 1 - 2 * (position % 2)) * rows)
    lane = lane_ids()
    weight = ((2 * lane + row_ids() % 2) % 16).astype(jnp.float32) / 16.0 + 0.5 / 16.0

    def piece(b, carry):
        col = links[b, 0, 1]
        start = jnp.clip(col // LANES, 0, width // LANES - 2) * LANES
        shift = lax.rem(span - (col - start), span)
        at = pl.ds(pl.multiple_of(start, LANES), span)
        for i, f in enumerate((0, 2)):
            chunk = None
            for source, top in zip((own, pair), tops):
                row = links[b, 0, 0] - top
                owned = jnp.logical_and(row >= 0, row < rows).astype(jnp.float32)
                part = source[f, pl.ds(jnp.clip(row, 0, rows - 1), 1), at] * owned
                chunk = part if chunk is None else chunk + part
            moved = pltpu.roll(chunk, shift, 1)[:, :LANES]
            strips[b, 2 * i : 2 * i + 2] = jnp.broadcast_to(moved, (2, LANES))
        values = strips[b]
        low, high = pick(values, lane // 8), pick(values, lane // 8 + 1)
        ghosts[b] = (1.0 - weight) * low + weight * high
        return carry

    strips[...] = jnp.zeros_like(strips)
    lax.fori_loop(0, count, piece, 0, unroll=8)


def make_strips(links, own, pair):
    count = links.shape[0]
    tiles = (count, SUB, LANES)
    vmem = pl.BlockSpec(memory_space=pltpu.VMEM)
    smem = pl.BlockSpec(memory_space=pltpu.SMEM)
    return pl.pallas_call(
        strips_kernel,
        out_shape=jax.ShapeDtypeStruct(tiles, jnp.float32),
        in_specs=[smem, vmem, vmem],
        out_specs=vmem,
        scratch_shapes=[pltpu.VMEM(tiles, jnp.float32)],
        compiler_params=pltpu.CompilerParams(vmem_limit_bytes=VMEM_LIMIT),
        name="strips",
    )(links, own, pair)


def local(basin_state, basin_depth, coast_depth, coast_flow, coast_link):
    devices = lax.axis_size("row")
    odd = lax.axis_index("row") % 2
    parity = [list(range(p, devices, 2))[::-1] for p in range(2)]
    sent = jnp.broadcast_to(coast_link, (devices // 2,) + coast_link.shape)
    links = lax.all_to_all(sent, "row", 0, 0, axis_index_groups=parity, tiled=True)

    twins = [(i, i ^ 1) for i in range(devices)]
    pair_state, pair_depth = [lax.ppermute(a, "row", twins) for a in (basin_state, basin_depth)]
    start = odd * (basin_depth.shape[0] - HALO)
    edge = jnp.concatenate(
        [
            lax.dynamic_slice_in_dim(basin_state, start, HALO, axis=1),
            lax.dynamic_slice_in_dim(basin_depth, start, HALO, axis=0)[None],
        ],
        axis=0,
    )
    across = [(i, i + 1) for i in range(1, devices - 1, 2)]
    edge = lax.ppermute(edge, "row", across + [(j, i) for i, j in across])

    basin_out = basin_run(basin_state, basin_depth, pair_state, pair_depth, edge)
    pair_state, basin_out = lax.optimization_barrier((pair_state, basin_out))
    ghosts = make_strips(links, basin_state, pair_state)
    coast_depth, ghosts = lax.optimization_barrier((coast_depth, ghosts))
    ghosts = lax.all_to_all(ghosts, "row", 0, 0, axis_index_groups=parity, tiled=True)
    depth, flow = coast_depth[0], coast_flow[0]
    folded, wet = coast_fold(coast_link, depth, flow)
    coast_out = coast_run(wet, ghosts, folded, depth, flow)
    return (basin_out, coast_out[None])


def solution(mesh):
    in_specs = (
        P("scen", "row", None),
        P("row", "scen"),
        P("row", "scen", None),
        P("row", "scen", None, None),
        P("row", "scen"),
    )
    out_specs = (P("scen", "row", None), P("row", "scen", None, None))
    return jax.shard_map(local, mesh=mesh, in_specs=in_specs, out_specs=out_specs, check_vma=False)
```

```python
import functools

import jax
import jax.numpy as jnp
from jax import lax
from jax.experimental import pallas as pl
from jax.experimental.pallas import tpu as pltpu
from jax.sharding import PartitionSpec as P

BSTEPS = 8
CSTEPS = 10

depth_floor = 0.2
ghost_level = 2.0

RATE = 0.05
DEPTH_UNIT = RATE * RATE
FLOW_UNIT = RATE * RATE * RATE
TINY = 1e-30

HALO = BSTEPS
SUB = 8
LANES = 128


def lane_ids():
    return lax.broadcasted_iota(jnp.int32, (SUB, LANES), 1)


def row_ids():
    return lax.broadcasted_iota(jnp.int32, (SUB, LANES), 0)


def cell_terms(u):
    h, mu, mv = u
    r = pl.reciprocal(jnp.maximum(h, depth_floor * DEPTH_UNIT), approx=True)
    vx, vy = mu * r, mv * r
    hp = jnp.maximum(h, TINY)
    c = hp * lax.rsqrt(hp)
    p = (0.5 * h) * h
    cross = mu * vy
    return {
        "u": u,
        "fx": (mu, mu * vx + p, cross),
        "fy": (mv, cross, mv * vy + p),
        "sx": jnp.abs(vx) + c,
        "sy": jnp.abs(vy) + c,
    }


def y_face(above, below):
    a = jnp.maximum(above["sy"], below["sy"])
    return [
        a * (ub - ua) - (fa + fb)
        for ua, ub, fa, fb in zip(above["u"], below["u"], above["fy"], below["fy"])
    ]


def coast_steps(state, terms, after, parts, opening, rows, group, steps, ghost):
    lane, sub = lane_ids(), row_ids()
    first, last = lane == 0, lane == LANES - 1
    top, bottom = sub == 0, sub == SUB - 1
    zero = jnp.zeros((SUB, LANES), jnp.float32)
    left = functools.partial(pltpu.roll, shift=LANES - 1, axis=1)
    right = functools.partial(pltpu.roll, shift=1, axis=1)

    def load(view, k):
        return [[view[f, half, 1 + k] for f in range(3)] for half in range(2)]

    def store(view, k, both):
        for half in range(2):
            for f in range(3):
                view[f, half, 1 + k] = both[half][f]

    def store_above(tails):
        store(state, -1, [[jnp.where(top, g, pltpu.roll(t, 1, 0)) for g, t in zip(*pair)] for pair in zip(ghost, tails)])

    def y_terms_of(view, k):
        both = [cell_terms(u) for u in load(view, k)]
        for half, cell in enumerate(both):
            terms[half, 1 + k, 0] = cell["sy"]
            terms[half, 1 + k, 1] = cell["fy"][2]
            terms[half, 1 + k, 2] = cell["fx"][2]
        return both

    def terms_of(view, k):
        even, odd = y_terms_of(view, k)
        for half, cell in enumerate((even, odd)):
            terms[half, 1 + k, 3] = cell["sx"]
            terms[half, 1 + k, 4] = cell["fx"][1]
        moved = zip(even["u"] + [even["sx"]] + list(even["fx"][1:]), odd["u"] + [odd["sx"]] + list(odd["fx"][1:]))
        for q, (e, o) in enumerate(moved):
            after[k, q] = jnp.where(last, o, left(e))

    def x_faces(view, k):
        even, odd = load(view, k)
        following = [after[k, f] for f in range(3)]
        sx_e, sx_o, sx_n = terms[0, 1 + k, 3], terms[1, 1 + k, 3], after[k, 3]
        fx_e = [even[1], terms[0, 1 + k, 4], terms[0, 1 + k, 2]]
        fx_o = [odd[1], terms[1, 1 + k, 4], terms[1, 1 + k, 2]]
        fx_n = [following[1], after[k, 4], after[k, 5]]
        a_in, a_out = jnp.maximum(sx_e, sx_o), jnp.maximum(sx_o, sx_n)
        for f in range(3):
            g_in = a_in * (odd[f] - even[f]) - (fx_e[f] + fx_o[f])
            g_out = a_out * (following[f] - odd[f]) - (fx_o[f] + fx_n[f])
            g_back = jnp.where(first, -2.0 * fx_e[f], right(g_out))
            parts[k, f] = even[f] + (g_in - g_back)
            parts[k, 3 + f] = odd[f] + (g_out - g_in)

    def y_cells(view, k):
        return [
            {
                "u": u,
                "fy": [u[2], terms[half, 1 + k, 2], terms[half, 1 + k, 1]],
                "sy": terms[half, 1 + k, 0],
            }
            for half, u in enumerate(load(view, k))
        ]

    def trip(i, acc):
        view = state.at[:, :, pl.ds(i * group, 1 + group)]
        y_terms_of(view, -1)
        for k in range(group):
            terms_of(view, k)
        for k in range(group):
            x_faces(view, k)
        prev = y_cells(view, -1)
        for k in range(group):
            cur = y_cells(view, k)
            face = [y_face(a, b) for a, b in zip(prev, cur)]
            if k == 0:
                for half in range(2):
                    for f in range(3):
                        opening[i, half, f] = pltpu.roll(face[half][f], SUB - 1, 0)
            store(view, k - 1, [[x + g for x, g in zip(*pair)] for pair in zip(acc, face)])
            acc = [[parts[k, 3 * half + f] - face[half][f] for f in range(3)] for half in range(2)]
            prev = cur
        return acc

    def step(_, carry):
        acc = lax.fori_loop(0, rows // group, trip, [[zero] * 3 for _ in range(2)])
        tails = [
            [
                x + jnp.where(bottom, -2.0 * f, opening[0, half, i])
                for i, (x, f) in enumerate(zip(xs, cell["fy"]))
            ]
            for half, (xs, cell) in enumerate(
                zip(acc, y_cells(state.at[:, :, rows - group :], group - 1))
            )
        ]
        store(state, rows - 1, tails)
        store_above(tails)
        return carry

    store_above(load(state, rows - 1))
    lax.fori_loop(0, steps, step, 0)


GROUP = 16
UNITS = (DEPTH_UNIT, FLOW_UNIT, FLOW_UNIT)
VMEM_LIMIT = 12 * 1024 * 1024
HALF = LANES // 2


def pick(values, ids):
    return jnp.take_along_axis(values, ids, axis=1, mode="promise_in_bounds")


def split_columns(west, east):
    lane = lane_ids()
    low = lane < HALF
    twice = 2 * jnp.where(low, lane, lane - HALF)
    w = pick(west, jnp.where(low, twice, twice + 1))
    e = pick(east, jnp.where(low, twice + 1, twice))
    return jnp.where(low, w, e), pltpu.roll(jnp.where(low, e, w), HALF, 1)


def join_columns(even, odd):
    lane = lane_ids()
    low = lane < HALF
    odd = pltpu.roll(odd, HALF, 1)
    w, e = jnp.where(low, even, odd), jnp.where(low, odd, even)
    half, is_odd = lane // 2, lane % 2
    return pick(w, half + HALF * is_odd), pick(e, half + HALF * (1 - is_odd))


HALVES = (slice(0, LANES), slice(LANES, 2 * LANES))
TALL = 32


def fold_kernel(link, depth, flow, state, wet, tmp):
    rows = depth.shape[0] // SUB
    wet[...] = jnp.broadcast_to(link[:, 2:3], wet.shape).astype(jnp.float32)

    def copy_in(i, carry):
        at = pl.ds(pl.multiple_of(i * TALL, TALL), TALL)
        for f in range(3):
            raw = depth[at] if f == 0 else flow[f - 1, at]
            for p in range(2):
                tmp[f, p, at] = raw[:, HALVES[p]] * UNITS[f]
        return carry

    def fold(k, carry):
        for f in range(3):
            both = split_columns(*[tmp[f, p, pl.ds(k, SUB, stride=rows), :] for p in range(2)])
            for p in range(2):
                state[f, p, k] = both[p]
        return carry

    lax.fori_loop(0, depth.shape[0] // TALL, copy_in, 0)
    lax.fori_loop(0, rows, fold, 0, unroll=4)


def coast_fold(link, depth, flow):
    cells = depth.shape[0]
    vmem = pl.BlockSpec(memory_space=pltpu.VMEM)
    return pl.pallas_call(
        fold_kernel,
        out_shape=(
            jax.ShapeDtypeStruct((3, 2, cells // SUB, SUB, LANES), jnp.float32),
            jax.ShapeDtypeStruct((SUB, LANES), jnp.float32),
        ),
        in_specs=[vmem, vmem, vmem],
        out_specs=(vmem, vmem),
        scratch_shapes=[pltpu.VMEM((3, 2, cells, LANES), jnp.float32)],
        compiler_params=pltpu.CompilerParams(vmem_limit_bytes=VMEM_LIMIT),
        cost_estimate=pl.CostEstimate(
            flops=CSTEPS * 70 * cells * cells, bytes_accessed=24 * cells * cells, transcendentals=0
        ),
        name="coast_fold",
    )(link, depth, flow)


def coast_kernel(
    wet, ghosts, folded, depth, flow, out, state, terms, after, parts, opening, tmp, done, sems
):
    rows = depth.shape[0] // SUB
    is_wet = jnp.max(wet[...]) > 0.0

    def copy_in(k, carry):
        for f in range(3):
            for p in range(2):
                state[f, p, 1 + k] = folded[f, p, k]
        return carry

    @pl.when(jnp.logical_not(is_wet))
    def _():
        copies = [
            pltpu.make_async_copy(depth, out.at[0], sems.at[0]),
            pltpu.make_async_copy(flow, out.at[1:], sems.at[1]),
        ]
        for copy in copies:
            copy.start()
        for copy in copies:
            copy.wait()

    @pl.when(is_wet)
    def _():
        lax.fori_loop(0, rows, copy_in, 0, unroll=4)
        values = jnp.sum(ghosts[...], axis=0)
        level = (ghost_level + values) * DEPTH_UNIT
        inflow = values * FLOW_UNIT
        h, mv = [
            [jnp.broadcast_to(v[i : i + 1], (SUB, LANES)) for i in range(at, at + 2)]
            for v, at in ((level, 0), (inflow, 2))
        ]
        ghost = [[h[p], jnp.zeros_like(h[p]), mv[p]] for p in range(2)]
        coast_steps(state, terms, after, parts, opening, rows, GROUP, CSTEPS, ghost)

        def write(f):
            return pltpu.make_async_copy(done.at[f], out.at[f], sems.at[f])

        def finish(f, carry):
            scale = jnp.where(f == 0, 1.0 / DEPTH_UNIT, 1.0 / FLOW_UNIT)

            def unfold(k, carry):
                both = join_columns(state[f, 0, 1 + k], state[f, 1, 1 + k])
                for p in range(2):
                    tmp[p, pl.ds(k, SUB, stride=rows), :] = both[p] * scale
                return carry

            def copy_out(i, carry):
                at = pl.ds(pl.multiple_of(i * TALL, TALL), TALL)
                for p in range(2):
                    done[f, at, HALVES[p]] = tmp[p, at]
                return carry

            lax.fori_loop(0, rows, unfold, 0, unroll=16)
            lax.fori_loop(0, depth.shape[0] // TALL, copy_out, 0, unroll=4)
            write(f).start()
            return carry

        lax.fori_loop(0, 3, finish, 0)
        for f in range(3):
            write(f).wait()


def coast_run(wet, ghosts, folded, depth, flow):
    cells = depth.shape[0]
    vmem = pl.BlockSpec(memory_space=pltpu.VMEM)
    return pl.pallas_call(
        coast_kernel,
        out_shape=jax.ShapeDtypeStruct((3, cells, cells), jnp.float32),
        in_specs=[vmem] * 5,
        out_specs=pl.BlockSpec(memory_space=pltpu.HBM),
        scratch_shapes=[
            pltpu.VMEM((3, 2, 1 + cells // SUB, SUB, LANES), jnp.float32),
            pltpu.VMEM((2, 1 + GROUP, 5, SUB, LANES), jnp.float32),
            pltpu.VMEM((GROUP, 6, SUB, LANES), jnp.float32),
            pltpu.VMEM((GROUP, 6, SUB, LANES), jnp.float32),
            pltpu.VMEM((cells // SUB // GROUP, 2, 3, SUB, LANES), jnp.float32),
            pltpu.VMEM((2, cells, LANES), jnp.float32),
            pltpu.VMEM((3, cells, cells), jnp.float32),
            pltpu.SemaphoreType.DMA((3,)),
        ],
        compiler_params=pltpu.CompilerParams(vmem_limit_bytes=VMEM_LIMIT),
        cost_estimate=pl.CostEstimate(
            flops=CSTEPS * 70 * cells * cells, bytes_accessed=24 * cells * cells, transcendentals=0
        ),
        name="coast_steps",
    )(wet, ghosts, folded, depth, flow)


def basin_kernel(state, depth, pair_state, pair_depth, edges, out, eta, hu, hv, dep):
    rows, width = depth.shape
    total = rows + 2 * HALO
    chunks = width // LANES
    position = lax.axis_index("row")
    odd = position % 2
    end = lax.axis_size("row") - 1
    north_inside = (position < end).astype(jnp.float32)
    edge_inside = jnp.logical_and(position > 0, position < end).astype(jnp.float32)
    pair_from = pl.multiple_of(odd * (rows - HALO), HALO)
    pair_at = pl.multiple_of((1 - odd) * (HALO + rows), HALO)
    edge_at = pl.multiple_of(odd * (HALO + rows), HALO)
    for ref, field, unit in ((eta, 0, 1.0), (hu, 1, 0.5), (hv, 2, 0.5), (dep, 3, 0.25)):
        own, pair = (depth, pair_depth) if field == 3 else (state.at[field], pair_state.at[field])
        ref[HALO : HALO + rows] = own[...] * unit
        ref[pl.ds(pair_at, HALO)] = pair[pl.ds(pair_from, HALO)] * unit
        ref[pl.ds(edge_at, HALO)] = edges[odd, field] * (unit * edge_inside)
    lane = lax.broadcasted_iota(jnp.int32, (total, LANES), 1)
    first, last = lane == 0, lane == LANES - 1
    row = lax.broadcasted_iota(jnp.int32, (total, LANES), 0)
    kept = jnp.where(row < HALO + rows, 1.0, north_inside)

    def step(_, carry):
        prev_west = jnp.zeros((total, LANES), jnp.float32)
        prev_eta, prev_east, prev_hu = None, None, None
        for c in range(chunks + 1):
            if c < chunks:
                at = slice(c * LANES, (c + 1) * LANES)
                u, v = hu[:, at], hv[:, at]
                west = pltpu.roll(u, 1, 1)
                du = u - jnp.where(first, prev_west, west)
                dv = v - pltpu.roll(v, 1, 0)
                new = (eta[:, at] - (du + dv)) * kept
                eta[:, at] = new
                east = pltpu.roll(new, LANES - 1, 1)
                hv[:, at] = v - dep[:, at] * (pltpu.roll(new, total - 1, 0) - new)
            else:
                east = jnp.zeros((total, LANES), jnp.float32)
            if c > 0:
                back = slice((c - 1) * LANES, c * LANES)
                hu[:, back] = prev_hu - dep[:, back] * (jnp.where(last, east, prev_east) - prev_eta)
            prev_west, prev_eta, prev_east, prev_hu = west, new, east, u
        return carry

    lax.fori_loop(0, BSTEPS, step, 0)
    own = slice(HALO, HALO + rows)
    out[0] = eta[own]
    out[1] = hu[own] * 2.0
    out[2] = hv[own] * 2.0


def basin_run(state, depth, pair_state, pair_depth, edges):
    rows, width = depth.shape
    total = rows + 2 * HALO
    vmem = pl.BlockSpec(memory_space=pltpu.VMEM)
    return pl.pallas_call(
        basin_kernel,
        out_shape=jax.ShapeDtypeStruct((3, rows, width), jnp.float32),
        in_specs=[vmem] * 5,
        out_specs=vmem,
        scratch_shapes=[pltpu.VMEM((total, width), jnp.float32)] * 4,
        compiler_params=pltpu.CompilerParams(vmem_limit_bytes=VMEM_LIMIT),
        cost_estimate=pl.CostEstimate(
            flops=BSTEPS * 16 * total * width, bytes_accessed=4 * 11 * rows * width, transcendentals=0
        ),
        name="basin_steps",
    )(state, depth, pair_state, pair_depth, edges)


def strips_kernel(links, own, pair, ghosts, strips):
    rows, width = own.shape[1], own.shape[2]
    count = ghosts.shape[0]
    span = 2 * LANES
    position = lax.axis_index("row")
    tops = (position * rows, (position + 1 - 2 * (position % 2)) * rows)
    lane = lane_ids()
    weight = ((2 * lane + row_ids() % 2) % 16).astype(jnp.float32) / 16.0 + 0.5 / 16.0

    def piece(b, carry):
        col = links[b, 0, 1]
        start = jnp.clip(col // LANES, 0, width // LANES - 2) * LANES
        shift = lax.rem(span - (col - start), span)
        at = pl.ds(pl.multiple_of(start, LANES), span)
        for i, f in enumerate((0, 2)):
            chunk = None
            for source, top in zip((own, pair), tops):
                row = links[b, 0, 0] - top
                owned = jnp.logical_and(row >= 0, row < rows).astype(jnp.float32)
                part = source[f, pl.ds(jnp.clip(row, 0, rows - 1), 1), at] * owned
                chunk = part if chunk is None else chunk + part
            moved = pltpu.roll(chunk, shift, 1)[:, :LANES]
            strips[b, 2 * i : 2 * i + 2] = jnp.broadcast_to(moved, (2, LANES))
        values = strips[b]
        low, high = pick(values, lane // 8), pick(values, lane // 8 + 1)
        ghosts[b] = (1.0 - weight) * low + weight * high
        return carry

    strips[...] = jnp.zeros_like(strips)
    lax.fori_loop(0, count, piece, 0, unroll=8)


def make_strips(links, own, pair):
    count = links.shape[0]
    tiles = (count, SUB, LANES)
    vmem = pl.BlockSpec(memory_space=pltpu.VMEM)
    smem = pl.BlockSpec(memory_space=pltpu.SMEM)
    return pl.pallas_call(
        strips_kernel,
        out_shape=jax.ShapeDtypeStruct(tiles, jnp.float32),
        in_specs=[smem, vmem, vmem],
        out_specs=vmem,
        scratch_shapes=[pltpu.VMEM(tiles, jnp.float32)],
        compiler_params=pltpu.CompilerParams(vmem_limit_bytes=VMEM_LIMIT),
        name="strips",
    )(links, own, pair)


def local(basin_state, basin_depth, coast_depth, coast_flow, coast_link):
    devices = lax.axis_size("row")
    odd = lax.axis_index("row") % 2
    parity = [list(range(p, devices, 2))[::-1] for p in range(2)]
    sent = jnp.broadcast_to(coast_link, (devices // 2,) + coast_link.shape)
    links = lax.all_to_all(sent, "row", 0, 0, axis_index_groups=parity, tiled=True)

    twins = [(i, i ^ 1) for i in range(devices)]
    pair_state, pair_depth = [lax.ppermute(a, "row", twins) for a in (basin_state, basin_depth)]
    start = odd * (basin_depth.shape[0] - HALO)
    edge = jnp.concatenate(
        [
            lax.dynamic_slice_in_dim(basin_state, start, HALO, axis=1),
            lax.dynamic_slice_in_dim(basin_depth, start, HALO, axis=0)[None],
        ],
        axis=0,
    )
    across = [[i, (i + 1) % devices] for i in range(1, devices, 2)]
    edges = jnp.broadcast_to(edge, (2,) + edge.shape)
    edges = lax.all_to_all(edges, "row", 0, 0, axis_index_groups=across, tiled=True)

    depth, flow = coast_depth[0], coast_flow[0]
    folded, wet = coast_fold(coast_link, depth, flow)
    pair_state, folded = lax.optimization_barrier((pair_state, folded))
    ghosts = make_strips(links, basin_state, pair_state)
    basin_depth, ghosts = lax.optimization_barrier((basin_depth, ghosts))
    ghosts = lax.all_to_all(ghosts, "row", 0, 0, axis_index_groups=parity, tiled=True)
    basin_out = basin_run(basin_state, basin_depth, pair_state, pair_depth, edges)
    folded, basin_out = lax.optimization_barrier((folded, basin_out))
    coast_out = coast_run(wet, ghosts, folded, depth, flow)
    return (basin_out, coast_out[None])


def solution(mesh):
    in_specs = (
        P("scen", "row", None),
        P("row", "scen"),
        P("row", "scen", None),
        P("row", "scen", None, None),
        P("row", "scen"),
    )
    out_specs = (P("scen", "row", None), P("row", "scen", None, None))
    return jax.shard_map(local, mesh=mesh, in_specs=in_specs, out_specs=out_specs, check_vma=False)
```

```python
import functools

import jax
import jax.numpy as jnp
from jax import lax
from jax.experimental import pallas as pl
from jax.experimental.pallas import tpu as pltpu
from jax.sharding import PartitionSpec as P

BSTEPS = 8
CSTEPS = 10

depth_floor = 0.2
ghost_level = 2.0

RATE = 0.05
DEPTH_UNIT = RATE * RATE
FLOW_UNIT = RATE * RATE * RATE
TINY = 1e-30

HALO = BSTEPS
SUB = 8
LANES = 128


def lane_ids():
    return lax.broadcasted_iota(jnp.int32, (SUB, LANES), 1)


def row_ids():
    return lax.broadcasted_iota(jnp.int32, (SUB, LANES), 0)


def cell_terms(u):
    h, mu, mv = u
    r = pl.reciprocal(jnp.maximum(h, depth_floor * DEPTH_UNIT), approx=True)
    vx, vy = mu * r, mv * r
    hp = jnp.maximum(h, TINY)
    c = hp * lax.rsqrt(hp)
    p = (0.5 * h) * h
    cross = mu * vy
    return {
        "u": u,
        "fx": (mu, mu * vx + p, cross),
        "fy": (mv, cross, mv * vy + p),
        "sx": jnp.abs(vx) + c,
        "sy": jnp.abs(vy) + c,
    }


def y_face(above, below):
    a = jnp.maximum(above["sy"], below["sy"])
    return [
        a * (ub - ua) - (fa + fb)
        for ua, ub, fa, fb in zip(above["u"], below["u"], above["fy"], below["fy"])
    ]


def coast_steps(state, terms, after, parts, opening, rows, group, steps, ghost):
    lane, sub = lane_ids(), row_ids()
    first, last = lane == 0, lane == LANES - 1
    top, bottom = sub == 0, sub == SUB - 1
    zero = jnp.zeros((SUB, LANES), jnp.float32)
    left = functools.partial(pltpu.roll, shift=LANES - 1, axis=1)
    right = functools.partial(pltpu.roll, shift=1, axis=1)

    def load(view, k):
        return [[view[f, half, 1 + k] for f in range(3)] for half in range(2)]

    def store(view, k, both):
        for half in range(2):
            for f in range(3):
                view[f, half, 1 + k] = both[half][f]

    def store_above(tails):
        store(state, -1, [[jnp.where(top, g, pltpu.roll(t, 1, 0)) for g, t in zip(*pair)] for pair in zip(ghost, tails)])

    def y_terms_of(view, k):
        both = [cell_terms(u) for u in load(view, k)]
        for half, cell in enumerate(both):
            terms[half, 1 + k, 0] = cell["sy"]
            terms[half, 1 + k, 1] = cell["fy"][2]
            terms[half, 1 + k, 2] = cell["fx"][2]
        return both

    def terms_of(view, k):
        even, odd = y_terms_of(view, k)
        for half, cell in enumerate((even, odd)):
            terms[half, 1 + k, 3] = cell["sx"]
            terms[half, 1 + k, 4] = cell["fx"][1]
        moved = zip(even["u"] + [even["sx"]] + list(even["fx"][1:]), odd["u"] + [odd["sx"]] + list(odd["fx"][1:]))
        for q, (e, o) in enumerate(moved):
            after[k, q] = jnp.where(last, o, left(e))

    def x_faces(view, k):
        even, odd = load(view, k)
        following = [after[k, f] for f in range(3)]
        sx_e, sx_o, sx_n = terms[0, 1 + k, 3], terms[1, 1 + k, 3], after[k, 3]
        fx_e = [even[1], terms[0, 1 + k, 4], terms[0, 1 + k, 2]]
        fx_o = [odd[1], terms[1, 1 + k, 4], terms[1, 1 + k, 2]]
        fx_n = [following[1], after[k, 4], after[k, 5]]
        a_in, a_out = jnp.maximum(sx_e, sx_o), jnp.maximum(sx_o, sx_n)
        for f in range(3):
            g_in = a_in * (odd[f] - even[f]) - (fx_e[f] + fx_o[f])
            g_out = a_out * (following[f] - odd[f]) - (fx_o[f] + fx_n[f])
            g_back = jnp.where(first, -2.0 * fx_e[f], right(g_out))
            parts[k, f] = even[f] + (g_in - g_back)
            parts[k, 3 + f] = odd[f] + (g_out - g_in)

    def y_cells(view, k):
        return [
            {
                "u": u,
                "fy": [u[2], terms[half, 1 + k, 2], terms[half, 1 + k, 1]],
                "sy": terms[half, 1 + k, 0],
            }
            for half, u in enumerate(load(view, k))
        ]

    def trip(i, acc):
        view = state.at[:, :, pl.ds(i * group, 1 + group)]
        y_terms_of(view, -1)
        for k in range(group):
            terms_of(view, k)
        for k in range(group):
            x_faces(view, k)
        prev = y_cells(view, -1)
        for k in range(group):
            cur = y_cells(view, k)
            face = [y_face(a, b) for a, b in zip(prev, cur)]
            if k == 0:
                for half in range(2):
                    for f in range(3):
                        opening[i, half, f] = pltpu.roll(face[half][f], SUB - 1, 0)
            store(view, k - 1, [[x + g for x, g in zip(*pair)] for pair in zip(acc, face)])
            acc = [[parts[k, 3 * half + f] - face[half][f] for f in range(3)] for half in range(2)]
            prev = cur
        return acc

    def step(_, carry):
        acc = lax.fori_loop(0, rows // group, trip, [[zero] * 3 for _ in range(2)])
        tails = [
            [
                x + jnp.where(bottom, -2.0 * f, opening[0, half, i])
                for i, (x, f) in enumerate(zip(xs, cell["fy"]))
            ]
            for half, (xs, cell) in enumerate(
                zip(acc, y_cells(state.at[:, :, rows - group :], group - 1))
            )
        ]
        store(state, rows - 1, tails)
        store_above(tails)
        return carry

    store_above(load(state, rows - 1))
    lax.fori_loop(0, steps, step, 0)


GROUP = 16
UNITS = (DEPTH_UNIT, FLOW_UNIT, FLOW_UNIT)
VMEM_LIMIT = 12 * 1024 * 1024
HALF = LANES // 2


def pick(values, ids):
    return jnp.take_along_axis(values, ids, axis=1, mode="promise_in_bounds")


def split_columns(west, east):
    lane = lane_ids()
    low = lane < HALF
    twice = 2 * jnp.where(low, lane, lane - HALF)
    w = pick(west, jnp.where(low, twice, twice + 1))
    e = pick(east, jnp.where(low, twice + 1, twice))
    return jnp.where(low, w, e), pltpu.roll(jnp.where(low, e, w), HALF, 1)


def join_columns(even, odd):
    lane = lane_ids()
    low = lane < HALF
    odd = pltpu.roll(odd, HALF, 1)
    w, e = jnp.where(low, even, odd), jnp.where(low, odd, even)
    half, is_odd = lane // 2, lane % 2
    return pick(w, half + HALF * is_odd), pick(e, half + HALF * (1 - is_odd))


HALVES = (slice(0, LANES), slice(LANES, 2 * LANES))
TALL = 32


def fold_kernel(link, depth, flow, state, wet, tmp):
    rows = depth.shape[0] // SUB
    wet[...] = jnp.broadcast_to(link[:, 2:3], wet.shape).astype(jnp.float32)

    def copy_in(i, carry):
        at = pl.ds(pl.multiple_of(i * TALL, TALL), TALL)
        for f in range(3):
            raw = depth[at] if f == 0 else flow[f - 1, at]
            for p in range(2):
                tmp[f, p, at] = raw[:, HALVES[p]] * UNITS[f]
        return carry

    def fold(k, carry):
        for f in range(3):
            both = split_columns(*[tmp[f, p, pl.ds(k, SUB, stride=rows), :] for p in range(2)])
            for p in range(2):
                state[f, p, k] = both[p]
        return carry

    lax.fori_loop(0, depth.shape[0] // TALL, copy_in, 0)
    lax.fori_loop(0, rows, fold, 0, unroll=4)


def coast_fold(link, depth, flow):
    cells = depth.shape[0]
    vmem = pl.BlockSpec(memory_space=pltpu.VMEM)
    return pl.pallas_call(
        fold_kernel,
        out_shape=(
            jax.ShapeDtypeStruct((3, 2, cells // SUB, SUB, LANES), jnp.float32),
            jax.ShapeDtypeStruct((SUB, LANES), jnp.float32),
        ),
        in_specs=[vmem, vmem, vmem],
        out_specs=(vmem, vmem),
        scratch_shapes=[pltpu.VMEM((3, 2, cells, LANES), jnp.float32)],
        compiler_params=pltpu.CompilerParams(vmem_limit_bytes=VMEM_LIMIT),
        cost_estimate=pl.CostEstimate(
            flops=CSTEPS * 70 * cells * cells, bytes_accessed=24 * cells * cells, transcendentals=0
        ),
        name="coast_fold",
    )(link, depth, flow)


def coast_kernel(
    wet, ghosts, folded, depth, flow, out, state, terms, after, parts, opening, tmp, done, sems
):
    rows = depth.shape[0] // SUB
    is_wet = jnp.max(wet[...]) > 0.0

    def copy_in(k, carry):
        for f in range(3):
            for p in range(2):
                state[f, p, 1 + k] = folded[f, p, k]
        return carry

    @pl.when(jnp.logical_not(is_wet))
    def _():
        copies = [
            pltpu.make_async_copy(depth, out.at[0], sems.at[0]),
            pltpu.make_async_copy(flow, out.at[1:], sems.at[1]),
        ]
        for copy in copies:
            copy.start()
        for copy in copies:
            copy.wait()

    @pl.when(is_wet)
    def _():
        lax.fori_loop(0, rows, copy_in, 0, unroll=4)
        values = jnp.sum(ghosts[...], axis=0)
        level = (ghost_level + values) * DEPTH_UNIT
        inflow = values * FLOW_UNIT
        h, mv = [
            [jnp.broadcast_to(v[i : i + 1], (SUB, LANES)) for i in range(at, at + 2)]
            for v, at in ((level, 0), (inflow, 2))
        ]
        ghost = [[h[p], jnp.zeros_like(h[p]), mv[p]] for p in range(2)]
        coast_steps(state, terms, after, parts, opening, rows, GROUP, CSTEPS, ghost)

        def write(f):
            return pltpu.make_async_copy(done.at[f], out.at[f], sems.at[f])

        def finish(f, carry):
            scale = jnp.where(f == 0, 1.0 / DEPTH_UNIT, 1.0 / FLOW_UNIT)

            def unfold(k, carry):
                both = join_columns(state[f, 0, 1 + k], state[f, 1, 1 + k])
                for p in range(2):
                    tmp[p, pl.ds(k, SUB, stride=rows), :] = both[p] * scale
                return carry

            def copy_out(i, carry):
                at = pl.ds(pl.multiple_of(i * TALL, TALL), TALL)
                for p in range(2):
                    done[f, at, HALVES[p]] = tmp[p, at]
                return carry

            lax.fori_loop(0, rows, unfold, 0, unroll=16)
            lax.fori_loop(0, depth.shape[0] // TALL, copy_out, 0, unroll=4)
            write(f).start()
            return carry

        lax.fori_loop(0, 3, finish, 0)
        for f in range(3):
            write(f).wait()


def coast_run(wet, ghosts, folded, depth, flow):
    cells = depth.shape[0]
    vmem = pl.BlockSpec(memory_space=pltpu.VMEM)
    return pl.pallas_call(
        coast_kernel,
        out_shape=jax.ShapeDtypeStruct((3, cells, cells), jnp.float32),
        in_specs=[vmem] * 5,
        out_specs=pl.BlockSpec(memory_space=pltpu.HBM),
        scratch_shapes=[
            pltpu.VMEM((3, 2, 1 + cells // SUB, SUB, LANES), jnp.float32),
            pltpu.VMEM((2, 1 + GROUP, 5, SUB, LANES), jnp.float32),
            pltpu.VMEM((GROUP, 6, SUB, LANES), jnp.float32),
            pltpu.VMEM((GROUP, 6, SUB, LANES), jnp.float32),
            pltpu.VMEM((cells // SUB // GROUP, 2, 3, SUB, LANES), jnp.float32),
            pltpu.VMEM((2, cells, LANES), jnp.float32),
            pltpu.VMEM((3, cells, cells), jnp.float32),
            pltpu.SemaphoreType.DMA((3,)),
        ],
        compiler_params=pltpu.CompilerParams(vmem_limit_bytes=VMEM_LIMIT),
        cost_estimate=pl.CostEstimate(
            flops=CSTEPS * 70 * cells * cells, bytes_accessed=24 * cells * cells, transcendentals=0
        ),
        name="coast_steps",
    )(wet, ghosts, folded, depth, flow)


def basin_kernel(state, depth, pair_state, pair_depth, edge, out, eta, hu, hv, dep):
    rows, width = depth.shape
    total = rows + 2 * HALO
    chunks = width // LANES
    position = lax.axis_index("row")
    odd = position % 2
    north_inside = (position < lax.axis_size("row") - 1).astype(jnp.float32)
    pair_from = pl.multiple_of(odd * (rows - HALO), HALO)
    pair_at = pl.multiple_of((1 - odd) * (HALO + rows), HALO)
    edge_at = pl.multiple_of(odd * (HALO + rows), HALO)
    for ref, field, unit in ((eta, 0, 1.0), (hu, 1, 0.5), (hv, 2, 0.5), (dep, 3, 0.25)):
        own, pair = (depth, pair_depth) if field == 3 else (state.at[field], pair_state.at[field])
        ref[HALO : HALO + rows] = own[...] * unit
        ref[pl.ds(pair_at, HALO)] = pair[pl.ds(pair_from, HALO)] * unit
        ref[pl.ds(edge_at, HALO)] = edge[field] * unit
    lane = lax.broadcasted_iota(jnp.int32, (total, LANES), 1)
    first, last = lane == 0, lane == LANES - 1
    row = lax.broadcasted_iota(jnp.int32, (total, LANES), 0)
    kept = jnp.where(row < HALO + rows, 1.0, north_inside)

    def step(_, carry):
        prev_west = jnp.zeros((total, LANES), jnp.float32)
        prev_eta, prev_east, prev_hu = None, None, None
        for c in range(chunks + 1):
            if c < chunks:
                at = slice(c * LANES, (c + 1) * LANES)
                u, v = hu[:, at], hv[:, at]
                west = pltpu.roll(u, 1, 1)
                du = u - jnp.where(first, prev_west, west)
                dv = v - pltpu.roll(v, 1, 0)
                new = (eta[:, at] - (du + dv)) * kept
                eta[:, at] = new
                east = pltpu.roll(new, LANES - 1, 1)
                hv[:, at] = v - dep[:, at] * (pltpu.roll(new, total - 1, 0) - new)
            else:
                east = jnp.zeros((total, LANES), jnp.float32)
            if c > 0:
                back = slice((c - 1) * LANES, c * LANES)
                hu[:, back] = prev_hu - dep[:, back] * (jnp.where(last, east, prev_east) - prev_eta)
            prev_west, prev_eta, prev_east, prev_hu = west, new, east, u
        return carry

    lax.fori_loop(0, BSTEPS, step, 0)
    own = slice(HALO, HALO + rows)
    out[0] = eta[own]
    out[1] = hu[own] * 2.0
    out[2] = hv[own] * 2.0


def basin_run(state, depth, pair_state, pair_depth, edge):
    rows, width = depth.shape
    total = rows + 2 * HALO
    vmem = pl.BlockSpec(memory_space=pltpu.VMEM)
    return pl.pallas_call(
        basin_kernel,
        out_shape=jax.ShapeDtypeStruct((3, rows, width), jnp.float32),
        in_specs=[vmem] * 5,
        out_specs=vmem,
        scratch_shapes=[pltpu.VMEM((total, width), jnp.float32)] * 4,
        compiler_params=pltpu.CompilerParams(vmem_limit_bytes=VMEM_LIMIT),
        cost_estimate=pl.CostEstimate(
            flops=BSTEPS * 16 * total * width, bytes_accessed=4 * 11 * rows * width, transcendentals=0
        ),
        name="basin_steps",
    )(state, depth, pair_state, pair_depth, edge)


def strips_kernel(links, own, pair, ghosts, strips):
    rows, width = own.shape[1], own.shape[2]
    count = ghosts.shape[0]
    span = 2 * LANES
    position = lax.axis_index("row")
    tops = (position * rows, (position + 1 - 2 * (position % 2)) * rows)
    lane = lane_ids()
    weight = ((2 * lane + row_ids() % 2) % 16).astype(jnp.float32) / 16.0 + 0.5 / 16.0

    def piece(b, carry):
        col = links[b, 0, 1]
        start = jnp.clip(col // LANES, 0, width // LANES - 2) * LANES
        shift = lax.rem(span - (col - start), span)
        at = pl.ds(pl.multiple_of(start, LANES), span)
        for i, f in enumerate((0, 2)):
            chunk = None
            for source, top in zip((own, pair), tops):
                row = links[b, 0, 0] - top
                owned = jnp.logical_and(row >= 0, row < rows).astype(jnp.float32)
                part = source[f, pl.ds(jnp.clip(row, 0, rows - 1), 1), at] * owned
                chunk = part if chunk is None else chunk + part
            moved = pltpu.roll(chunk, shift, 1)[:, :LANES]
            strips[b, 2 * i : 2 * i + 2] = jnp.broadcast_to(moved, (2, LANES))
        values = strips[b]
        low, high = pick(values, lane // 8), pick(values, lane // 8 + 1)
        ghosts[b] = (1.0 - weight) * low + weight * high
        return carry

    strips[...] = jnp.zeros_like(strips)
    lax.fori_loop(0, count, piece, 0, unroll=8)


def make_strips(links, own, pair):
    count = links.shape[0]
    tiles = (count, SUB, LANES)
    vmem = pl.BlockSpec(memory_space=pltpu.VMEM)
    smem = pl.BlockSpec(memory_space=pltpu.SMEM)
    return pl.pallas_call(
        strips_kernel,
        out_shape=jax.ShapeDtypeStruct(tiles, jnp.float32),
        in_specs=[smem, vmem, vmem],
        out_specs=vmem,
        scratch_shapes=[pltpu.VMEM(tiles, jnp.float32)],
        compiler_params=pltpu.CompilerParams(vmem_limit_bytes=VMEM_LIMIT),
        cost_estimate=pl.CostEstimate(flops=2 * 10**11, bytes_accessed=own.size, transcendentals=0),
        name="strips",
    )(links, own, pair)


def local(basin_state, basin_depth, coast_depth, coast_flow, coast_link):
    devices = lax.axis_size("row")
    odd = lax.axis_index("row") % 2
    parity = [list(range(p, devices, 2))[::-1] for p in range(2)]
    sent = jnp.broadcast_to(coast_link, (devices // 2,) + coast_link.shape)
    links = lax.all_to_all(sent, "row", 0, 0, axis_index_groups=parity, tiled=True)

    twins = [(i, i ^ 1) for i in range(devices)]
    pair_state, pair_depth = [lax.ppermute(a, "row", twins) for a in (basin_state, basin_depth)]
    start = odd * (basin_depth.shape[0] - HALO)
    edge = jnp.concatenate(
        [
            lax.dynamic_slice_in_dim(basin_state, start, HALO, axis=1),
            lax.dynamic_slice_in_dim(basin_depth, start, HALO, axis=0)[None],
        ],
        axis=0,
    )
    across = [(i, i + 1) for i in range(1, devices - 1, 2)]
    edge = lax.ppermute(edge, "row", across + [(j, i) for i, j in across])

    depth, flow = coast_depth[0], coast_flow[0]
    folded, wet = coast_fold(coast_link, depth, flow)
    pair_state, folded = lax.optimization_barrier((pair_state, folded))
    ghosts = make_strips(links, basin_state, pair_state)
    basin_depth, ghosts = lax.optimization_barrier((basin_depth, ghosts))
    ghosts = lax.all_to_all(ghosts, "row", 0, 0, axis_index_groups=parity, tiled=True)
    basin_out = basin_run(basin_state, basin_depth, pair_state, pair_depth, edge)
    folded, basin_out = lax.optimization_barrier((folded, basin_out))
    coast_out = coast_run(wet, ghosts, folded, depth, flow)
    return (basin_out, coast_out[None])


def solution(mesh):
    in_specs = (
        P("scen", "row", None),
        P("row", "scen"),
        P("row", "scen", None),
        P("row", "scen", None, None),
        P("row", "scen"),
    )
    out_specs = (P("scen", "row", None), P("row", "scen", None, None))
    return jax.shard_map(local, mesh=mesh, in_specs=in_specs, out_specs=out_specs, check_vma=False)
```

```python
import functools

import jax
import jax.numpy as jnp
from jax import lax
from jax.experimental import pallas as pl
from jax.experimental.pallas import tpu as pltpu
from jax.sharding import PartitionSpec as P

BSTEPS = 8
CSTEPS = 10

depth_floor = 0.2
ghost_level = 2.0

RATE = 0.05
DEPTH_UNIT = RATE * RATE
FLOW_UNIT = RATE * RATE * RATE
TINY = 1e-30

HALO = BSTEPS
SUB = 8
LANES = 128


def lane_ids():
    return lax.broadcasted_iota(jnp.int32, (SUB, LANES), 1)


def row_ids():
    return lax.broadcasted_iota(jnp.int32, (SUB, LANES), 0)


def cell_terms(u):
    h, mu, mv = u
    r = pl.reciprocal(jnp.maximum(h, depth_floor * DEPTH_UNIT), approx=True)
    vx, vy = mu * r, mv * r
    hp = jnp.maximum(h, TINY)
    c = hp * lax.rsqrt(hp)
    p = (0.5 * h) * h
    cross = mu * vy
    return {
        "u": u,
        "fx": (mu, mu * vx + p, cross),
        "fy": (mv, cross, mv * vy + p),
        "sx": jnp.abs(vx) + c,
        "sy": jnp.abs(vy) + c,
    }


def y_face(above, below):
    a = jnp.maximum(above["sy"], below["sy"])
    return [
        a * (ub - ua) - (fa + fb)
        for ua, ub, fa, fb in zip(above["u"], below["u"], above["fy"], below["fy"])
    ]


def coast_steps(state, terms, after, parts, opening, rows, group, steps, ghost):
    lane, sub = lane_ids(), row_ids()
    first, last = lane == 0, lane == LANES - 1
    top, bottom = sub == 0, sub == SUB - 1
    zero = jnp.zeros((SUB, LANES), jnp.float32)
    left = functools.partial(pltpu.roll, shift=LANES - 1, axis=1)
    right = functools.partial(pltpu.roll, shift=1, axis=1)

    def load(view, k):
        return [[view[f, half, 1 + k] for f in range(3)] for half in range(2)]

    def store(view, k, both):
        for half in range(2):
            for f in range(3):
                view[f, half, 1 + k] = both[half][f]

    def store_above(tails):
        store(state, -1, [[jnp.where(top, g, pltpu.roll(t, 1, 0)) for g, t in zip(*pair)] for pair in zip(ghost, tails)])

    def y_terms_of(view, k):
        both = [cell_terms(u) for u in load(view, k)]
        for half, cell in enumerate(both):
            terms[half, 1 + k, 0] = cell["sy"]
            terms[half, 1 + k, 1] = cell["fy"][2]
            terms[half, 1 + k, 2] = cell["fx"][2]
        return both

    def terms_of(view, k):
        even, odd = y_terms_of(view, k)
        for half, cell in enumerate((even, odd)):
            terms[half, 1 + k, 3] = cell["sx"]
            terms[half, 1 + k, 4] = cell["fx"][1]
        moved = zip(even["u"] + [even["sx"]] + list(even["fx"][1:]), odd["u"] + [odd["sx"]] + list(odd["fx"][1:]))
        for q, (e, o) in enumerate(moved):
            after[k, q] = jnp.where(last, o, left(e))

    def x_faces(view, k):
        even, odd = load(view, k)
        following = [after[k, f] for f in range(3)]
        sx_e, sx_o, sx_n = terms[0, 1 + k, 3], terms[1, 1 + k, 3], after[k, 3]
        fx_e = [even[1], terms[0, 1 + k, 4], terms[0, 1 + k, 2]]
        fx_o = [odd[1], terms[1, 1 + k, 4], terms[1, 1 + k, 2]]
        fx_n = [following[1], after[k, 4], after[k, 5]]
        a_in, a_out = jnp.maximum(sx_e, sx_o), jnp.maximum(sx_o, sx_n)
        for f in range(3):
            g_in = a_in * (odd[f] - even[f]) - (fx_e[f] + fx_o[f])
            g_out = a_out * (following[f] - odd[f]) - (fx_o[f] + fx_n[f])
            g_back = jnp.where(first, -2.0 * fx_e[f], right(g_out))
            parts[k, f] = even[f] + (g_in - g_back)
            parts[k, 3 + f] = odd[f] + (g_out - g_in)

    def y_cells(view, k):
        return [
            {
                "u": u,
                "fy": [u[2], terms[half, 1 + k, 2], terms[half, 1 + k, 1]],
                "sy": terms[half, 1 + k, 0],
            }
            for half, u in enumerate(load(view, k))
        ]

    def trip(i, acc):
        view = state.at[:, :, pl.ds(i * group, 1 + group)]
        y_terms_of(view, -1)
        for k in range(group):
            terms_of(view, k)
        for k in range(group):
            x_faces(view, k)
        prev = y_cells(view, -1)
        for k in range(group):
            cur = y_cells(view, k)
            face = [y_face(a, b) for a, b in zip(prev, cur)]
            if k == 0:
                for half in range(2):
                    for f in range(3):
                        opening[i, half, f] = pltpu.roll(face[half][f], SUB - 1, 0)
            store(view, k - 1, [[x + g for x, g in zip(*pair)] for pair in zip(acc, face)])
            acc = [[parts[k, 3 * half + f] - face[half][f] for f in range(3)] for half in range(2)]
            prev = cur
        return acc

    def step(_, carry):
        acc = lax.fori_loop(0, rows // group, trip, [[zero] * 3 for _ in range(2)])
        tails = [
            [
                x + jnp.where(bottom, -2.0 * f, opening[0, half, i])
                for i, (x, f) in enumerate(zip(xs, cell["fy"]))
            ]
            for half, (xs, cell) in enumerate(
                zip(acc, y_cells(state.at[:, :, rows - group :], group - 1))
            )
        ]
        store(state, rows - 1, tails)
        store_above(tails)
        return carry

    store_above(load(state, rows - 1))
    lax.fori_loop(0, steps, step, 0)


GROUP = 16
UNITS = (DEPTH_UNIT, FLOW_UNIT, FLOW_UNIT)
VMEM_LIMIT = 12 * 1024 * 1024
HALF = LANES // 2


def pick(values, ids):
    return jnp.take_along_axis(values, ids, axis=1, mode="promise_in_bounds")


def split_columns(west, east):
    lane = lane_ids()
    low = lane < HALF
    twice = 2 * jnp.where(low, lane, lane - HALF)
    w = pick(west, jnp.where(low, twice, twice + 1))
    e = pick(east, jnp.where(low, twice + 1, twice))
    return jnp.where(low, w, e), pltpu.roll(jnp.where(low, e, w), HALF, 1)


def join_columns(even, odd):
    lane = lane_ids()
    low = lane < HALF
    odd = pltpu.roll(odd, HALF, 1)
    w, e = jnp.where(low, even, odd), jnp.where(low, odd, even)
    half, is_odd = lane // 2, lane % 2
    return pick(w, half + HALF * is_odd), pick(e, half + HALF * (1 - is_odd))


HALVES = (slice(0, LANES), slice(LANES, 2 * LANES))
TALL = 32


def fold_kernel(link, depth, flow, state, wet, tmp):
    rows = depth.shape[0] // SUB
    wet[...] = jnp.broadcast_to(link[:, 2:3], wet.shape).astype(jnp.float32)

    def copy_in(i, carry):
        at = pl.ds(pl.multiple_of(i * TALL, TALL), TALL)
        for f in range(3):
            raw = depth[at] if f == 0 else flow[f - 1, at]
            for p in range(2):
                tmp[f, p, at] = raw[:, HALVES[p]] * UNITS[f]
        return carry

    def fold(k, carry):
        for f in range(3):
            both = split_columns(*[tmp[f, p, pl.ds(k, SUB, stride=rows), :] for p in range(2)])
            for p in range(2):
                state[f, p, k] = both[p]
        return carry

    lax.fori_loop(0, depth.shape[0] // TALL, copy_in, 0)
    lax.fori_loop(0, rows, fold, 0, unroll=16)


def coast_fold(link, depth, flow):
    cells = depth.shape[0]
    vmem = pl.BlockSpec(memory_space=pltpu.VMEM)
    return pl.pallas_call(
        fold_kernel,
        out_shape=(
            jax.ShapeDtypeStruct((3, 2, cells // SUB, SUB, LANES), jnp.float32),
            jax.ShapeDtypeStruct((SUB, LANES), jnp.float32),
        ),
        in_specs=[vmem, vmem, vmem],
        out_specs=(vmem, vmem),
        scratch_shapes=[pltpu.VMEM((3, 2, cells, LANES), jnp.float32)],
        compiler_params=pltpu.CompilerParams(vmem_limit_bytes=VMEM_LIMIT),
        cost_estimate=pl.CostEstimate(
            flops=CSTEPS * 70 * cells * cells, bytes_accessed=24 * cells * cells, transcendentals=0
        ),
        name="coast_fold",
    )(link, depth, flow)


def coast_kernel(
    wet, ghosts, folded, depth, flow, out, state, terms, after, parts, opening, tmp, done, sems
):
    rows = depth.shape[0] // SUB
    is_wet = jnp.max(wet[...]) > 0.0

    def copy_in(k, carry):
        for f in range(3):
            for p in range(2):
                state[f, p, 1 + k] = folded[f, p, k]
        return carry

    @pl.when(jnp.logical_not(is_wet))
    def _():
        copies = [
            pltpu.make_async_copy(depth, out.at[0], sems.at[0]),
            pltpu.make_async_copy(flow, out.at[1:], sems.at[1]),
        ]
        for copy in copies:
            copy.start()
        for copy in copies:
            copy.wait()

    @pl.when(is_wet)
    def _():
        lax.fori_loop(0, rows, copy_in, 0, unroll=4)
        values = jnp.sum(ghosts[...], axis=0)
        level = (ghost_level + values) * DEPTH_UNIT
        inflow = values * FLOW_UNIT
        h, mv = [
            [jnp.broadcast_to(v[i : i + 1], (SUB, LANES)) for i in range(at, at + 2)]
            for v, at in ((level, 0), (inflow, 2))
        ]
        ghost = [[h[p], jnp.zeros_like(h[p]), mv[p]] for p in range(2)]
        coast_steps(state, terms, after, parts, opening, rows, GROUP, CSTEPS, ghost)

        def write(f):
            return pltpu.make_async_copy(done.at[f], out.at[f], sems.at[f])

        def finish(f, carry):
            scale = jnp.where(f == 0, 1.0 / DEPTH_UNIT, 1.0 / FLOW_UNIT)

            def unfold(k, carry):
                both = join_columns(state[f, 0, 1 + k], state[f, 1, 1 + k])
                for p in range(2):
                    tmp[p, pl.ds(k, SUB, stride=rows), :] = both[p] * scale
                return carry

            def copy_out(i, carry):
                at = pl.ds(pl.multiple_of(i * TALL, TALL), TALL)
                for p in range(2):
                    done[f, at, HALVES[p]] = tmp[p, at]
                return carry

            lax.fori_loop(0, rows, unfold, 0, unroll=16)
            lax.fori_loop(0, depth.shape[0] // TALL, copy_out, 0, unroll=4)
            write(f).start()
            return carry

        lax.fori_loop(0, 3, finish, 0)
        for f in range(3):
            write(f).wait()


def coast_run(wet, ghosts, folded, depth, flow):
    cells = depth.shape[0]
    vmem = pl.BlockSpec(memory_space=pltpu.VMEM)
    return pl.pallas_call(
        coast_kernel,
        out_shape=jax.ShapeDtypeStruct((3, cells, cells), jnp.float32),
        in_specs=[vmem] * 5,
        out_specs=pl.BlockSpec(memory_space=pltpu.HBM),
        scratch_shapes=[
            pltpu.VMEM((3, 2, 1 + cells // SUB, SUB, LANES), jnp.float32),
            pltpu.VMEM((2, 1 + GROUP, 5, SUB, LANES), jnp.float32),
            pltpu.VMEM((GROUP, 6, SUB, LANES), jnp.float32),
            pltpu.VMEM((GROUP, 6, SUB, LANES), jnp.float32),
            pltpu.VMEM((cells // SUB // GROUP, 2, 3, SUB, LANES), jnp.float32),
            pltpu.VMEM((2, cells, LANES), jnp.float32),
            pltpu.VMEM((3, cells, cells), jnp.float32),
            pltpu.SemaphoreType.DMA((3,)),
        ],
        compiler_params=pltpu.CompilerParams(vmem_limit_bytes=VMEM_LIMIT),
        cost_estimate=pl.CostEstimate(
            flops=CSTEPS * 70 * cells * cells, bytes_accessed=24 * cells * cells, transcendentals=0
        ),
        name="coast_steps",
    )(wet, ghosts, folded, depth, flow)


def basin_kernel(state, depth, pair_state, pair_depth, edge, out, eta, hu, hv, dep):
    rows, width = depth.shape
    total = rows + 2 * HALO
    chunks = width // LANES
    position = lax.axis_index("row")
    odd = position % 2
    north_inside = (position < lax.axis_size("row") - 1).astype(jnp.float32)
    pair_from = pl.multiple_of(odd * (rows - HALO), HALO)
    pair_at = pl.multiple_of((1 - odd) * (HALO + rows), HALO)
    edge_at = pl.multiple_of(odd * (HALO + rows), HALO)
    for ref, field, unit in ((eta, 0, 1.0), (hu, 1, 0.5), (hv, 2, 0.5), (dep, 3, 0.25)):
        own, pair = (depth, pair_depth) if field == 3 else (state.at[field], pair_state.at[field])
        ref[HALO : HALO + rows] = own[...] * unit
        ref[pl.ds(pair_at, HALO)] = pair[pl.ds(pair_from, HALO)] * unit
        ref[pl.ds(edge_at, HALO)] = edge[field] * unit
    lane = lax.broadcasted_iota(jnp.int32, (total, LANES), 1)
    first, last = lane == 0, lane == LANES - 1
    row = lax.broadcasted_iota(jnp.int32, (total, LANES), 0)
    kept = jnp.where(row < HALO + rows, 1.0, north_inside)

    def step(_, carry):
        prev_west = jnp.zeros((total, LANES), jnp.float32)
        prev_eta, prev_east, prev_hu = None, None, None
        for c in range(chunks + 1):
            if c < chunks:
                at = slice(c * LANES, (c + 1) * LANES)
                u, v = hu[:, at], hv[:, at]
                west = pltpu.roll(u, 1, 1)
                du = u - jnp.where(first, prev_west, west)
                dv = v - pltpu.roll(v, 1, 0)
                new = (eta[:, at] - (du + dv)) * kept
                eta[:, at] = new
                east = pltpu.roll(new, LANES - 1, 1)
                hv[:, at] = v - dep[:, at] * (pltpu.roll(new, total - 1, 0) - new)
            else:
                east = jnp.zeros((total, LANES), jnp.float32)
            if c > 0:
                back = slice((c - 1) * LANES, c * LANES)
                hu[:, back] = prev_hu - dep[:, back] * (jnp.where(last, east, prev_east) - prev_eta)
            prev_west, prev_eta, prev_east, prev_hu = west, new, east, u
        return carry

    lax.fori_loop(0, BSTEPS, step, 0)
    own = slice(HALO, HALO + rows)
    out[0] = eta[own]
    out[1] = hu[own] * 2.0
    out[2] = hv[own] * 2.0


def basin_run(state, depth, pair_state, pair_depth, edge):
    rows, width = depth.shape
    total = rows + 2 * HALO
    vmem = pl.BlockSpec(memory_space=pltpu.VMEM)
    return pl.pallas_call(
        basin_kernel,
        out_shape=jax.ShapeDtypeStruct((3, rows, width), jnp.float32),
        in_specs=[vmem] * 5,
        out_specs=vmem,
        scratch_shapes=[pltpu.VMEM((total, width), jnp.float32)] * 4,
        compiler_params=pltpu.CompilerParams(vmem_limit_bytes=VMEM_LIMIT),
        cost_estimate=pl.CostEstimate(
            flops=BSTEPS * 16 * total * width, bytes_accessed=4 * 11 * rows * width, transcendentals=0
        ),
        name="basin_steps",
    )(state, depth, pair_state, pair_depth, edge)


def strips_kernel(links, own, pair, ghosts, strips):
    rows, width = own.shape[1], own.shape[2]
    count = ghosts.shape[0]
    span = 2 * LANES
    position = lax.axis_index("row")
    tops = (position * rows, (position + 1 - 2 * (position % 2)) * rows)
    lane = lane_ids()
    weight = ((2 * lane + row_ids() % 2) % 16).astype(jnp.float32) / 16.0 + 0.5 / 16.0

    def piece(b, carry):
        col = links[b, 0, 1]
        start = jnp.clip(col // LANES, 0, width // LANES - 2) * LANES
        shift = lax.rem(span - (col - start), span)
        at = pl.ds(pl.multiple_of(start, LANES), span)
        for i, f in enumerate((0, 2)):
            chunk = None
            for source, top in zip((own, pair), tops):
                row = links[b, 0, 0] - top
                owned = jnp.logical_and(row >= 0, row < rows).astype(jnp.float32)
                part = source[f, pl.ds(jnp.clip(row, 0, rows - 1), 1), at] * owned
                chunk = part if chunk is None else chunk + part
            moved = pltpu.roll(chunk, shift, 1)[:, :LANES]
            strips[b, 2 * i : 2 * i + 2] = jnp.broadcast_to(moved, (2, LANES))
        values = strips[b]
        low, high = pick(values, lane // 8), pick(values, lane // 8 + 1)
        ghosts[b] = (1.0 - weight) * low + weight * high
        return carry

    strips[...] = jnp.zeros_like(strips)
    lax.fori_loop(0, count, piece, 0, unroll=8)


def make_strips(links, own, pair):
    count = links.shape[0]
    tiles = (count, SUB, LANES)
    vmem = pl.BlockSpec(memory_space=pltpu.VMEM)
    smem = pl.BlockSpec(memory_space=pltpu.SMEM)
    return pl.pallas_call(
        strips_kernel,
        out_shape=jax.ShapeDtypeStruct(tiles, jnp.float32),
        in_specs=[smem, vmem, vmem],
        out_specs=vmem,
        scratch_shapes=[pltpu.VMEM(tiles, jnp.float32)],
        compiler_params=pltpu.CompilerParams(vmem_limit_bytes=VMEM_LIMIT),
        cost_estimate=pl.CostEstimate(flops=2 * 10**10, bytes_accessed=own.size, transcendentals=0),
        name="strips",
    )(links, own, pair)


def local(basin_state, basin_depth, coast_depth, coast_flow, coast_link):
    devices = lax.axis_size("row")
    odd = lax.axis_index("row") % 2
    parity = [list(range(p, devices, 2))[::-1] for p in range(2)]
    start = odd * (basin_depth.shape[0] - HALO)
    edge = jnp.concatenate(
        [
            lax.dynamic_slice_in_dim(basin_state, start, HALO, axis=1),
            lax.dynamic_slice_in_dim(basin_depth, start, HALO, axis=0)[None],
        ],
        axis=0,
    )
    coast_link, edge = lax.optimization_barrier((coast_link, edge))
    sent = jnp.broadcast_to(coast_link, (devices // 2,) + coast_link.shape)
    links = lax.all_to_all(sent, "row", 0, 0, axis_index_groups=parity, tiled=True)

    twins = [(i, i ^ 1) for i in range(devices)]
    pair_state, pair_depth = [lax.ppermute(a, "row", twins) for a in (basin_state, basin_depth)]
    across = [(i, i + 1) for i in range(1, devices - 1, 2)]
    edge = lax.ppermute(edge, "row", across + [(j, i) for i, j in across])

    depth, flow = coast_depth[0], coast_flow[0]
    folded, wet = coast_fold(coast_link, depth, flow)
    pair_state, folded = lax.optimization_barrier((pair_state, folded))
    ghosts = make_strips(links, basin_state, pair_state)
    basin_depth, ghosts = lax.optimization_barrier((basin_depth, ghosts))
    ghosts = lax.all_to_all(ghosts, "row", 0, 0, axis_index_groups=parity, tiled=True)
    basin_out = basin_run(basin_state, basin_depth, pair_state, pair_depth, edge)
    folded, basin_out = lax.optimization_barrier((folded, basin_out))
    coast_out = coast_run(wet, ghosts, folded, depth, flow)
    return (basin_out, coast_out[None])


def solution(mesh):
    in_specs = (
        P("scen", "row", None),
        P("row", "scen"),
        P("row", "scen", None),
        P("row", "scen", None, None),
        P("row", "scen"),
    )
    out_specs = (P("scen", "row", None), P("row", "scen", None, None))
    return jax.shard_map(local, mesh=mesh, in_specs=in_specs, out_specs=out_specs, check_vma=False)
```

```python
import functools

import jax
import jax.numpy as jnp
from jax import lax
from jax.experimental import pallas as pl
from jax.experimental.pallas import tpu as pltpu
from jax.sharding import PartitionSpec as P

BSTEPS = 8
CSTEPS = 10

depth_floor = 0.2
ghost_level = 2.0

RATE = 0.05
DEPTH_UNIT = RATE * RATE
FLOW_UNIT = RATE * RATE * RATE
TINY = 1e-30

HALO = BSTEPS
SUB = 8
LANES = 128


def lane_ids():
    return lax.broadcasted_iota(jnp.int32, (SUB, LANES), 1)


def row_ids():
    return lax.broadcasted_iota(jnp.int32, (SUB, LANES), 0)


def cell_terms(u):
    h, mu, mv = u
    r = pl.reciprocal(jnp.maximum(h, depth_floor * DEPTH_UNIT), approx=True)
    vx, vy = mu * r, mv * r
    hp = jnp.maximum(h, TINY)
    c = hp * lax.rsqrt(hp)
    p = (0.5 * h) * h
    cross = mu * vy
    return {
        "u": u,
        "fx": (mu, mu * vx + p, cross),
        "fy": (mv, cross, mv * vy + p),
        "sx": jnp.abs(vx) + c,
        "sy": jnp.abs(vy) + c,
    }


def y_face(above, below):
    a = jnp.maximum(above["sy"], below["sy"])
    return [
        a * (ub - ua) - (fa + fb)
        for ua, ub, fa, fb in zip(above["u"], below["u"], above["fy"], below["fy"])
    ]


def coast_steps(state, terms, after, parts, opening, rows, group, steps, ghost):
    lane, sub = lane_ids(), row_ids()
    first, last = lane == 0, lane == LANES - 1
    top, bottom = sub == 0, sub == SUB - 1
    zero = jnp.zeros((SUB, LANES), jnp.float32)
    left = functools.partial(pltpu.roll, shift=LANES - 1, axis=1)
    right = functools.partial(pltpu.roll, shift=1, axis=1)

    def load(view, k):
        return [[view[f, half, 1 + k] for f in range(3)] for half in range(2)]

    def store(view, k, both):
        for half in range(2):
            for f in range(3):
                view[f, half, 1 + k] = both[half][f]

    def store_above(tails):
        store(state, -1, [[jnp.where(top, g, pltpu.roll(t, 1, 0)) for g, t in zip(*pair)] for pair in zip(ghost, tails)])

    def y_terms_of(view, k):
        both = [cell_terms(u) for u in load(view, k)]
        for half, cell in enumerate(both):
            terms[half, 1 + k, 0] = cell["sy"]
            terms[half, 1 + k, 1] = cell["fy"][2]
            terms[half, 1 + k, 2] = cell["fx"][2]
        return both

    def terms_of(view, k):
        even, odd = y_terms_of(view, k)
        for half, cell in enumerate((even, odd)):
            terms[half, 1 + k, 3] = cell["sx"]
            terms[half, 1 + k, 4] = cell["fx"][1]
        moved = zip(even["u"] + [even["sx"]] + list(even["fx"][1:]), odd["u"] + [odd["sx"]] + list(odd["fx"][1:]))
        for q, (e, o) in enumerate(moved):
            after[k, q] = jnp.where(last, o, left(e))

    def x_faces(view, k):
        even, odd = load(view, k)
        following = [after[k, f] for f in range(3)]
        sx_e, sx_o, sx_n = terms[0, 1 + k, 3], terms[1, 1 + k, 3], after[k, 3]
        fx_e = [even[1], terms[0, 1 + k, 4], terms[0, 1 + k, 2]]
        fx_o = [odd[1], terms[1, 1 + k, 4], terms[1, 1 + k, 2]]
        fx_n = [following[1], after[k, 4], after[k, 5]]
        a_in, a_out = jnp.maximum(sx_e, sx_o), jnp.maximum(sx_o, sx_n)
        for f in range(3):
            g_in = a_in * (odd[f] - even[f]) - (fx_e[f] + fx_o[f])
            g_out = a_out * (following[f] - odd[f]) - (fx_o[f] + fx_n[f])
            g_back = jnp.where(first, -2.0 * fx_e[f], right(g_out))
            parts[k, f] = even[f] + (g_in - g_back)
            parts[k, 3 + f] = odd[f] + (g_out - g_in)

    def y_cells(view, k):
        return [
            {
                "u": u,
                "fy": [u[2], terms[half, 1 + k, 2], terms[half, 1 + k, 1]],
                "sy": terms[half, 1 + k, 0],
            }
            for half, u in enumerate(load(view, k))
        ]

    def trip(i, acc):
        view = state.at[:, :, pl.ds(i * group, 1 + group)]
        y_terms_of(view, -1)
        for k in range(group):
            terms_of(view, k)
        for k in range(group):
            x_faces(view, k)
        prev = y_cells(view, -1)
        for k in range(group):
            cur = y_cells(view, k)
            face = [y_face(a, b) for a, b in zip(prev, cur)]
            if k == 0:
                for half in range(2):
                    for f in range(3):
                        opening[i, half, f] = pltpu.roll(face[half][f], SUB - 1, 0)
            store(view, k - 1, [[x + g for x, g in zip(*pair)] for pair in zip(acc, face)])
            acc = [[parts[k, 3 * half + f] - face[half][f] for f in range(3)] for half in range(2)]
            prev = cur
        return acc

    def step(_, carry):
        acc = lax.fori_loop(0, rows // group, trip, [[zero] * 3 for _ in range(2)])
        tails = [
            [
                x + jnp.where(bottom, -2.0 * f, opening[0, half, i])
                for i, (x, f) in enumerate(zip(xs, cell["fy"]))
            ]
            for half, (xs, cell) in enumerate(
                zip(acc, y_cells(state.at[:, :, rows - group :], group - 1))
            )
        ]
        store(state, rows - 1, tails)
        store_above(tails)
        return carry

    store_above(load(state, rows - 1))
    lax.fori_loop(0, steps, step, 0)


GROUP = 16
UNITS = (DEPTH_UNIT, FLOW_UNIT, FLOW_UNIT)
VMEM_LIMIT = 12 * 1024 * 1024
HALF = LANES // 2


def pick(values, ids):
    return jnp.take_along_axis(values, ids, axis=1, mode="promise_in_bounds")


def split_columns(west, east):
    lane = lane_ids()
    low = lane < HALF
    twice = 2 * jnp.where(low, lane, lane - HALF)
    w = pick(west, jnp.where(low, twice, twice + 1))
    e = pick(east, jnp.where(low, twice + 1, twice))
    return jnp.where(low, w, e), pltpu.roll(jnp.where(low, e, w), HALF, 1)


def join_columns(even, odd):
    lane = lane_ids()
    low = lane < HALF
    odd = pltpu.roll(odd, HALF, 1)
    w, e = jnp.where(low, even, odd), jnp.where(low, odd, even)
    half, is_odd = lane // 2, lane % 2
    return pick(w, half + HALF * is_odd), pick(e, half + HALF * (1 - is_odd))


HALVES = (slice(0, LANES), slice(LANES, 2 * LANES))
TALL = 32


def fold_kernel(link, depth, flow, state, wet, tmp):
    rows = depth.shape[0] // SUB
    wet[...] = jnp.broadcast_to(link[:, 2:3], wet.shape).astype(jnp.float32)

    def copy_in(i, carry):
        at = pl.ds(pl.multiple_of(i * TALL, TALL), TALL)
        for f in range(3):
            raw = depth[at] if f == 0 else flow[f - 1, at]
            for p in range(2):
                tmp[f, p, at] = raw[:, HALVES[p]] * UNITS[f]
        return carry

    def fold(k, carry):
        for f in range(3):
            both = split_columns(*[tmp[f, p, pl.ds(k, SUB, stride=rows), :] for p in range(2)])
            for p in range(2):
                state[f, p, k] = both[p]
        return carry

    lax.fori_loop(0, depth.shape[0] // TALL, copy_in, 0)
    lax.fori_loop(0, rows, fold, 0, unroll=4)


def coast_fold(link, depth, flow):
    cells = depth.shape[0]
    vmem = pl.BlockSpec(memory_space=pltpu.VMEM)
    return pl.pallas_call(
        fold_kernel,
        out_shape=(
            jax.ShapeDtypeStruct((3, 2, cells // SUB, SUB, LANES), jnp.float32),
            jax.ShapeDtypeStruct((SUB, LANES), jnp.float32),
        ),
        in_specs=[vmem, vmem, vmem],
        out_specs=(vmem, vmem),
        scratch_shapes=[pltpu.VMEM((3, 2, cells, LANES), jnp.float32)],
        compiler_params=pltpu.CompilerParams(vmem_limit_bytes=VMEM_LIMIT),
        cost_estimate=pl.CostEstimate(
            flops=CSTEPS * 70 * cells * cells, bytes_accessed=24 * cells * cells, transcendentals=0
        ),
        name="coast_fold",
    )(link, depth, flow)


def coast_kernel(
    wet, ghosts, folded, depth, flow, out, state, terms, after, parts, opening, tmp, done, sems
):
    rows = depth.shape[0] // SUB
    is_wet = jnp.max(wet[...]) > 0.0

    def copy_in(k, carry):
        for f in range(3):
            for p in range(2):
                state[f, p, 1 + k] = folded[f, p, k]
        return carry

    @pl.when(jnp.logical_not(is_wet))
    def _():
        copies = [
            pltpu.make_async_copy(depth, out.at[0], sems.at[0]),
            pltpu.make_async_copy(flow, out.at[1:], sems.at[1]),
        ]
        for copy in copies:
            copy.start()
        for copy in copies:
            copy.wait()

    @pl.when(is_wet)
    def _():
        lax.fori_loop(0, rows, copy_in, 0, unroll=4)
        values = jnp.sum(ghosts[...], axis=0)
        level = (ghost_level + values) * DEPTH_UNIT
        inflow = values * FLOW_UNIT
        h, mv = [
            [jnp.broadcast_to(v[i : i + 1], (SUB, LANES)) for i in range(at, at + 2)]
            for v, at in ((level, 0), (inflow, 2))
        ]
        ghost = [[h[p], jnp.zeros_like(h[p]), mv[p]] for p in range(2)]
        coast_steps(state, terms, after, parts, opening, rows, GROUP, CSTEPS, ghost)

        def write(f):
            return pltpu.make_async_copy(done.at[f], out.at[f], sems.at[f])

        def finish(f, carry):
            scale = jnp.where(f == 0, 1.0 / DEPTH_UNIT, 1.0 / FLOW_UNIT)

            def unfold(k, carry):
                both = join_columns(state[f, 0, 1 + k], state[f, 1, 1 + k])
                for p in range(2):
                    tmp[p, pl.ds(k, SUB, stride=rows), :] = both[p] * scale
                return carry

            def copy_out(i, carry):
                at = pl.ds(pl.multiple_of(i * TALL, TALL), TALL)
                for p in range(2):
                    done[f, at, HALVES[p]] = tmp[p, at]
                return carry

            lax.fori_loop(0, rows, unfold, 0, unroll=4)
            lax.fori_loop(0, depth.shape[0] // TALL, copy_out, 0, unroll=2)
            write(f).start()
            return carry

        lax.fori_loop(0, 3, finish, 0)
        for f in range(3):
            write(f).wait()


def coast_run(wet, ghosts, folded, depth, flow):
    cells = depth.shape[0]
    vmem = pl.BlockSpec(memory_space=pltpu.VMEM)
    return pl.pallas_call(
        coast_kernel,
        out_shape=jax.ShapeDtypeStruct((3, cells, cells), jnp.float32),
        in_specs=[vmem] * 5,
        out_specs=pl.BlockSpec(memory_space=pltpu.HBM),
        scratch_shapes=[
            pltpu.VMEM((3, 2, 1 + cells // SUB, SUB, LANES), jnp.float32),
            pltpu.VMEM((2, 1 + GROUP, 5, SUB, LANES), jnp.float32),
            pltpu.VMEM((GROUP, 6, SUB, LANES), jnp.float32),
            pltpu.VMEM((GROUP, 6, SUB, LANES), jnp.float32),
            pltpu.VMEM((cells // SUB // GROUP, 2, 3, SUB, LANES), jnp.float32),
            pltpu.VMEM((2, cells, LANES), jnp.float32),
            pltpu.VMEM((3, cells, cells), jnp.float32),
            pltpu.SemaphoreType.DMA((3,)),
        ],
        compiler_params=pltpu.CompilerParams(vmem_limit_bytes=VMEM_LIMIT),
        cost_estimate=pl.CostEstimate(
            flops=CSTEPS * 70 * cells * cells, bytes_accessed=24 * cells * cells, transcendentals=0
        ),
        name="coast_steps",
    )(wet, ghosts, folded, depth, flow)


def basin_kernel(state, depth, pair_state, pair_depth, edge, out, eta, hu, hv, dep):
    rows, width = depth.shape
    total = rows + 2 * HALO
    chunks = width // LANES
    position = lax.axis_index("row")
    odd = position % 2
    north_inside = (position < lax.axis_size("row") - 1).astype(jnp.float32)
    pair_from = pl.multiple_of(odd * (rows - HALO), HALO)
    pair_at = pl.multiple_of((1 - odd) * (HALO + rows), HALO)
    edge_at = pl.multiple_of(odd * (HALO + rows), HALO)
    for ref, field, unit in ((eta, 0, 1.0), (hu, 1, 0.5), (hv, 2, 0.5), (dep, 3, 0.25)):
        own, pair = (depth, pair_depth) if field == 3 else (state.at[field], pair_state.at[field])
        ref[HALO : HALO + rows] = own[...] * unit
        ref[pl.ds(pair_at, HALO)] = pair[pl.ds(pair_from, HALO)] * unit
        ref[pl.ds(edge_at, HALO)] = edge[field] * unit
    lane = lax.broadcasted_iota(jnp.int32, (total, LANES), 1)
    first, last = lane == 0, lane == LANES - 1
    row = lax.broadcasted_iota(jnp.int32, (total, LANES), 0)
    kept = jnp.where(row < HALO + rows, 1.0, north_inside)

    def step(_, carry):
        prev_west = jnp.zeros((total, LANES), jnp.float32)
        prev_eta, prev_east, prev_hu = None, None, None
        for c in range(chunks + 1):
            if c < chunks:
                at = slice(c * LANES, (c + 1) * LANES)
                u, v = hu[:, at], hv[:, at]
                west = pltpu.roll(u, 1, 1)
                du = u - jnp.where(first, prev_west, west)
                dv = v - pltpu.roll(v, 1, 0)
                new = (eta[:, at] - (du + dv)) * kept
                eta[:, at] = new
                east = pltpu.roll(new, LANES - 1, 1)
                hv[:, at] = v - dep[:, at] * (pltpu.roll(new, total - 1, 0) - new)
            else:
                east = jnp.zeros((total, LANES), jnp.float32)
            if c > 0:
                back = slice((c - 1) * LANES, c * LANES)
                hu[:, back] = prev_hu - dep[:, back] * (jnp.where(last, east, prev_east) - prev_eta)
            prev_west, prev_eta, prev_east, prev_hu = west, new, east, u
        return carry

    lax.fori_loop(0, BSTEPS, step, 0)
    own = slice(HALO, HALO + rows)
    out[0] = eta[own]
    out[1] = hu[own] * 2.0
    out[2] = hv[own] * 2.0


def basin_run(state, depth, pair_state, pair_depth, edge):
    rows, width = depth.shape
    total = rows + 2 * HALO
    vmem = pl.BlockSpec(memory_space=pltpu.VMEM)
    return pl.pallas_call(
        basin_kernel,
        out_shape=jax.ShapeDtypeStruct((3, rows, width), jnp.float32),
        in_specs=[vmem] * 5,
        out_specs=vmem,
        scratch_shapes=[pltpu.VMEM((total, width), jnp.float32)] * 4,
        compiler_params=pltpu.CompilerParams(vmem_limit_bytes=VMEM_LIMIT),
        cost_estimate=pl.CostEstimate(
            flops=BSTEPS * 16 * total * width, bytes_accessed=4 * 11 * rows * width, transcendentals=0
        ),
        name="basin_steps",
    )(state, depth, pair_state, pair_depth, edge)


def strips_kernel(links, own, pair, ghosts, strips):
    rows, width = own.shape[1], own.shape[2]
    count = ghosts.shape[0]
    span = 2 * LANES
    position = lax.axis_index("row")
    tops = (position * rows, (position + 1 - 2 * (position % 2)) * rows)
    lane = lane_ids()
    weight = ((2 * lane + row_ids() % 2) % 16).astype(jnp.float32) / 16.0 + 0.5 / 16.0

    def piece(b, carry):
        col = links[b, 0, 1]
        start = jnp.clip(col // LANES, 0, width // LANES - 2) * LANES
        shift = lax.rem(span - (col - start), span)
        at = pl.ds(pl.multiple_of(start, LANES), span)
        for i, f in enumerate((0, 2)):
            chunk = None
            for source, top in zip((own, pair), tops):
                row = links[b, 0, 0] - top
                owned = jnp.logical_and(row >= 0, row < rows).astype(jnp.float32)
                part = source[f, pl.ds(jnp.clip(row, 0, rows - 1), 1), at] * owned
                chunk = part if chunk is None else chunk + part
            moved = pltpu.roll(chunk, shift, 1)[:, :LANES]
            strips[b, 2 * i : 2 * i + 2] = jnp.broadcast_to(moved, (2, LANES))
        values = strips[b]
        low, high = pick(values, lane // 8), pick(values, lane // 8 + 1)
        ghosts[b] = (1.0 - weight) * low + weight * high
        return carry

    strips[...] = jnp.zeros_like(strips)
    lax.fori_loop(0, count, piece, 0, unroll=8)


def make_strips(links, own, pair):
    count = links.shape[0]
    tiles = (count, SUB, LANES)
    vmem = pl.BlockSpec(memory_space=pltpu.VMEM)
    smem = pl.BlockSpec(memory_space=pltpu.SMEM)
    return pl.pallas_call(
        strips_kernel,
        out_shape=jax.ShapeDtypeStruct(tiles, jnp.float32),
        in_specs=[smem, vmem, vmem],
        out_specs=vmem,
        scratch_shapes=[pltpu.VMEM(tiles, jnp.float32)],
        compiler_params=pltpu.CompilerParams(vmem_limit_bytes=VMEM_LIMIT),
        cost_estimate=pl.CostEstimate(flops=2 * 10**10, bytes_accessed=own.size, transcendentals=0),
        name="strips",
    )(links, own, pair)


def local(basin_state, basin_depth, coast_depth, coast_flow, coast_link):
    devices = lax.axis_size("row")
    odd = lax.axis_index("row") % 2
    parity = [list(range(p, devices, 2))[::-1] for p in range(2)]
    start = odd * (basin_depth.shape[0] - HALO)
    edge = jnp.concatenate(
        [
            lax.dynamic_slice_in_dim(basin_state, start, HALO, axis=1),
            lax.dynamic_slice_in_dim(basin_depth, start, HALO, axis=0)[None],
        ],
        axis=0,
    )
    sent = jnp.broadcast_to(coast_link, (devices // 2,) + coast_link.shape)
    sent, edge = lax.optimization_barrier((sent, edge))
    links = lax.all_to_all(sent, "row", 0, 0, axis_index_groups=parity, tiled=True)

    twins = [(i, i ^ 1) for i in range(devices)]
    pair_state, pair_depth = [lax.ppermute(a, "row", twins) for a in (basin_state, basin_depth)]
    across = [(i, i + 1) for i in range(1, devices - 1, 2)]
    edge = lax.ppermute(edge, "row", across + [(j, i) for i, j in across])

    depth, flow = coast_depth[0], coast_flow[0]
    folded, wet = coast_fold(coast_link, depth, flow)
    pair_state, folded = lax.optimization_barrier((pair_state, folded))
    ghosts = make_strips(links, basin_state, pair_state)
    basin_depth, ghosts = lax.optimization_barrier((basin_depth, ghosts))
    ghosts = lax.all_to_all(ghosts, "row", 0, 0, axis_index_groups=parity, tiled=True)
    basin_out = basin_run(basin_state, basin_depth, pair_state, pair_depth, edge)
    folded, basin_out = lax.optimization_barrier((folded, basin_out))
    coast_out = coast_run(wet, ghosts, folded, depth, flow)
    return (basin_out, coast_out[None])


def solution(mesh):
    in_specs = (
        P("scen", "row", None),
        P("row", "scen"),
        P("row", "scen", None),
        P("row", "scen", None, None),
        P("row", "scen"),
    )
    out_specs = (P("scen", "row", None), P("row", "scen", None, None))
    return jax.shard_map(local, mesh=mesh, in_specs=in_specs, out_specs=out_specs, check_vma=False)
```

```python
import functools

import jax
import jax.numpy as jnp
from jax import lax
from jax.experimental import pallas as pl
from jax.experimental.pallas import tpu as pltpu
from jax.sharding import PartitionSpec as P

BSTEPS = 8
CSTEPS = 10

depth_floor = 0.2
ghost_level = 2.0

RATE = 0.05
DEPTH_UNIT = RATE * RATE
FLOW_UNIT = RATE * RATE * RATE
TINY = 1e-30

HALO = BSTEPS
SUB = 8
LANES = 128


def lane_ids():
    return lax.broadcasted_iota(jnp.int32, (SUB, LANES), 1)


def row_ids():
    return lax.broadcasted_iota(jnp.int32, (SUB, LANES), 0)


def cell_terms(u):
    h, mu, mv = u
    r = pl.reciprocal(jnp.maximum(h, depth_floor * DEPTH_UNIT), approx=True)
    vx, vy = mu * r, mv * r
    hp = jnp.maximum(h, TINY)
    c = hp * lax.rsqrt(hp)
    p = (0.5 * h) * h
    cross = mu * vy
    return {
        "u": u,
        "fx": (mu, mu * vx + p, cross),
        "fy": (mv, cross, mv * vy + p),
        "sx": jnp.abs(vx) + c,
        "sy": jnp.abs(vy) + c,
    }


def y_face(above, below):
    a = jnp.maximum(above["sy"], below["sy"])
    return [
        a * (ub - ua) - (fa + fb)
        for ua, ub, fa, fb in zip(above["u"], below["u"], above["fy"], below["fy"])
    ]


def coast_steps(state, terms, after, parts, opening, rows, group, steps, ghost):
    lane, sub = lane_ids(), row_ids()
    first, last = lane == 0, lane == LANES - 1
    top, bottom = sub == 0, sub == SUB - 1
    zero = jnp.zeros((SUB, LANES), jnp.float32)
    left = functools.partial(pltpu.roll, shift=LANES - 1, axis=1)
    right = functools.partial(pltpu.roll, shift=1, axis=1)

    def load(view, k):
        return [[view[f, half, 1 + k] for f in range(3)] for half in range(2)]

    def store(view, k, both):
        for half in range(2):
            for f in range(3):
                view[f, half, 1 + k] = both[half][f]

    def store_above(tails):
        store(state, -1, [[jnp.where(top, g, pltpu.roll(t, 1, 0)) for g, t in zip(*pair)] for pair in zip(ghost, tails)])

    def y_terms_of(view, k):
        both = [cell_terms(u) for u in load(view, k)]
        for half, cell in enumerate(both):
            terms[half, 1 + k, 0] = cell["sy"]
            terms[half, 1 + k, 1] = cell["fy"][2]
            terms[half, 1 + k, 2] = cell["fx"][2]
        return both

    def terms_of(view, k):
        even, odd = y_terms_of(view, k)
        for half, cell in enumerate((even, odd)):
            terms[half, 1 + k, 3] = cell["sx"]
            terms[half, 1 + k, 4] = cell["fx"][1]
        moved = zip(even["u"] + [even["sx"]] + list(even["fx"][1:]), odd["u"] + [odd["sx"]] + list(odd["fx"][1:]))
        for q, (e, o) in enumerate(moved):
            after[k, q] = jnp.where(last, o, left(e))

    def x_faces(view, k):
        even, odd = load(view, k)
        following = [after[k, f] for f in range(3)]
        sx_e, sx_o, sx_n = terms[0, 1 + k, 3], terms[1, 1 + k, 3], after[k, 3]
        fx_e = [even[1], terms[0, 1 + k, 4], terms[0, 1 + k, 2]]
        fx_o = [odd[1], terms[1, 1 + k, 4], terms[1, 1 + k, 2]]
        fx_n = [following[1], after[k, 4], after[k, 5]]
        a_in, a_out = jnp.maximum(sx_e, sx_o), jnp.maximum(sx_o, sx_n)
        for f in range(3):
            g_in = a_in * (odd[f] - even[f]) - (fx_e[f] + fx_o[f])
            g_out = a_out * (following[f] - odd[f]) - (fx_o[f] + fx_n[f])
            g_back = jnp.where(first, -2.0 * fx_e[f], right(g_out))
            parts[k, f] = even[f] + (g_in - g_back)
            parts[k, 3 + f] = odd[f] + (g_out - g_in)

    def y_cells(view, k):
        return [
            {
                "u": u,
                "fy": [u[2], terms[half, 1 + k, 2], terms[half, 1 + k, 1]],
                "sy": terms[half, 1 + k, 0],
            }
            for half, u in enumerate(load(view, k))
        ]

    def trip(i, acc):
        view = state.at[:, :, pl.ds(i * group, 1 + group)]
        y_terms_of(view, -1)
        for k in range(group):
            terms_of(view, k)
        for k in range(group):
            x_faces(view, k)
        prev = y_cells(view, -1)
        for k in range(group):
            cur = y_cells(view, k)
            face = [y_face(a, b) for a, b in zip(prev, cur)]
            if k == 0:
                for half in range(2):
                    for f in range(3):
                        opening[i, half, f] = pltpu.roll(face[half][f], SUB - 1, 0)
            store(view, k - 1, [[x + g for x, g in zip(*pair)] for pair in zip(acc, face)])
            acc = [[parts[k, 3 * half + f] - face[half][f] for f in range(3)] for half in range(2)]
            prev = cur
        return acc

    def step(_, carry):
        acc = lax.fori_loop(0, rows // group, trip, [[zero] * 3 for _ in range(2)])
        tails = [
            [
                x + jnp.where(bottom, -2.0 * f, opening[0, half, i])
                for i, (x, f) in enumerate(zip(xs, cell["fy"]))
            ]
            for half, (xs, cell) in enumerate(
                zip(acc, y_cells(state.at[:, :, rows - group :], group - 1))
            )
        ]
        store(state, rows - 1, tails)
        store_above(tails)
        return carry

    store_above(load(state, rows - 1))
    lax.fori_loop(0, steps, step, 0)


GROUP = 16
UNITS = (DEPTH_UNIT, FLOW_UNIT, FLOW_UNIT)
VMEM_LIMIT = 12 * 1024 * 1024
HALF = LANES // 2


def pick(values, ids):
    return jnp.take_along_axis(values, ids, axis=1, mode="promise_in_bounds")


def split_columns(west, east):
    lane = lane_ids()
    low = lane < HALF
    twice = 2 * jnp.where(low, lane, lane - HALF)
    w = pick(west, jnp.where(low, twice, twice + 1))
    e = pick(east, jnp.where(low, twice + 1, twice))
    return jnp.where(low, w, e), pltpu.roll(jnp.where(low, e, w), HALF, 1)


def join_columns(even, odd):
    lane = lane_ids()
    low = lane < HALF
    odd = pltpu.roll(odd, HALF, 1)
    w, e = jnp.where(low, even, odd), jnp.where(low, odd, even)
    half, is_odd = lane // 2, lane % 2
    return pick(w, half + HALF * is_odd), pick(e, half + HALF * (1 - is_odd))


HALVES = (slice(0, LANES), slice(LANES, 2 * LANES))
TALL = 32


def fold_kernel(link, depth, flow, state, wet, tmp):
    rows = depth.shape[0] // SUB
    wet[...] = jnp.broadcast_to(link[:, 2:3], wet.shape).astype(jnp.float32)

    def copy_in(i, carry):
        at = pl.ds(pl.multiple_of(i * TALL, TALL), TALL)
        for f in range(3):
            raw = depth[at] if f == 0 else flow[f - 1, at]
            for p in range(2):
                tmp[f, p, at] = raw[:, HALVES[p]] * UNITS[f]
        return carry

    def fold(k, carry):
        for f in range(3):
            both = split_columns(*[tmp[f, p, pl.ds(k, SUB, stride=rows), :] for p in range(2)])
            for p in range(2):
                state[f, p, k] = both[p]
        return carry

    lax.fori_loop(0, depth.shape[0] // TALL, copy_in, 0)
    lax.fori_loop(0, rows, fold, 0, unroll=4)


def coast_fold(link, depth, flow):
    cells = depth.shape[0]
    vmem = pl.BlockSpec(memory_space=pltpu.VMEM)
    return pl.pallas_call(
        fold_kernel,
        out_shape=(
            jax.ShapeDtypeStruct((3, 2, cells // SUB, SUB, LANES), jnp.float32),
            jax.ShapeDtypeStruct((SUB, LANES), jnp.float32),
        ),
        in_specs=[vmem, vmem, vmem],
        out_specs=(vmem, vmem),
        scratch_shapes=[pltpu.VMEM((3, 2, cells, LANES), jnp.float32)],
        compiler_params=pltpu.CompilerParams(vmem_limit_bytes=VMEM_LIMIT),
        cost_estimate=pl.CostEstimate(
            flops=CSTEPS * 70 * cells * cells, bytes_accessed=24 * cells * cells, transcendentals=0
        ),
        name="coast_fold",
    )(link, depth, flow)


def coast_kernel(
    wet, ghosts, folded, depth, flow, out, state, terms, after, parts, opening, tmp, done, sems
):
    rows = depth.shape[0] // SUB
    is_wet = jnp.max(wet[...]) > 0.0

    def copy_in(k, carry):
        for f in range(3):
            for p in range(2):
                state[f, p, 1 + k] = folded[f, p, k]
        return carry

    @pl.when(jnp.logical_not(is_wet))
    def _():
        copies = [
            pltpu.make_async_copy(depth, out.at[0], sems.at[0]),
            pltpu.make_async_copy(flow, out.at[1:], sems.at[1]),
        ]
        for copy in copies:
            copy.start()
        for copy in copies:
            copy.wait()

    @pl.when(is_wet)
    def _():
        lax.fori_loop(0, rows, copy_in, 0, unroll=4)
        values = jnp.sum(ghosts[...], axis=0)
        level = (ghost_level + values) * DEPTH_UNIT
        inflow = values * FLOW_UNIT
        h, mv = [
            [jnp.broadcast_to(v[i : i + 1], (SUB, LANES)) for i in range(at, at + 2)]
            for v, at in ((level, 0), (inflow, 2))
        ]
        ghost = [[h[p], jnp.zeros_like(h[p]), mv[p]] for p in range(2)]
        coast_steps(state, terms, after, parts, opening, rows, GROUP, CSTEPS, ghost)

        def write(f):
            return pltpu.make_async_copy(done.at[f], out.at[f], sems.at[f])

        def finish(f, carry):
            scale = jnp.where(f == 0, 1.0 / DEPTH_UNIT, 1.0 / FLOW_UNIT)

            def unfold(k, carry):
                both = join_columns(state[f, 0, 1 + k], state[f, 1, 1 + k])
                for p in range(2):
                    tmp[p, pl.ds(k, SUB, stride=rows), :] = both[p] * scale
                return carry

            def copy_out(i, carry):
                at = pl.ds(pl.multiple_of(i * TALL, TALL), TALL)
                for p in range(2):
                    done[f, at, HALVES[p]] = tmp[p, at]
                return carry

            lax.fori_loop(0, rows, unfold, 0, unroll=rows)
            lax.fori_loop(0, depth.shape[0] // TALL, copy_out, 0, unroll=2)
            write(f).start()
            return carry

        lax.fori_loop(0, 3, finish, 0)
        for f in range(3):
            write(f).wait()


def coast_run(wet, ghosts, folded, depth, flow):
    cells = depth.shape[0]
    vmem = pl.BlockSpec(memory_space=pltpu.VMEM)
    return pl.pallas_call(
        coast_kernel,
        out_shape=jax.ShapeDtypeStruct((3, cells, cells), jnp.float32),
        in_specs=[vmem] * 5,
        out_specs=pl.BlockSpec(memory_space=pltpu.HBM),
        scratch_shapes=[
            pltpu.VMEM((3, 2, 1 + cells // SUB, SUB, LANES), jnp.float32),
            pltpu.VMEM((2, 1 + GROUP, 5, SUB, LANES), jnp.float32),
            pltpu.VMEM((GROUP, 6, SUB, LANES), jnp.float32),
            pltpu.VMEM((GROUP, 6, SUB, LANES), jnp.float32),
            pltpu.VMEM((cells // SUB // GROUP, 2, 3, SUB, LANES), jnp.float32),
            pltpu.VMEM((2, cells, LANES), jnp.float32),
            pltpu.VMEM((3, cells, cells), jnp.float32),
            pltpu.SemaphoreType.DMA((3,)),
        ],
        compiler_params=pltpu.CompilerParams(vmem_limit_bytes=VMEM_LIMIT),
        cost_estimate=pl.CostEstimate(
            flops=CSTEPS * 70 * cells * cells, bytes_accessed=24 * cells * cells, transcendentals=0
        ),
        name="coast_steps",
    )(wet, ghosts, folded, depth, flow)


def basin_kernel(state, depth, pair_state, pair_depth, edge, out, eta, hu, hv, dep):
    rows, width = depth.shape
    total = rows + 2 * HALO
    chunks = width // LANES
    position = lax.axis_index("row")
    odd = position % 2
    north_inside = (position < lax.axis_size("row") - 1).astype(jnp.float32)
    pair_from = pl.multiple_of(odd * (rows - HALO), HALO)
    pair_at = pl.multiple_of((1 - odd) * (HALO + rows), HALO)
    edge_at = pl.multiple_of(odd * (HALO + rows), HALO)
    for ref, field, unit in ((eta, 0, 1.0), (hu, 1, 0.5), (hv, 2, 0.5), (dep, 3, 0.25)):
        own, pair = (depth, pair_depth) if field == 3 else (state.at[field], pair_state.at[field])
        ref[HALO : HALO + rows] = own[...] * unit
        ref[pl.ds(pair_at, HALO)] = pair[pl.ds(pair_from, HALO)] * unit
        ref[pl.ds(edge_at, HALO)] = edge[field] * unit
    lane = lax.broadcasted_iota(jnp.int32, (total, LANES), 1)
    first, last = lane == 0, lane == LANES - 1
    row = lax.broadcasted_iota(jnp.int32, (total, LANES), 0)
    kept = jnp.where(row < HALO + rows, 1.0, north_inside)

    def step(_, carry):
        prev_west = jnp.zeros((total, LANES), jnp.float32)
        prev_eta, prev_east, prev_hu = None, None, None
        for c in range(chunks + 1):
            if c < chunks:
                at = slice(c * LANES, (c + 1) * LANES)
                u, v = hu[:, at], hv[:, at]
                west = pltpu.roll(u, 1, 1)
                du = u - jnp.where(first, prev_west, west)
                dv = v - pltpu.roll(v, 1, 0)
                new = (eta[:, at] - (du + dv)) * kept
                eta[:, at] = new
                east = pltpu.roll(new, LANES - 1, 1)
                hv[:, at] = v - dep[:, at] * (pltpu.roll(new, total - 1, 0) - new)
            else:
                east = jnp.zeros((total, LANES), jnp.float32)
            if c > 0:
                back = slice((c - 1) * LANES, c * LANES)
                hu[:, back] = prev_hu - dep[:, back] * (jnp.where(last, east, prev_east) - prev_eta)
            prev_west, prev_eta, prev_east, prev_hu = west, new, east, u
        return carry

    lax.fori_loop(0, BSTEPS, step, 0)
    own = slice(HALO, HALO + rows)
    out[0] = eta[own]
    out[1] = hu[own] * 2.0
    out[2] = hv[own] * 2.0


def basin_run(state, depth, pair_state, pair_depth, edge):
    rows, width = depth.shape
    total = rows + 2 * HALO
    vmem = pl.BlockSpec(memory_space=pltpu.VMEM)
    return pl.pallas_call(
        basin_kernel,
        out_shape=jax.ShapeDtypeStruct((3, rows, width), jnp.float32),
        in_specs=[vmem] * 5,
        out_specs=vmem,
        scratch_shapes=[pltpu.VMEM((total, width), jnp.float32)] * 4,
        compiler_params=pltpu.CompilerParams(vmem_limit_bytes=VMEM_LIMIT),
        cost_estimate=pl.CostEstimate(
            flops=BSTEPS * 16 * total * width, bytes_accessed=4 * 11 * rows * width, transcendentals=0
        ),
        name="basin_steps",
    )(state, depth, pair_state, pair_depth, edge)


def strips_kernel(links, own, pair, ghosts, strips):
    rows, width = own.shape[1], own.shape[2]
    count = ghosts.shape[0]
    span = 2 * LANES
    position = lax.axis_index("row")
    tops = (position * rows, (position + 1 - 2 * (position % 2)) * rows)
    lane = lane_ids()
    weight = ((2 * lane + row_ids() % 2) % 16).astype(jnp.float32) / 16.0 + 0.5 / 16.0

    def piece(b, carry):
        col = links[b, 0, 1]
        start = jnp.clip(col // LANES, 0, width // LANES - 2) * LANES
        shift = lax.rem(span - (col - start), span)
        at = pl.ds(pl.multiple_of(start, LANES), span)
        for i, f in enumerate((0, 2)):
            chunk = None
            for source, top in zip((own, pair), tops):
                row = links[b, 0, 0] - top
                owned = jnp.logical_and(row >= 0, row < rows).astype(jnp.float32)
                part = source[f, pl.ds(jnp.clip(row, 0, rows - 1), 1), at] * owned
                chunk = part if chunk is None else chunk + part
            moved = pltpu.roll(chunk, shift, 1)[:, :LANES]
            strips[b, 2 * i : 2 * i + 2] = jnp.broadcast_to(moved, (2, LANES))
        values = strips[b]
        low, high = pick(values, lane // 8), pick(values, lane // 8 + 1)
        ghosts[b] = (1.0 - weight) * low + weight * high
        return carry

    strips[...] = jnp.zeros_like(strips)
    lax.fori_loop(0, count, piece, 0, unroll=8)


def make_strips(links, own, pair):
    count = links.shape[0]
    tiles = (count, SUB, LANES)
    vmem = pl.BlockSpec(memory_space=pltpu.VMEM)
    smem = pl.BlockSpec(memory_space=pltpu.SMEM)
    return pl.pallas_call(
        strips_kernel,
        out_shape=jax.ShapeDtypeStruct(tiles, jnp.float32),
        in_specs=[smem, vmem, vmem],
        out_specs=vmem,
        scratch_shapes=[pltpu.VMEM(tiles, jnp.float32)],
        compiler_params=pltpu.CompilerParams(vmem_limit_bytes=VMEM_LIMIT),
        cost_estimate=pl.CostEstimate(flops=2 * 10**10, bytes_accessed=own.size, transcendentals=0),
        name="strips",
    )(links, own, pair)


def local(basin_state, basin_depth, coast_depth, coast_flow, coast_link):
    devices = lax.axis_size("row")
    odd = lax.axis_index("row") % 2
    parity = [list(range(p, devices, 2))[::-1] for p in range(2)]
    sent = jnp.broadcast_to(coast_link, (devices // 2,) + coast_link.shape)
    sent, later_state = lax.optimization_barrier((sent, basin_state))
    start = odd * (basin_depth.shape[0] - HALO)
    edge = jnp.concatenate(
        [
            lax.dynamic_slice_in_dim(later_state, start, HALO, axis=1),
            lax.dynamic_slice_in_dim(basin_depth, start, HALO, axis=0)[None],
        ],
        axis=0,
    )
    sent, edge = lax.optimization_barrier((sent, edge))
    links = lax.all_to_all(sent, "row", 0, 0, axis_index_groups=parity, tiled=True)

    twins = [(i, i ^ 1) for i in range(devices)]
    pair_state, pair_depth = [lax.ppermute(a, "row", twins) for a in (basin_state, basin_depth)]
    across = [(i, i + 1) for i in range(1, devices - 1, 2)]
    edge = lax.ppermute(edge, "row", across + [(j, i) for i, j in across])

    depth, flow = coast_depth[0], coast_flow[0]
    folded, wet = coast_fold(coast_link, depth, flow)
    pair_state, folded = lax.optimization_barrier((pair_state, folded))
    ghosts = make_strips(links, basin_state, pair_state)
    basin_depth, ghosts = lax.optimization_barrier((basin_depth, ghosts))
    ghosts = lax.all_to_all(ghosts, "row", 0, 0, axis_index_groups=parity, tiled=True)
    basin_out = basin_run(basin_state, basin_depth, pair_state, pair_depth, edge)
    folded, basin_out = lax.optimization_barrier((folded, basin_out))
    coast_out = coast_run(wet, ghosts, folded, depth, flow)
    return (basin_out, coast_out[None])


def solution(mesh):
    in_specs = (
        P("scen", "row", None),
        P("row", "scen"),
        P("row", "scen", None),
        P("row", "scen", None, None),
        P("row", "scen"),
    )
    out_specs = (P("scen", "row", None), P("row", "scen", None, None))
    return jax.shard_map(local, mesh=mesh, in_specs=in_specs, out_specs=out_specs, check_vma=False)
```

```python
import functools

import jax
import jax.numpy as jnp
from jax import lax
from jax.experimental import pallas as pl
from jax.experimental.pallas import tpu as pltpu
from jax.sharding import PartitionSpec as P

BSTEPS = 8
CSTEPS = 10

depth_floor = 0.2
ghost_level = 2.0

RATE = 0.05
DEPTH_UNIT = RATE * RATE
FLOW_UNIT = RATE * RATE * RATE
TINY = 1e-30

HALO = BSTEPS
SUB = 8
LANES = 128


def lane_ids():
    return lax.broadcasted_iota(jnp.int32, (SUB, LANES), 1)


def row_ids():
    return lax.broadcasted_iota(jnp.int32, (SUB, LANES), 0)


def cell_terms(u):
    h, mu, mv = u
    r = pl.reciprocal(jnp.maximum(h, depth_floor * DEPTH_UNIT), approx=True)
    vx, vy = mu * r, mv * r
    hp = jnp.maximum(h, TINY)
    c = hp * lax.rsqrt(hp)
    p = (0.5 * h) * h
    cross = mu * vy
    return {
        "u": u,
        "fx": (mu, mu * vx + p, cross),
        "fy": (mv, cross, mv * vy + p),
        "sx": jnp.abs(vx) + c,
        "sy": jnp.abs(vy) + c,
    }


def y_face(above, below):
    a = jnp.maximum(above["sy"], below["sy"])
    return [
        a * (ub - ua) - (fa + fb)
        for ua, ub, fa, fb in zip(above["u"], below["u"], above["fy"], below["fy"])
    ]


def coast_steps(state, terms, after, parts, opening, rows, group, steps, ghost):
    lane, sub = lane_ids(), row_ids()
    first, last = lane == 0, lane == LANES - 1
    top, bottom = sub == 0, sub == SUB - 1
    zero = jnp.zeros((SUB, LANES), jnp.float32)
    left = functools.partial(pltpu.roll, shift=LANES - 1, axis=1)
    right = functools.partial(pltpu.roll, shift=1, axis=1)

    def load(view, k):
        return [[view[f, half, 1 + k] for f in range(3)] for half in range(2)]

    def store(view, k, both):
        for half in range(2):
            for f in range(3):
                view[f, half, 1 + k] = both[half][f]

    def store_above(tails):
        store(state, -1, [[jnp.where(top, g, pltpu.roll(t, 1, 0)) for g, t in zip(*pair)] for pair in zip(ghost, tails)])

    def y_terms_of(view, k):
        both = [cell_terms(u) for u in load(view, k)]
        for half, cell in enumerate(both):
            terms[half, 1 + k, 0] = cell["sy"]
            terms[half, 1 + k, 1] = cell["fy"][2]
            terms[half, 1 + k, 2] = cell["fx"][2]
        return both

    def terms_of(view, k):
        even, odd = y_terms_of(view, k)
        for half, cell in enumerate((even, odd)):
            terms[half, 1 + k, 3] = cell["sx"]
            terms[half, 1 + k, 4] = cell["fx"][1]
        moved = zip(even["u"] + [even["sx"]] + list(even["fx"][1:]), odd["u"] + [odd["sx"]] + list(odd["fx"][1:]))
        for q, (e, o) in enumerate(moved):
            after[k, q] = jnp.where(last, o, left(e))

    def x_faces(view, k):
        even, odd = load(view, k)
        following = [after[k, f] for f in range(3)]
        sx_e, sx_o, sx_n = terms[0, 1 + k, 3], terms[1, 1 + k, 3], after[k, 3]
        fx_e = [even[1], terms[0, 1 + k, 4], terms[0, 1 + k, 2]]
        fx_o = [odd[1], terms[1, 1 + k, 4], terms[1, 1 + k, 2]]
        fx_n = [following[1], after[k, 4], after[k, 5]]
        a_in, a_out = jnp.maximum(sx_e, sx_o), jnp.maximum(sx_o, sx_n)
        for f in range(3):
            g_in = a_in * (odd[f] - even[f]) - (fx_e[f] + fx_o[f])
            g_out = a_out * (following[f] - odd[f]) - (fx_o[f] + fx_n[f])
            g_back = jnp.where(first, -2.0 * fx_e[f], right(g_out))
            parts[k, f] = even[f] + (g_in - g_back)
            parts[k, 3 + f] = odd[f] + (g_out - g_in)

    def y_cells(view, k):
        return [
            {
                "u": u,
                "fy": [u[2], terms[half, 1 + k, 2], terms[half, 1 + k, 1]],
                "sy": terms[half, 1 + k, 0],
            }
            for half, u in enumerate(load(view, k))
        ]

    def trip(i, acc):
        view = state.at[:, :, pl.ds(i * group, 1 + group)]
        y_terms_of(view, -1)
        for k in range(group):
            terms_of(view, k)
        for k in range(group):
            x_faces(view, k)
        prev = y_cells(view, -1)
        for k in range(group):
            cur = y_cells(view, k)
            face = [y_face(a, b) for a, b in zip(prev, cur)]
            if k == 0:
                for half in range(2):
                    for f in range(3):
                        opening[i, half, f] = pltpu.roll(face[half][f], SUB - 1, 0)
            store(view, k - 1, [[x + g for x, g in zip(*pair)] for pair in zip(acc, face)])
            acc = [[parts[k, 3 * half + f] - face[half][f] for f in range(3)] for half in range(2)]
            prev = cur
        return acc

    def step(_, carry):
        acc = lax.fori_loop(0, rows // group, trip, [[zero] * 3 for _ in range(2)])
        tails = [
            [
                x + jnp.where(bottom, -2.0 * f, opening[0, half, i])
                for i, (x, f) in enumerate(zip(xs, cell["fy"]))
            ]
            for half, (xs, cell) in enumerate(
                zip(acc, y_cells(state.at[:, :, rows - group :], group - 1))
            )
        ]
        store(state, rows - 1, tails)
        store_above(tails)
        return carry

    store_above(load(state, rows - 1))
    lax.fori_loop(0, steps, step, 0)


GROUP = 16
UNITS = (DEPTH_UNIT, FLOW_UNIT, FLOW_UNIT)
VMEM_LIMIT = 12 * 1024 * 1024
HALF = LANES // 2


def pick(values, ids):
    return jnp.take_along_axis(values, ids, axis=1, mode="promise_in_bounds")


def split_columns(west, east):
    lane = lane_ids()
    low = lane < HALF
    twice = 2 * jnp.where(low, lane, lane - HALF)
    w = pick(west, jnp.where(low, twice, twice + 1))
    e = pick(east, jnp.where(low, twice + 1, twice))
    return jnp.where(low, w, e), pltpu.roll(jnp.where(low, e, w), HALF, 1)


def join_columns(even, odd):
    lane = lane_ids()
    low = lane < HALF
    odd = pltpu.roll(odd, HALF, 1)
    w, e = jnp.where(low, even, odd), jnp.where(low, odd, even)
    half, is_odd = lane // 2, lane % 2
    return pick(w, half + HALF * is_odd), pick(e, half + HALF * (1 - is_odd))


HALVES = (slice(0, LANES), slice(LANES, 2 * LANES))
TALL = 32


def fold_kernel(link, depth, flow, state, wet, tmp):
    rows = depth.shape[0] // SUB
    wet[...] = jnp.broadcast_to(link[:, 2:3], wet.shape).astype(jnp.float32)

    def copy_in(i, carry):
        at = pl.ds(pl.multiple_of(i * TALL, TALL), TALL)
        for f in range(3):
            raw = depth[at] if f == 0 else flow[f - 1, at]
            for p in range(2):
                tmp[f, p, at] = raw[:, HALVES[p]] * UNITS[f]
        return carry

    def fold_field(f, carry):
        def fold(k, carry):
            both = split_columns(*[tmp[f, p, pl.ds(k, SUB, stride=rows), :] for p in range(2)])
            for p in range(2):
                state[f, p, k] = both[p]
            return carry

        return lax.fori_loop(0, rows, fold, carry, unroll=16)

    lax.fori_loop(0, depth.shape[0] // TALL, copy_in, 0)
    lax.fori_loop(0, 3, fold_field, 0)


def coast_fold(link, depth, flow):
    cells = depth.shape[0]
    vmem = pl.BlockSpec(memory_space=pltpu.VMEM)
    return pl.pallas_call(
        fold_kernel,
        out_shape=(
            jax.ShapeDtypeStruct((3, 2, cells // SUB, SUB, LANES), jnp.float32),
            jax.ShapeDtypeStruct((SUB, LANES), jnp.float32),
        ),
        in_specs=[vmem, vmem, vmem],
        out_specs=(vmem, vmem),
        scratch_shapes=[pltpu.VMEM((3, 2, cells, LANES), jnp.float32)],
        compiler_params=pltpu.CompilerParams(vmem_limit_bytes=VMEM_LIMIT),
        cost_estimate=pl.CostEstimate(
            flops=CSTEPS * 70 * cells * cells, bytes_accessed=24 * cells * cells, transcendentals=0
        ),
        name="coast_fold",
    )(link, depth, flow)


def coast_kernel(
    wet, ghosts, folded, depth, flow, out, state, terms, after, parts, opening, tmp, done, sems
):
    rows = depth.shape[0] // SUB
    is_wet = jnp.max(wet[...]) > 0.0

    def copy_in(k, carry):
        for f in range(3):
            for p in range(2):
                state[f, p, 1 + k] = folded[f, p, k]
        return carry

    @pl.when(jnp.logical_not(is_wet))
    def _():
        copies = [
            pltpu.make_async_copy(depth, out.at[0], sems.at[0]),
            pltpu.make_async_copy(flow, out.at[1:], sems.at[1]),
        ]
        for copy in copies:
            copy.start()
        for copy in copies:
            copy.wait()

    @pl.when(is_wet)
    def _():
        lax.fori_loop(0, rows, copy_in, 0, unroll=4)
        values = jnp.sum(ghosts[...], axis=0)
        level = (ghost_level + values) * DEPTH_UNIT
        inflow = values * FLOW_UNIT
        h, mv = [
            [jnp.broadcast_to(v[i : i + 1], (SUB, LANES)) for i in range(at, at + 2)]
            for v, at in ((level, 0), (inflow, 2))
        ]
        ghost = [[h[p], jnp.zeros_like(h[p]), mv[p]] for p in range(2)]
        coast_steps(state, terms, after, parts, opening, rows, GROUP, CSTEPS, ghost)

        def write(f):
            return pltpu.make_async_copy(done.at[f], out.at[f], sems.at[f])

        def finish(f, carry):
            scale = jnp.where(f == 0, 1.0 / DEPTH_UNIT, 1.0 / FLOW_UNIT)

            def unfold(k, carry):
                both = join_columns(state[f, 0, 1 + k], state[f, 1, 1 + k])
                for p in range(2):
                    tmp[p, pl.ds(k, SUB, stride=rows), :] = both[p] * scale
                return carry

            def copy_out(i, carry):
                at = pl.ds(pl.multiple_of(i * TALL, TALL), TALL)
                for p in range(2):
                    done[f, at, HALVES[p]] = tmp[p, at]
                return carry

            lax.fori_loop(0, rows, unfold, 0, unroll=rows)
            lax.fori_loop(0, depth.shape[0] // TALL, copy_out, 0, unroll=2)
            write(f).start()
            return carry

        lax.fori_loop(0, 3, finish, 0)
        for f in range(3):
            write(f).wait()


def coast_run(wet, ghosts, folded, depth, flow):
    cells = depth.shape[0]
    vmem = pl.BlockSpec(memory_space=pltpu.VMEM)
    return pl.pallas_call(
        coast_kernel,
        out_shape=jax.ShapeDtypeStruct((3, cells, cells), jnp.float32),
        in_specs=[vmem] * 5,
        out_specs=pl.BlockSpec(memory_space=pltpu.HBM),
        scratch_shapes=[
            pltpu.VMEM((3, 2, 1 + cells // SUB, SUB, LANES), jnp.float32),
            pltpu.VMEM((2, 1 + GROUP, 5, SUB, LANES), jnp.float32),
            pltpu.VMEM((GROUP, 6, SUB, LANES), jnp.float32),
            pltpu.VMEM((GROUP, 6, SUB, LANES), jnp.float32),
            pltpu.VMEM((cells // SUB // GROUP, 2, 3, SUB, LANES), jnp.float32),
            pltpu.VMEM((2, cells, LANES), jnp.float32),
            pltpu.VMEM((3, cells, cells), jnp.float32),
            pltpu.SemaphoreType.DMA((3,)),
        ],
        compiler_params=pltpu.CompilerParams(vmem_limit_bytes=VMEM_LIMIT),
        cost_estimate=pl.CostEstimate(
            flops=CSTEPS * 70 * cells * cells, bytes_accessed=24 * cells * cells, transcendentals=0
        ),
        name="coast_steps",
    )(wet, ghosts, folded, depth, flow)


def basin_kernel(state, depth, pair_state, pair_depth, edge, out, eta, hu, hv, dep):
    rows, width = depth.shape
    total = rows + 2 * HALO
    chunks = width // LANES
    position = lax.axis_index("row")
    odd = position % 2
    north_inside = (position < lax.axis_size("row") - 1).astype(jnp.float32)
    pair_from = pl.multiple_of(odd * (rows - HALO), HALO)
    pair_at = pl.multiple_of((1 - odd) * (HALO + rows), HALO)
    edge_at = pl.multiple_of(odd * (HALO + rows), HALO)
    for ref, field, unit in ((eta, 0, 1.0), (hu, 1, 0.5), (hv, 2, 0.5), (dep, 3, 0.25)):
        own, pair = (depth, pair_depth) if field == 3 else (state.at[field], pair_state.at[field])
        for c in range(chunks):
            at = slice(c * LANES, (c + 1) * LANES)
            ref[c, HALO : HALO + rows] = own[:, at] * unit
            ref[c, pl.ds(pair_at, HALO)] = pair[pl.ds(pair_from, HALO), at] * unit
            ref[c, pl.ds(edge_at, HALO)] = edge[field, :, at] * unit
    apart = total // SUB
    lane = lane_ids()
    first, last = lane == 0, lane == LANES - 1
    kept = jnp.where(row_ids() * apart < HALO + rows, 1.0, north_inside)
    zero = jnp.zeros((SUB, LANES), jnp.float32)

    def load(ref, c):
        return [ref[c, pl.ds(k, SUB, stride=apart), :] for k in range(apart)]

    def store(ref, c, values):
        for k in range(apart):
            ref[c, pl.ds(k, SUB, stride=apart), :] = values[k]

    def step(_, carry):
        prev_west = [zero] * apart
        prev_eta, prev_east, prev_hu = None, None, None
        for c in range(chunks + 1):
            if c < chunks:
                u, v, d = load(hu, c), load(hv, c), load(dep, c)
                west = [pltpu.roll(x, 1, 1) for x in u]
                south = [pltpu.roll(v[-1], 1, 0)] + v[:-1]
                new = [
                    (e - ((x - jnp.where(first, p, w)) + (y - t))) * kept
                    for e, x, p, w, y, t in zip(load(eta, c), u, prev_west, west, v, south)
                ]
                store(eta, c, new)
                east = [pltpu.roll(x, LANES - 1, 1) for x in new]
                north = new[1:] + [pltpu.roll(new[0], SUB - 1, 0)]
                store(hv, c, [y - g * (n - x) for y, g, n, x in zip(v, d, north, new)])
            else:
                east = [zero] * apart
            if c > 0:
                d = load(dep, c - 1)
                store(
                    hu,
                    c - 1,
                    [
                        x - g * (jnp.where(last, e, p) - n)
                        for x, g, e, p, n in zip(prev_hu, d, east, prev_east, prev_eta)
                    ],
                )
            prev_west, prev_eta, prev_east, prev_hu = west, new, east, u
        return carry

    lax.fori_loop(0, BSTEPS, step, 0)
    for c in range(chunks):
        at = slice(c * LANES, (c + 1) * LANES)
        for f, (ref, unit) in enumerate(((eta, 1.0), (hu, 2.0), (hv, 2.0))):
            out[f, :, at] = ref[c, HALO : HALO + rows] * unit


def basin_run(state, depth, pair_state, pair_depth, edge):
    rows, width = depth.shape
    total = rows + 2 * HALO
    vmem = pl.BlockSpec(memory_space=pltpu.VMEM)
    return pl.pallas_call(
        basin_kernel,
        out_shape=jax.ShapeDtypeStruct((3, rows, width), jnp.float32),
        in_specs=[vmem] * 5,
        out_specs=vmem,
        scratch_shapes=[pltpu.VMEM((width // LANES, total, LANES), jnp.float32)] * 4,
        compiler_params=pltpu.CompilerParams(vmem_limit_bytes=VMEM_LIMIT),
        cost_estimate=pl.CostEstimate(
            flops=BSTEPS * 16 * total * width, bytes_accessed=4 * 11 * rows * width, transcendentals=0
        ),
        name="basin_steps",
    )(state, depth, pair_state, pair_depth, edge)


def strips_kernel(links, own, pair, ghosts, strips):
    rows, width = own.shape[1], own.shape[2]
    count = ghosts.shape[0]
    span = 2 * LANES
    position = lax.axis_index("row")
    tops = (position * rows, (position + 1 - 2 * (position % 2)) * rows)
    lane = lane_ids()
    weight = ((2 * lane + row_ids() % 2) % 16).astype(jnp.float32) / 16.0 + 0.5 / 16.0

    def piece(b, carry):
        col = links[b, 0, 1]
        start = jnp.clip(col // LANES, 0, width // LANES - 2) * LANES
        shift = lax.rem(span - (col - start), span)
        at = pl.ds(pl.multiple_of(start, LANES), span)
        for i, f in enumerate((0, 2)):
            chunk = None
            for source, top in zip((own, pair), tops):
                row = links[b, 0, 0] - top
                owned = jnp.logical_and(row >= 0, row < rows).astype(jnp.float32)
                part = source[f, pl.ds(jnp.clip(row, 0, rows - 1), 1), at] * owned
                chunk = part if chunk is None else chunk + part
            moved = pltpu.roll(chunk, shift, 1)[:, :LANES]
            strips[b, 2 * i : 2 * i + 2] = jnp.broadcast_to(moved, (2, LANES))
        values = strips[b]
        low, high = pick(values, lane // 8), pick(values, lane // 8 + 1)
        ghosts[b] = (1.0 - weight) * low + weight * high
        return carry

    strips[...] = jnp.zeros_like(strips)
    lax.fori_loop(0, count, piece, 0, unroll=8)


def make_strips(links, own, pair):
    count = links.shape[0]
    tiles = (count, SUB, LANES)
    vmem = pl.BlockSpec(memory_space=pltpu.VMEM)
    smem = pl.BlockSpec(memory_space=pltpu.SMEM)
    return pl.pallas_call(
        strips_kernel,
        out_shape=jax.ShapeDtypeStruct(tiles, jnp.float32),
        in_specs=[smem, vmem, vmem],
        out_specs=vmem,
        scratch_shapes=[pltpu.VMEM(tiles, jnp.float32)],
        compiler_params=pltpu.CompilerParams(vmem_limit_bytes=VMEM_LIMIT),
        cost_estimate=pl.CostEstimate(flops=2 * 10**10, bytes_accessed=own.size, transcendentals=0),
        name="strips",
    )(links, own, pair)


def local(basin_state, basin_depth, coast_depth, coast_flow, coast_link):
    devices = lax.axis_size("row")
    odd = lax.axis_index("row") % 2
    parity = [list(range(p, devices, 2))[::-1] for p in range(2)]
    sent = jnp.broadcast_to(coast_link, (devices // 2,) + coast_link.shape)
    sent, later_state = lax.optimization_barrier((sent, basin_state))
    start = odd * (basin_depth.shape[0] - HALO)
    edge = jnp.concatenate(
        [
            lax.dynamic_slice_in_dim(later_state, start, HALO, axis=1),
            lax.dynamic_slice_in_dim(basin_depth, start, HALO, axis=0)[None],
        ],
        axis=0,
    )
    sent, edge = lax.optimization_barrier((sent, edge))
    links = lax.all_to_all(sent, "row", 0, 0, axis_index_groups=parity, tiled=True)

    twins = [(i, i ^ 1) for i in range(devices)]
    pair_state, pair_depth = [lax.ppermute(a, "row", twins) for a in (basin_state, basin_depth)]
    across = [(i, i + 1) for i in range(1, devices - 1, 2)]
    edge = lax.ppermute(edge, "row", across + [(j, i) for i, j in across])

    depth, flow = coast_depth[0], coast_flow[0]
    folded, wet = coast_fold(coast_link, depth, flow)
    pair_state, folded = lax.optimization_barrier((pair_state, folded))
    ghosts = make_strips(links, basin_state, pair_state)
    basin_depth, ghosts = lax.optimization_barrier((basin_depth, ghosts))
    ghosts = lax.all_to_all(ghosts, "row", 0, 0, axis_index_groups=parity, tiled=True)
    basin_out = basin_run(basin_state, basin_depth, pair_state, pair_depth, edge)
    folded, basin_out = lax.optimization_barrier((folded, basin_out))
    coast_out = coast_run(wet, ghosts, folded, depth, flow)
    return (basin_out, coast_out[None])


def solution(mesh):
    in_specs = (
        P("scen", "row", None),
        P("row", "scen"),
        P("row", "scen", None),
        P("row", "scen", None, None),
        P("row", "scen"),
    )
    out_specs = (P("scen", "row", None), P("row", "scen", None, None))
    return jax.shard_map(local, mesh=mesh, in_specs=in_specs, out_specs=out_specs, check_vma=False)
```

```python
import functools

import jax
import jax.numpy as jnp
from jax import lax
from jax.experimental import pallas as pl
from jax.experimental.pallas import tpu as pltpu
from jax.sharding import PartitionSpec as P

BSTEPS = 8
CSTEPS = 10

depth_floor = 0.2
ghost_level = 2.0

RATE = 0.05
DEPTH_UNIT = RATE * RATE
FLOW_UNIT = RATE * RATE * RATE
TINY = 1e-30

HALO = BSTEPS
SUB = 8
LANES = 128


def lane_ids():
    return lax.broadcasted_iota(jnp.int32, (SUB, LANES), 1)


def row_ids():
    return lax.broadcasted_iota(jnp.int32, (SUB, LANES), 0)


def cell_terms(u):
    h, mu, mv = u
    r = pl.reciprocal(jnp.maximum(h, depth_floor * DEPTH_UNIT), approx=True)
    vx, vy = mu * r, mv * r
    hp = jnp.maximum(h, TINY)
    c = hp * lax.rsqrt(hp)
    p = (0.5 * h) * h
    cross = mu * vy
    return {
        "u": u,
        "fx": (mu, mu * vx + p, cross),
        "fy": (mv, cross, mv * vy + p),
        "sx": jnp.abs(vx) + c,
        "sy": jnp.abs(vy) + c,
    }


def y_face(above, below):
    a = jnp.maximum(above["sy"], below["sy"])
    return [
        a * (ub - ua) - (fa + fb)
        for ua, ub, fa, fb in zip(above["u"], below["u"], above["fy"], below["fy"])
    ]


def coast_steps(state, terms, after, parts, opening, rows, group, steps, ghost):
    lane, sub = lane_ids(), row_ids()
    first, last = lane == 0, lane == LANES - 1
    top, bottom = sub == 0, sub == SUB - 1
    zero = jnp.zeros((SUB, LANES), jnp.float32)
    left = functools.partial(pltpu.roll, shift=LANES - 1, axis=1)
    right = functools.partial(pltpu.roll, shift=1, axis=1)

    def load(view, k):
        return [[view[f, half, 1 + k] for f in range(3)] for half in range(2)]

    def store(view, k, both):
        for half in range(2):
            for f in range(3):
                view[f, half, 1 + k] = both[half][f]

    def store_above(tails):
        store(state, -1, [[jnp.where(top, g, pltpu.roll(t, 1, 0)) for g, t in zip(*pair)] for pair in zip(ghost, tails)])

    def y_terms_of(view, k):
        both = [cell_terms(u) for u in load(view, k)]
        for half, cell in enumerate(both):
            terms[half, 1 + k, 0] = cell["sy"]
            terms[half, 1 + k, 1] = cell["fy"][2]
            terms[half, 1 + k, 2] = cell["fx"][2]
        return both

    def terms_of(view, k):
        even, odd = y_terms_of(view, k)
        for half, cell in enumerate((even, odd)):
            terms[half, 1 + k, 3] = cell["sx"]
            terms[half, 1 + k, 4] = cell["fx"][1]
        moved = zip(even["u"] + [even["sx"]] + list(even["fx"][1:]), odd["u"] + [odd["sx"]] + list(odd["fx"][1:]))
        for q, (e, o) in enumerate(moved):
            after[k, q] = jnp.where(last, o, left(e))

    def x_faces(view, k):
        even, odd = load(view, k)
        following = [after[k, f] for f in range(3)]
        sx_e, sx_o, sx_n = terms[0, 1 + k, 3], terms[1, 1 + k, 3], after[k, 3]
        fx_e = [even[1], terms[0, 1 + k, 4], terms[0, 1 + k, 2]]
        fx_o = [odd[1], terms[1, 1 + k, 4], terms[1, 1 + k, 2]]
        fx_n = [following[1], after[k, 4], after[k, 5]]
        a_in, a_out = jnp.maximum(sx_e, sx_o), jnp.maximum(sx_o, sx_n)
        for f in range(3):
            g_in = a_in * (odd[f] - even[f]) - (fx_e[f] + fx_o[f])
            g_out = a_out * (following[f] - odd[f]) - (fx_o[f] + fx_n[f])
            g_back = jnp.where(first, -2.0 * fx_e[f], right(g_out))
            parts[k, f] = even[f] + (g_in - g_back)
            parts[k, 3 + f] = odd[f] + (g_out - g_in)

    def y_cells(view, k):
        return [
            {
                "u": u,
                "fy": [u[2], terms[half, 1 + k, 2], terms[half, 1 + k, 1]],
                "sy": terms[half, 1 + k, 0],
            }
            for half, u in enumerate(load(view, k))
        ]

    def trip(i, acc):
        view = state.at[:, :, pl.ds(i * group, 1 + group)]
        y_terms_of(view, -1)
        for k in range(group):
            terms_of(view, k)
        for k in range(group):
            x_faces(view, k)
        prev = y_cells(view, -1)
        for k in range(group):
            cur = y_cells(view, k)
            face = [y_face(a, b) for a, b in zip(prev, cur)]
            if k == 0:
                for half in range(2):
                    for f in range(3):
                        opening[i, half, f] = pltpu.roll(face[half][f], SUB - 1, 0)
            store(view, k - 1, [[x + g for x, g in zip(*pair)] for pair in zip(acc, face)])
            acc = [[parts[k, 3 * half + f] - face[half][f] for f in range(3)] for half in range(2)]
            prev = cur
        return acc

    def step(_, carry):
        acc = lax.fori_loop(0, rows // group, trip, [[zero] * 3 for _ in range(2)])
        tails = [
            [
                x + jnp.where(bottom, -2.0 * f, opening[0, half, i])
                for i, (x, f) in enumerate(zip(xs, cell["fy"]))
            ]
            for half, (xs, cell) in enumerate(
                zip(acc, y_cells(state.at[:, :, rows - group :], group - 1))
            )
        ]
        store(state, rows - 1, tails)
        store_above(tails)
        return carry

    store_above(load(state, rows - 1))
    lax.fori_loop(0, steps, step, 0)


GROUP = 16
UNITS = (DEPTH_UNIT, FLOW_UNIT, FLOW_UNIT)
VMEM_LIMIT = 12 * 1024 * 1024
HALF = LANES // 2


def pick(values, ids):
    return jnp.take_along_axis(values, ids, axis=1, mode="promise_in_bounds")


def split_columns(west, east):
    lane = lane_ids()
    low = lane < HALF
    twice = 2 * jnp.where(low, lane, lane - HALF)
    w = pick(west, jnp.where(low, twice, twice + 1))
    e = pick(east, jnp.where(low, twice + 1, twice))
    return jnp.where(low, w, e), pltpu.roll(jnp.where(low, e, w), HALF, 1)


def join_columns(even, odd):
    lane = lane_ids()
    low = lane < HALF
    odd = pltpu.roll(odd, HALF, 1)
    w, e = jnp.where(low, even, odd), jnp.where(low, odd, even)
    half, is_odd = lane // 2, lane % 2
    return pick(w, half + HALF * is_odd), pick(e, half + HALF * (1 - is_odd))


HALVES = (slice(0, LANES), slice(LANES, 2 * LANES))
TALL = 32


def fold_kernel(link, depth, flow, state, wet, tmp):
    rows = depth.shape[0] // SUB
    wet[...] = jnp.broadcast_to(link[:, 2:3], wet.shape).astype(jnp.float32)

    def copy_in(i, carry):
        at = pl.ds(pl.multiple_of(i * TALL, TALL), TALL)
        for f in range(3):
            raw = depth[at] if f == 0 else flow[f - 1, at]
            for p in range(2):
                tmp[f, p, at] = raw[:, HALVES[p]] * UNITS[f]
        return carry

    def fold_field(f, carry):
        def fold(k, carry):
            both = split_columns(*[tmp[f, p, pl.ds(k, SUB, stride=rows), :] for p in range(2)])
            for p in range(2):
                state[f, p, k] = both[p]
            return carry

        return lax.fori_loop(0, rows, fold, carry, unroll=16)

    lax.fori_loop(0, depth.shape[0] // TALL, copy_in, 0)
    lax.fori_loop(0, 3, fold_field, 0)


def coast_fold(link, depth, flow):
    cells = depth.shape[0]
    vmem = pl.BlockSpec(memory_space=pltpu.VMEM)
    return pl.pallas_call(
        fold_kernel,
        out_shape=(
            jax.ShapeDtypeStruct((3, 2, cells // SUB, SUB, LANES), jnp.float32),
            jax.ShapeDtypeStruct((SUB, LANES), jnp.float32),
        ),
        in_specs=[vmem, vmem, vmem],
        out_specs=(vmem, vmem),
        scratch_shapes=[pltpu.VMEM((3, 2, cells, LANES), jnp.float32)],
        compiler_params=pltpu.CompilerParams(vmem_limit_bytes=VMEM_LIMIT),
        cost_estimate=pl.CostEstimate(
            flops=CSTEPS * 70 * cells * cells, bytes_accessed=24 * cells * cells, transcendentals=0
        ),
        name="coast_fold",
    )(link, depth, flow)


def coast_kernel(
    wet, ghosts, folded, depth, flow, out, state, terms, after, parts, opening, tmp, done, sems
):
    rows = depth.shape[0] // SUB
    is_wet = jnp.max(wet[...]) > 0.0

    def copy_in(k, carry):
        for f in range(3):
            for p in range(2):
                state[f, p, 1 + k] = folded[f, p, k]
        return carry

    @pl.when(jnp.logical_not(is_wet))
    def _():
        copies = [
            pltpu.make_async_copy(depth, out.at[0], sems.at[0]),
            pltpu.make_async_copy(flow, out.at[1:], sems.at[1]),
        ]
        for copy in copies:
            copy.start()
        for copy in copies:
            copy.wait()

    @pl.when(is_wet)
    def _():
        lax.fori_loop(0, rows, copy_in, 0, unroll=4)
        values = jnp.sum(ghosts[...], axis=0)
        level = (ghost_level + values) * DEPTH_UNIT
        inflow = values * FLOW_UNIT
        h, mv = [
            [jnp.broadcast_to(v[i : i + 1], (SUB, LANES)) for i in range(at, at + 2)]
            for v, at in ((level, 0), (inflow, 2))
        ]
        ghost = [[h[p], jnp.zeros_like(h[p]), mv[p]] for p in range(2)]
        coast_steps(state, terms, after, parts, opening, rows, GROUP, CSTEPS, ghost)

        def write(f):
            return pltpu.make_async_copy(done.at[f], out.at[f], sems.at[f])

        def finish(f, carry):
            scale = jnp.where(f == 0, 1.0 / DEPTH_UNIT, 1.0 / FLOW_UNIT)

            def unfold(k, carry):
                both = join_columns(state[f, 0, 1 + k], state[f, 1, 1 + k])
                for p in range(2):
                    tmp[p, pl.ds(k, SUB, stride=rows), :] = both[p] * scale
                return carry

            def copy_out(i, carry):
                at = pl.ds(pl.multiple_of(i * TALL, TALL), TALL)
                for p in range(2):
                    done[f, at, HALVES[p]] = tmp[p, at]
                return carry

            lax.fori_loop(0, rows, unfold, 0, unroll=rows)
            lax.fori_loop(0, depth.shape[0] // TALL, copy_out, 0, unroll=2)
            write(f).start()
            return carry

        lax.fori_loop(0, 3, finish, 0)
        for f in range(3):
            write(f).wait()


def coast_run(wet, ghosts, folded, depth, flow):
    cells = depth.shape[0]
    vmem = pl.BlockSpec(memory_space=pltpu.VMEM)
    return pl.pallas_call(
        coast_kernel,
        out_shape=jax.ShapeDtypeStruct((3, cells, cells), jnp.float32),
        in_specs=[vmem] * 5,
        out_specs=pl.BlockSpec(memory_space=pltpu.HBM),
        scratch_shapes=[
            pltpu.VMEM((3, 2, 1 + cells // SUB, SUB, LANES), jnp.float32),
            pltpu.VMEM((2, 1 + GROUP, 5, SUB, LANES), jnp.float32),
            pltpu.VMEM((GROUP, 6, SUB, LANES), jnp.float32),
            pltpu.VMEM((GROUP, 6, SUB, LANES), jnp.float32),
            pltpu.VMEM((cells // SUB // GROUP, 2, 3, SUB, LANES), jnp.float32),
            pltpu.VMEM((2, cells, LANES), jnp.float32),
            pltpu.VMEM((3, cells, cells), jnp.float32),
            pltpu.SemaphoreType.DMA((3,)),
        ],
        compiler_params=pltpu.CompilerParams(vmem_limit_bytes=VMEM_LIMIT),
        cost_estimate=pl.CostEstimate(
            flops=CSTEPS * 70 * cells * cells, bytes_accessed=24 * cells * cells, transcendentals=0
        ),
        name="coast_steps",
    )(wet, ghosts, folded, depth, flow)


def basin_kernel(state, depth, pair_state, pair_depth, edge, out, eta, hu, hv, dep):
    rows, width = depth.shape
    total = rows + 2 * HALO
    chunks = width // LANES
    position = lax.axis_index("row")
    odd = position % 2
    north_inside = (position < lax.axis_size("row") - 1).astype(jnp.float32)
    pair_from = pl.multiple_of(odd * (rows - HALO), HALO)
    pair_at = pl.multiple_of((1 - odd) * (HALO + rows), HALO)
    edge_at = pl.multiple_of(odd * (HALO + rows), HALO)
    for ref, field, unit in ((eta, 0, 1.0), (hu, 1, 0.5), (hv, 2, 0.5), (dep, 3, 0.25)):
        own, pair = (depth, pair_depth) if field == 3 else (state.at[field], pair_state.at[field])
        for c in range(chunks):
            at = slice(c * LANES, (c + 1) * LANES)
            ref[c, HALO : HALO + rows] = own[:, at] * unit
            ref[c, pl.ds(pair_at, HALO)] = pair[pl.ds(pair_from, HALO), at] * unit
            ref[c, pl.ds(edge_at, HALO)] = edge[field, :, at] * unit
    apart = total // SUB
    lane = lane_ids()
    first, last = lane == 0, lane == LANES - 1
    kept = jnp.where(row_ids() * apart < HALO + rows, 1.0, north_inside)
    zero = jnp.zeros((SUB, LANES), jnp.float32)

    def load(ref, c):
        return [ref[c, pl.ds(k, SUB, stride=apart), :] for k in range(apart)]

    def store(ref, c, values):
        for k in range(apart):
            ref[c, pl.ds(k, SUB, stride=apart), :] = values[k]

    def step(_, carry):
        prev_west = [zero] * apart
        prev_eta, prev_east, prev_hu = None, None, None
        for c in range(chunks + 1):
            if c < chunks:
                u, v, d = load(hu, c), load(hv, c), load(dep, c)
                west = [pltpu.roll(x, 1, 1) for x in u]
                south = [pltpu.roll(v[-1], 1, 0)] + v[:-1]
                new = [
                    (e - ((x - jnp.where(first, p, w)) + (y - t))) * kept
                    for e, x, p, w, y, t in zip(load(eta, c), u, prev_west, west, v, south)
                ]
                store(eta, c, new)
                east = [pltpu.roll(x, LANES - 1, 1) for x in new]
                north = new[1:] + [pltpu.roll(new[0], SUB - 1, 0)]
                store(hv, c, [y - g * (n - x) for y, g, n, x in zip(v, d, north, new)])
            else:
                east = [zero] * apart
            if c > 0:
                d = load(dep, c - 1)
                store(
                    hu,
                    c - 1,
                    [
                        x - g * (jnp.where(last, e, p) - n)
                        for x, g, e, p, n in zip(prev_hu, d, east, prev_east, prev_eta)
                    ],
                )
            prev_west, prev_eta, prev_east, prev_hu = west, new, east, u
        return carry

    lax.fori_loop(0, BSTEPS, step, 0)
    for c in range(chunks):
        at = slice(c * LANES, (c + 1) * LANES)
        for f, (ref, unit) in enumerate(((eta, 1.0), (hu, 2.0), (hv, 2.0))):
            out[f, :, at] = ref[c, HALO : HALO + rows] * unit


def basin_run(state, depth, pair_state, pair_depth, edge):
    rows, width = depth.shape
    total = rows + 2 * HALO
    vmem = pl.BlockSpec(memory_space=pltpu.VMEM)
    return pl.pallas_call(
        basin_kernel,
        out_shape=jax.ShapeDtypeStruct((3, rows, width), jnp.float32),
        in_specs=[vmem] * 5,
        out_specs=vmem,
        scratch_shapes=[pltpu.VMEM((width // LANES, total, LANES), jnp.float32)] * 4,
        compiler_params=pltpu.CompilerParams(vmem_limit_bytes=VMEM_LIMIT),
        cost_estimate=pl.CostEstimate(
            flops=BSTEPS * 16 * total * width, bytes_accessed=4 * 11 * rows * width, transcendentals=0
        ),
        name="basin_steps",
    )(state, depth, pair_state, pair_depth, edge)


def strips_kernel(links, own, pair, ghosts, strips):
    rows, width = own.shape[1], own.shape[2]
    count = ghosts.shape[0]
    span = 2 * LANES
    position = lax.axis_index("row")
    tops = (position * rows, (position + 1 - 2 * (position % 2)) * rows)
    lane = lane_ids()
    weight = ((2 * lane + row_ids() % 2) % 16).astype(jnp.float32) / 16.0 + 0.5 / 16.0

    def piece(b, carry):
        col = links[b, 0, 1]
        start = jnp.clip(col // LANES, 0, width // LANES - 2) * LANES
        shift = lax.rem(span - (col - start), span)
        at = pl.ds(pl.multiple_of(start, LANES), span)
        for i, f in enumerate((0, 2)):
            chunk = None
            for source, top in zip((own, pair), tops):
                row = links[b, 0, 0] - top
                owned = jnp.logical_and(row >= 0, row < rows).astype(jnp.float32)
                part = source[f, pl.ds(jnp.clip(row, 0, rows - 1), 1), at] * owned
                chunk = part if chunk is None else chunk + part
            moved = pltpu.roll(chunk, shift, 1)[:, :LANES]
            strips[b, 2 * i : 2 * i + 2] = jnp.broadcast_to(moved, (2, LANES))
        values = strips[b]
        low, high = pick(values, lane // 8), pick(values, lane // 8 + 1)
        ghosts[b] = (1.0 - weight) * low + weight * high
        return carry

    strips[...] = jnp.zeros_like(strips)
    lax.fori_loop(0, count, piece, 0, unroll=8)


def make_strips(links, own, pair):
    count = links.shape[0]
    tiles = (count, SUB, LANES)
    vmem = pl.BlockSpec(memory_space=pltpu.VMEM)
    smem = pl.BlockSpec(memory_space=pltpu.SMEM)
    return pl.pallas_call(
        strips_kernel,
        out_shape=jax.ShapeDtypeStruct(tiles, jnp.float32),
        in_specs=[smem, vmem, vmem],
        out_specs=vmem,
        scratch_shapes=[pltpu.VMEM(tiles, jnp.float32)],
        compiler_params=pltpu.CompilerParams(vmem_limit_bytes=VMEM_LIMIT),
        cost_estimate=pl.CostEstimate(flops=2 * 10**10, bytes_accessed=own.size, transcendentals=0),
        name="strips",
    )(links, own, pair)


def local(basin_state, basin_depth, coast_depth, coast_flow, coast_link):
    devices = lax.axis_size("row")
    odd = lax.axis_index("row") % 2
    chips = list(range(devices // 2))[::-1]
    chips.insert(0, chips.pop(len(chips) - 1 - devices // 4))
    parity = [[2 * chip + p for chip in chips] for p in range(2)]
    sent = jnp.broadcast_to(coast_link, (devices // 2,) + coast_link.shape)
    sent, later_state = lax.optimization_barrier((sent, basin_state))
    start = odd * (basin_depth.shape[0] - HALO)
    edge = jnp.concatenate(
        [
            lax.dynamic_slice_in_dim(later_state, start, HALO, axis=1),
            lax.dynamic_slice_in_dim(basin_depth, start, HALO, axis=0)[None],
        ],
        axis=0,
    )
    sent, edge = lax.optimization_barrier((sent, edge))
    links = lax.all_to_all(sent, "row", 0, 0, axis_index_groups=parity, tiled=True)

    twins = [(i, i ^ 1) for i in range(devices)]
    pair_state, pair_depth = [lax.ppermute(a, "row", twins) for a in (basin_state, basin_depth)]
    across = [(i, i + 1) for i in range(1, devices - 1, 2)]
    edge = lax.ppermute(edge, "row", across + [(j, i) for i, j in across])

    depth, flow = coast_depth[0], coast_flow[0]
    folded, wet = coast_fold(coast_link, depth, flow)
    pair_state, folded = lax.optimization_barrier((pair_state, folded))
    ghosts = make_strips(links, basin_state, pair_state)
    basin_depth, ghosts = lax.optimization_barrier((basin_depth, ghosts))
    ghosts = lax.all_to_all(ghosts, "row", 0, 0, axis_index_groups=parity, tiled=True)
    basin_out = basin_run(basin_state, basin_depth, pair_state, pair_depth, edge)
    folded, basin_out = lax.optimization_barrier((folded, basin_out))
    coast_out = coast_run(wet, ghosts, folded, depth, flow)
    return (basin_out, coast_out[None])


def solution(mesh):
    in_specs = (
        P("scen", "row", None),
        P("row", "scen"),
        P("row", "scen", None),
        P("row", "scen", None, None),
        P("row", "scen"),
    )
    out_specs = (P("scen", "row", None), P("row", "scen", None, None))
    return jax.shard_map(local, mesh=mesh, in_specs=in_specs, out_specs=out_specs, check_vma=False)
```

```python
import functools

import jax
import jax.numpy as jnp
from jax import lax
from jax.experimental import pallas as pl
from jax.experimental.pallas import tpu as pltpu
from jax.sharding import PartitionSpec as P

BSTEPS = 8
CSTEPS = 10

depth_floor = 0.2
ghost_level = 2.0

RATE = 0.05
DEPTH_UNIT = RATE * RATE
FLOW_UNIT = RATE * RATE * RATE
TINY = 1e-30

HALO = BSTEPS
SUB = 8
LANES = 128


def lane_ids():
    return lax.broadcasted_iota(jnp.int32, (SUB, LANES), 1)


def row_ids():
    return lax.broadcasted_iota(jnp.int32, (SUB, LANES), 0)


def cell_terms(u):
    h, mu, mv = u
    r = pl.reciprocal(jnp.maximum(h, depth_floor * DEPTH_UNIT), approx=True)
    vx, vy = mu * r, mv * r
    hp = jnp.maximum(h, TINY)
    c = hp * lax.rsqrt(hp)
    p = (0.5 * h) * h
    cross = mu * vy
    return {
        "u": u,
        "fx": (mu, mu * vx + p, cross),
        "fy": (mv, cross, mv * vy + p),
        "sx": jnp.abs(vx) + c,
        "sy": jnp.abs(vy) + c,
    }


def y_face(above, below):
    a = jnp.maximum(above["sy"], below["sy"])
    return [
        a * (ub - ua) - (fa + fb)
        for ua, ub, fa, fb in zip(above["u"], below["u"], above["fy"], below["fy"])
    ]


def coast_steps(state, terms, after, parts, opening, rows, group, steps, ghost):
    lane, sub = lane_ids(), row_ids()
    first, last = lane == 0, lane == LANES - 1
    top, bottom = sub == 0, sub == SUB - 1
    zero = jnp.zeros((SUB, LANES), jnp.float32)
    left = functools.partial(pltpu.roll, shift=LANES - 1, axis=1)
    right = functools.partial(pltpu.roll, shift=1, axis=1)

    def load(view, k):
        return [[view[f, half, 1 + k] for f in range(3)] for half in range(2)]

    def store(view, k, both):
        for half in range(2):
            for f in range(3):
                view[f, half, 1 + k] = both[half][f]

    def store_above(tails):
        store(state, -1, [[jnp.where(top, g, pltpu.roll(t, 1, 0)) for g, t in zip(*pair)] for pair in zip(ghost, tails)])

    def y_terms_of(view, k):
        both = [cell_terms(u) for u in load(view, k)]
        for half, cell in enumerate(both):
            terms[half, 1 + k, 0] = cell["sy"]
            terms[half, 1 + k, 1] = cell["fy"][2]
            terms[half, 1 + k, 2] = cell["fx"][2]
        return both

    def terms_of(view, k):
        even, odd = y_terms_of(view, k)
        for half, cell in enumerate((even, odd)):
            terms[half, 1 + k, 3] = cell["sx"]
            terms[half, 1 + k, 4] = cell["fx"][1]
        moved = zip(even["u"] + [even["sx"]] + list(even["fx"][1:]), odd["u"] + [odd["sx"]] + list(odd["fx"][1:]))
        for q, (e, o) in enumerate(moved):
            after[k, q] = jnp.where(last, o, left(e))

    def x_faces(view, k):
        even, odd = load(view, k)
        following = [after[k, f] for f in range(3)]
        sx_e, sx_o, sx_n = terms[0, 1 + k, 3], terms[1, 1 + k, 3], after[k, 3]
        fx_e = [even[1], terms[0, 1 + k, 4], terms[0, 1 + k, 2]]
        fx_o = [odd[1], terms[1, 1 + k, 4], terms[1, 1 + k, 2]]
        fx_n = [following[1], after[k, 4], after[k, 5]]
        a_in, a_out = jnp.maximum(sx_e, sx_o), jnp.maximum(sx_o, sx_n)
        for f in range(3):
            g_in = a_in * (odd[f] - even[f]) - (fx_e[f] + fx_o[f])
            g_out = a_out * (following[f] - odd[f]) - (fx_o[f] + fx_n[f])
            g_back = jnp.where(first, -2.0 * fx_e[f], right(g_out))
            parts[k, f] = even[f] + (g_in - g_back)
            parts[k, 3 + f] = odd[f] + (g_out - g_in)

    def y_cells(view, k):
        return [
            {
                "u": u,
                "fy": [u[2], terms[half, 1 + k, 2], terms[half, 1 + k, 1]],
                "sy": terms[half, 1 + k, 0],
            }
            for half, u in enumerate(load(view, k))
        ]

    def trip(i, acc):
        view = state.at[:, :, pl.ds(i * group, 1 + group)]
        y_terms_of(view, -1)
        for k in range(group):
            terms_of(view, k)
        for k in range(group):
            x_faces(view, k)
        prev = y_cells(view, -1)
        for k in range(group):
            cur = y_cells(view, k)
            face = [y_face(a, b) for a, b in zip(prev, cur)]
            if k == 0:
                for half in range(2):
                    for f in range(3):
                        opening[i, half, f] = pltpu.roll(face[half][f], SUB - 1, 0)
            store(view, k - 1, [[x + g for x, g in zip(*pair)] for pair in zip(acc, face)])
            acc = [[parts[k, 3 * half + f] - face[half][f] for f in range(3)] for half in range(2)]
            prev = cur
        return acc

    def step(_, carry):
        acc = lax.fori_loop(0, rows // group, trip, [[zero] * 3 for _ in range(2)])
        tails = [
            [
                x + jnp.where(bottom, -2.0 * f, opening[0, half, i])
                for i, (x, f) in enumerate(zip(xs, cell["fy"]))
            ]
            for half, (xs, cell) in enumerate(
                zip(acc, y_cells(state.at[:, :, rows - group :], group - 1))
            )
        ]
        store(state, rows - 1, tails)
        store_above(tails)
        return carry

    store_above(load(state, rows - 1))
    lax.fori_loop(0, steps, step, 0)


GROUP = 8
UNITS = (DEPTH_UNIT, FLOW_UNIT, FLOW_UNIT)
VMEM_LIMIT = 12 * 1024 * 1024
HALF = LANES // 2


def pick(values, ids):
    return jnp.take_along_axis(values, ids, axis=1, mode="promise_in_bounds")


def split_columns(west, east):
    lane = lane_ids()
    low = lane < HALF
    twice = 2 * jnp.where(low, lane, lane - HALF)
    w = pick(west, jnp.where(low, twice, twice + 1))
    e = pick(east, jnp.where(low, twice + 1, twice))
    return jnp.where(low, w, e), pltpu.roll(jnp.where(low, e, w), HALF, 1)


def join_columns(even, odd):
    lane = lane_ids()
    low = lane < HALF
    odd = pltpu.roll(odd, HALF, 1)
    w, e = jnp.where(low, even, odd), jnp.where(low, odd, even)
    half, is_odd = lane // 2, lane % 2
    return pick(w, half + HALF * is_odd), pick(e, half + HALF * (1 - is_odd))


HALVES = (slice(0, LANES), slice(LANES, 2 * LANES))
TALL = 32


def fold_kernel(link, depth, flow, state, wet, tmp):
    rows = depth.shape[0] // SUB
    wet[...] = jnp.broadcast_to(link[:, 2:3], wet.shape).astype(jnp.float32)

    def copy_in(i, carry):
        at = pl.ds(pl.multiple_of(i * TALL, TALL), TALL)
        for f in range(3):
            raw = depth[at] if f == 0 else flow[f - 1, at]
            for p in range(2):
                tmp[f, p, at] = raw[:, HALVES[p]] * UNITS[f]
        return carry

    def fold_field(f, carry):
        def fold(k, carry):
            both = split_columns(*[tmp[f, p, pl.ds(k, SUB, stride=rows), :] for p in range(2)])
            for p in range(2):
                state[f, p, k] = both[p]
            return carry

        return lax.fori_loop(0, rows, fold, carry, unroll=rows)

    lax.fori_loop(0, depth.shape[0] // TALL, copy_in, 0)
    lax.fori_loop(0, 3, fold_field, 0)


def coast_fold(link, depth, flow):
    cells = depth.shape[0]
    vmem = pl.BlockSpec(memory_space=pltpu.VMEM)
    return pl.pallas_call(
        fold_kernel,
        out_shape=(
            jax.ShapeDtypeStruct((3, 2, cells // SUB, SUB, LANES), jnp.float32),
            jax.ShapeDtypeStruct((SUB, LANES), jnp.float32),
        ),
        in_specs=[vmem, vmem, vmem],
        out_specs=(vmem, vmem),
        scratch_shapes=[pltpu.VMEM((3, 2, cells, LANES), jnp.float32)],
        compiler_params=pltpu.CompilerParams(vmem_limit_bytes=VMEM_LIMIT),
        cost_estimate=pl.CostEstimate(
            flops=CSTEPS * 70 * cells * cells, bytes_accessed=24 * cells * cells, transcendentals=0
        ),
        name="coast_fold",
    )(link, depth, flow)


def coast_kernel(
    wet, ghosts, folded, depth, flow, out, state, terms, after, parts, opening, tmp, done, sems
):
    rows = depth.shape[0] // SUB
    is_wet = jnp.max(wet[...]) > 0.0

    def copy_in(k, carry):
        for f in range(3):
            for p in range(2):
                state[f, p, 1 + k] = folded[f, p, k]
        return carry

    @pl.when(jnp.logical_not(is_wet))
    def _():
        copies = [
            pltpu.make_async_copy(depth, out.at[0], sems.at[0]),
            pltpu.make_async_copy(flow, out.at[1:], sems.at[1]),
        ]
        for copy in copies:
            copy.start()
        for copy in copies:
            copy.wait()

    @pl.when(is_wet)
    def _():
        lax.fori_loop(0, rows, copy_in, 0, unroll=4)
        values = jnp.sum(ghosts[...], axis=0)
        level = (ghost_level + values) * DEPTH_UNIT
        inflow = values * FLOW_UNIT
        h, mv = [
            [jnp.broadcast_to(v[i : i + 1], (SUB, LANES)) for i in range(at, at + 2)]
            for v, at in ((level, 0), (inflow, 2))
        ]
        ghost = [[h[p], jnp.zeros_like(h[p]), mv[p]] for p in range(2)]
        coast_steps(state, terms, after, parts, opening, rows, GROUP, CSTEPS, ghost)

        def write(f):
            return pltpu.make_async_copy(done.at[f], out.at[f], sems.at[f])

        def finish(f, carry):
            scale = jnp.where(f == 0, 1.0 / DEPTH_UNIT, 1.0 / FLOW_UNIT)

            def unfold(k, carry):
                both = join_columns(state[f, 0, 1 + k], state[f, 1, 1 + k])
                for p in range(2):
                    tmp[p, pl.ds(k, SUB, stride=rows), :] = both[p] * scale
                return carry

            def copy_out(i, carry):
                at = pl.ds(pl.multiple_of(i * TALL, TALL), TALL)
                for p in range(2):
                    done[f, at, HALVES[p]] = tmp[p, at]
                return carry

            lax.fori_loop(0, rows, unfold, 0, unroll=rows)
            lax.fori_loop(0, depth.shape[0] // TALL, copy_out, 0, unroll=2)
            write(f).start()
            return carry

        lax.fori_loop(0, 3, finish, 0)
        for f in range(3):
            write(f).wait()


def coast_run(wet, ghosts, folded, depth, flow):
    cells = depth.shape[0]
    vmem = pl.BlockSpec(memory_space=pltpu.VMEM)
    return pl.pallas_call(
        coast_kernel,
        out_shape=jax.ShapeDtypeStruct((3, cells, cells), jnp.float32),
        in_specs=[vmem] * 5,
        out_specs=pl.BlockSpec(memory_space=pltpu.HBM),
        scratch_shapes=[
            pltpu.VMEM((3, 2, 1 + cells // SUB, SUB, LANES), jnp.float32),
            pltpu.VMEM((2, 1 + GROUP, 5, SUB, LANES), jnp.float32),
            pltpu.VMEM((GROUP, 6, SUB, LANES), jnp.float32),
            pltpu.VMEM((GROUP, 6, SUB, LANES), jnp.float32),
            pltpu.VMEM((cells // SUB // GROUP, 2, 3, SUB, LANES), jnp.float32),
            pltpu.VMEM((2, cells, LANES), jnp.float32),
            pltpu.VMEM((3, cells, cells), jnp.float32),
            pltpu.SemaphoreType.DMA((3,)),
        ],
        compiler_params=pltpu.CompilerParams(vmem_limit_bytes=VMEM_LIMIT),
        cost_estimate=pl.CostEstimate(
            flops=CSTEPS * 70 * cells * cells, bytes_accessed=24 * cells * cells, transcendentals=0
        ),
        name="coast_steps",
    )(wet, ghosts, folded, depth, flow)


def basin_kernel(state, depth, pair_state, pair_depth, edge, out, eta, hu, hv, dep):
    rows, width = depth.shape
    total = rows + 2 * HALO
    chunks = width // LANES
    position = lax.axis_index("row")
    odd = position % 2
    north_inside = (position < lax.axis_size("row") - 1).astype(jnp.float32)
    pair_from = pl.multiple_of(odd * (rows - HALO), HALO)
    pair_at = pl.multiple_of((1 - odd) * (HALO + rows), HALO)
    edge_at = pl.multiple_of(odd * (HALO + rows), HALO)
    for ref, field, unit in ((eta, 0, 1.0), (hu, 1, 0.5), (hv, 2, 0.5), (dep, 3, 0.25)):
        own, pair = (depth, pair_depth) if field == 3 else (state.at[field], pair_state.at[field])
        for c in range(chunks):
            at = slice(c * LANES, (c + 1) * LANES)
            ref[c, HALO : HALO + rows] = own[:, at] * unit
            ref[c, pl.ds(pair_at, HALO)] = pair[pl.ds(pair_from, HALO), at] * unit
            ref[c, pl.ds(edge_at, HALO)] = edge[field, :, at] * unit
    apart = total // SUB
    lane = lane_ids()
    first, last = lane == 0, lane == LANES - 1
    kept = jnp.where(row_ids() * apart < HALO + rows, 1.0, north_inside)
    zero = jnp.zeros((SUB, LANES), jnp.float32)

    def load(ref, c):
        return [ref[c, pl.ds(k, SUB, stride=apart), :] for k in range(apart)]

    def store(ref, c, values):
        for k in range(apart):
            ref[c, pl.ds(k, SUB, stride=apart), :] = values[k]

    def step(_, carry):
        prev_west = [zero] * apart
        prev_eta, prev_east, prev_hu = None, None, None
        for c in range(chunks + 1):
            if c < chunks:
                u, v, d = load(hu, c), load(hv, c), load(dep, c)
                west = [pltpu.roll(x, 1, 1) for x in u]
                south = [pltpu.roll(v[-1], 1, 0)] + v[:-1]
                new = [
                    (e - ((x - jnp.where(first, p, w)) + (y - t))) * kept
                    for e, x, p, w, y, t in zip(load(eta, c), u, prev_west, west, v, south)
                ]
                store(eta, c, new)
                east = [pltpu.roll(x, LANES - 1, 1) for x in new]
                north = new[1:] + [pltpu.roll(new[0], SUB - 1, 0)]
                store(hv, c, [y - g * (n - x) for y, g, n, x in zip(v, d, north, new)])
            else:
                east = [zero] * apart
            if c > 0:
                d = load(dep, c - 1)
                store(
                    hu,
                    c - 1,
                    [
                        x - g * (jnp.where(last, e, p) - n)
                        for x, g, e, p, n in zip(prev_hu, d, east, prev_east, prev_eta)
                    ],
                )
            prev_west, prev_eta, prev_east, prev_hu = west, new, east, u
        return carry

    lax.fori_loop(0, BSTEPS, step, 0)
    for c in range(chunks):
        at = slice(c * LANES, (c + 1) * LANES)
        for f, (ref, unit) in enumerate(((eta, 1.0), (hu, 2.0), (hv, 2.0))):
            out[f, :, at] = ref[c, HALO : HALO + rows] * unit


def basin_run(state, depth, pair_state, pair_depth, edge):
    rows, width = depth.shape
    total = rows + 2 * HALO
    vmem = pl.BlockSpec(memory_space=pltpu.VMEM)
    return pl.pallas_call(
        basin_kernel,
        out_shape=jax.ShapeDtypeStruct((3, rows, width), jnp.float32),
        in_specs=[vmem] * 5,
        out_specs=vmem,
        scratch_shapes=[pltpu.VMEM((width // LANES, total, LANES), jnp.float32)] * 4,
        compiler_params=pltpu.CompilerParams(vmem_limit_bytes=VMEM_LIMIT),
        cost_estimate=pl.CostEstimate(
            flops=BSTEPS * 16 * total * width, bytes_accessed=4 * 11 * rows * width, transcendentals=0
        ),
        name="basin_steps",
    )(state, depth, pair_state, pair_depth, edge)


def strips_kernel(links, own, pair, ghosts, strips):
    rows, width = own.shape[1], own.shape[2]
    count = ghosts.shape[0]
    span = 2 * LANES
    position = lax.axis_index("row")
    tops = (position * rows, (position + 1 - 2 * (position % 2)) * rows)
    lane = lane_ids()
    weight = ((2 * lane + row_ids() % 2) % 16).astype(jnp.float32) / 16.0 + 0.5 / 16.0

    def piece(b, carry):
        col = links[b, 0, 1]
        start = jnp.clip(col // LANES, 0, width // LANES - 2) * LANES
        shift = lax.rem(span - (col - start), span)
        at = pl.ds(pl.multiple_of(start, LANES), span)
        for i, f in enumerate((0, 2)):
            chunk = None
            for source, top in zip((own, pair), tops):
                row = links[b, 0, 0] - top
                owned = jnp.logical_and(row >= 0, row < rows).astype(jnp.float32)
                part = source[f, pl.ds(jnp.clip(row, 0, rows - 1), 1), at] * owned
                chunk = part if chunk is None else chunk + part
            moved = pltpu.roll(chunk, shift, 1)[:, :LANES]
            strips[b, 2 * i : 2 * i + 2] = jnp.broadcast_to(moved, (2, LANES))
        values = strips[b]
        low, high = pick(values, lane // 8), pick(values, lane // 8 + 1)
        ghosts[b] = (1.0 - weight) * low + weight * high
        return carry

    strips[...] = jnp.zeros_like(strips)
    lax.fori_loop(0, count, piece, 0, unroll=8)


def make_strips(links, own, pair):
    count = links.shape[0]
    tiles = (count, SUB, LANES)
    vmem = pl.BlockSpec(memory_space=pltpu.VMEM)
    smem = pl.BlockSpec(memory_space=pltpu.SMEM)
    return pl.pallas_call(
        strips_kernel,
        out_shape=jax.ShapeDtypeStruct(tiles, jnp.float32),
        in_specs=[smem, vmem, vmem],
        out_specs=vmem,
        scratch_shapes=[pltpu.VMEM(tiles, jnp.float32)],
        compiler_params=pltpu.CompilerParams(vmem_limit_bytes=VMEM_LIMIT),
        cost_estimate=pl.CostEstimate(flops=2 * 10**10, bytes_accessed=own.size, transcendentals=0),
        name="strips",
    )(links, own, pair)


def local(basin_state, basin_depth, coast_depth, coast_flow, coast_link):
    devices = lax.axis_size("row")
    odd = lax.axis_index("row") % 2
    chips = list(range(devices // 2))[::-1]
    chips.insert(0, chips.pop(len(chips) - 1 - devices // 4))
    parity = [[2 * chip + p for chip in chips] for p in range(2)]
    sent = jnp.broadcast_to(coast_link, (devices // 2,) + coast_link.shape)
    sent, later_state = lax.optimization_barrier((sent, basin_state))
    start = odd * (basin_depth.shape[0] - HALO)
    edge = jnp.concatenate(
        [
            lax.dynamic_slice_in_dim(later_state, start, HALO, axis=1),
            lax.dynamic_slice_in_dim(basin_depth, start, HALO, axis=0)[None],
        ],
        axis=0,
    )
    sent, edge = lax.optimization_barrier((sent, edge))
    links = lax.all_to_all(sent, "row", 0, 0, axis_index_groups=parity, tiled=True)

    twins = [(i, i ^ 1) for i in range(devices)]
    pair_state, pair_depth = [lax.ppermute(a, "row", twins) for a in (basin_state, basin_depth)]
    across = [(i, i + 1) for i in range(1, devices - 1, 2)]
    edge = lax.ppermute(edge, "row", across + [(j, i) for i, j in across])

    depth, flow = coast_depth[0], coast_flow[0]
    folded, wet = coast_fold(coast_link, depth, flow)
    pair_state, folded = lax.optimization_barrier((pair_state, folded))
    ghosts = make_strips(links, basin_state, pair_state)
    basin_depth, ghosts = lax.optimization_barrier((basin_depth, ghosts))
    ghosts = lax.all_to_all(ghosts, "row", 0, 0, axis_index_groups=parity, tiled=True)
    basin_out = basin_run(basin_state, basin_depth, pair_state, pair_depth, edge)
    folded, basin_out = lax.optimization_barrier((folded, basin_out))
    coast_out = coast_run(wet, ghosts, folded, depth, flow)
    return (basin_out, coast_out[None])


def solution(mesh):
    in_specs = (
        P("scen", "row", None),
        P("row", "scen"),
        P("row", "scen", None),
        P("row", "scen", None, None),
        P("row", "scen"),
    )
    out_specs = (P("scen", "row", None), P("row", "scen", None, None))
    return jax.shard_map(local, mesh=mesh, in_specs=in_specs, out_specs=out_specs, check_vma=False)
```

```python
import functools

import jax
import jax.numpy as jnp
from jax import lax
from jax.experimental import pallas as pl
from jax.experimental.pallas import tpu as pltpu
from jax.sharding import PartitionSpec as P

BSTEPS = 8
CSTEPS = 10

depth_floor = 0.2
ghost_level = 2.0

RATE = 0.05
DEPTH_UNIT = RATE * RATE
FLOW_UNIT = RATE * RATE * RATE
TINY = 1e-30

HALO = BSTEPS
SUB = 8
LANES = 128


def lane_ids():
    return lax.broadcasted_iota(jnp.int32, (SUB, LANES), 1)


def row_ids():
    return lax.broadcasted_iota(jnp.int32, (SUB, LANES), 0)


def cell_terms(u):
    h, mu, mv = u
    r = pl.reciprocal(jnp.maximum(h, depth_floor * DEPTH_UNIT), approx=True)
    vx, vy = mu * r, mv * r
    hp = jnp.maximum(h, TINY)
    c = hp * lax.rsqrt(hp)
    p = (0.5 * h) * h
    cross = mu * vy
    return {
        "u": u,
        "fx": (mu, mu * vx + p, cross),
        "fy": (mv, cross, mv * vy + p),
        "sx": jnp.abs(vx) + c,
        "sy": jnp.abs(vy) + c,
    }


def y_face(above, below):
    a = jnp.maximum(above["sy"], below["sy"])
    return [
        a * (ub - ua) - (fa + fb)
        for ua, ub, fa, fb in zip(above["u"], below["u"], above["fy"], below["fy"])
    ]


def coast_steps(state, terms, after, parts, opening, rows, group, steps, ghost):
    lane, sub = lane_ids(), row_ids()
    first, last = lane == 0, lane == LANES - 1
    top, bottom = sub == 0, sub == SUB - 1
    zero = jnp.zeros((SUB, LANES), jnp.float32)
    left = functools.partial(pltpu.roll, shift=LANES - 1, axis=1)
    right = functools.partial(pltpu.roll, shift=1, axis=1)

    def load(view, k):
        return [[view[f, half, 1 + k] for f in range(3)] for half in range(2)]

    def store(view, k, both):
        for half in range(2):
            for f in range(3):
                view[f, half, 1 + k] = both[half][f]

    def store_above(tails):
        store(state, -1, [[jnp.where(top, g, pltpu.roll(t, 1, 0)) for g, t in zip(*pair)] for pair in zip(ghost, tails)])

    def y_terms_of(view, k):
        both = [cell_terms(u) for u in load(view, k)]
        for half, cell in enumerate(both):
            terms[half, 1 + k, 0] = cell["sy"]
            terms[half, 1 + k, 1] = cell["fy"][2]
            terms[half, 1 + k, 2] = cell["fx"][2]
        return both

    def terms_of(view, k):
        even, odd = y_terms_of(view, k)
        for half, cell in enumerate((even, odd)):
            terms[half, 1 + k, 3] = cell["sx"]
            terms[half, 1 + k, 4] = cell["fx"][1]
        moved = zip(even["u"] + [even["sx"]] + list(even["fx"][1:]), odd["u"] + [odd["sx"]] + list(odd["fx"][1:]))
        for q, (e, o) in enumerate(moved):
            after[k, q] = jnp.where(last, o, left(e))

    def x_faces(view, k):
        even, odd = load(view, k)
        following = [after[k, f] for f in range(3)]
        sx_e, sx_o, sx_n = terms[0, 1 + k, 3], terms[1, 1 + k, 3], after[k, 3]
        fx_e = [even[1], terms[0, 1 + k, 4], terms[0, 1 + k, 2]]
        fx_o = [odd[1], terms[1, 1 + k, 4], terms[1, 1 + k, 2]]
        fx_n = [following[1], after[k, 4], after[k, 5]]
        a_in, a_out = jnp.maximum(sx_e, sx_o), jnp.maximum(sx_o, sx_n)
        for f in range(3):
            g_in = a_in * (odd[f] - even[f]) - (fx_e[f] + fx_o[f])
            g_out = a_out * (following[f] - odd[f]) - (fx_o[f] + fx_n[f])
            g_back = jnp.where(first, -2.0 * fx_e[f], right(g_out))
            parts[k, f] = even[f] + (g_in - g_back)
            parts[k, 3 + f] = odd[f] + (g_out - g_in)

    def y_cells(view, k):
        return [
            {
                "u": u,
                "fy": [u[2], terms[half, 1 + k, 2], terms[half, 1 + k, 1]],
                "sy": terms[half, 1 + k, 0],
            }
            for half, u in enumerate(load(view, k))
        ]

    def trip(i, acc):
        view = state.at[:, :, pl.ds(i * group, 1 + group)]
        y_terms_of(view, -1)
        for k in range(group):
            terms_of(view, k)
        for k in range(group):
            x_faces(view, k)
        prev = y_cells(view, -1)
        for k in range(group):
            cur = y_cells(view, k)
            face = [y_face(a, b) for a, b in zip(prev, cur)]
            if k == 0:
                for half in range(2):
                    for f in range(3):
                        opening[i, half, f] = pltpu.roll(face[half][f], SUB - 1, 0)
            store(view, k - 1, [[x + g for x, g in zip(*pair)] for pair in zip(acc, face)])
            acc = [[parts[k, 3 * half + f] - face[half][f] for f in range(3)] for half in range(2)]
            prev = cur
        return acc

    def step(_, carry):
        acc = lax.fori_loop(0, rows // group, trip, [[zero] * 3 for _ in range(2)])
        tails = [
            [
                x + jnp.where(bottom, -2.0 * f, opening[0, half, i])
                for i, (x, f) in enumerate(zip(xs, cell["fy"]))
            ]
            for half, (xs, cell) in enumerate(
                zip(acc, y_cells(state.at[:, :, rows - group :], group - 1))
            )
        ]
        store(state, rows - 1, tails)
        store_above(tails)
        return carry

    store_above(load(state, rows - 1))
    lax.fori_loop(0, steps, step, 0)


GROUP = 16
UNITS = (DEPTH_UNIT, FLOW_UNIT, FLOW_UNIT)
VMEM_LIMIT = 12 * 1024 * 1024
HALF = LANES // 2


def pick(values, ids):
    return jnp.take_along_axis(values, ids, axis=1, mode="promise_in_bounds")


def split_columns(west, east):
    lane = lane_ids()
    low = lane < HALF
    twice = 2 * jnp.where(low, lane, lane - HALF)
    w = pick(west, jnp.where(low, twice, twice + 1))
    e = pick(east, jnp.where(low, twice + 1, twice))
    return jnp.where(low, w, e), pltpu.roll(jnp.where(low, e, w), HALF, 1)


def join_columns(even, odd):
    lane = lane_ids()
    low = lane < HALF
    odd = pltpu.roll(odd, HALF, 1)
    w, e = jnp.where(low, even, odd), jnp.where(low, odd, even)
    half, is_odd = lane // 2, lane % 2
    return pick(w, half + HALF * is_odd), pick(e, half + HALF * (1 - is_odd))


HALVES = (slice(0, LANES), slice(LANES, 2 * LANES))
TALL = 32


def fold_kernel(link, depth, flow, state, wet, tmp):
    rows = depth.shape[0] // SUB
    wet[...] = jnp.broadcast_to(link[:, 2:3], wet.shape).astype(jnp.float32)

    def copy_in(i, carry):
        at = pl.ds(pl.multiple_of(i * TALL, TALL), TALL)
        for f in range(3):
            raw = depth[at] if f == 0 else flow[f - 1, at]
            for p in range(2):
                tmp[f, p, at] = raw[:, HALVES[p]] * UNITS[f]
        return carry

    def fold_field(f, carry):
        def fold(k, carry):
            both = split_columns(*[tmp[f, p, pl.ds(k, SUB, stride=rows), :] for p in range(2)])
            for p in range(2):
                state[f, p, k] = both[p]
            return carry

        return lax.fori_loop(0, rows, fold, carry, unroll=rows)

    lax.fori_loop(0, depth.shape[0] // TALL, copy_in, 0)
    lax.fori_loop(0, 3, fold_field, 0)


def coast_fold(link, depth, flow):
    cells = depth.shape[0]
    vmem = pl.BlockSpec(memory_space=pltpu.VMEM)
    return pl.pallas_call(
        fold_kernel,
        out_shape=(
            jax.ShapeDtypeStruct((3, 2, cells // SUB, SUB, LANES), jnp.float32),
            jax.ShapeDtypeStruct((SUB, LANES), jnp.float32),
        ),
        in_specs=[vmem, vmem, vmem],
        out_specs=(vmem, vmem),
        scratch_shapes=[pltpu.VMEM((3, 2, cells, LANES), jnp.float32)],
        compiler_params=pltpu.CompilerParams(vmem_limit_bytes=VMEM_LIMIT),
        cost_estimate=pl.CostEstimate(
            flops=CSTEPS * 70 * cells * cells, bytes_accessed=24 * cells * cells, transcendentals=0
        ),
        name="coast_fold",
    )(link, depth, flow)


def coast_kernel(
    wet, ghosts, folded, depth, flow, out, state, terms, after, parts, opening, tmp, done, sems
):
    rows = depth.shape[0] // SUB
    is_wet = jnp.max(wet[...]) > 0.0

    def copy_in(k, carry):
        for f in range(3):
            for p in range(2):
                state[f, p, 1 + k] = folded[f, p, k]
        return carry

    @pl.when(jnp.logical_not(is_wet))
    def _():
        copies = [
            pltpu.make_async_copy(depth, out.at[0], sems.at[0]),
            pltpu.make_async_copy(flow, out.at[1:], sems.at[1]),
        ]
        for copy in copies:
            copy.start()
        for copy in copies:
            copy.wait()

    @pl.when(is_wet)
    def _():
        lax.fori_loop(0, rows, copy_in, 0, unroll=4)
        values = jnp.sum(ghosts[...], axis=0)
        level = (ghost_level + values) * DEPTH_UNIT
        inflow = values * FLOW_UNIT
        h, mv = [
            [jnp.broadcast_to(v[i : i + 1], (SUB, LANES)) for i in range(at, at + 2)]
            for v, at in ((level, 0), (inflow, 2))
        ]
        ghost = [[h[p], jnp.zeros_like(h[p]), mv[p]] for p in range(2)]
        coast_steps(state, terms, after, parts, opening, rows, GROUP, CSTEPS, ghost)

        def write(f):
            return pltpu.make_async_copy(done.at[f], out.at[f], sems.at[f])

        def finish(f, carry):
            scale = jnp.where(f == 0, 1.0 / DEPTH_UNIT, 1.0 / FLOW_UNIT)

            def unfold(k, carry):
                both = join_columns(state[f, 0, 1 + k], state[f, 1, 1 + k])
                for p in range(2):
                    tmp[p, pl.ds(k, SUB, stride=rows), :] = both[p] * scale
                return carry

            def copy_out(i, carry):
                at = pl.ds(pl.multiple_of(i * TALL, TALL), TALL)
                for p in range(2):
                    done[f, at, HALVES[p]] = tmp[p, at]
                return carry

            lax.fori_loop(0, rows, unfold, 0, unroll=rows)
            lax.fori_loop(0, depth.shape[0] // TALL, copy_out, 0, unroll=2)
            write(f).start()
            return carry

        lax.fori_loop(0, 3, finish, 0)
        for f in range(3):
            write(f).wait()


def coast_run(wet, ghosts, folded, depth, flow):
    cells = depth.shape[0]
    vmem = pl.BlockSpec(memory_space=pltpu.VMEM)
    return pl.pallas_call(
        coast_kernel,
        out_shape=jax.ShapeDtypeStruct((3, cells, cells), jnp.float32),
        in_specs=[vmem] * 5,
        out_specs=pl.BlockSpec(memory_space=pltpu.HBM),
        scratch_shapes=[
            pltpu.VMEM((3, 2, 1 + cells // SUB, SUB, LANES), jnp.float32),
            pltpu.VMEM((2, 1 + GROUP, 5, SUB, LANES), jnp.float32),
            pltpu.VMEM((GROUP, 6, SUB, LANES), jnp.float32),
            pltpu.VMEM((GROUP, 6, SUB, LANES), jnp.float32),
            pltpu.VMEM((cells // SUB // GROUP, 2, 3, SUB, LANES), jnp.float32),
            pltpu.VMEM((2, cells, LANES), jnp.float32),
            pltpu.VMEM((3, cells, cells), jnp.float32),
            pltpu.SemaphoreType.DMA((3,)),
        ],
        compiler_params=pltpu.CompilerParams(vmem_limit_bytes=VMEM_LIMIT),
        cost_estimate=pl.CostEstimate(
            flops=CSTEPS * 70 * cells * cells, bytes_accessed=24 * cells * cells, transcendentals=0
        ),
        name="coast_steps",
    )(wet, ghosts, folded, depth, flow)


def basin_kernel(state, depth, pair_state, pair_depth, edge, out, eta, hu, hv, dep):
    rows, width = depth.shape
    total = rows + 2 * HALO
    chunks = width // LANES
    position = lax.axis_index("row")
    odd = position % 2
    north_inside = (position < lax.axis_size("row") - 1).astype(jnp.float32)
    pair_from = pl.multiple_of(odd * (rows - HALO), HALO)
    pair_at = pl.multiple_of((1 - odd) * (HALO + rows), HALO)
    edge_at = pl.multiple_of(odd * (HALO + rows), HALO)
    for ref, field, unit in ((eta, 0, 1.0), (hu, 1, 0.5), (hv, 2, 0.5), (dep, 3, 0.25)):
        own, pair = (depth, pair_depth) if field == 3 else (state.at[field], pair_state.at[field])
        for c in range(chunks):
            at = slice(c * LANES, (c + 1) * LANES)
            ref[c, HALO : HALO + rows] = own[:, at] * unit
            ref[c, pl.ds(pair_at, HALO)] = pair[pl.ds(pair_from, HALO), at] * unit
            ref[c, pl.ds(edge_at, HALO)] = edge[field, :, at] * unit
    apart = total // SUB
    lane = lane_ids()
    first, last = lane == 0, lane == LANES - 1
    kept = jnp.where(row_ids() * apart < HALO + rows, 1.0, north_inside)
    zero = jnp.zeros((SUB, LANES), jnp.float32)

    def load(ref, c):
        return [ref[c, pl.ds(k, SUB, stride=apart), :] for k in range(apart)]

    def store(ref, c, values):
        for k in range(apart):
            ref[c, pl.ds(k, SUB, stride=apart), :] = values[k]

    def step(_, carry):
        prev_west = [zero] * apart
        prev_eta, prev_east, prev_hu = None, None, None
        for c in range(chunks + 1):
            if c < chunks:
                u, v, d = load(hu, c), load(hv, c), load(dep, c)
                west = [pltpu.roll(x, 1, 1) for x in u]
                south = [pltpu.roll(v[-1], 1, 0)] + v[:-1]
                new = [
                    (e - ((x - jnp.where(first, p, w)) + (y - t))) * kept
                    for e, x, p, w, y, t in zip(load(eta, c), u, prev_west, west, v, south)
                ]
                store(eta, c, new)
                east = [pltpu.roll(x, LANES - 1, 1) for x in new]
                north = new[1:] + [pltpu.roll(new[0], SUB - 1, 0)]
                store(hv, c, [y - g * (n - x) for y, g, n, x in zip(v, d, north, new)])
            else:
                east = [zero] * apart
            if c > 0:
                d = load(dep, c - 1)
                store(
                    hu,
                    c - 1,
                    [
                        x - g * (jnp.where(last, e, p) - n)
                        for x, g, e, p, n in zip(prev_hu, d, east, prev_east, prev_eta)
                    ],
                )
            prev_west, prev_eta, prev_east, prev_hu = west, new, east, u
        return carry

    lax.fori_loop(0, BSTEPS, step, 0)
    for c in range(chunks):
        at = slice(c * LANES, (c + 1) * LANES)
        for f, (ref, unit) in enumerate(((eta, 1.0), (hu, 2.0), (hv, 2.0))):
            out[f, :, at] = ref[c, HALO : HALO + rows] * unit


def basin_run(state, depth, pair_state, pair_depth, edge):
    rows, width = depth.shape
    total = rows + 2 * HALO
    vmem = pl.BlockSpec(memory_space=pltpu.VMEM)
    return pl.pallas_call(
        basin_kernel,
        out_shape=jax.ShapeDtypeStruct((3, rows, width), jnp.float32),
        in_specs=[vmem] * 5,
        out_specs=vmem,
        scratch_shapes=[pltpu.VMEM((width // LANES, total, LANES), jnp.float32)] * 4,
        compiler_params=pltpu.CompilerParams(vmem_limit_bytes=VMEM_LIMIT),
        cost_estimate=pl.CostEstimate(
            flops=BSTEPS * 16 * total * width, bytes_accessed=4 * 11 * rows * width, transcendentals=0
        ),
        name="basin_steps",
    )(state, depth, pair_state, pair_depth, edge)


def strips_kernel(links, own, pair, ghosts, strips):
    rows, width = own.shape[1], own.shape[2]
    count = ghosts.shape[0]
    span = 2 * LANES
    position = lax.axis_index("row")
    tops = (position * rows, (position + 1 - 2 * (position % 2)) * rows)
    lane = lane_ids()
    weight = ((2 * lane + row_ids() % 2) % 16).astype(jnp.float32) / 16.0 + 0.5 / 16.0

    def piece(b, carry):
        col = links[b, 0, 1]
        start = jnp.clip(col // LANES, 0, width // LANES - 2) * LANES
        shift = lax.rem(span - (col - start), span)
        at = pl.ds(pl.multiple_of(start, LANES), span)
        for i, f in enumerate((0, 2)):
            chunk = None
            for source, top in zip((own, pair), tops):
                row = links[b, 0, 0] - top
                owned = jnp.logical_and(row >= 0, row < rows).astype(jnp.float32)
                part = source[f, pl.ds(jnp.clip(row, 0, rows - 1), 1), at] * owned
                chunk = part if chunk is None else chunk + part
            moved = pltpu.roll(chunk, shift, 1)[:, :LANES]
            strips[b, 2 * i : 2 * i + 2] = jnp.broadcast_to(moved, (2, LANES))
        values = strips[b]
        low, high = pick(values, lane // 8), pick(values, lane // 8 + 1)
        ghosts[b] = (1.0 - weight) * low + weight * high
        return carry

    strips[...] = jnp.zeros_like(strips)
    lax.fori_loop(0, count, piece, 0, unroll=8)


def make_strips(links, own, pair):
    count = links.shape[0]
    tiles = (count, SUB, LANES)
    vmem = pl.BlockSpec(memory_space=pltpu.VMEM)
    smem = pl.BlockSpec(memory_space=pltpu.SMEM)
    return pl.pallas_call(
        strips_kernel,
        out_shape=jax.ShapeDtypeStruct(tiles, jnp.float32),
        in_specs=[smem, vmem, vmem],
        out_specs=vmem,
        scratch_shapes=[pltpu.VMEM(tiles, jnp.float32)],
        compiler_params=pltpu.CompilerParams(vmem_limit_bytes=VMEM_LIMIT),
        cost_estimate=pl.CostEstimate(flops=2 * 10**10, bytes_accessed=own.size, transcendentals=0),
        name="strips",
    )(links, own, pair)


def local(basin_state, basin_depth, coast_depth, coast_flow, coast_link):
    devices = lax.axis_size("row")
    odd = lax.axis_index("row") % 2
    chips = list(range(devices // 2))[::-1]
    chips.insert(0, chips.pop(len(chips) - 1 - devices // 4))
    parity = [[2 * chip + p for chip in chips] for p in range(2)]
    sent = jnp.broadcast_to(coast_link, (devices // 2,) + coast_link.shape)
    sent, later_state = lax.optimization_barrier((sent, basin_state))
    start = odd * (basin_depth.shape[0] - HALO)
    edge = jnp.concatenate(
        [
            lax.dynamic_slice_in_dim(later_state, start, HALO, axis=1),
            lax.dynamic_slice_in_dim(basin_depth, start, HALO, axis=0)[None],
        ],
        axis=0,
    )
    sent, edge = lax.optimization_barrier((sent, edge))
    links = lax.all_to_all(sent, "row", 0, 0, axis_index_groups=parity, tiled=True)

    twins = [(i, i ^ 1) for i in range(devices)]
    pair_state, pair_depth = [lax.ppermute(a, "row", twins) for a in (basin_state, basin_depth)]
    across = [(i, i + 1) for i in range(1, devices - 1, 2)]
    edge = lax.ppermute(edge, "row", across + [(j, i) for i, j in across])

    depth, flow = coast_depth[0], coast_flow[0]
    folded, wet = coast_fold(coast_link, depth, flow)
    pair_state, folded = lax.optimization_barrier((pair_state, folded))
    ghosts = make_strips(links, basin_state, pair_state)
    basin_depth, ghosts = lax.optimization_barrier((basin_depth, ghosts))
    ghosts = lax.all_to_all(ghosts, "row", 0, 0, axis_index_groups=parity, tiled=True)
    basin_out = basin_run(basin_state, basin_depth, pair_state, pair_depth, edge)
    folded, basin_out = lax.optimization_barrier((folded, basin_out))
    coast_out = coast_run(wet, ghosts, folded, depth, flow)
    return (basin_out, coast_out[None])


def solution(mesh):
    in_specs = (
        P("scen", "row", None),
        P("row", "scen"),
        P("row", "scen", None),
        P("row", "scen", None, None),
        P("row", "scen"),
    )
    out_specs = (P("scen", "row", None), P("row", "scen", None, None))
    return jax.shard_map(local, mesh=mesh, in_specs=in_specs, out_specs=out_specs, check_vma=False)
```

```python
import functools

import jax
import jax.numpy as jnp
from jax import lax
from jax.experimental import pallas as pl
from jax.experimental.pallas import tpu as pltpu
from jax.sharding import PartitionSpec as P

BSTEPS = 8
CSTEPS = 10

depth_floor = 0.2
ghost_level = 2.0

RATE = 0.05
DEPTH_UNIT = RATE * RATE
FLOW_UNIT = RATE * RATE * RATE
TINY = 1e-30

HALO = BSTEPS
SUB = 8
LANES = 128


def lane_ids():
    return lax.broadcasted_iota(jnp.int32, (SUB, LANES), 1)


def row_ids():
    return lax.broadcasted_iota(jnp.int32, (SUB, LANES), 0)


def cell_terms(u):
    h, mu, mv = u
    r = pl.reciprocal(jnp.maximum(h, depth_floor * DEPTH_UNIT), approx=True)
    vx, vy = mu * r, mv * r
    hp = jnp.maximum(h, TINY)
    c = hp * lax.rsqrt(hp)
    p = (0.5 * h) * h
    cross = mu * vy
    return {
        "u": u,
        "fx": (mu, mu * vx + p, cross),
        "fy": (mv, cross, mv * vy + p),
        "sx": jnp.abs(vx) + c,
        "sy": jnp.abs(vy) + c,
    }


def y_face(above, below):
    a = jnp.maximum(above["sy"], below["sy"])
    return [
        a * (ub - ua) - (fa + fb)
        for ua, ub, fa, fb in zip(above["u"], below["u"], above["fy"], below["fy"])
    ]


def coast_steps(state, terms, after, parts, opening, rows, group, steps, ghost):
    lane, sub = lane_ids(), row_ids()
    first, last = lane == 0, lane == LANES - 1
    top, bottom = sub == 0, sub == SUB - 1
    zero = jnp.zeros((SUB, LANES), jnp.float32)
    left = functools.partial(pltpu.roll, shift=LANES - 1, axis=1)
    right = functools.partial(pltpu.roll, shift=1, axis=1)

    def load(view, k):
        return [[view[f, half, 1 + k] for f in range(3)] for half in range(2)]

    def store(view, k, both):
        for half in range(2):
            for f in range(3):
                view[f, half, 1 + k] = both[half][f]

    def store_above(tails):
        store(state, -1, [[jnp.where(top, g, pltpu.roll(t, 1, 0)) for g, t in zip(*pair)] for pair in zip(ghost, tails)])

    def y_terms_of(view, k):
        both = [cell_terms(u) for u in load(view, k)]
        for half, cell in enumerate(both):
            terms[half, 1 + k, 0] = cell["sy"]
            terms[half, 1 + k, 1] = cell["fy"][2]
            terms[half, 1 + k, 2] = cell["fx"][2]
        return both

    def terms_of(view, k):
        even, odd = y_terms_of(view, k)
        for half, cell in enumerate((even, odd)):
            terms[half, 1 + k, 3] = cell["sx"]
            terms[half, 1 + k, 4] = cell["fx"][1]
        moved = zip(even["u"] + [even["sx"]] + list(even["fx"][1:]), odd["u"] + [odd["sx"]] + list(odd["fx"][1:]))
        for q, (e, o) in enumerate(moved):
            after[k, q] = jnp.where(last, o, left(e))

    def x_faces(view, k):
        even, odd = load(view, k)
        following = [after[k, f] for f in range(3)]
        sx_e, sx_o, sx_n = terms[0, 1 + k, 3], terms[1, 1 + k, 3], after[k, 3]
        fx_e = [even[1], terms[0, 1 + k, 4], terms[0, 1 + k, 2]]
        fx_o = [odd[1], terms[1, 1 + k, 4], terms[1, 1 + k, 2]]
        fx_n = [following[1], after[k, 4], after[k, 5]]
        a_in, a_out = jnp.maximum(sx_e, sx_o), jnp.maximum(sx_o, sx_n)
        for f in range(3):
            g_in = a_in * (odd[f] - even[f]) - (fx_e[f] + fx_o[f])
            g_out = a_out * (following[f] - odd[f]) - (fx_o[f] + fx_n[f])
            g_back = jnp.where(first, -2.0 * fx_e[f], right(g_out))
            parts[k, f] = even[f] + (g_in - g_back)
            parts[k, 3 + f] = odd[f] + (g_out - g_in)

    def y_cells(view, k):
        return [
            {
                "u": u,
                "fy": [u[2], terms[half, 1 + k, 2], terms[half, 1 + k, 1]],
                "sy": terms[half, 1 + k, 0],
            }
            for half, u in enumerate(load(view, k))
        ]

    def trip(i, acc):
        view = state.at[:, :, pl.ds(i * group, 1 + group)]
        y_terms_of(view, -1)
        for k in range(group):
            terms_of(view, k)
        for k in range(group):
            x_faces(view, k)
        prev = y_cells(view, -1)
        for k in range(group):
            cur = y_cells(view, k)
            face = [y_face(a, b) for a, b in zip(prev, cur)]
            if k == 0:
                for half in range(2):
                    for f in range(3):
                        opening[i, half, f] = pltpu.roll(face[half][f], SUB - 1, 0)
            store(view, k - 1, [[x + g for x, g in zip(*pair)] for pair in zip(acc, face)])
            acc = [[parts[k, 3 * half + f] - face[half][f] for f in range(3)] for half in range(2)]
            prev = cur
        return acc

    def step(_, carry):
        acc = lax.fori_loop(0, rows // group, trip, [[zero] * 3 for _ in range(2)])
        tails = [
            [
                x + jnp.where(bottom, -2.0 * f, opening[0, half, i])
                for i, (x, f) in enumerate(zip(xs, cell["fy"]))
            ]
            for half, (xs, cell) in enumerate(
                zip(acc, y_cells(state.at[:, :, rows - group :], group - 1))
            )
        ]
        store(state, rows - 1, tails)
        store_above(tails)
        return carry

    store_above(load(state, rows - 1))
    lax.fori_loop(0, steps, step, 0)


GROUP = 16
UNITS = (DEPTH_UNIT, FLOW_UNIT, FLOW_UNIT)
VMEM_LIMIT = 12 * 1024 * 1024
HALF = LANES // 2


def pick(values, ids):
    return jnp.take_along_axis(values, ids, axis=1, mode="promise_in_bounds")


def split_columns(west, east):
    lane = lane_ids()
    low = lane < HALF
    twice = 2 * jnp.where(low, lane, lane - HALF)
    w = pick(west, jnp.where(low, twice, twice + 1))
    e = pick(east, jnp.where(low, twice + 1, twice))
    return jnp.where(low, w, e), pltpu.roll(jnp.where(low, e, w), HALF, 1)


def join_columns(even, odd):
    lane = lane_ids()
    low = lane < HALF
    odd = pltpu.roll(odd, HALF, 1)
    w, e = jnp.where(low, even, odd), jnp.where(low, odd, even)
    half, is_odd = lane // 2, lane % 2
    return pick(w, half + HALF * is_odd), pick(e, half + HALF * (1 - is_odd))


HALVES = (slice(0, LANES), slice(LANES, 2 * LANES))
TALL = 32


def fold_kernel(link, depth, flow, state, wet, tmp):
    rows = depth.shape[0] // SUB
    wet[...] = jnp.broadcast_to(link[:, 2:3], wet.shape).astype(jnp.float32)

    def copy_in(i, carry):
        at = pl.ds(pl.multiple_of(i * TALL, TALL), TALL)
        for f in range(3):
            raw = depth[at] if f == 0 else flow[f - 1, at]
            for p in range(2):
                tmp[f, p, at] = raw[:, HALVES[p]] * UNITS[f]
        return carry

    def fold_field(f, carry):
        def fold(k, carry):
            both = split_columns(*[tmp[f, p, pl.ds(k, SUB, stride=rows), :] for p in range(2)])
            for p in range(2):
                state[f, p, k] = both[p]
            return carry

        return lax.fori_loop(0, rows, fold, carry, unroll=rows)

    lax.fori_loop(0, depth.shape[0] // TALL, copy_in, 0)
    lax.fori_loop(0, 3, fold_field, 0)


def coast_fold(link, depth, flow):
    cells = depth.shape[0]
    vmem = pl.BlockSpec(memory_space=pltpu.VMEM)
    return pl.pallas_call(
        fold_kernel,
        out_shape=(
            jax.ShapeDtypeStruct((3, 2, cells // SUB, SUB, LANES), jnp.float32),
            jax.ShapeDtypeStruct((SUB, LANES), jnp.float32),
        ),
        in_specs=[vmem, vmem, vmem],
        out_specs=(vmem, vmem),
        scratch_shapes=[pltpu.VMEM((3, 2, cells, LANES), jnp.float32)],
        compiler_params=pltpu.CompilerParams(vmem_limit_bytes=VMEM_LIMIT),
        cost_estimate=pl.CostEstimate(
            flops=CSTEPS * 70 * cells * cells, bytes_accessed=24 * cells * cells, transcendentals=0
        ),
        name="coast_fold",
    )(link, depth, flow)


def coast_kernel(
    wet, ghosts, folded, depth, flow, out, state, terms, after, parts, opening, tmp, done, sems
):
    rows = depth.shape[0] // SUB
    is_wet = jnp.max(wet[...]) > 0.0

    def copy_in(k, carry):
        for f in range(3):
            for p in range(2):
                state[f, p, 1 + k] = folded[f, p, k]
        return carry

    @pl.when(jnp.logical_not(is_wet))
    def _():
        copies = [
            pltpu.make_async_copy(depth, out.at[0], sems.at[0]),
            pltpu.make_async_copy(flow, out.at[1:], sems.at[1]),
        ]
        for copy in copies:
            copy.start()
        for copy in copies:
            copy.wait()

    @pl.when(is_wet)
    def _():
        lax.fori_loop(0, rows, copy_in, 0, unroll=4)
        values = jnp.sum(ghosts[...], axis=0)
        level = (ghost_level + values) * DEPTH_UNIT
        inflow = values * FLOW_UNIT
        h, mv = [
            [jnp.broadcast_to(v[i : i + 1], (SUB, LANES)) for i in range(at, at + 2)]
            for v, at in ((level, 0), (inflow, 2))
        ]
        ghost = [[h[p], jnp.zeros_like(h[p]), mv[p]] for p in range(2)]
        coast_steps(state, terms, after, parts, opening, rows, GROUP, CSTEPS, ghost)

        def write(f):
            return pltpu.make_async_copy(done.at[f], out.at[f], sems.at[f])

        def finish(f, carry):
            scale = jnp.where(f == 0, 1.0 / DEPTH_UNIT, 1.0 / FLOW_UNIT)

            def unfold(k, carry):
                both = join_columns(state[f, 0, 1 + k], state[f, 1, 1 + k])
                for p in range(2):
                    tmp[p, pl.ds(k, SUB, stride=rows), :] = both[p] * scale
                return carry

            def copy_out(i, carry):
                at = pl.ds(pl.multiple_of(i * TALL, TALL), TALL)
                for p in range(2):
                    done[f, at, HALVES[p]] = tmp[p, at]
                return carry

            lax.fori_loop(0, rows, unfold, 0, unroll=rows)
            lax.fori_loop(0, depth.shape[0] // TALL, copy_out, 0, unroll=2)
            write(f).start()
            return carry

        lax.fori_loop(0, 3, finish, 0)
        for f in range(3):
            write(f).wait()


def coast_run(wet, ghosts, folded, depth, flow):
    cells = depth.shape[0]
    vmem = pl.BlockSpec(memory_space=pltpu.VMEM)
    return pl.pallas_call(
        coast_kernel,
        out_shape=jax.ShapeDtypeStruct((3, cells, cells), jnp.float32),
        in_specs=[vmem] * 5,
        out_specs=pl.BlockSpec(memory_space=pltpu.HBM),
        scratch_shapes=[
            pltpu.VMEM((3, 2, 1 + cells // SUB, SUB, LANES), jnp.float32),
            pltpu.VMEM((2, 1 + GROUP, 5, SUB, LANES), jnp.float32),
            pltpu.VMEM((GROUP, 6, SUB, LANES), jnp.float32),
            pltpu.VMEM((GROUP, 6, SUB, LANES), jnp.float32),
            pltpu.VMEM((cells // SUB // GROUP, 2, 3, SUB, LANES), jnp.float32),
            pltpu.VMEM((2, cells, LANES), jnp.float32),
            pltpu.VMEM((3, cells, cells), jnp.float32),
            pltpu.SemaphoreType.DMA((3,)),
        ],
        compiler_params=pltpu.CompilerParams(vmem_limit_bytes=VMEM_LIMIT),
        cost_estimate=pl.CostEstimate(
            flops=CSTEPS * 70 * cells * cells, bytes_accessed=24 * cells * cells, transcendentals=0
        ),
        name="coast_steps",
    )(wet, ghosts, folded, depth, flow)


def basin_kernel(state, depth, pair_state, pair_depth, edge, out, eta, hu, hv, dep):
    rows, width = depth.shape
    total = rows + 2 * HALO
    chunks = width // LANES
    position = lax.axis_index("row")
    odd = position % 2
    north_inside = (position < lax.axis_size("row") - 1).astype(jnp.float32)
    pair_from = pl.multiple_of(odd * (rows - HALO), HALO)
    pair_at = pl.multiple_of((1 - odd) * (HALO + rows), HALO)
    edge_at = pl.multiple_of(odd * (HALO + rows), HALO)
    for ref, field, unit in ((eta, 0, 1.0), (hu, 1, 0.5), (hv, 2, 0.5), (dep, 3, 0.25)):
        own, pair = (depth, pair_depth) if field == 3 else (state.at[field], pair_state.at[field])
        for c in range(chunks):
            at = slice(c * LANES, (c + 1) * LANES)
            ref[c, HALO : HALO + rows] = own[:, at] * unit
            ref[c, pl.ds(pair_at, HALO)] = pair[pl.ds(pair_from, HALO), at] * unit
            ref[c, pl.ds(edge_at, HALO)] = edge[field, :, at] * unit
    apart = total // SUB
    lane = lane_ids()
    first, last = lane == 0, lane == LANES - 1
    kept = jnp.where(row_ids() * apart < HALO + rows, 1.0, north_inside)
    zero = jnp.zeros((SUB, LANES), jnp.float32)

    def load(ref, c):
        return [ref[c, pl.ds(k, SUB, stride=apart), :] for k in range(apart)]

    def store(ref, c, values):
        for k in range(apart):
            ref[c, pl.ds(k, SUB, stride=apart), :] = values[k]

    def step(_, carry):
        prev_west = [zero] * apart
        prev_eta, prev_east, prev_hu = None, None, None
        for c in range(chunks + 1):
            if c < chunks:
                u, v, d = load(hu, c), load(hv, c), load(dep, c)
                west = [pltpu.roll(x, 1, 1) for x in u]
                south = [pltpu.roll(v[-1], 1, 0)] + v[:-1]
                new = [
                    (e - ((x - jnp.where(first, p, w)) + (y - t))) * kept
                    for e, x, p, w, y, t in zip(load(eta, c), u, prev_west, west, v, south)
                ]
                store(eta, c, new)
                east = [pltpu.roll(x, LANES - 1, 1) for x in new]
                north = new[1:] + [pltpu.roll(new[0], SUB - 1, 0)]
                store(hv, c, [y - g * (n - x) for y, g, n, x in zip(v, d, north, new)])
            else:
                east = [zero] * apart
            if c > 0:
                d = load(dep, c - 1)
                store(
                    hu,
                    c - 1,
                    [
                        x - g * (jnp.where(last, e, p) - n)
                        for x, g, e, p, n in zip(prev_hu, d, east, prev_east, prev_eta)
                    ],
                )
            prev_west, prev_eta, prev_east, prev_hu = west, new, east, u
        return carry

    lax.fori_loop(0, BSTEPS, step, 0)
    for c in range(chunks):
        at = slice(c * LANES, (c + 1) * LANES)
        for f, (ref, unit) in enumerate(((eta, 1.0), (hu, 2.0), (hv, 2.0))):
            out[f, :, at] = ref[c, HALO : HALO + rows] * unit


def basin_run(state, depth, pair_state, pair_depth, edge):
    rows, width = depth.shape
    total = rows + 2 * HALO
    vmem = pl.BlockSpec(memory_space=pltpu.VMEM)
    return pl.pallas_call(
        basin_kernel,
        out_shape=jax.ShapeDtypeStruct((3, rows, width), jnp.float32),
        in_specs=[vmem] * 5,
        out_specs=vmem,
        scratch_shapes=[pltpu.VMEM((width // LANES, total, LANES), jnp.float32)] * 4,
        compiler_params=pltpu.CompilerParams(vmem_limit_bytes=VMEM_LIMIT),
        cost_estimate=pl.CostEstimate(
            flops=BSTEPS * 16 * total * width, bytes_accessed=4 * 11 * rows * width, transcendentals=0
        ),
        name="basin_steps",
    )(state, depth, pair_state, pair_depth, edge)


def strips_kernel(links, own, pair, ghosts, strips):
    rows, width = own.shape[1], own.shape[2]
    count = ghosts.shape[0]
    span = 2 * LANES
    position = lax.axis_index("row")
    tops = (position * rows, (position + 1 - 2 * (position % 2)) * rows)
    lane = lane_ids()
    weight = ((2 * lane + row_ids() % 2) % 16).astype(jnp.float32) / 16.0 + 0.5 / 16.0

    def piece(b, carry):
        col = links[b, 0, 1]
        start = jnp.clip(col // LANES, 0, width // LANES - 2) * LANES
        shift = lax.rem(span - (col - start), span)
        at = pl.ds(pl.multiple_of(start, LANES), span)
        for i, f in enumerate((0, 2)):
            chunk = None
            for source, top in zip((own, pair), tops):
                row = links[b, 0, 0] - top
                owned = jnp.logical_and(row >= 0, row < rows).astype(jnp.float32)
                part = source[f, pl.ds(jnp.clip(row, 0, rows - 1), 1), at] * owned
                chunk = part if chunk is None else chunk + part
            moved = pltpu.roll(chunk, shift, 1)[:, :LANES]
            strips[b, 2 * i : 2 * i + 2] = jnp.broadcast_to(moved, (2, LANES))
        values = strips[b]
        low, high = pick(values, lane // 8), pick(values, lane // 8 + 1)
        ghosts[b] = (1.0 - weight) * low + weight * high
        return carry

    strips[...] = jnp.zeros_like(strips)
    lax.fori_loop(0, count, piece, 0, unroll=8)


def make_strips(links, own, pair):
    count = links.shape[0]
    tiles = (count, SUB, LANES)
    vmem = pl.BlockSpec(memory_space=pltpu.VMEM)
    smem = pl.BlockSpec(memory_space=pltpu.SMEM)
    return pl.pallas_call(
        strips_kernel,
        out_shape=jax.ShapeDtypeStruct(tiles, jnp.float32),
        in_specs=[smem, vmem, vmem],
        out_specs=vmem,
        scratch_shapes=[pltpu.VMEM(tiles, jnp.float32)],
        compiler_params=pltpu.CompilerParams(vmem_limit_bytes=VMEM_LIMIT),
        cost_estimate=pl.CostEstimate(flops=2 * 10**10, bytes_accessed=own.size, transcendentals=0),
        name="strips",
    )(links, own, pair)


def local(basin_state, basin_depth, coast_depth, coast_flow, coast_link):
    devices = lax.axis_size("row")
    odd = lax.axis_index("row") % 2
    chips = list(range(devices // 2))[::-1]
    chips.insert(0, chips.pop(len(chips) - 1 - devices // 4))
    parity = [[2 * chip + p for chip in chips] for p in range(2)]
    sent = jnp.broadcast_to(coast_link, (devices // 2,) + coast_link.shape)
    start = odd * (basin_depth.shape[0] - HALO)
    edge = jnp.concatenate(
        [
            lax.dynamic_slice_in_dim(basin_state, start, HALO, axis=1),
            lax.dynamic_slice_in_dim(basin_depth, start, HALO, axis=0)[None],
        ],
        axis=0,
    )
    links = lax.all_to_all(sent, "row", 0, 0, axis_index_groups=parity, tiled=True)

    twins = [(i, i ^ 1) for i in range(devices)]
    pair_state, pair_depth = [lax.ppermute(a, "row", twins) for a in (basin_state, basin_depth)]
    across = [(i, i + 1) for i in range(1, devices - 1, 2)]
    edge = lax.ppermute(edge, "row", across + [(j, i) for i, j in across])

    depth, flow = coast_depth[0], coast_flow[0]
    folded, wet = coast_fold(coast_link, depth, flow)
    pair_state, folded = lax.optimization_barrier((pair_state, folded))
    ghosts = make_strips(links, basin_state, pair_state)
    basin_depth, ghosts = lax.optimization_barrier((basin_depth, ghosts))
    ghosts = lax.all_to_all(ghosts, "row", 0, 0, axis_index_groups=parity, tiled=True)
    basin_out = basin_run(basin_state, basin_depth, pair_state, pair_depth, edge)
    folded, basin_out = lax.optimization_barrier((folded, basin_out))
    coast_out = coast_run(wet, ghosts, folded, depth, flow)
    return (basin_out, coast_out[None])


def solution(mesh):
    in_specs = (
        P("scen", "row", None),
        P("row", "scen"),
        P("row", "scen", None),
        P("row", "scen", None, None),
        P("row", "scen"),
    )
    out_specs = (P("scen", "row", None), P("row", "scen", None, None))
    return jax.shard_map(local, mesh=mesh, in_specs=in_specs, out_specs=out_specs, check_vma=False)
```

```python
import functools

import jax
import jax.numpy as jnp
from jax import lax
from jax.experimental import pallas as pl
from jax.experimental.pallas import tpu as pltpu
from jax.sharding import PartitionSpec as P

BSTEPS = 8
CSTEPS = 10

depth_floor = 0.2
ghost_level = 2.0

RATE = 0.05
DEPTH_UNIT = RATE * RATE
FLOW_UNIT = RATE * RATE * RATE
TINY = 1e-30

HALO = BSTEPS
SUB = 8
LANES = 128


def lane_ids():
    return lax.broadcasted_iota(jnp.int32, (SUB, LANES), 1)


def row_ids():
    return lax.broadcasted_iota(jnp.int32, (SUB, LANES), 0)


def cell_terms(u):
    h, mu, mv = u
    r = pl.reciprocal(jnp.maximum(h, depth_floor * DEPTH_UNIT), approx=True)
    vx, vy = mu * r, mv * r
    hp = jnp.maximum(h, TINY)
    c = hp * lax.rsqrt(hp)
    p = (0.5 * h) * h
    cross = mu * vy
    return {
        "u": u,
        "fx": (mu, mu * vx + p, cross),
        "fy": (mv, cross, mv * vy + p),
        "sx": jnp.abs(vx) + c,
        "sy": jnp.abs(vy) + c,
    }


def y_face(above, below):
    a = jnp.maximum(above["sy"], below["sy"])
    return [
        a * (ub - ua) - (fa + fb)
        for ua, ub, fa, fb in zip(above["u"], below["u"], above["fy"], below["fy"])
    ]


def coast_steps(state, terms, after, parts, opening, rows, group, steps, ghost):
    lane, sub = lane_ids(), row_ids()
    first, last = lane == 0, lane == LANES - 1
    top, bottom = sub == 0, sub == SUB - 1
    zero = jnp.zeros((SUB, LANES), jnp.float32)
    left = functools.partial(pltpu.roll, shift=LANES - 1, axis=1)
    right = functools.partial(pltpu.roll, shift=1, axis=1)

    def load(view, k):
        return [[view[f, half, 1 + k] for f in range(3)] for half in range(2)]

    def store(view, k, both):
        for half in range(2):
            for f in range(3):
                view[f, half, 1 + k] = both[half][f]

    def store_above(tails):
        store(state, -1, [[jnp.where(top, g, pltpu.roll(t, 1, 0)) for g, t in zip(*pair)] for pair in zip(ghost, tails)])

    def y_terms_of(view, k):
        both = [cell_terms(u) for u in load(view, k)]
        for half, cell in enumerate(both):
            terms[half, 1 + k, 0] = cell["sy"]
            terms[half, 1 + k, 1] = cell["fy"][2]
            terms[half, 1 + k, 2] = cell["fx"][2]
        return both

    def terms_of(view, k):
        even, odd = y_terms_of(view, k)
        for half, cell in enumerate((even, odd)):
            terms[half, 1 + k, 3] = cell["sx"]
            terms[half, 1 + k, 4] = cell["fx"][1]
        moved = zip(even["u"] + [even["sx"]] + list(even["fx"][1:]), odd["u"] + [odd["sx"]] + list(odd["fx"][1:]))
        for q, (e, o) in enumerate(moved):
            after[k, q] = jnp.where(last, o, left(e))

    def x_faces(view, k):
        even, odd = load(view, k)
        following = [after[k, f] for f in range(3)]
        sx_e, sx_o, sx_n = terms[0, 1 + k, 3], terms[1, 1 + k, 3], after[k, 3]
        fx_e = [even[1], terms[0, 1 + k, 4], terms[0, 1 + k, 2]]
        fx_o = [odd[1], terms[1, 1 + k, 4], terms[1, 1 + k, 2]]
        fx_n = [following[1], after[k, 4], after[k, 5]]
        a_in, a_out = jnp.maximum(sx_e, sx_o), jnp.maximum(sx_o, sx_n)
        for f in range(3):
            g_in = a_in * (odd[f] - even[f]) - (fx_e[f] + fx_o[f])
            g_out = a_out * (following[f] - odd[f]) - (fx_o[f] + fx_n[f])
            g_back = jnp.where(first, -2.0 * fx_e[f], right(g_out))
            parts[k, f] = even[f] + (g_in - g_back)
            parts[k, 3 + f] = odd[f] + (g_out - g_in)

    def y_cells(view, k):
        return [
            {
                "u": u,
                "fy": [u[2], terms[half, 1 + k, 2], terms[half, 1 + k, 1]],
                "sy": terms[half, 1 + k, 0],
            }
            for half, u in enumerate(load(view, k))
        ]

    def trip(i, acc):
        view = state.at[:, :, pl.ds(i * group, 1 + group)]
        y_terms_of(view, -1)
        for k in range(group):
            terms_of(view, k)
        for k in range(group):
            x_faces(view, k)
        prev = y_cells(view, -1)
        for k in range(group):
            cur = y_cells(view, k)
            face = [y_face(a, b) for a, b in zip(prev, cur)]
            if k == 0:
                for half in range(2):
                    for f in range(3):
                        opening[i, half, f] = pltpu.roll(face[half][f], SUB - 1, 0)
            store(view, k - 1, [[x + g for x, g in zip(*pair)] for pair in zip(acc, face)])
            acc = [[parts[k, 3 * half + f] - face[half][f] for f in range(3)] for half in range(2)]
            prev = cur
        return acc

    def step(_, carry):
        acc = lax.fori_loop(0, rows // group, trip, [[zero] * 3 for _ in range(2)])
        tails = [
            [
                x + jnp.where(bottom, -2.0 * f, opening[0, half, i])
                for i, (x, f) in enumerate(zip(xs, cell["fy"]))
            ]
            for half, (xs, cell) in enumerate(
                zip(acc, y_cells(state.at[:, :, rows - group :], group - 1))
            )
        ]
        store(state, rows - 1, tails)
        store_above(tails)
        return carry

    store_above(load(state, rows - 1))
    lax.fori_loop(0, steps, step, 0)


GROUP = 16
UNITS = (DEPTH_UNIT, FLOW_UNIT, FLOW_UNIT)
VMEM_LIMIT = 12 * 1024 * 1024
HALF = LANES // 2


def pick(values, ids):
    return jnp.take_along_axis(values, ids, axis=1, mode="promise_in_bounds")


def split_columns(west, east):
    lane = lane_ids()
    low = lane < HALF
    twice = 2 * jnp.where(low, lane, lane - HALF)
    w = pick(west, jnp.where(low, twice, twice + 1))
    e = pick(east, jnp.where(low, twice + 1, twice))
    return jnp.where(low, w, e), pltpu.roll(jnp.where(low, e, w), HALF, 1)


def join_columns(even, odd):
    lane = lane_ids()
    low = lane < HALF
    odd = pltpu.roll(odd, HALF, 1)
    w, e = jnp.where(low, even, odd), jnp.where(low, odd, even)
    half, is_odd = lane // 2, lane % 2
    return pick(w, half + HALF * is_odd), pick(e, half + HALF * (1 - is_odd))


HALVES = (slice(0, LANES), slice(LANES, 2 * LANES))
TALL = 32


def fold_kernel(link, depth, flow, state, wet, tmp):
    rows = depth.shape[0] // SUB
    wet[...] = jnp.broadcast_to(link[:, 2:3], wet.shape).astype(jnp.float32)

    def copy_in(i, carry):
        at = pl.ds(pl.multiple_of(i * TALL, TALL), TALL)
        for f in range(3):
            raw = depth[at] if f == 0 else flow[f - 1, at]
            for p in range(2):
                tmp[f, p, at] = raw[:, HALVES[p]] * UNITS[f]
        return carry

    def fold_field(f, carry):
        def fold(k, carry):
            both = split_columns(*[tmp[f, p, pl.ds(k, SUB, stride=rows), :] for p in range(2)])
            for p in range(2):
                state[f, p, k] = both[p]
            return carry

        return lax.fori_loop(0, rows, fold, carry, unroll=rows)

    lax.fori_loop(0, depth.shape[0] // TALL, copy_in, 0)
    lax.fori_loop(0, 3, fold_field, 0)


def coast_fold(link, depth, flow):
    cells = depth.shape[0]
    vmem = pl.BlockSpec(memory_space=pltpu.VMEM)
    return pl.pallas_call(
        fold_kernel,
        out_shape=(
            jax.ShapeDtypeStruct((3, 2, cells // SUB, SUB, LANES), jnp.float32),
            jax.ShapeDtypeStruct((SUB, LANES), jnp.float32),
        ),
        in_specs=[vmem, vmem, vmem],
        out_specs=(vmem, vmem),
        scratch_shapes=[pltpu.VMEM((3, 2, cells, LANES), jnp.float32)],
        compiler_params=pltpu.CompilerParams(vmem_limit_bytes=VMEM_LIMIT),
        cost_estimate=pl.CostEstimate(
            flops=CSTEPS * 70 * cells * cells, bytes_accessed=24 * cells * cells, transcendentals=0
        ),
        name="coast_fold",
    )(link, depth, flow)


def coast_kernel(
    wet, ghosts, folded, depth, flow, out, state, terms, after, parts, opening, tmp, done, sems
):
    rows = depth.shape[0] // SUB
    is_wet = jnp.max(wet[...]) > 0.0

    def copy_in(k, carry):
        for f in range(3):
            for p in range(2):
                state[f, p, 1 + k] = folded[f, p, k]
        return carry

    @pl.when(jnp.logical_not(is_wet))
    def _():
        copies = [
            pltpu.make_async_copy(depth, out.at[0], sems.at[0]),
            pltpu.make_async_copy(flow, out.at[1:], sems.at[1]),
        ]
        for copy in copies:
            copy.start()
        for copy in copies:
            copy.wait()

    @pl.when(is_wet)
    def _():
        lax.fori_loop(0, rows, copy_in, 0, unroll=4)
        values = jnp.sum(ghosts[...], axis=0)
        level = (ghost_level + values) * DEPTH_UNIT
        inflow = values * FLOW_UNIT
        h, mv = [
            [jnp.broadcast_to(v[i : i + 1], (SUB, LANES)) for i in range(at, at + 2)]
            for v, at in ((level, 0), (inflow, 2))
        ]
        ghost = [[h[p], jnp.zeros_like(h[p]), mv[p]] for p in range(2)]
        coast_steps(state, terms, after, parts, opening, rows, GROUP, CSTEPS, ghost)

        def write(f):
            return pltpu.make_async_copy(done.at[f], out.at[f], sems.at[f])

        def finish(f, carry):
            scale = jnp.where(f == 0, 1.0 / DEPTH_UNIT, 1.0 / FLOW_UNIT)

            def unfold(k, carry):
                both = join_columns(state[f, 0, 1 + k], state[f, 1, 1 + k])
                for p in range(2):
                    tmp[p, pl.ds(k, SUB, stride=rows), :] = both[p] * scale
                return carry

            def copy_out(i, carry):
                at = pl.ds(pl.multiple_of(i * TALL, TALL), TALL)
                for p in range(2):
                    done[f, at, HALVES[p]] = tmp[p, at]
                return carry

            lax.fori_loop(0, rows, unfold, 0, unroll=rows)
            lax.fori_loop(0, depth.shape[0] // TALL, copy_out, 0, unroll=2)
            write(f).start()
            return carry

        lax.fori_loop(0, 3, finish, 0)
        for f in range(3):
            write(f).wait()


def coast_run(wet, ghosts, folded, depth, flow):
    cells = depth.shape[0]
    vmem = pl.BlockSpec(memory_space=pltpu.VMEM)
    return pl.pallas_call(
        coast_kernel,
        out_shape=jax.ShapeDtypeStruct((3, cells, cells), jnp.float32),
        in_specs=[vmem] * 5,
        out_specs=pl.BlockSpec(memory_space=pltpu.HBM),
        scratch_shapes=[
            pltpu.VMEM((3, 2, 1 + cells // SUB, SUB, LANES), jnp.float32),
            pltpu.VMEM((2, 1 + GROUP, 5, SUB, LANES), jnp.float32),
            pltpu.VMEM((GROUP, 6, SUB, LANES), jnp.float32),
            pltpu.VMEM((GROUP, 6, SUB, LANES), jnp.float32),
            pltpu.VMEM((cells // SUB // GROUP, 2, 3, SUB, LANES), jnp.float32),
            pltpu.VMEM((2, cells, LANES), jnp.float32),
            pltpu.VMEM((3, cells, cells), jnp.float32),
            pltpu.SemaphoreType.DMA((3,)),
        ],
        compiler_params=pltpu.CompilerParams(vmem_limit_bytes=VMEM_LIMIT),
        cost_estimate=pl.CostEstimate(
            flops=CSTEPS * 70 * cells * cells, bytes_accessed=24 * cells * cells, transcendentals=0
        ),
        name="coast_steps",
    )(wet, ghosts, folded, depth, flow)


def basin_kernel(state, depth, pair_state, pair_depth, edge, out, eta, hu, hv, dep):
    rows, width = depth.shape
    total = rows + 2 * HALO
    chunks = width // LANES
    position = lax.axis_index("row")
    odd = position % 2
    north_inside = (position < lax.axis_size("row") - 1).astype(jnp.float32)
    pair_from = pl.multiple_of(odd * (rows - HALO), HALO)
    pair_at = pl.multiple_of((1 - odd) * (HALO + rows), HALO)
    edge_at = pl.multiple_of(odd * (HALO + rows), HALO)
    for ref, field, unit in ((eta, 0, 1.0), (hu, 1, 0.5), (hv, 2, 0.5), (dep, 3, 0.25)):
        own, pair = (depth, pair_depth) if field == 3 else (state.at[field], pair_state.at[field])
        for c in range(chunks):
            at = slice(c * LANES, (c + 1) * LANES)
            ref[c, HALO : HALO + rows] = own[:, at] * unit
            ref[c, pl.ds(pair_at, HALO)] = pair[pl.ds(pair_from, HALO), at] * unit
            ref[c, pl.ds(edge_at, HALO)] = edge[field, :, at] * unit
    apart = total // SUB
    lane = lane_ids()
    first, last = lane == 0, lane == LANES - 1
    kept = jnp.where(row_ids() * apart < HALO + rows, 1.0, north_inside)
    zero = jnp.zeros((SUB, LANES), jnp.float32)

    def load(ref, c):
        return [ref[c, pl.ds(k, SUB, stride=apart), :] for k in range(apart)]

    def store(ref, c, values):
        for k in range(apart):
            ref[c, pl.ds(k, SUB, stride=apart), :] = values[k]

    def step(_, carry):
        prev_west = [zero] * apart
        prev_eta, prev_east, prev_hu = None, None, None
        for c in range(chunks + 1):
            if c < chunks:
                u, v, d = load(hu, c), load(hv, c), load(dep, c)
                west = [pltpu.roll(x, 1, 1) for x in u]
                south = [pltpu.roll(v[-1], 1, 0)] + v[:-1]
                new = [
                    (e - ((x - jnp.where(first, p, w)) + (y - t))) * kept
                    for e, x, p, w, y, t in zip(load(eta, c), u, prev_west, west, v, south)
                ]
                store(eta, c, new)
                east = [pltpu.roll(x, LANES - 1, 1) for x in new]
                north = new[1:] + [pltpu.roll(new[0], SUB - 1, 0)]
                store(hv, c, [y - g * (n - x) for y, g, n, x in zip(v, d, north, new)])
            else:
                east = [zero] * apart
            if c > 0:
                d = load(dep, c - 1)
                store(
                    hu,
                    c - 1,
                    [
                        x - g * (jnp.where(last, e, p) - n)
                        for x, g, e, p, n in zip(prev_hu, d, east, prev_east, prev_eta)
                    ],
                )
            prev_west, prev_eta, prev_east, prev_hu = west, new, east, u
        return carry

    lax.fori_loop(0, BSTEPS, step, 0)
    for c in range(chunks):
        at = slice(c * LANES, (c + 1) * LANES)
        for f, (ref, unit) in enumerate(((eta, 1.0), (hu, 2.0), (hv, 2.0))):
            out[f, :, at] = ref[c, HALO : HALO + rows] * unit


def basin_run(state, depth, pair_state, pair_depth, edge):
    rows, width = depth.shape
    total = rows + 2 * HALO
    vmem = pl.BlockSpec(memory_space=pltpu.VMEM)
    return pl.pallas_call(
        basin_kernel,
        out_shape=jax.ShapeDtypeStruct((3, rows, width), jnp.float32),
        in_specs=[vmem] * 5,
        out_specs=vmem,
        scratch_shapes=[pltpu.VMEM((width // LANES, total, LANES), jnp.float32)] * 4,
        compiler_params=pltpu.CompilerParams(vmem_limit_bytes=VMEM_LIMIT),
        cost_estimate=pl.CostEstimate(
            flops=BSTEPS * 16 * total * width, bytes_accessed=4 * 11 * rows * width, transcendentals=0
        ),
        name="basin_steps",
    )(state, depth, pair_state, pair_depth, edge)


def strips_kernel(links, own, pair, ghosts, strips):
    rows, width = own.shape[1], own.shape[2]
    count = ghosts.shape[0]
    span = 2 * LANES
    position = lax.axis_index("row")
    tops = (position * rows, (position + 1 - 2 * (position % 2)) * rows)
    lane = lane_ids()
    weight = ((2 * lane + row_ids() % 2) % 16).astype(jnp.float32) / 16.0 + 0.5 / 16.0

    def piece(b, carry):
        col = links[b, 0, 1]
        start = jnp.clip(col // LANES, 0, width // LANES - 2) * LANES
        shift = lax.rem(span - (col - start), span)
        at = pl.ds(pl.multiple_of(start, LANES), span)
        for i, f in enumerate((0, 2)):
            chunk = None
            for source, top in zip((own, pair), tops):
                row = links[b, 0, 0] - top
                owned = jnp.logical_and(row >= 0, row < rows).astype(jnp.float32)
                part = source[f, pl.ds(jnp.clip(row, 0, rows - 1), 1), at] * owned
                chunk = part if chunk is None else chunk + part
            moved = pltpu.roll(chunk, shift, 1)[:, :LANES]
            strips[b, 2 * i : 2 * i + 2] = jnp.broadcast_to(moved, (2, LANES))
        values = strips[b]
        low, high = pick(values, lane // 8), pick(values, lane // 8 + 1)
        ghosts[b] = (1.0 - weight) * low + weight * high
        return carry

    strips[...] = jnp.zeros_like(strips)
    lax.fori_loop(0, count, piece, 0, unroll=8)


def make_strips(links, own, pair):
    count = links.shape[0]
    tiles = (count, SUB, LANES)
    vmem = pl.BlockSpec(memory_space=pltpu.VMEM)
    smem = pl.BlockSpec(memory_space=pltpu.SMEM)
    return pl.pallas_call(
        strips_kernel,
        out_shape=jax.ShapeDtypeStruct(tiles, jnp.float32),
        in_specs=[smem, vmem, vmem],
        out_specs=vmem,
        scratch_shapes=[pltpu.VMEM(tiles, jnp.float32)],
        compiler_params=pltpu.CompilerParams(vmem_limit_bytes=VMEM_LIMIT),
        cost_estimate=pl.CostEstimate(flops=2 * 10**10, bytes_accessed=own.size, transcendentals=0),
        name="strips",
    )(links, own, pair)


def local(basin_state, basin_depth, coast_depth, coast_flow, coast_link):
    devices = lax.axis_size("row")
    odd = lax.axis_index("row") % 2
    chips = list(range(devices // 2))[::-1]
    chips.insert(0, chips.pop(len(chips) - 1 - devices // 4))
    parity = [[2 * chip + p for chip in chips] for p in range(2)]
    sent = jnp.broadcast_to(coast_link, (devices // 2,) + coast_link.shape)
    start = odd * (basin_depth.shape[0] - HALO)
    edge = jnp.concatenate(
        [
            lax.dynamic_slice_in_dim(basin_state, start, HALO, axis=1),
            lax.dynamic_slice_in_dim(basin_depth, start, HALO, axis=0)[None],
        ],
        axis=0,
    )
    links = lax.all_to_all(sent, "row", 0, 0, axis_index_groups=parity, tiled=True)

    twins = [(i, i ^ 1) for i in range(devices)]
    pair_state, pair_depth = [lax.ppermute(a, "row", twins) for a in (basin_state, basin_depth)]
    across = [(i, i + 1) for i in range(1, devices - 1, 2)]
    edge = lax.ppermute(edge, "row", across + [(j, i) for i, j in across])

    ghosts = make_strips(links, basin_state, pair_state)
    basin_depth, coast_depth, ghosts = lax.optimization_barrier((basin_depth, coast_depth, ghosts))
    ghosts = lax.all_to_all(ghosts, "row", 0, 0, axis_index_groups=parity, tiled=True)
    depth, flow = coast_depth[0], coast_flow[0]
    folded, wet = coast_fold(coast_link, depth, flow)
    basin_out = basin_run(basin_state, basin_depth, pair_state, pair_depth, edge)
    folded, basin_out = lax.optimization_barrier((folded, basin_out))
    coast_out = coast_run(wet, ghosts, folded, depth, flow)
    return (basin_out, coast_out[None])


def solution(mesh):
    in_specs = (
        P("scen", "row", None),
        P("row", "scen"),
        P("row", "scen", None),
        P("row", "scen", None, None),
        P("row", "scen"),
    )
    out_specs = (P("scen", "row", None), P("row", "scen", None, None))
    return jax.shard_map(local, mesh=mesh, in_specs=in_specs, out_specs=out_specs, check_vma=False)
```

```python
import functools

import jax
import jax.numpy as jnp
from jax import lax
from jax.experimental import pallas as pl
from jax.experimental.pallas import tpu as pltpu
from jax.sharding import PartitionSpec as P

BSTEPS = 8
CSTEPS = 10

depth_floor = 0.2
ghost_level = 2.0

RATE = 0.05
DEPTH_UNIT = RATE * RATE
FLOW_UNIT = RATE * RATE * RATE
TINY = 1e-30

HALO = BSTEPS
SUB = 8
LANES = 128


def lane_ids():
    return lax.broadcasted_iota(jnp.int32, (SUB, LANES), 1)


def row_ids():
    return lax.broadcasted_iota(jnp.int32, (SUB, LANES), 0)


def cell_terms(u):
    h, mu, mv = u
    r = pl.reciprocal(jnp.maximum(h, depth_floor * DEPTH_UNIT), approx=True)
    vx, vy = mu * r, mv * r
    hp = jnp.maximum(h, TINY)
    c = hp * lax.rsqrt(hp)
    p = (0.5 * h) * h
    cross = mu * vy
    return {
        "u": u,
        "fx": (mu, mu * vx + p, cross),
        "fy": (mv, cross, mv * vy + p),
        "sx": jnp.abs(vx) + c,
        "sy": jnp.abs(vy) + c,
    }


def y_face(above, below):
    a = jnp.maximum(above["sy"], below["sy"])
    return [
        a * (ub - ua) - (fa + fb)
        for ua, ub, fa, fb in zip(above["u"], below["u"], above["fy"], below["fy"])
    ]


def coast_steps(state, terms, after, parts, opening, rows, group, steps, ghost):
    lane, sub = lane_ids(), row_ids()
    first, last = lane == 0, lane == LANES - 1
    top, bottom = sub == 0, sub == SUB - 1
    zero = jnp.zeros((SUB, LANES), jnp.float32)
    left = functools.partial(pltpu.roll, shift=LANES - 1, axis=1)
    right = functools.partial(pltpu.roll, shift=1, axis=1)

    def load(view, k):
        return [[view[f, half, 1 + k] for f in range(3)] for half in range(2)]

    def store(view, k, both):
        for half in range(2):
            for f in range(3):
                view[f, half, 1 + k] = both[half][f]

    def store_above(tails):
        store(state, -1, [[jnp.where(top, g, pltpu.roll(t, 1, 0)) for g, t in zip(*pair)] for pair in zip(ghost, tails)])

    def y_terms_of(view, k):
        both = [cell_terms(u) for u in load(view, k)]
        for half, cell in enumerate(both):
            terms[half, 1 + k, 0] = cell["sy"]
            terms[half, 1 + k, 1] = cell["fy"][2]
            terms[half, 1 + k, 2] = cell["fx"][2]
        return both

    def terms_of(view, k):
        even, odd = y_terms_of(view, k)
        for half, cell in enumerate((even, odd)):
            terms[half, 1 + k, 3] = cell["sx"]
            terms[half, 1 + k, 4] = cell["fx"][1]
        moved = zip(even["u"] + [even["sx"]] + list(even["fx"][1:]), odd["u"] + [odd["sx"]] + list(odd["fx"][1:]))
        for q, (e, o) in enumerate(moved):
            after[k, q] = jnp.where(last, o, left(e))

    def x_faces(view, k):
        even, odd = load(view, k)
        following = [after[k, f] for f in range(3)]
        sx_e, sx_o, sx_n = terms[0, 1 + k, 3], terms[1, 1 + k, 3], after[k, 3]
        fx_e = [even[1], terms[0, 1 + k, 4], terms[0, 1 + k, 2]]
        fx_o = [odd[1], terms[1, 1 + k, 4], terms[1, 1 + k, 2]]
        fx_n = [following[1], after[k, 4], after[k, 5]]
        a_in, a_out = jnp.maximum(sx_e, sx_o), jnp.maximum(sx_o, sx_n)
        for f in range(3):
            g_in = a_in * (odd[f] - even[f]) - (fx_e[f] + fx_o[f])
            g_out = a_out * (following[f] - odd[f]) - (fx_o[f] + fx_n[f])
            g_back = jnp.where(first, -2.0 * fx_e[f], right(g_out))
            parts[k, f] = even[f] + (g_in - g_back)
            parts[k, 3 + f] = odd[f] + (g_out - g_in)

    def y_cells(view, k):
        return [
            {
                "u": u,
                "fy": [u[2], terms[half, 1 + k, 2], terms[half, 1 + k, 1]],
                "sy": terms[half, 1 + k, 0],
            }
            for half, u in enumerate(load(view, k))
        ]

    def trip(i, acc):
        view = state.at[:, :, pl.ds(i * group, 1 + group)]
        y_terms_of(view, -1)
        for k in range(group):
            terms_of(view, k)
        for k in range(group):
            x_faces(view, k)
        prev = y_cells(view, -1)
        for k in range(group):
            cur = y_cells(view, k)
            face = [y_face(a, b) for a, b in zip(prev, cur)]
            if k == 0:
                for half in range(2):
                    for f in range(3):
                        opening[i, half, f] = pltpu.roll(face[half][f], SUB - 1, 0)
            store(view, k - 1, [[x + g for x, g in zip(*pair)] for pair in zip(acc, face)])
            acc = [[parts[k, 3 * half + f] - face[half][f] for f in range(3)] for half in range(2)]
            prev = cur
        return acc

    def step(_, carry):
        acc = lax.fori_loop(0, rows // group, trip, [[zero] * 3 for _ in range(2)])
        tails = [
            [
                x + jnp.where(bottom, -2.0 * f, opening[0, half, i])
                for i, (x, f) in enumerate(zip(xs, cell["fy"]))
            ]
            for half, (xs, cell) in enumerate(
                zip(acc, y_cells(state.at[:, :, rows - group :], group - 1))
            )
        ]
        store(state, rows - 1, tails)
        store_above(tails)
        return carry

    store_above(load(state, rows - 1))
    lax.fori_loop(0, steps, step, 0)


GROUP = 16
UNITS = (DEPTH_UNIT, FLOW_UNIT, FLOW_UNIT)
VMEM_LIMIT = 12 * 1024 * 1024
HALF = LANES // 2


def pick(values, ids):
    return jnp.take_along_axis(values, ids, axis=1, mode="promise_in_bounds")


def split_columns(west, east):
    lane = lane_ids()
    low = lane < HALF
    twice = 2 * jnp.where(low, lane, lane - HALF)
    w = pick(west, jnp.where(low, twice, twice + 1))
    e = pick(east, jnp.where(low, twice + 1, twice))
    return jnp.where(low, w, e), pltpu.roll(jnp.where(low, e, w), HALF, 1)


def join_columns(even, odd):
    lane = lane_ids()
    low = lane < HALF
    odd = pltpu.roll(odd, HALF, 1)
    w, e = jnp.where(low, even, odd), jnp.where(low, odd, even)
    half, is_odd = lane // 2, lane % 2
    return pick(w, half + HALF * is_odd), pick(e, half + HALF * (1 - is_odd))


HALVES = (slice(0, LANES), slice(LANES, 2 * LANES))
TALL = 32


def fold_kernel(link, depth, flow, state, wet, tmp):
    rows = depth.shape[0] // SUB
    wet[...] = jnp.broadcast_to(link[:, 2:3], wet.shape).astype(jnp.float32)

    def copy_in(i, carry):
        at = pl.ds(pl.multiple_of(i * TALL, TALL), TALL)
        for f in range(3):
            raw = depth[at] if f == 0 else flow[f - 1, at]
            for p in range(2):
                tmp[f, p, at] = raw[:, HALVES[p]] * UNITS[f]
        return carry

    def fold_field(f, carry):
        def fold(k, carry):
            both = split_columns(*[tmp[f, p, pl.ds(k, SUB, stride=rows), :] for p in range(2)])
            for p in range(2):
                state[f, p, k] = both[p]
            return carry

        return lax.fori_loop(0, rows, fold, carry, unroll=rows)

    lax.fori_loop(0, depth.shape[0] // TALL, copy_in, 0)
    lax.fori_loop(0, 3, fold_field, 0)


def coast_fold(link, depth, flow):
    cells = depth.shape[0]
    vmem = pl.BlockSpec(memory_space=pltpu.VMEM)
    return pl.pallas_call(
        fold_kernel,
        out_shape=(
            jax.ShapeDtypeStruct((3, 2, cells // SUB, SUB, LANES), jnp.float32),
            jax.ShapeDtypeStruct((SUB, LANES), jnp.float32),
        ),
        in_specs=[vmem, vmem, vmem],
        out_specs=(vmem, vmem),
        scratch_shapes=[pltpu.VMEM((3, 2, cells, LANES), jnp.float32)],
        compiler_params=pltpu.CompilerParams(vmem_limit_bytes=VMEM_LIMIT),
        cost_estimate=pl.CostEstimate(
            flops=CSTEPS * 70 * cells * cells, bytes_accessed=24 * cells * cells, transcendentals=0
        ),
        name="coast_fold",
    )(link, depth, flow)


def coast_kernel(
    wet, ghosts, folded, depth, flow, out, state, terms, after, parts, opening, tmp, done, sems
):
    rows = depth.shape[0] // SUB
    is_wet = jnp.max(wet[...]) > 0.0

    def copy_in(k, carry):
        for f in range(3):
            for p in range(2):
                state[f, p, 1 + k] = folded[f, p, k]
        return carry

    @pl.when(jnp.logical_not(is_wet))
    def _():
        copies = [
            pltpu.make_async_copy(depth, out.at[0], sems.at[0]),
            pltpu.make_async_copy(flow, out.at[1:], sems.at[1]),
        ]
        for copy in copies:
            copy.start()
        for copy in copies:
            copy.wait()

    @pl.when(is_wet)
    def _():
        lax.fori_loop(0, rows, copy_in, 0, unroll=4)
        values = jnp.sum(ghosts[...], axis=0)
        level = (ghost_level + values) * DEPTH_UNIT
        inflow = values * FLOW_UNIT
        h, mv = [
            [jnp.broadcast_to(v[i : i + 1], (SUB, LANES)) for i in range(at, at + 2)]
            for v, at in ((level, 0), (inflow, 2))
        ]
        ghost = [[h[p], jnp.zeros_like(h[p]), mv[p]] for p in range(2)]
        coast_steps(state, terms, after, parts, opening, rows, GROUP, CSTEPS, ghost)

        def write(f):
            return pltpu.make_async_copy(done.at[f], out.at[f], sems.at[f])

        def finish(f, carry):
            scale = jnp.where(f == 0, 1.0 / DEPTH_UNIT, 1.0 / FLOW_UNIT)

            def unfold(k, carry):
                both = join_columns(state[f, 0, 1 + k], state[f, 1, 1 + k])
                for p in range(2):
                    tmp[p, pl.ds(k, SUB, stride=rows), :] = both[p] * scale
                return carry

            def copy_out(i, carry):
                at = pl.ds(pl.multiple_of(i * TALL, TALL), TALL)
                for p in range(2):
                    done[f, at, HALVES[p]] = tmp[p, at]
                return carry

            lax.fori_loop(0, rows, unfold, 0, unroll=rows)
            lax.fori_loop(0, depth.shape[0] // TALL, copy_out, 0, unroll=2)
            write(f).start()
            return carry

        lax.fori_loop(0, 3, finish, 0)
        for f in range(3):
            write(f).wait()


def coast_run(wet, ghosts, folded, depth, flow):
    cells = depth.shape[0]
    vmem = pl.BlockSpec(memory_space=pltpu.VMEM)
    return pl.pallas_call(
        coast_kernel,
        out_shape=jax.ShapeDtypeStruct((3, cells, cells), jnp.float32),
        in_specs=[vmem] * 5,
        out_specs=pl.BlockSpec(memory_space=pltpu.HBM),
        scratch_shapes=[
            pltpu.VMEM((3, 2, 1 + cells // SUB, SUB, LANES), jnp.float32),
            pltpu.VMEM((2, 1 + GROUP, 5, SUB, LANES), jnp.float32),
            pltpu.VMEM((GROUP, 6, SUB, LANES), jnp.float32),
            pltpu.VMEM((GROUP, 6, SUB, LANES), jnp.float32),
            pltpu.VMEM((cells // SUB // GROUP, 2, 3, SUB, LANES), jnp.float32),
            pltpu.VMEM((2, cells, LANES), jnp.float32),
            pltpu.VMEM((3, cells, cells), jnp.float32),
            pltpu.SemaphoreType.DMA((3,)),
        ],
        compiler_params=pltpu.CompilerParams(vmem_limit_bytes=VMEM_LIMIT),
        cost_estimate=pl.CostEstimate(
            flops=CSTEPS * 70 * cells * cells, bytes_accessed=24 * cells * cells, transcendentals=0
        ),
        name="coast_steps",
    )(wet, ghosts, folded, depth, flow)


def basin_kernel(state, depth, pair_state, pair_depth, edge, out, eta, hu, hv, dep):
    rows, width = depth.shape
    total = rows + 2 * HALO
    chunks = width // LANES
    position = lax.axis_index("row")
    odd = position % 2
    north_inside = (position < lax.axis_size("row") - 1).astype(jnp.float32)
    pair_from = pl.multiple_of(odd * (rows - HALO), HALO)
    pair_at = pl.multiple_of((1 - odd) * (HALO + rows), HALO)
    edge_at = pl.multiple_of(odd * (HALO + rows), HALO)
    for ref, field, unit in ((eta, 0, 1.0), (hu, 1, 0.5), (hv, 2, 0.5), (dep, 3, 0.25)):
        own, pair = (depth, pair_depth) if field == 3 else (state.at[field], pair_state.at[field])
        for c in range(chunks):
            at = slice(c * LANES, (c + 1) * LANES)
            ref[c, HALO : HALO + rows] = own[:, at] * unit
            ref[c, pl.ds(pair_at, HALO)] = pair[pl.ds(pair_from, HALO), at] * unit
            ref[c, pl.ds(edge_at, HALO)] = edge[field, :, at] * unit
    apart = total // SUB
    lane = lane_ids()
    first, last = lane == 0, lane == LANES - 1
    kept = jnp.where(row_ids() * apart < HALO + rows, 1.0, north_inside)
    zero = jnp.zeros((SUB, LANES), jnp.float32)

    def load(ref, c):
        return [ref[c, pl.ds(k, SUB, stride=apart), :] for k in range(apart)]

    def store(ref, c, values):
        for k in range(apart):
            ref[c, pl.ds(k, SUB, stride=apart), :] = values[k]

    def step(_, carry):
        prev_west = [zero] * apart
        prev_eta, prev_east, prev_hu = None, None, None
        for c in range(chunks + 1):
            if c < chunks:
                u, v, d = load(hu, c), load(hv, c), load(dep, c)
                west = [pltpu.roll(x, 1, 1) for x in u]
                south = [pltpu.roll(v[-1], 1, 0)] + v[:-1]
                new = [
                    (e - ((x - jnp.where(first, p, w)) + (y - t))) * kept
                    for e, x, p, w, y, t in zip(load(eta, c), u, prev_west, west, v, south)
                ]
                store(eta, c, new)
                east = [pltpu.roll(x, LANES - 1, 1) for x in new]
                north = new[1:] + [pltpu.roll(new[0], SUB - 1, 0)]
                store(hv, c, [y - g * (n - x) for y, g, n, x in zip(v, d, north, new)])
            else:
                east = [zero] * apart
            if c > 0:
                d = load(dep, c - 1)
                store(
                    hu,
                    c - 1,
                    [
                        x - g * (jnp.where(last, e, p) - n)
                        for x, g, e, p, n in zip(prev_hu, d, east, prev_east, prev_eta)
                    ],
                )
            prev_west, prev_eta, prev_east, prev_hu = west, new, east, u
        return carry

    lax.fori_loop(0, BSTEPS, step, 0)
    for c in range(chunks):
        at = slice(c * LANES, (c + 1) * LANES)
        for f, (ref, unit) in enumerate(((eta, 1.0), (hu, 2.0), (hv, 2.0))):
            out[f, :, at] = ref[c, HALO : HALO + rows] * unit


def basin_run(state, depth, pair_state, pair_depth, edge):
    rows, width = depth.shape
    total = rows + 2 * HALO
    vmem = pl.BlockSpec(memory_space=pltpu.VMEM)
    return pl.pallas_call(
        basin_kernel,
        out_shape=jax.ShapeDtypeStruct((3, rows, width), jnp.float32),
        in_specs=[vmem] * 5,
        out_specs=vmem,
        scratch_shapes=[pltpu.VMEM((width // LANES, total, LANES), jnp.float32)] * 4,
        compiler_params=pltpu.CompilerParams(vmem_limit_bytes=VMEM_LIMIT),
        cost_estimate=pl.CostEstimate(
            flops=BSTEPS * 16 * total * width, bytes_accessed=4 * 11 * rows * width, transcendentals=0
        ),
        name="basin_steps",
    )(state, depth, pair_state, pair_depth, edge)


def strips_kernel(links, own, pair, ghosts, strips):
    rows, width = own.shape[1], own.shape[2]
    count = ghosts.shape[0]
    span = 2 * LANES
    position = lax.axis_index("row")
    tops = (position * rows, (position + 1 - 2 * (position % 2)) * rows)
    lane = lane_ids()
    weight = ((2 * lane + row_ids() % 2) % 16).astype(jnp.float32) / 16.0 + 0.5 / 16.0

    def piece(b, carry):
        col = links[b, 0, 1]
        start = jnp.clip(col // LANES, 0, width // LANES - 2) * LANES
        shift = lax.rem(span - (col - start), span)
        at = pl.ds(pl.multiple_of(start, LANES), span)
        for i, f in enumerate((0, 2)):
            chunk = None
            for source, top in zip((own, pair), tops):
                row = links[b, 0, 0] - top
                owned = jnp.logical_and(row >= 0, row < rows).astype(jnp.float32)
                part = source[f, pl.ds(jnp.clip(row, 0, rows - 1), 1), at] * owned
                chunk = part if chunk is None else chunk + part
            moved = pltpu.roll(chunk, shift, 1)[:, :LANES]
            strips[b, 2 * i : 2 * i + 2] = jnp.broadcast_to(moved, (2, LANES))
        values = strips[b]
        low, high = pick(values, lane // 8), pick(values, lane // 8 + 1)
        ghosts[b] = (1.0 - weight) * low + weight * high
        return carry

    strips[...] = jnp.zeros_like(strips)
    lax.fori_loop(0, count, piece, 0, unroll=8)


def make_strips(links, own, pair):
    count = links.shape[0]
    tiles = (count, SUB, LANES)
    vmem = pl.BlockSpec(memory_space=pltpu.VMEM)
    smem = pl.BlockSpec(memory_space=pltpu.SMEM)
    return pl.pallas_call(
        strips_kernel,
        out_shape=jax.ShapeDtypeStruct(tiles, jnp.float32),
        in_specs=[smem, vmem, vmem],
        out_specs=vmem,
        scratch_shapes=[pltpu.VMEM(tiles, jnp.float32)],
        compiler_params=pltpu.CompilerParams(vmem_limit_bytes=VMEM_LIMIT),
        cost_estimate=pl.CostEstimate(flops=2 * 10**10, bytes_accessed=own.size, transcendentals=0),
        name="strips",
    )(links, own, pair)


def local(basin_state, basin_depth, coast_depth, coast_flow, coast_link):
    devices = lax.axis_size("row")
    odd = lax.axis_index("row") % 2
    chips = list(range(devices // 2))[::-1]
    chips.insert(0, chips.pop(len(chips) - 1 - devices // 4))
    parity = [[2 * chip + p for chip in chips] for p in range(2)]
    sent = jnp.broadcast_to(coast_link, (devices // 2,) + coast_link.shape)
    start = odd * (basin_depth.shape[0] - HALO)
    edge = jnp.concatenate(
        [
            lax.dynamic_slice_in_dim(basin_state, start, HALO, axis=1),
            lax.dynamic_slice_in_dim(basin_depth, start, HALO, axis=0)[None],
        ],
        axis=0,
    )
    links = lax.all_to_all(sent, "row", 0, 0, axis_index_groups=parity, tiled=True)

    twins = [(i, i ^ 1) for i in range(devices)]
    pair_state, pair_depth = [lax.ppermute(a, "row", twins) for a in (basin_state, basin_depth)]
    across = [(i, i + 1) for i in range(1, devices - 1, 2)]
    edge = lax.ppermute(edge, "row", across + [(j, i) for i, j in across])

    ghosts = make_strips(links, basin_state, pair_state)
    basin_depth, coast_depth, ghosts = lax.optimization_barrier((basin_depth, coast_depth, ghosts))
    ghosts = lax.all_to_all(ghosts, "row", 0, 0, axis_index_groups=parity, tiled=True)
    depth, flow = coast_depth[0], coast_flow[0]
    folded, wet = coast_fold(coast_link, depth, flow)
    basin_depth, folded = lax.optimization_barrier((basin_depth, folded))
    basin_out = basin_run(basin_state, basin_depth, pair_state, pair_depth, edge)
    folded, basin_out = lax.optimization_barrier((folded, basin_out))
    coast_out = coast_run(wet, ghosts, folded, depth, flow)
    return (basin_out, coast_out[None])


def solution(mesh):
    in_specs = (
        P("scen", "row", None),
        P("row", "scen"),
        P("row", "scen", None),
        P("row", "scen", None, None),
        P("row", "scen"),
    )
    out_specs = (P("scen", "row", None), P("row", "scen", None, None))
    return jax.shard_map(local, mesh=mesh, in_specs=in_specs, out_specs=out_specs, check_vma=False)
```

```python
import functools

import jax
import jax.numpy as jnp
from jax import lax
from jax.experimental import pallas as pl
from jax.experimental.pallas import tpu as pltpu
from jax.sharding import PartitionSpec as P

BSTEPS = 8
CSTEPS = 10

depth_floor = 0.2
ghost_level = 2.0

RATE = 0.05
DEPTH_UNIT = RATE * RATE
FLOW_UNIT = RATE * RATE * RATE
TINY = 1e-30

HALO = BSTEPS
SUB = 8
LANES = 128


def lane_ids():
    return lax.broadcasted_iota(jnp.int32, (SUB, LANES), 1)


def row_ids():
    return lax.broadcasted_iota(jnp.int32, (SUB, LANES), 0)


def cell_terms(u):
    h, mu, mv = u
    r = pl.reciprocal(jnp.maximum(h, depth_floor * DEPTH_UNIT), approx=True)
    vx, vy = mu * r, mv * r
    hp = jnp.maximum(h, TINY)
    c = hp * lax.rsqrt(hp)
    p = (0.5 * h) * h
    cross = mu * vy
    return {
        "u": u,
        "fx": (mu, mu * vx + p, cross),
        "fy": (mv, cross, mv * vy + p),
        "sx": jnp.abs(vx) + c,
        "sy": jnp.abs(vy) + c,
    }


def y_face(above, below):
    a = jnp.maximum(above["sy"], below["sy"])
    return [
        a * (ub - ua) - (fa + fb)
        for ua, ub, fa, fb in zip(above["u"], below["u"], above["fy"], below["fy"])
    ]


def coast_steps(state, terms, after, parts, opening, rows, group, steps, ghost):
    lane, sub = lane_ids(), row_ids()
    first, last = lane == 0, lane == LANES - 1
    top, bottom = sub == 0, sub == SUB - 1
    zero = jnp.zeros((SUB, LANES), jnp.float32)
    left = functools.partial(pltpu.roll, shift=LANES - 1, axis=1)
    right = functools.partial(pltpu.roll, shift=1, axis=1)

    def load(view, k):
        return [[view[f, half, 1 + k] for f in range(3)] for half in range(2)]

    def store(view, k, both):
        for half in range(2):
            for f in range(3):
                view[f, half, 1 + k] = both[half][f]

    def store_above(tails):
        store(state, -1, [[jnp.where(top, g, pltpu.roll(t, 1, 0)) for g, t in zip(*pair)] for pair in zip(ghost, tails)])

    def y_terms_of(view, k):
        both = [cell_terms(u) for u in load(view, k)]
        for half, cell in enumerate(both):
            terms[half, 1 + k, 0] = cell["sy"]
            terms[half, 1 + k, 1] = cell["fy"][2]
            terms[half, 1 + k, 2] = cell["fx"][2]
        return both

    def terms_of(view, k):
        even, odd = y_terms_of(view, k)
        for half, cell in enumerate((even, odd)):
            terms[half, 1 + k, 3] = cell["sx"]
            terms[half, 1 + k, 4] = cell["fx"][1]
        moved = zip(even["u"] + [even["sx"]] + list(even["fx"][1:]), odd["u"] + [odd["sx"]] + list(odd["fx"][1:]))
        for q, (e, o) in enumerate(moved):
            after[k, q] = jnp.where(last, o, left(e))

    def x_faces(view, k):
        even, odd = load(view, k)
        following = [after[k, f] for f in range(3)]
        sx_e, sx_o, sx_n = terms[0, 1 + k, 3], terms[1, 1 + k, 3], after[k, 3]
        fx_e = [even[1], terms[0, 1 + k, 4], terms[0, 1 + k, 2]]
        fx_o = [odd[1], terms[1, 1 + k, 4], terms[1, 1 + k, 2]]
        fx_n = [following[1], after[k, 4], after[k, 5]]
        a_in, a_out = jnp.maximum(sx_e, sx_o), jnp.maximum(sx_o, sx_n)
        for f in range(3):
            g_in = a_in * (odd[f] - even[f]) - (fx_e[f] + fx_o[f])
            g_out = a_out * (following[f] - odd[f]) - (fx_o[f] + fx_n[f])
            g_back = jnp.where(first, -2.0 * fx_e[f], right(g_out))
            parts[k, f] = even[f] + (g_in - g_back)
            parts[k, 3 + f] = odd[f] + (g_out - g_in)

    def y_cells(view, k):
        return [
            {
                "u": u,
                "fy": [u[2], terms[half, 1 + k, 2], terms[half, 1 + k, 1]],
                "sy": terms[half, 1 + k, 0],
            }
            for half, u in enumerate(load(view, k))
        ]

    def trip(i, acc):
        view = state.at[:, :, pl.ds(i * group, 1 + group)]
        y_terms_of(view, -1)
        for k in range(group):
            terms_of(view, k)
        for k in range(group):
            x_faces(view, k)
        prev = y_cells(view, -1)
        for k in range(group):
            cur = y_cells(view, k)
            face = [y_face(a, b) for a, b in zip(prev, cur)]
            if k == 0:
                for half in range(2):
                    for f in range(3):
                        opening[i, half, f] = pltpu.roll(face[half][f], SUB - 1, 0)
            store(view, k - 1, [[x + g for x, g in zip(*pair)] for pair in zip(acc, face)])
            acc = [[parts[k, 3 * half + f] - face[half][f] for f in range(3)] for half in range(2)]
            prev = cur
        return acc

    def step(_, carry):
        acc = lax.fori_loop(0, rows // group, trip, [[zero] * 3 for _ in range(2)])
        tails = [
            [
                x + jnp.where(bottom, -2.0 * f, opening[0, half, i])
                for i, (x, f) in enumerate(zip(xs, cell["fy"]))
            ]
            for half, (xs, cell) in enumerate(
                zip(acc, y_cells(state.at[:, :, rows - group :], group - 1))
            )
        ]
        store(state, rows - 1, tails)
        store_above(tails)
        return carry

    store_above(load(state, rows - 1))
    lax.fori_loop(0, steps, step, 0)


GROUP = 16
UNITS = (DEPTH_UNIT, FLOW_UNIT, FLOW_UNIT)
VMEM_LIMIT = 12 * 1024 * 1024
HALF = LANES // 2


def pick(values, ids):
    return jnp.take_along_axis(values, ids, axis=1, mode="promise_in_bounds")


def split_columns(west, east):
    lane = lane_ids()
    low = lane < HALF
    twice = 2 * jnp.where(low, lane, lane - HALF)
    w = pick(west, jnp.where(low, twice, twice + 1))
    e = pick(east, jnp.where(low, twice + 1, twice))
    return jnp.where(low, w, e), pltpu.roll(jnp.where(low, e, w), HALF, 1)


def join_columns(even, odd):
    lane = lane_ids()
    low = lane < HALF
    odd = pltpu.roll(odd, HALF, 1)
    w, e = jnp.where(low, even, odd), jnp.where(low, odd, even)
    half, is_odd = lane // 2, lane % 2
    return pick(w, half + HALF * is_odd), pick(e, half + HALF * (1 - is_odd))


HALVES = (slice(0, LANES), slice(LANES, 2 * LANES))
TALL = 32


def fold_kernel(link, depth, flow, state, wet, tmp):
    rows = depth.shape[0] // SUB
    wet[...] = jnp.broadcast_to(link[:, 2:3], wet.shape).astype(jnp.float32)

    def copy_in(i, carry):
        at = pl.ds(pl.multiple_of(i * TALL, TALL), TALL)
        for f in range(3):
            raw = depth[at] if f == 0 else flow[f - 1, at]
            for p in range(2):
                tmp[f, p, at] = raw[:, HALVES[p]] * UNITS[f]
        return carry

    def fold_field(f, carry):
        def fold(k, carry):
            both = split_columns(*[tmp[f, p, pl.ds(k, SUB, stride=rows), :] for p in range(2)])
            for p in range(2):
                state[f, p, k] = both[p]
            return carry

        return lax.fori_loop(0, rows, fold, carry, unroll=rows)

    lax.fori_loop(0, depth.shape[0] // TALL, copy_in, 0)
    lax.fori_loop(0, 3, fold_field, 0)


def coast_fold(link, depth, flow):
    cells = depth.shape[0]
    vmem = pl.BlockSpec(memory_space=pltpu.VMEM)
    return pl.pallas_call(
        fold_kernel,
        out_shape=(
            jax.ShapeDtypeStruct((3, 2, cells // SUB, SUB, LANES), jnp.float32),
            jax.ShapeDtypeStruct((SUB, LANES), jnp.float32),
        ),
        in_specs=[vmem, vmem, vmem],
        out_specs=(vmem, vmem),
        scratch_shapes=[pltpu.VMEM((3, 2, cells, LANES), jnp.float32)],
        compiler_params=pltpu.CompilerParams(vmem_limit_bytes=VMEM_LIMIT),
        cost_estimate=pl.CostEstimate(
            flops=CSTEPS * 70 * cells * cells, bytes_accessed=24 * cells * cells, transcendentals=0
        ),
        name="coast_fold",
    )(link, depth, flow)


def coast_kernel(
    wet, ghosts, folded, depth, flow, out, state, terms, after, parts, opening, tmp, done, sems
):
    rows = depth.shape[0] // SUB
    is_wet = jnp.max(wet[...]) > 0.0

    def copy_in(k, carry):
        for f in range(3):
            for p in range(2):
                state[f, p, 1 + k] = folded[f, p, k]
        return carry

    @pl.when(jnp.logical_not(is_wet))
    def _():
        copies = [
            pltpu.make_async_copy(depth, out.at[0], sems.at[0]),
            pltpu.make_async_copy(flow, out.at[1:], sems.at[1]),
        ]
        for copy in copies:
            copy.start()
        for copy in copies:
            copy.wait()

    @pl.when(is_wet)
    def _():
        lax.fori_loop(0, rows, copy_in, 0, unroll=8)
        values = jnp.sum(ghosts[...], axis=0)
        level = (ghost_level + values) * DEPTH_UNIT
        inflow = values * FLOW_UNIT
        h, mv = [
            [jnp.broadcast_to(v[i : i + 1], (SUB, LANES)) for i in range(at, at + 2)]
            for v, at in ((level, 0), (inflow, 2))
        ]
        ghost = [[h[p], jnp.zeros_like(h[p]), mv[p]] for p in range(2)]
        coast_steps(state, terms, after, parts, opening, rows, GROUP, CSTEPS, ghost)

        def write(f):
            return pltpu.make_async_copy(done.at[f], out.at[f], sems.at[f])

        def finish(f, carry):
            scale = jnp.where(f == 0, 1.0 / DEPTH_UNIT, 1.0 / FLOW_UNIT)

            def unfold(k, carry):
                both = join_columns(state[f, 0, 1 + k], state[f, 1, 1 + k])
                for p in range(2):
                    tmp[p, pl.ds(k, SUB, stride=rows), :] = both[p] * scale
                return carry

            def copy_out(i, carry):
                at = pl.ds(pl.multiple_of(i * TALL, TALL), TALL)
                for p in range(2):
                    done[f, at, HALVES[p]] = tmp[p, at]
                return carry

            lax.fori_loop(0, rows, unfold, 0, unroll=rows)
            lax.fori_loop(0, depth.shape[0] // TALL, copy_out, 0, unroll=8)
            write(f).start()
            return carry

        lax.fori_loop(0, 3, finish, 0)
        for f in range(3):
            write(f).wait()


def coast_run(wet, ghosts, folded, depth, flow):
    cells = depth.shape[0]
    vmem = pl.BlockSpec(memory_space=pltpu.VMEM)
    return pl.pallas_call(
        coast_kernel,
        out_shape=jax.ShapeDtypeStruct((3, cells, cells), jnp.float32),
        in_specs=[vmem] * 5,
        out_specs=pl.BlockSpec(memory_space=pltpu.HBM),
        scratch_shapes=[
            pltpu.VMEM((3, 2, 1 + cells // SUB, SUB, LANES), jnp.float32),
            pltpu.VMEM((2, 1 + GROUP, 5, SUB, LANES), jnp.float32),
            pltpu.VMEM((GROUP, 6, SUB, LANES), jnp.float32),
            pltpu.VMEM((GROUP, 6, SUB, LANES), jnp.float32),
            pltpu.VMEM((cells // SUB // GROUP, 2, 3, SUB, LANES), jnp.float32),
            pltpu.VMEM((2, cells, LANES), jnp.float32),
            pltpu.VMEM((3, cells, cells), jnp.float32),
            pltpu.SemaphoreType.DMA((3,)),
        ],
        compiler_params=pltpu.CompilerParams(vmem_limit_bytes=VMEM_LIMIT),
        cost_estimate=pl.CostEstimate(
            flops=CSTEPS * 70 * cells * cells, bytes_accessed=24 * cells * cells, transcendentals=0
        ),
        name="coast_steps",
    )(wet, ghosts, folded, depth, flow)


def basin_kernel(state, depth, pair_state, pair_depth, edge, out, eta, hu, hv, dep):
    rows, width = depth.shape
    total = rows + 2 * HALO
    chunks = width // LANES
    position = lax.axis_index("row")
    odd = position % 2
    north_inside = (position < lax.axis_size("row") - 1).astype(jnp.float32)
    pair_from = pl.multiple_of(odd * (rows - HALO), HALO)
    pair_at = pl.multiple_of((1 - odd) * (HALO + rows), HALO)
    edge_at = pl.multiple_of(odd * (HALO + rows), HALO)
    for ref, field, unit in ((eta, 0, 1.0), (hu, 1, 0.5), (hv, 2, 0.5), (dep, 3, 0.25)):
        own, pair = (depth, pair_depth) if field == 3 else (state.at[field], pair_state.at[field])
        for c in range(chunks):
            at = slice(c * LANES, (c + 1) * LANES)
            ref[c, HALO : HALO + rows] = own[:, at] * unit
            ref[c, pl.ds(pair_at, HALO)] = pair[pl.ds(pair_from, HALO), at] * unit
            ref[c, pl.ds(edge_at, HALO)] = edge[field, :, at] * unit
    apart = total // SUB
    lane = lane_ids()
    first, last = lane == 0, lane == LANES - 1
    kept = jnp.where(row_ids() * apart < HALO + rows, 1.0, north_inside)
    zero = jnp.zeros((SUB, LANES), jnp.float32)

    def load(ref, c):
        return [ref[c, pl.ds(k, SUB, stride=apart), :] for k in range(apart)]

    def store(ref, c, values):
        for k in range(apart):
            ref[c, pl.ds(k, SUB, stride=apart), :] = values[k]

    def step(_, carry):
        prev_west = [zero] * apart
        prev_eta, prev_east, prev_hu = None, None, None
        for c in range(chunks + 1):
            if c < chunks:
                u, v, d = load(hu, c), load(hv, c), load(dep, c)
                west = [pltpu.roll(x, 1, 1) for x in u]
                south = [pltpu.roll(v[-1], 1, 0)] + v[:-1]
                new = [
                    (e - ((x - jnp.where(first, p, w)) + (y - t))) * kept
                    for e, x, p, w, y, t in zip(load(eta, c), u, prev_west, west, v, south)
                ]
                store(eta, c, new)
                east = [pltpu.roll(x, LANES - 1, 1) for x in new]
                north = new[1:] + [pltpu.roll(new[0], SUB - 1, 0)]
                store(hv, c, [y - g * (n - x) for y, g, n, x in zip(v, d, north, new)])
            else:
                east = [zero] * apart
            if c > 0:
                d = load(dep, c - 1)
                store(
                    hu,
                    c - 1,
                    [
                        x - g * (jnp.where(last, e, p) - n)
                        for x, g, e, p, n in zip(prev_hu, d, east, prev_east, prev_eta)
                    ],
                )
            prev_west, prev_eta, prev_east, prev_hu = west, new, east, u
        return carry

    lax.fori_loop(0, BSTEPS, step, 0)
    for c in range(chunks):
        at = slice(c * LANES, (c + 1) * LANES)
        for f, (ref, unit) in enumerate(((eta, 1.0), (hu, 2.0), (hv, 2.0))):
            out[f, :, at] = ref[c, HALO : HALO + rows] * unit


def basin_run(state, depth, pair_state, pair_depth, edge):
    rows, width = depth.shape
    total = rows + 2 * HALO
    vmem = pl.BlockSpec(memory_space=pltpu.VMEM)
    return pl.pallas_call(
        basin_kernel,
        out_shape=jax.ShapeDtypeStruct((3, rows, width), jnp.float32),
        in_specs=[vmem] * 5,
        out_specs=vmem,
        scratch_shapes=[pltpu.VMEM((width // LANES, total, LANES), jnp.float32)] * 4,
        compiler_params=pltpu.CompilerParams(vmem_limit_bytes=VMEM_LIMIT),
        cost_estimate=pl.CostEstimate(
            flops=BSTEPS * 16 * total * width, bytes_accessed=4 * 11 * rows * width, transcendentals=0
        ),
        name="basin_steps",
    )(state, depth, pair_state, pair_depth, edge)


def strips_kernel(links, own, pair, ghosts, strips):
    rows, width = own.shape[1], own.shape[2]
    count = ghosts.shape[0]
    span = 2 * LANES
    position = lax.axis_index("row")
    tops = (position * rows, (position + 1 - 2 * (position % 2)) * rows)
    lane = lane_ids()
    weight = ((2 * lane + row_ids() % 2) % 16).astype(jnp.float32) / 16.0 + 0.5 / 16.0

    def piece(b, carry):
        col = links[b, 0, 1]
        start = jnp.clip(col // LANES, 0, width // LANES - 2) * LANES
        shift = lax.rem(span - (col - start), span)
        at = pl.ds(pl.multiple_of(start, LANES), span)
        for i, f in enumerate((0, 2)):
            chunk = None
            for source, top in zip((own, pair), tops):
                row = links[b, 0, 0] - top
                owned = jnp.logical_and(row >= 0, row < rows).astype(jnp.float32)
                part = source[f, pl.ds(jnp.clip(row, 0, rows - 1), 1), at] * owned
                chunk = part if chunk is None else chunk + part
            moved = pltpu.roll(chunk, shift, 1)[:, :LANES]
            strips[b, 2 * i : 2 * i + 2] = jnp.broadcast_to(moved, (2, LANES))
        values = strips[b]
        low, high = pick(values, lane // 8), pick(values, lane // 8 + 1)
        ghosts[b] = (1.0 - weight) * low + weight * high
        return carry

    strips[...] = jnp.zeros_like(strips)
    lax.fori_loop(0, count, piece, 0, unroll=8)


def make_strips(links, own, pair):
    count = links.shape[0]
    tiles = (count, SUB, LANES)
    vmem = pl.BlockSpec(memory_space=pltpu.VMEM)
    smem = pl.BlockSpec(memory_space=pltpu.SMEM)
    return pl.pallas_call(
        strips_kernel,
        out_shape=jax.ShapeDtypeStruct(tiles, jnp.float32),
        in_specs=[smem, vmem, vmem],
        out_specs=vmem,
        scratch_shapes=[pltpu.VMEM(tiles, jnp.float32)],
        compiler_params=pltpu.CompilerParams(vmem_limit_bytes=VMEM_LIMIT),
        cost_estimate=pl.CostEstimate(flops=2 * 10**10, bytes_accessed=own.size, transcendentals=0),
        name="strips",
    )(links, own, pair)


def local(basin_state, basin_depth, coast_depth, coast_flow, coast_link):
    devices = lax.axis_size("row")
    odd = lax.axis_index("row") % 2
    chips = list(range(devices // 2))[::-1]
    chips.insert(0, chips.pop(len(chips) - 1 - devices // 4))
    parity = [[2 * chip + p for chip in chips] for p in range(2)]
    sent = jnp.broadcast_to(coast_link, (devices // 2,) + coast_link.shape)
    start = odd * (basin_depth.shape[0] - HALO)
    edge = jnp.concatenate(
        [
            lax.dynamic_slice_in_dim(basin_state, start, HALO, axis=1),
            lax.dynamic_slice_in_dim(basin_depth, start, HALO, axis=0)[None],
        ],
        axis=0,
    )
    links = lax.all_to_all(sent, "row", 0, 0, axis_index_groups=parity, tiled=True)

    twins = [(i, i ^ 1) for i in range(devices)]
    pair_state, pair_depth = [lax.ppermute(a, "row", twins) for a in (basin_state, basin_depth)]
    across = [(i, i + 1) for i in range(1, devices - 1, 2)]
    edge = lax.ppermute(edge, "row", across + [(j, i) for i, j in across])

    ghosts = make_strips(links, basin_state, pair_state)
    basin_depth, coast_depth, ghosts = lax.optimization_barrier((basin_depth, coast_depth, ghosts))
    ghosts = lax.all_to_all(ghosts, "row", 0, 0, axis_index_groups=parity, tiled=True)
    depth, flow = coast_depth[0], coast_flow[0]
    folded, wet = coast_fold(coast_link, depth, flow)
    basin_depth, folded = lax.optimization_barrier((basin_depth, folded))
    basin_out = basin_run(basin_state, basin_depth, pair_state, pair_depth, edge)
    folded, basin_out = lax.optimization_barrier((folded, basin_out))
    coast_out = coast_run(wet, ghosts, folded, depth, flow)
    return (basin_out, coast_out[None])


def solution(mesh):
    in_specs = (
        P("scen", "row", None),
        P("row", "scen"),
        P("row", "scen", None),
        P("row", "scen", None, None),
        P("row", "scen"),
    )
    out_specs = (P("scen", "row", None), P("row", "scen", None, None))
    return jax.shard_map(local, mesh=mesh, in_specs=in_specs, out_specs=out_specs, check_vma=False)
```
